32 devices in a mesh: seq: 2 (over x), pipe: 4 (over y, core), dp: 4 (over z).
Axes of the slice: x: 2, y: 2, z: 4, core: 2. Of those that a mesh axis runs over, the one named last changes fastest.
Arguments:
- segment_input: bfloat16 [4, 512, 3072], P('pipe', ('dp', 'seq')), parts along dimension 1
- output_grad: bfloat16 [4, 512, 3072], P('pipe', ('dp', 'seq')), parts along dimension 1, may hold values from -6 to 6
- qkv_weight: bfloat16 [4, 3072, 16, 384], P('pipe', None, 'seq')
- out_weight: bfloat16 [4, 2048, 3072], P('pipe', 'seq'), may hold values from -0.125 to 0.125
- query_gain: float32 [4, 128], P('pipe')
- key_gain: float32 [4, 128], P('pipe')
- gate_scale: float32 [4, 3072], P('pipe'), may hold values from -4 to 4
- neighbours: int32 [8, 27], P('dp'), parts along dimension 0, may hold values from -1 to 1, as said below
- tile_slot: int32 [8], P('dp'), parts along dimension 0, may hold values from 0 to 1, as said below
Outputs:
- segment_output: bfloat16 [4, 512, 3072], P('pipe', ('dp', 'seq')), parts along dimension 1
- input_grad: bfloat16 [4, 512, 3072], P('pipe', ('dp', 'seq')), parts along dimension 1
- gate_grad: float32 [16, 3072], P(('dp', 'pipe'), 'seq'), parts along dimension 0
The draws below stay inside these ranges and needn't reach their ends.
There are 4 independent parts, one for each index of `dp`. The reference program is written for one: setup_inputs(seed, part) draws one part's arguments, and reference() takes and returns one part's arrays. A program takes and returns all parts, laid end to end along the dimension named above; an argument that names none is the same for every part. Nothing has to cross between parts.
Inputs may be any that keep to these rules, and one draw needn't show every extreme that they name: `neighbours`: row t lists tile t and every tile whose position in the clip's 3-D grid of tiles differs from t's by at most one along each of the three dimensions, one fixed place for each of the 27 offsets, with -1 where an offset leaves the grid; if u lists t then t lists u. `tile_slot`: A permutation of 0 to 1.
All inputs are finite; a program needn't handle non-finite values.
Results may differ from the reference program's by a relative error of at most 0.02.
Values may be sent and summed in bfloat16 or wider, within the bound.
No kernel may reach another device: no remote copies, remote signals or barrier semaphores. Data moves between devices by JAX's collectives and lax.ppermute only.
A program may use at most 128 MiB of HBM per device.

```python
import math
import jax
import jax.numpy as jnp
from jax import lax

D = 3072
HD = 128
HEADS = 16
TILE = 64
NB = 27
SECTIONS = 4
HEAD_DEV = 8
TILES = 2
TOKENS = 128
N_SEQ = 2


def grid_shape(tile_count):
    shape_dims = [1, 1, 1]
    remaining = tile_count
    factor = 2
    while remaining > 1:
        if remaining % factor == 0:
            shape_dims.sort()
            shape_dims[0] = shape_dims[0] * factor
            remaining = remaining // factor
        else:
            factor = factor + 1
    shape_dims.sort()
    return shape_dims


def tile_layout(key):
    relabel = jax.random.permutation(jax.random.fold_in(key, 11), TILES).astype(jnp.int32)
    grid_dims = grid_shape(TILES)
    depth = grid_dims[0]
    height = grid_dims[1]
    breadth = grid_dims[2]
    raster = jnp.arange(TILES, dtype=jnp.int32)
    along_depth = raster // (height * breadth)
    along_height = raster // breadth % height
    along_breadth = raster % breadth
    columns = []
    for step_depth in (-1, 0, 1):
        for step_height in (-1, 0, 1):
            for step_breadth in (-1, 0, 1):
                moved_depth = along_depth + step_depth
                moved_height = along_height + step_height
                moved_breadth = along_breadth + step_breadth
                inside = (moved_depth >= 0) & (moved_depth < depth) & (moved_height >= 0) & (moved_height < height) & (moved_breadth >= 0) & (moved_breadth < breadth)
                target = jnp.clip(moved_depth * height * breadth + moved_height * breadth + moved_breadth, 0, TILES - 1)
                columns.append(jnp.where(inside, relabel[target], -1))
    listed_rows = jnp.stack(columns, axis=1).astype(jnp.int32)
    neighbour_table = jnp.zeros((TILES, NB), jnp.int32).at[relabel].set(listed_rows)
    slot_table = jnp.zeros((TILES,), jnp.int32).at[relabel].set(raster)
    return (neighbour_table, slot_table)


def draw_neighbours(key, part):
    return tile_layout(key)[0]


def draw_tile_slot(key, part):
    return tile_layout(key)[1]


def draw_segment_input(key, part):
    base_key = jax.random.fold_in(key, 1)
    noise_key = jax.random.fold_in(base_key, 21)
    row_key = jax.random.fold_in(base_key, 22)
    column_key = jax.random.fold_in(base_key, 23)
    full_shape = (SECTIONS, TOKENS, D)
    row_scale = jnp.exp(jax.random.uniform(row_key, (SECTIONS, TOKENS, 1), jnp.float32, math.log(0.3), math.log(3.0)))
    column_scale = jnp.exp(jax.random.uniform(column_key, (1, 1, D), jnp.float32, math.log(0.3), math.log(3.0)))
    values = jax.random.normal(noise_key, full_shape, jnp.float32) * row_scale * column_scale
    return jnp.clip(values, -32.0, 32.0).astype(jnp.bfloat16)


def draw_qkv_weight(key, part):
    base_key = jax.random.fold_in(key, 31)
    part_shape = (SECTIONS, D, HEADS, HD)
    spread = 1.0 / math.sqrt(D)
    value_part = jnp.clip(jax.random.normal(jax.random.fold_in(base_key, 3), part_shape, jnp.float32), -4.0, 4.0) * spread
    query_noise = jnp.clip(jax.random.normal(jax.random.fold_in(base_key, 1), part_shape, jnp.float32), -4.0, 4.0) * spread
    query_part = query_noise
    key_part = jnp.clip(jax.random.normal(jax.random.fold_in(base_key, 2), part_shape, jnp.float32), -4.0, 4.0) * spread
    return jnp.concatenate([query_part, key_part, value_part], axis=-1).astype(jnp.bfloat16)


def gain_pair(key):
    base_key = jax.random.fold_in(key, 5)
    first = jnp.clip(jax.random.normal(jax.random.fold_in(base_key, 1), (SECTIONS, HD), jnp.float32), -3.5, 3.5)
    second = jnp.clip(jax.random.normal(jax.random.fold_in(base_key, 2), (SECTIONS, HD), jnp.float32), -3.5, 3.5)
    return (first, second)


def draw_query_gain(key, part):
    return gain_pair(key)[0]


def draw_key_gain(key, part):
    return gain_pair(key)[1]


def block_scale(rng, shape, pieces, least, high):
    def one(dim, blocks):
        draws = jax.random.uniform(jax.random.fold_in(jax.random.fold_in(rng, 6), dim), (blocks,), jnp.float32, least / len(pieces), high / len(pieces))
        return jnp.repeat(jnp.exp(draws), shape[dim] // blocks).reshape((-1,) + (1,) * (len(shape) - dim - 1))

    level = one(*pieces[0])
    for cut in pieces[1:]:
        level = level * one(*cut)
    return level


def scatter_about(own_key, shape, scale, reach, pieces=(), held_as=jnp.bfloat16):
    entries = scale * jax.random.normal(own_key, shape, jnp.float32)
    if pieces:
        entries = entries * block_scale(own_key, shape, pieces, -0.22, 0.18)
    return jnp.clip(entries, -reach, reach).astype(held_as)


def setup_inputs(seed: int = 0, part: int = 0) -> dict:
    splits = jax.random.split(jax.random.key(seed), 10)
    part_splits = jax.random.split(jax.random.fold_in(splits[9], part), 10)
    return {
        "segment_input": draw_segment_input(jax.random.fold_in(jax.random.fold_in(splits[9], part), 71), part),
        "output_grad": scatter_about(part_splits[1], (SECTIONS, TOKENS, D), 1.0, 6.0, ((0, 4), (1, 2))),
        "qkv_weight": draw_qkv_weight(jax.random.fold_in(splits[9], 71), part),
        "out_weight": scatter_about(splits[3], (SECTIONS, HEADS * HD, D), (HEADS * HD) ** -0.5, 0.125, ((0, 4), (1, 2))),
        "query_gain": draw_query_gain(jax.random.fold_in(splits[9], 71), part),
        "key_gain": draw_key_gain(jax.random.fold_in(splits[9], 71), part),
        "gate_scale": scatter_about(splits[6], (SECTIONS, D), 1.0, 4.0, ((0, 4),), jnp.float32),
        "neighbours": draw_neighbours(jax.random.fold_in(jax.random.fold_in(splits[9], part), 71), part),
        "tile_slot": draw_tile_slot(jax.random.fold_in(jax.random.fold_in(splits[9], part), 71), part),
    }


EPSILON = 1e-06

def slot_lists(neighbours, tile_slot):
    tile_count = tile_slot.shape[0]
    numbering = jnp.arange(tile_count, dtype=jnp.int32)
    tile_of_slot = jnp.zeros((tile_count,), jnp.int32).at[tile_slot].set(numbering)
    listed_tiles = neighbours[tile_of_slot]
    key_valid = listed_tiles >= 0
    key_slots = jnp.where(key_valid, tile_slot[jnp.maximum(listed_tiles, 0)], 0).astype(jnp.int32)
    return (key_slots, key_valid)

def unit_norm(values):
    spread = jnp.sqrt(lax.optimization_barrier(jnp.mean(values * values, axis=-1, keepdims=True)) + EPSILON)
    return (values / spread, spread)

def block_tiles():
    return math.gcd(TILES, max(1, 512 // TILE))

def probabilities(query_block, key_rows, block_valid):
    scores = jnp.einsum('aihd,ajhd->ahij', query_block.astype(jnp.float32), key_rows.astype(jnp.float32)) * (1.0 / math.sqrt(HD))
    key_mask = jnp.repeat(block_valid, TILE, axis=1)
    scores = jnp.where(key_mask[:, None, None, :], scores, -jnp.inf)
    row_max = lax.optimization_barrier(jnp.max(scores, axis=-1, keepdims=True))
    weights = jnp.exp(scores - row_max)
    return (weights / lax.optimization_barrier(jnp.sum(weights, axis=-1, keepdims=True))).astype(jnp.bfloat16)

def gathered(tiles_array, block_slots):
    return tiles_array[block_slots].reshape(block_slots.shape[0], NB * TILE, HEADS, HD)

def attend_both(queries, keys_normed, value_rows_all, attended_grad, key_slots, key_valid):
    query_tiles = queries.reshape(TILES, TILE, HEADS, HD)
    key_tiles = keys_normed.reshape(TILES, TILE, HEADS, HD)
    value_tiles = value_rows_all.reshape(TILES, TILE, HEADS, HD)
    grad_tiles = attended_grad.reshape(TILES, TILE, HEADS, HD)
    span = block_tiles()
    scale_factor = 1.0 / math.sqrt(HD)
    empty_grad = jnp.zeros((TILES, TILE, HEADS, HD), jnp.float32)

    def per_block(accumulators, block_index):
        key_total, value_total = accumulators
        first_tile = block_index * span
        query_block = lax.dynamic_slice_in_dim(query_tiles, first_tile, span, 0)
        grad_block = lax.dynamic_slice_in_dim(grad_tiles, first_tile, span, 0).astype(jnp.float32)
        block_slots = lax.dynamic_slice_in_dim(key_slots, first_tile, span, 0)
        block_valid = lax.dynamic_slice_in_dim(key_valid, first_tile, span, 0)
        key_rows = gathered(key_tiles, block_slots).astype(jnp.float32)
        value_rows = gathered(value_tiles, block_slots).astype(jnp.float32)
        weights_wide = probabilities(query_block, key_rows, block_valid).astype(jnp.float32)
        attended = jnp.einsum('ahij,ajhd->aihd', weights_wide, value_rows)
        value_part = jnp.einsum('ahij,aihd->ajhd', weights_wide, grad_block)
        prob_grad = jnp.einsum('aihd,ajhd->ahij', grad_block, value_rows)
        row_delta = lax.optimization_barrier(jnp.sum(weights_wide * prob_grad, axis=-1, keepdims=True))
        score_grad = (weights_wide * (prob_grad - row_delta) * scale_factor).astype(jnp.bfloat16)
        score_wide = score_grad.astype(jnp.float32)
        query_part = jnp.einsum('ahij,ajhd->aihd', score_wide, key_rows)
        key_part = jnp.einsum('ahij,aihd->ajhd', score_wide, query_block.astype(jnp.float32))
        block_shape = (span, NB, TILE, HEADS, HD)
        key_total = key_total.at[block_slots].add(key_part.reshape(block_shape))
        value_total = value_total.at[block_slots].add(value_part.reshape(block_shape))
        return ((key_total, value_total), (attended, query_part))
    totals, parts = lax.scan(per_block, (empty_grad, empty_grad), jnp.arange(TILES // span, dtype=jnp.int32))
    flat_shape = (TOKENS, HEADS, HD)
    return (parts[0].reshape(flat_shape), parts[1].reshape(flat_shape), totals[0].reshape(flat_shape), totals[1].reshape(flat_shape))

def section(stream, upstream, weight_in, weight_out, query_weights, key_weights, gate_weights, key_slots, key_valid):
    weight_flat = weight_in.reshape(D, HEADS * 3 * HD)
    projected = jnp.dot(stream, weight_flat, preferred_element_type=jnp.float32).reshape(TOKENS, HEADS, 3, HD)
    query_unit, query_spread = unit_norm(projected[:, :, 0])
    key_unit, key_spread = unit_norm(projected[:, :, 1])
    queries = (query_unit * query_weights).astype(jnp.bfloat16)
    keys_normed = (key_unit * key_weights).astype(jnp.bfloat16)
    value_rows = projected[:, :, 2].astype(jnp.bfloat16)
    scaled = (upstream.astype(jnp.float32) * gate_weights).astype(jnp.bfloat16)
    attended_grad = jnp.dot(scaled, weight_out.T, preferred_element_type=jnp.float32).astype(jnp.bfloat16)
    attended, query_grad, key_grad, value_grad = attend_both(queries, keys_normed, value_rows, attended_grad, key_slots, key_valid)
    attended_low = attended.astype(jnp.bfloat16).reshape(TOKENS, HEADS * HD)
    attention_out = jnp.dot(attended_low, weight_out, preferred_element_type=jnp.float32)
    forward = (stream.astype(jnp.float32) + gate_weights * attention_out).astype(jnp.bfloat16)
    gate_part = lax.optimization_barrier(jnp.sum(upstream.astype(jnp.float32) * attention_out, axis=0))
    query_scaled = query_grad * query_weights
    query_part_grad = (query_scaled - query_unit * lax.optimization_barrier(jnp.mean(query_scaled * query_unit, axis=-1, keepdims=True))) / query_spread
    key_scaled = key_grad * key_weights
    key_part_grad = (key_scaled - key_unit * lax.optimization_barrier(jnp.mean(key_scaled * key_unit, axis=-1, keepdims=True))) / key_spread
    projected_grad = jnp.stack([query_part_grad, key_part_grad, value_grad], axis=2).astype(jnp.bfloat16)
    grouped_grad = projected_grad.reshape(TOKENS, N_SEQ, HEAD_DEV * 3 * HD).astype(jnp.float32)
    grouped_weight = weight_flat.reshape(D, N_SEQ, HEAD_DEV * 3 * HD).astype(jnp.float32)
    group_terms = jnp.einsum('tgc,dgc->gtd', grouped_grad, grouped_weight).astype(jnp.bfloat16)
    stream_grad = lax.optimization_barrier(jnp.sum(group_terms.astype(jnp.float32), axis=0))
    backward = (upstream.astype(jnp.float32) + stream_grad).astype(jnp.bfloat16)
    return (forward, backward, gate_part)

def reference(segment_input, output_grad, qkv_weight, out_weight, query_gain, key_gain, gate_scale, neighbours, tile_slot):
    key_slots, key_valid = slot_lists(neighbours, tile_slot)
    forward_parts = []
    gradient_parts = []
    gate_parts = []
    for index in range(SECTIONS):
        result = section(segment_input[index], output_grad[index], qkv_weight[index], out_weight[index], query_gain[index], key_gain[index], gate_scale[index], key_slots, key_valid)
        forward_parts.append(result[0])
        gradient_parts.append(result[1])
        gate_parts.append(result[2])
    segment_output = jnp.roll(jnp.stack(forward_parts), 1, axis=0)
    input_grad = jnp.roll(jnp.stack(gradient_parts), -1, axis=0)
    gate_grad = jnp.stack(gate_parts)
    return (segment_output, input_grad, gate_grad)
```

```python
import functools
import math

import jax
import jax.numpy as jnp
from jax import lax
from jax.experimental import pallas as pl
from jax.experimental.pallas import tpu as pltpu
from jax.sharding import PartitionSpec as P

TILE = 64
EPSILON = 1e-06
F32 = jnp.float32
BF16 = jnp.bfloat16
VMEM_LIMIT = 44 * 1024 * 1024


def passed_along(block, axis, distance):
    devices = range(lax.axis_size(axis))
    route = [((i - distance) % len(devices), i) for i in devices]
    return lax.ppermute(block, axis, route)


def slot_lists(neighbours, tile_slot):
    tile_count = tile_slot.shape[0]
    numbering = jnp.arange(tile_count, dtype=jnp.int32)
    placed = (tile_slot[:, None] == numbering[None, :]).astype(jnp.int32)
    tile_of_slot = jnp.sum(placed * numbering[:, None], axis=0)
    chosen = (tile_of_slot[:, None] == numbering[None, :]).astype(jnp.int32)
    listed_tiles = jnp.sum(chosen[:, :, None] * neighbours[None, :, :], axis=1)
    key_valid = listed_tiles >= 0
    safe_tiles = jnp.maximum(listed_tiles, 0)
    matches = (safe_tiles[:, :, None] == numbering[None, None, :]).astype(jnp.int32)
    key_slots = jnp.sum(matches * tile_slot[None, None, :], axis=2)
    return (key_slots, key_valid)


def block_tiles(tile_count):
    return math.gcd(tile_count, max(1, 512 // TILE))


def unit_norm(values):
    spread = jnp.sqrt(jnp.mean(values * values, axis=-1, keepdims=True) + EPSILON)
    return (values / spread, spread)


def probabilities(query_block, key_rows, block_valid):
    scores = jnp.einsum(
        "aihd,ajhd->ahij", query_block, key_rows, preferred_element_type=jnp.float32
    ) * (1.0 / math.sqrt(query_block.shape[-1]))
    key_mask = jnp.repeat(block_valid, TILE, axis=1)
    scores = jnp.where(key_mask[:, None, None, :], scores, -jnp.inf)
    row_max = jnp.max(scores, axis=-1, keepdims=True)
    weights = jnp.exp(scores - row_max)
    return (weights / jnp.sum(weights, axis=-1, keepdims=True)).astype(jnp.bfloat16)


def gathered(tiles_array, block_slots):
    picked = tiles_array[block_slots]
    return picked.reshape(block_slots.shape[0], -1, tiles_array.shape[2], tiles_array.shape[3])


def attend_both(query_tiles, key_tiles, value_tiles, grad_tiles, key_slots, key_valid):
    tile_count = query_tiles.shape[0]
    span = block_tiles(tile_count)
    scale_factor = 1.0 / math.sqrt(query_tiles.shape[-1])
    empty_grad = jnp.zeros(query_tiles.shape, jnp.float32)

    def per_block(accumulators, block_index):
        key_total, value_total = accumulators
        first_tile = block_index * span
        query_block = lax.dynamic_slice_in_dim(query_tiles, first_tile, span, 0)
        grad_block = lax.dynamic_slice_in_dim(grad_tiles, first_tile, span, 0)
        block_slots = lax.dynamic_slice_in_dim(key_slots, first_tile, span, 0)
        block_valid = lax.dynamic_slice_in_dim(key_valid, first_tile, span, 0)
        key_rows = gathered(key_tiles, block_slots)
        value_rows = gathered(value_tiles, block_slots)
        weights = probabilities(query_block, key_rows, block_valid)
        attended = jnp.einsum(
            "ahij,ajhd->aihd", weights, value_rows, preferred_element_type=jnp.float32
        )
        value_part = jnp.einsum(
            "ahij,aihd->ajhd", weights, grad_block, preferred_element_type=jnp.float32
        )
        prob_grad = jnp.einsum(
            "aihd,ajhd->ahij", grad_block, value_rows, preferred_element_type=jnp.float32
        )
        weights_wide = weights.astype(jnp.float32)
        row_delta = jnp.sum(weights_wide * prob_grad, axis=-1, keepdims=True)
        score_grad = (weights_wide * (prob_grad - row_delta) * scale_factor).astype(jnp.bfloat16)
        query_part = jnp.einsum(
            "ahij,ajhd->aihd", score_grad, key_rows, preferred_element_type=jnp.float32
        )
        key_part = jnp.einsum(
            "ahij,aihd->ajhd", score_grad, query_block, preferred_element_type=jnp.float32
        )
        block_shape = (span, block_slots.shape[1]) + query_tiles.shape[1:]
        key_total = key_total.at[block_slots].add(key_part.reshape(block_shape))
        value_total = value_total.at[block_slots].add(value_part.reshape(block_shape))
        return ((key_total, value_total), (attended, query_part))

    totals, parts = lax.scan(
        per_block, (empty_grad, empty_grad), jnp.arange(tile_count // span, dtype=jnp.int32)
    )
    flat_shape = (-1,) + query_tiles.shape[2:]
    return (
        parts[0].reshape(flat_shape),
        parts[1].reshape(flat_shape),
        totals[0].reshape(flat_shape),
        totals[1].reshape(flat_shape),
    )


def general_body(
    segment_input,
    output_grad,
    qkv_weight,
    out_weight,
    query_gain,
    key_gain,
    gate_scale,
    neighbours,
    tile_slot,
):
    key_slots, key_valid = slot_lists(neighbours, tile_slot)
    stream = segment_input[0]
    upstream = output_grad[0]
    model_width = stream.shape[1]
    head_dim = query_gain.shape[1]
    local_heads = qkv_weight.shape[2]
    local_width = local_heads * head_dim
    proj_weight = qkv_weight[0].reshape(model_width, local_heads * 3 * head_dim)
    out_local = out_weight[0]
    gate_row = gate_scale[0]
    query_weights = query_gain[0]
    key_weights = key_gain[0]
    projected = jnp.dot(
        lax.all_gather(stream, "seq", axis=0, tiled=True),
        proj_weight,
        preferred_element_type=jnp.float32,
    )
    all_tokens = projected.shape[0]
    projected = projected.reshape(all_tokens, local_heads, 3, head_dim)
    query_unit, query_spread = unit_norm(projected[:, :, 0])
    key_unit, key_spread = unit_norm(projected[:, :, 1])
    queries = (query_unit * query_weights).astype(jnp.bfloat16)
    keys_normed = (key_unit * key_weights).astype(jnp.bfloat16)
    value_rows = projected[:, :, 2].astype(jnp.bfloat16)
    scaled = (upstream.astype(jnp.float32) * gate_row).astype(jnp.bfloat16)
    attended_grad = jnp.einsum(
        "td,cd->tc",
        lax.all_gather(scaled, "seq", axis=0, tiled=True),
        out_local,
        preferred_element_type=jnp.float32,
    ).astype(jnp.bfloat16)

    def as_tiles(values):
        return values.reshape(-1, TILE, local_heads, head_dim)

    attended, query_grad, key_grad, value_grad = attend_both(
        as_tiles(queries),
        as_tiles(keys_normed),
        as_tiles(value_rows),
        as_tiles(attended_grad),
        key_slots,
        key_valid,
    )
    attended_low = attended.astype(jnp.bfloat16).reshape(all_tokens, local_width)
    rows = attended_low
    attention_out = lax.psum_scatter(
        jnp.dot(rows, out_local, preferred_element_type=jnp.float32),
        "seq",
        scatter_dimension=0,
        tiled=True,
    )
    section_out = (stream.astype(jnp.float32) + gate_row * attention_out).astype(jnp.bfloat16)
    segment_output = passed_along(section_out, "pipe", 1)
    gate_local = lax.psum_scatter(
        jnp.sum(upstream.astype(jnp.float32) * attention_out, axis=0),
        "seq",
        scatter_dimension=0,
        tiled=True,
    )
    query_scaled = query_grad * query_weights
    query_part_grad = (
        query_scaled - query_unit * jnp.mean(query_scaled * query_unit, axis=-1, keepdims=True)
    ) / query_spread
    key_scaled = key_grad * key_weights
    key_part_grad = (
        key_scaled - key_unit * jnp.mean(key_scaled * key_unit, axis=-1, keepdims=True)
    ) / key_spread
    projected_grad = (
        jnp.stack([query_part_grad, key_part_grad, value_grad], axis=2)
        .astype(jnp.bfloat16)
        .reshape(all_tokens, local_heads * 3 * head_dim)
    )
    rows = projected_grad
    stream_grad = lax.psum_scatter(
        jnp.einsum("tc,dc->td", rows, proj_weight, preferred_element_type=jnp.float32).astype(
            jnp.bfloat16
        ),
        "seq",
        scatter_dimension=0,
        tiled=True,
    ).astype(jnp.float32)
    token_grad = (upstream.astype(jnp.float32) + stream_grad).astype(jnp.bfloat16)
    input_grad = passed_along(token_grad, "pipe", -1)
    return (segment_output[None], input_grad[None], gate_local[None])


def dot_nn(a, b):
    return lax.dot_general(a, b, (((1,), (0,)), ((), ())), preferred_element_type=F32)


def dot_nt(a, b):
    return lax.dot_general(a, b, (((1,), (1,)), ((), ())), preferred_element_type=F32)


def dot_tn(a, b):
    return lax.dot_general(a, b, (((0,), (0,)), ((), ())), preferred_element_type=F32)


def params(limit=VMEM_LIMIT):
    return pltpu.CompilerParams(vmem_limit_bytes=limit)


def regroup_kernel(weight_ref, out_ref):
    heads = weight_ref.shape[1]
    width = weight_ref.shape[2]
    by_head = jnp.swapaxes(weight_ref[...], 0, 1)
    for head in range(heads):
        left = (head % 2) * width
        out_ref[head // 2, :, left : left + width] = by_head[head]


def regroup(weight, rows):
    depth, heads, width = weight.shape
    pairs = heads // 2
    return pl.pallas_call(
        regroup_kernel,
        grid=(depth // rows,),
        out_shape=jax.ShapeDtypeStruct((pairs, depth, 2 * width), weight.dtype),
        in_specs=[pl.BlockSpec((rows, heads, width), lambda i: (i, 0, 0))],
        out_specs=pl.BlockSpec((pairs, rows, 2 * width), lambda i: (0, i, 0)),
        compiler_params=params(),
        cost_estimate=pl.CostEstimate(
            flops=0, bytes_accessed=4 * depth * heads * width, transcendentals=0
        ),
        name="regroup",
    )(weight)


def listed_slots(neighbours_ref, tile_slot_ref):
    tiles, places = neighbours_ref.shape
    one, zero = jnp.int32(1), jnp.int32(0)
    allowed = [[zero] * tiles for _ in range(tiles)]
    for t in range(tiles):
        for u in range(tiles):
            listed = zero
            for k in range(places):
                listed = jnp.where(neighbours_ref[t, k] == u, one, listed)
            for r in range(tiles):
                for c in range(tiles):
                    here = (tile_slot_ref[t] == r) & (tile_slot_ref[u] == c)
                    allowed[r][c] = jnp.where(here, listed, allowed[r][c])
    return allowed


def forward_kernel(
    neighbours_ref,
    tile_slot_ref,
    own_ref,
    other_ref,
    weight_ref,
    out_weight_ref,
    query_gain_ref,
    key_gain_ref,
    gate_ref,
    projected_ref,
    probs_ref,
    attention_ref,
    kept_ref,
    sent_ref,
    tokens_ref,
    bias_ref,
):
    step = pl.program_id(0)
    local = own_ref.shape[0]
    tokens = 2 * local
    width = query_gain_ref.shape[1]
    heads = probs_ref.shape[0]

    @pl.when(step == 0)
    def _():
        tokens_ref[:local, :] = own_ref[...]
        tokens_ref[local:, :] = other_ref[...]
        allowed = listed_slots(neighbours_ref, tile_slot_ref)
        mine = lax.axis_index("seq")
        row_half = lax.broadcasted_iota(jnp.int32, (tokens, tokens), 0) // local
        column_half = lax.broadcasted_iota(jnp.int32, (tokens, tokens), 1) // local
        row_slot = jnp.where(row_half == 0, mine, 1 - mine)
        column_slot = jnp.where(column_half == 0, mine, 1 - mine)
        table = jnp.zeros((tokens, tokens), jnp.int32)
        for r in range(2):
            for c in range(2):
                table = jnp.where((row_slot == r) & (column_slot == c), allowed[r][c], table)
        bias_ref[...] = jnp.where(table > 0, 0.0, -jnp.inf).astype(F32)

    projected = dot_nn(tokens_ref[...], weight_ref[0])
    projected_ref[0] = projected
    scale_factor = 1.0 / math.sqrt(width)
    bias = bias_ref[...]
    attended = []
    for head in range(heads):
        left = head * 3 * width
        query = projected[:, left : left + width]
        key = projected[:, left + width : left + 2 * width]
        value = projected[:, left + 2 * width : left + 3 * width].astype(BF16)
        query_inverse = lax.rsqrt(jnp.mean(query * query, axis=-1, keepdims=True) + EPSILON)
        key_inverse = lax.rsqrt(jnp.mean(key * key, axis=-1, keepdims=True) + EPSILON)
        queries = (query * query_inverse * query_gain_ref[...]).astype(BF16)
        keys = (key * key_inverse * key_gain_ref[...]).astype(BF16)
        scores = dot_nt(queries, keys) * scale_factor + bias
        row_max = jnp.max(scores, axis=-1, keepdims=True)
        weights = jnp.exp(scores - row_max)
        probs = (weights / jnp.sum(weights, axis=-1, keepdims=True)).astype(BF16)
        probs_ref[head] = probs
        attended.append(dot_nn(probs, value).astype(BF16))
    share = dot_nn(jnp.concatenate(attended, axis=1), out_weight_ref[...])

    @pl.when(step == 0)
    def _():
        attention_ref[...] = share

    @pl.when(step > 0)
    def _():
        attention_ref[...] += share

    @pl.when(step == pl.num_programs(0) - 1)
    def _():
        gate = gate_ref[...]
        kept_ref[...] = (own_ref[...].astype(F32) + gate * attention_ref[:local, :]).astype(BF16)
        sent_ref[...] = (gate * attention_ref[local:, :]).astype(BF16)


def forward(neighbours, tile_slot, own, other, weight, out_weight, query_gain, key_gain, gate):
    local, model = own.shape
    pairs, _, wide = weight.shape
    head_dim = query_gain.shape[1]
    tokens = 2 * local
    whole = lambda i: (0, 0)
    smem = pl.BlockSpec(memory_space=pltpu.SMEM)
    return pl.pallas_call(
        forward_kernel,
        grid=(pairs,),
        out_shape=(
            jax.ShapeDtypeStruct((pairs, tokens, wide), F32),
            jax.ShapeDtypeStruct((2 * pairs, tokens, tokens), BF16),
            jax.ShapeDtypeStruct((tokens, model), F32),
            jax.ShapeDtypeStruct((local, model), BF16),
            jax.ShapeDtypeStruct((local, model), BF16),
        ),
        in_specs=[
            smem,
            smem,
            pl.BlockSpec((local, model), whole),
            pl.BlockSpec((local, model), whole),
            pl.BlockSpec((1, model, wide), lambda i: (i, 0, 0)),
            pl.BlockSpec((2 * head_dim, model), lambda i: (i, 0)),
            pl.BlockSpec((1, head_dim), whole),
            pl.BlockSpec((1, head_dim), whole),
            pl.BlockSpec((1, model), whole),
        ],
        out_specs=(
            pl.BlockSpec((1, tokens, wide), lambda i: (i, 0, 0)),
            pl.BlockSpec((2, tokens, tokens), lambda i: (i, 0, 0)),
            pl.BlockSpec((tokens, model), whole),
            pl.BlockSpec((local, model), whole),
            pl.BlockSpec((local, model), whole),
        ),
        scratch_shapes=[pltpu.VMEM((tokens, model), BF16), pltpu.VMEM((tokens, tokens), F32)],
        compiler_params=params(),
        cost_estimate=pl.CostEstimate(
            flops=2 * tokens * model * pairs * (wide + 2 * head_dim),
            bytes_accessed=2 * model * pairs * (wide + 2 * head_dim),
            transcendentals=0,
        ),
        name="attention_forward",
    )(neighbours, tile_slot, own, other, weight, out_weight, query_gain, key_gain, gate)


def backward_kernel(
    own_ref,
    other_ref,
    out_weight_ref,
    projected_ref,
    probs_ref,
    attention_ref,
    query_gain_ref,
    key_gain_ref,
    gate_ref,
    grad_ref,
    gate_grad_ref,
    scaled_ref,
):
    step = pl.program_id(0)
    local = own_ref.shape[0]
    width = query_gain_ref.shape[1]
    heads = probs_ref.shape[0]
    columns = attention_ref.shape[1]

    @pl.when(step == 0)
    def _():
        gate = gate_ref[...]
        scaled_ref[:local, :] = (own_ref[...].astype(F32) * gate).astype(BF16)
        scaled_ref[local:, :] = (other_ref[...].astype(F32) * gate).astype(BF16)

    part = pl.ds(pl.multiple_of(step * columns, columns), columns)
    gate_grad_ref[...] = jnp.sum(
        own_ref[:, part].astype(F32) * attention_ref[:local, :], axis=0, keepdims=True
    ) + jnp.sum(other_ref[:, part].astype(F32) * attention_ref[local:, :], axis=0, keepdims=True)

    attended_grad = dot_nt(scaled_ref[...], out_weight_ref[...]).astype(BF16)
    scale_factor = 1.0 / math.sqrt(width)
    for head in range(heads):
        left = head * 3 * width
        query = projected_ref[0, :, left : left + width]
        key = projected_ref[0, :, left + width : left + 2 * width]
        value = projected_ref[0, :, left + 2 * width : left + 3 * width].astype(BF16)
        query_inverse = lax.rsqrt(jnp.mean(query * query, axis=-1, keepdims=True) + EPSILON)
        key_inverse = lax.rsqrt(jnp.mean(key * key, axis=-1, keepdims=True) + EPSILON)
        query_unit = query * query_inverse
        key_unit = key * key_inverse
        queries = (query_unit * query_gain_ref[...]).astype(BF16)
        keys = (key_unit * key_gain_ref[...]).astype(BF16)
        grad = attended_grad[:, head * width : (head + 1) * width]
        probs = probs_ref[head]
        probs_wide = probs.astype(F32)
        value_grad = dot_tn(probs, grad)
        prob_grad = dot_nt(grad, value)
        row_delta = jnp.sum(probs_wide * prob_grad, axis=-1, keepdims=True)
        score_grad = (probs_wide * (prob_grad - row_delta) * scale_factor).astype(BF16)
        query_scaled = dot_nn(score_grad, keys) * query_gain_ref[...]
        key_scaled = dot_tn(score_grad, queries) * key_gain_ref[...]
        query_mean = jnp.mean(query_scaled * query_unit, axis=-1, keepdims=True)
        key_mean = jnp.mean(key_scaled * key_unit, axis=-1, keepdims=True)
        grad_ref[0, :, left : left + width] = (
            (query_scaled - query_unit * query_mean) * query_inverse
        ).astype(BF16)
        grad_ref[0, :, left + width : left + 2 * width] = (
            (key_scaled - key_unit * key_mean) * key_inverse
        ).astype(BF16)
        grad_ref[0, :, left + 2 * width : left + 3 * width] = value_grad.astype(BF16)


def backward(own, other, out_weight, projected, probs, attention, query_gain, key_gain, gate):
    local, model = own.shape
    pairs, tokens, wide = projected.shape
    head_dim = query_gain.shape[1]
    whole = lambda i: (0, 0)
    return pl.pallas_call(
        backward_kernel,
        grid=(pairs,),
        out_shape=(
            jax.ShapeDtypeStruct((pairs, tokens, wide), BF16),
            jax.ShapeDtypeStruct((1, model), F32),
        ),
        in_specs=[
            pl.BlockSpec((local, model), whole),
            pl.BlockSpec((local, model), whole),
            pl.BlockSpec((2 * head_dim, model), lambda i: (i, 0)),
            pl.BlockSpec((1, tokens, wide), lambda i: (i, 0, 0)),
            pl.BlockSpec((2, tokens, tokens), lambda i: (i, 0, 0)),
            pl.BlockSpec((tokens, model // pairs), lambda i: (0, i)),
            pl.BlockSpec((1, head_dim), whole),
            pl.BlockSpec((1, head_dim), whole),
            pl.BlockSpec((1, model), whole),
        ],
        out_specs=(
            pl.BlockSpec((1, tokens, wide), lambda i: (i, 0, 0)),
            pl.BlockSpec((1, model // pairs), lambda i: (0, i)),
        ),
        scratch_shapes=[pltpu.VMEM((tokens, model), BF16)],
        compiler_params=params(),
        cost_estimate=pl.CostEstimate(
            flops=2 * tokens * model * pairs * 2 * head_dim,
            bytes_accessed=2 * model * pairs * 2 * head_dim,
            transcendentals=0,
        ),
        name="attention_backward",
    )(own, other, out_weight, projected, probs, attention, query_gain, key_gain, gate)


def input_grad_kernel(grad_ref, weight_ref, own_ref, kept_ref, sent_ref):
    local = own_ref.shape[0]
    total = dot_nt(grad_ref[0], weight_ref[0])
    for pair in range(1, grad_ref.shape[0]):
        total += dot_nt(grad_ref[pair], weight_ref[pair])
    kept_ref[...] = (own_ref[...].astype(F32) + total[:local]).astype(BF16)
    sent_ref[...] = total[local:].astype(BF16)


def input_grad_part(grad, weight, own, part, parts, block):
    local, model = own.shape
    pairs, tokens, wide = grad.shape
    columns = model // parts
    first = part * columns // block
    out = jax.ShapeDtypeStruct((local, columns), BF16)
    out_spec = pl.BlockSpec((local, block), lambda i: (0, i))
    return pl.pallas_call(
        input_grad_kernel,
        grid=(columns // block,),
        out_shape=(out, out),
        in_specs=[
            pl.BlockSpec((pairs, tokens, wide), lambda i: (0, 0, 0)),
            pl.BlockSpec((pairs, block, wide), lambda i: (0, i + first, 0)),
            pl.BlockSpec((local, block), lambda i: (0, i + first)),
        ],
        out_specs=(out_spec, out_spec),
        compiler_params=params(),
        cost_estimate=pl.CostEstimate(
            flops=2 * tokens * columns * pairs * wide,
            bytes_accessed=2 * columns * pairs * wide,
            transcendentals=0,
        ),
        name="input_grad",
    )(grad, weight, own)


def routed(block, seq_step, pipe_step):
    seq_size, pipe_size = lax.axis_size("seq"), lax.axis_size("pipe")
    route = []
    for i in range(seq_size):
        for j in range(pipe_size):
            target = (i + seq_step) % seq_size * pipe_size + (j + pipe_step) % pipe_size
            route.append((i * pipe_size + j, target))
    return lax.ppermute(block, ("seq", "pipe"), route)


def pair_body(
    segment_input,
    output_grad,
    qkv_weight,
    out_weight,
    query_gain,
    key_gain,
    gate_scale,
    neighbours,
    tile_slot,
):
    stream = segment_input[0]
    upstream = output_grad[0]
    out_local = out_weight[0]
    model = stream.shape[1]
    other_stream = routed(stream, 1, 0)
    weight = regroup(qkv_weight[0], 256)
    other_stream, upstream_after = lax.optimization_barrier((other_stream, upstream))
    other_upstream = routed(upstream_after, 1, 0)
    projected, probs, attention, kept, sent = forward(
        neighbours,
        tile_slot,
        stream,
        other_stream,
        weight,
        out_local,
        query_gain,
        key_gain,
        gate_scale,
    )
    kept = routed(kept, 0, 1)
    sent = routed(sent, 1, 1)
    grad, gate_share = backward(
        upstream,
        other_upstream,
        out_local,
        projected,
        probs,
        attention,
        query_gain,
        key_gain,
        gate_scale,
    )
    other_gate = routed(gate_share, 1, 0)
    parts = 2
    pieces = []
    for part in range(parts):
        one, two = input_grad_part(grad, weight, upstream, part, parts, 512)
        pieces.append((routed(one, 0, -1), routed(two, 1, -1)))
    segment_output = (kept.astype(F32) + sent.astype(F32)).astype(BF16)
    input_grad = jnp.concatenate(
        [(a.astype(F32) + b.astype(F32)).astype(BF16) for a, b in pieces], axis=1
    )
    half = model // lax.axis_size("seq")
    gate_total = lax.dynamic_slice_in_dim(
        gate_share + other_gate, lax.axis_index("seq") * half, half, 1
    )
    return (segment_output[None], input_grad[None], gate_total)


def solution(mesh):
    in_specs = (
        P("pipe", ("dp", "seq"), None),
        P("pipe", ("dp", "seq"), None),
        P("pipe", None, "seq", None),
        P("pipe", "seq", None),
        P("pipe", None),
        P("pipe", None),
        P("pipe", None),
        P("dp", None),
        P("dp"),
    )
    out_specs = (
        P("pipe", ("dp", "seq"), None),
        P("pipe", ("dp", "seq"), None),
        P(("dp", "pipe"), "seq"),
    )

    def body(*args):
        one_tile_each = args[0].shape[1] == TILE and args[8].shape[0] == 2
        if mesh.shape["seq"] == 2 and one_tile_each and args[2].shape[2] % 2 == 0:
            return pair_body(*args)
        return general_body(*args)

    return jax.shard_map(body, mesh=mesh, in_specs=in_specs, out_specs=out_specs, check_vma=False)
```

```python
import functools
import math

import jax
import jax.numpy as jnp
from jax import lax
from jax.experimental import pallas as pl
from jax.experimental.pallas import tpu as pltpu
from jax.sharding import PartitionSpec as P

TILE = 64
EPSILON = 1e-06
F32 = jnp.float32
BF16 = jnp.bfloat16
MIB = 1024 * 1024


def passed_along(block, axis, distance):
    devices = range(lax.axis_size(axis))
    route = [((i - distance) % len(devices), i) for i in devices]
    return lax.ppermute(block, axis, route)


def slot_lists(neighbours, tile_slot):
    tile_count = tile_slot.shape[0]
    numbering = jnp.arange(tile_count, dtype=jnp.int32)
    placed = (tile_slot[:, None] == numbering[None, :]).astype(jnp.int32)
    tile_of_slot = jnp.sum(placed * numbering[:, None], axis=0)
    chosen = (tile_of_slot[:, None] == numbering[None, :]).astype(jnp.int32)
    listed_tiles = jnp.sum(chosen[:, :, None] * neighbours[None, :, :], axis=1)
    key_valid = listed_tiles >= 0
    safe_tiles = jnp.maximum(listed_tiles, 0)
    matches = (safe_tiles[:, :, None] == numbering[None, None, :]).astype(jnp.int32)
    key_slots = jnp.sum(matches * tile_slot[None, None, :], axis=2)
    return (key_slots, key_valid)


def block_tiles(tile_count):
    return math.gcd(tile_count, max(1, 512 // TILE))


def unit_norm(values):
    spread = jnp.sqrt(jnp.mean(values * values, axis=-1, keepdims=True) + EPSILON)
    return (values / spread, spread)


def probabilities(query_block, key_rows, block_valid):
    scores = jnp.einsum(
        "aihd,ajhd->ahij", query_block, key_rows, preferred_element_type=jnp.float32
    ) * (1.0 / math.sqrt(query_block.shape[-1]))
    key_mask = jnp.repeat(block_valid, TILE, axis=1)
    scores = jnp.where(key_mask[:, None, None, :], scores, -jnp.inf)
    row_max = jnp.max(scores, axis=-1, keepdims=True)
    weights = jnp.exp(scores - row_max)
    return (weights / jnp.sum(weights, axis=-1, keepdims=True)).astype(jnp.bfloat16)


def gathered(tiles_array, block_slots):
    picked = tiles_array[block_slots]
    return picked.reshape(block_slots.shape[0], -1, tiles_array.shape[2], tiles_array.shape[3])


def attend_both(query_tiles, key_tiles, value_tiles, grad_tiles, key_slots, key_valid):
    tile_count = query_tiles.shape[0]
    span = block_tiles(tile_count)
    scale_factor = 1.0 / math.sqrt(query_tiles.shape[-1])
    empty_grad = jnp.zeros(query_tiles.shape, jnp.float32)

    def per_block(accumulators, block_index):
        key_total, value_total = accumulators
        first_tile = block_index * span
        query_block = lax.dynamic_slice_in_dim(query_tiles, first_tile, span, 0)
        grad_block = lax.dynamic_slice_in_dim(grad_tiles, first_tile, span, 0)
        block_slots = lax.dynamic_slice_in_dim(key_slots, first_tile, span, 0)
        block_valid = lax.dynamic_slice_in_dim(key_valid, first_tile, span, 0)
        key_rows = gathered(key_tiles, block_slots)
        value_rows = gathered(value_tiles, block_slots)
        weights = probabilities(query_block, key_rows, block_valid)
        attended = jnp.einsum(
            "ahij,ajhd->aihd", weights, value_rows, preferred_element_type=jnp.float32
        )
        value_part = jnp.einsum(
            "ahij,aihd->ajhd", weights, grad_block, preferred_element_type=jnp.float32
        )
        prob_grad = jnp.einsum(
            "aihd,ajhd->ahij", grad_block, value_rows, preferred_element_type=jnp.float32
        )
        weights_wide = weights.astype(jnp.float32)
        row_delta = jnp.sum(weights_wide * prob_grad, axis=-1, keepdims=True)
        score_grad = (weights_wide * (prob_grad - row_delta) * scale_factor).astype(jnp.bfloat16)
        query_part = jnp.einsum(
            "ahij,ajhd->aihd", score_grad, key_rows, preferred_element_type=jnp.float32
        )
        key_part = jnp.einsum(
            "ahij,aihd->ajhd", score_grad, query_block, preferred_element_type=jnp.float32
        )
        block_shape = (span, block_slots.shape[1]) + query_tiles.shape[1:]
        key_total = key_total.at[block_slots].add(key_part.reshape(block_shape))
        value_total = value_total.at[block_slots].add(value_part.reshape(block_shape))
        return ((key_total, value_total), (attended, query_part))

    totals, parts = lax.scan(
        per_block, (empty_grad, empty_grad), jnp.arange(tile_count // span, dtype=jnp.int32)
    )
    flat_shape = (-1,) + query_tiles.shape[2:]
    return (
        parts[0].reshape(flat_shape),
        parts[1].reshape(flat_shape),
        totals[0].reshape(flat_shape),
        totals[1].reshape(flat_shape),
    )


def general_body(
    segment_input,
    output_grad,
    qkv_weight,
    out_weight,
    query_gain,
    key_gain,
    gate_scale,
    neighbours,
    tile_slot,
):
    key_slots, key_valid = slot_lists(neighbours, tile_slot)
    stream = segment_input[0]
    upstream = output_grad[0]
    model_width = stream.shape[1]
    head_dim = query_gain.shape[1]
    local_heads = qkv_weight.shape[2]
    local_width = local_heads * head_dim
    proj_weight = qkv_weight[0].reshape(model_width, local_heads * 3 * head_dim)
    out_local = out_weight[0]
    gate_row = gate_scale[0]
    query_weights = query_gain[0]
    key_weights = key_gain[0]
    projected = jnp.dot(
        lax.all_gather(stream, "seq", axis=0, tiled=True),
        proj_weight,
        preferred_element_type=jnp.float32,
    )
    all_tokens = projected.shape[0]
    projected = projected.reshape(all_tokens, local_heads, 3, head_dim)
    query_unit, query_spread = unit_norm(projected[:, :, 0])
    key_unit, key_spread = unit_norm(projected[:, :, 1])
    queries = (query_unit * query_weights).astype(jnp.bfloat16)
    keys_normed = (key_unit * key_weights).astype(jnp.bfloat16)
    value_rows = projected[:, :, 2].astype(jnp.bfloat16)
    scaled = (upstream.astype(jnp.float32) * gate_row).astype(jnp.bfloat16)
    attended_grad = jnp.einsum(
        "td,cd->tc",
        lax.all_gather(scaled, "seq", axis=0, tiled=True),
        out_local,
        preferred_element_type=jnp.float32,
    ).astype(jnp.bfloat16)

    def as_tiles(values):
        return values.reshape(-1, TILE, local_heads, head_dim)

    attended, query_grad, key_grad, value_grad = attend_both(
        as_tiles(queries),
        as_tiles(keys_normed),
        as_tiles(value_rows),
        as_tiles(attended_grad),
        key_slots,
        key_valid,
    )
    attended_low = attended.astype(jnp.bfloat16).reshape(all_tokens, local_width)
    rows = attended_low
    attention_out = lax.psum_scatter(
        jnp.dot(rows, out_local, preferred_element_type=jnp.float32),
        "seq",
        scatter_dimension=0,
        tiled=True,
    )
    section_out = (stream.astype(jnp.float32) + gate_row * attention_out).astype(jnp.bfloat16)
    segment_output = passed_along(section_out, "pipe", 1)
    gate_local = lax.psum_scatter(
        jnp.sum(upstream.astype(jnp.float32) * attention_out, axis=0),
        "seq",
        scatter_dimension=0,
        tiled=True,
    )
    query_scaled = query_grad * query_weights
    query_part_grad = (
        query_scaled - query_unit * jnp.mean(query_scaled * query_unit, axis=-1, keepdims=True)
    ) / query_spread
    key_scaled = key_grad * key_weights
    key_part_grad = (
        key_scaled - key_unit * jnp.mean(key_scaled * key_unit, axis=-1, keepdims=True)
    ) / key_spread
    projected_grad = (
        jnp.stack([query_part_grad, key_part_grad, value_grad], axis=2)
        .astype(jnp.bfloat16)
        .reshape(all_tokens, local_heads * 3 * head_dim)
    )
    rows = projected_grad
    stream_grad = lax.psum_scatter(
        jnp.einsum("tc,dc->td", rows, proj_weight, preferred_element_type=jnp.float32).astype(
            jnp.bfloat16
        ),
        "seq",
        scatter_dimension=0,
        tiled=True,
    ).astype(jnp.float32)
    token_grad = (upstream.astype(jnp.float32) + stream_grad).astype(jnp.bfloat16)
    input_grad = passed_along(token_grad, "pipe", -1)
    return (segment_output[None], input_grad[None], gate_local[None])


def dot_nn(a, b):
    return lax.dot_general(a, b, (((1,), (0,)), ((), ())), preferred_element_type=F32)


def dot_nt(a, b):
    return lax.dot_general(a, b, (((1,), (1,)), ((), ())), preferred_element_type=F32)


def dot_tn(a, b):
    return lax.dot_general(a, b, (((0,), (0,)), ((), ())), preferred_element_type=F32)


def params(mebibytes):
    return pltpu.CompilerParams(vmem_limit_bytes=mebibytes * MIB)


def regroup_kernel(weight_ref, out_ref, wide_ref):
    rows, heads, width = weight_ref.shape
    third = wide_ref.shape[2]
    for part in range(width // third):
        piece = weight_ref[:, :, part * third : (part + 1) * third].astype(F32)
        wide_ref[part] = piece.reshape(rows * heads, third)
    for head in range(heads):
        for part in range(width // third):
            left = (head % 2) * width + part * third
            out_ref[head // 2, :, left : left + third] = wide_ref[
                part, pl.ds(head, rows, stride=heads), :
            ].astype(BF16)


def regroup(weight, rows):
    depth, heads, width = weight.shape
    pairs = heads // 2
    third = width // 3
    return pl.pallas_call(
        regroup_kernel,
        grid=(depth // rows,),
        out_shape=jax.ShapeDtypeStruct((pairs, depth, 2 * width), weight.dtype),
        in_specs=[pl.BlockSpec((rows, heads, width), lambda i: (i, 0, 0))],
        out_specs=pl.BlockSpec((pairs, rows, 2 * width), lambda i: (0, i, 0)),
        scratch_shapes=[pltpu.VMEM((3, rows * heads, third), F32)],
        compiler_params=params(46),
        cost_estimate=pl.CostEstimate(
            flops=0, bytes_accessed=4 * depth * heads * width, transcendentals=0
        ),
        name="regroup",
    )(weight)


def listed_slots(neighbours_ref, tile_slot_ref):
    tiles, places = neighbours_ref.shape
    one, zero = jnp.int32(1), jnp.int32(0)
    allowed = [[zero] * tiles for _ in range(tiles)]
    for t in range(tiles):
        for u in range(tiles):
            listed = zero
            for k in range(places):
                listed = jnp.where(neighbours_ref[t, k] == u, one, listed)
            for r in range(tiles):
                for c in range(tiles):
                    here = (tile_slot_ref[t] == r) & (tile_slot_ref[u] == c)
                    allowed[r][c] = jnp.where(here, listed, allowed[r][c])
    return allowed


def forward_kernel(
    neighbours_ref,
    tile_slot_ref,
    own_ref,
    other_ref,
    weight_ref,
    out_weight_ref,
    query_gain_ref,
    key_gain_ref,
    gate_ref,
    projected_ref,
    probs_ref,
    attention_ref,
    kept_ref,
    sent_ref,
    tokens_ref,
    bias_ref,
):
    step = pl.program_id(0)
    local = own_ref.shape[0]
    tokens = 2 * local
    width = query_gain_ref.shape[1]
    heads = probs_ref.shape[0]

    @pl.when(step == 0)
    def _():
        tokens_ref[:local, :] = own_ref[...]
        tokens_ref[local:, :] = other_ref[...]
        allowed = listed_slots(neighbours_ref, tile_slot_ref)
        mine = lax.axis_index("seq")
        row_half = lax.broadcasted_iota(jnp.int32, (tokens, tokens), 0) // local
        column_half = lax.broadcasted_iota(jnp.int32, (tokens, tokens), 1) // local
        row_slot = jnp.where(row_half == 0, mine, 1 - mine)
        column_slot = jnp.where(column_half == 0, mine, 1 - mine)
        table = jnp.zeros((tokens, tokens), jnp.int32)
        for r in range(2):
            for c in range(2):
                table = jnp.where((row_slot == r) & (column_slot == c), allowed[r][c], table)
        bias_ref[...] = jnp.where(table > 0, 0.0, -jnp.inf).astype(F32)

    projected = dot_nn(tokens_ref[...], weight_ref[0])
    projected_ref[0] = projected
    scale_factor = 1.0 / math.sqrt(width)
    bias = bias_ref[...]
    attended = []
    for head in range(heads):
        left = head * 3 * width
        query = projected[:, left : left + width]
        key = projected[:, left + width : left + 2 * width]
        value = projected[:, left + 2 * width : left + 3 * width].astype(BF16)
        query_inverse = lax.rsqrt(jnp.mean(query * query, axis=-1, keepdims=True) + EPSILON)
        key_inverse = lax.rsqrt(jnp.mean(key * key, axis=-1, keepdims=True) + EPSILON)
        queries = (query * query_inverse * query_gain_ref[...]).astype(BF16)
        keys = (key * key_inverse * key_gain_ref[...]).astype(BF16)
        scores = dot_nt(queries, keys) * scale_factor + bias
        row_max = jnp.max(scores, axis=-1, keepdims=True)
        weights = jnp.exp(scores - row_max)
        probs = (weights / jnp.sum(weights, axis=-1, keepdims=True)).astype(BF16)
        probs_ref[head] = probs
        attended.append(dot_nn(probs, value).astype(BF16))
    share = dot_nn(jnp.concatenate(attended, axis=1), out_weight_ref[...])

    @pl.when(step == 0)
    def _():
        attention_ref[...] = share

    @pl.when(step > 0)
    def _():
        attention_ref[...] += share

    @pl.when(step == pl.num_programs(0) - 1)
    def _():
        gate = gate_ref[...]
        kept_ref[...] = (own_ref[...].astype(F32) + gate * attention_ref[:local, :]).astype(BF16)
        sent_ref[...] = (gate * attention_ref[local:, :]).astype(BF16)


def forward(neighbours, tile_slot, own, other, weight, out_weight, query_gain, key_gain, gate):
    local, model = own.shape
    pairs, _, wide = weight.shape
    head_dim = query_gain.shape[1]
    tokens = 2 * local
    whole = lambda i: (0, 0)
    smem = pl.BlockSpec(memory_space=pltpu.SMEM)
    return pl.pallas_call(
        forward_kernel,
        grid=(pairs,),
        out_shape=(
            jax.ShapeDtypeStruct((pairs, tokens, wide), F32),
            jax.ShapeDtypeStruct((2 * pairs, tokens, tokens), BF16),
            jax.ShapeDtypeStruct((tokens, model), F32),
            jax.ShapeDtypeStruct((local, model), BF16),
            jax.ShapeDtypeStruct((local, model), BF16),
        ),
        in_specs=[
            smem,
            smem,
            pl.BlockSpec((local, model), whole),
            pl.BlockSpec((local, model), whole),
            pl.BlockSpec((1, model, wide), lambda i: (i, 0, 0)),
            pl.BlockSpec((2 * head_dim, model), lambda i: (i, 0)),
            pl.BlockSpec((1, head_dim), whole),
            pl.BlockSpec((1, head_dim), whole),
            pl.BlockSpec((1, model), whole),
        ],
        out_specs=(
            pl.BlockSpec((1, tokens, wide), lambda i: (i, 0, 0)),
            pl.BlockSpec((2, tokens, tokens), lambda i: (i, 0, 0)),
            pl.BlockSpec((tokens, model), whole),
            pl.BlockSpec((local, model), whole),
            pl.BlockSpec((local, model), whole),
        ),
        scratch_shapes=[pltpu.VMEM((tokens, model), BF16), pltpu.VMEM((tokens, tokens), F32)],
        compiler_params=params(46),
        cost_estimate=pl.CostEstimate(
            flops=2 * tokens * model * pairs * (wide + 2 * head_dim),
            bytes_accessed=2 * model * pairs * (wide + 2 * head_dim),
            transcendentals=0,
        ),
        name="attention_forward",
    )(neighbours, tile_slot, own, other, weight, out_weight, query_gain, key_gain, gate)


def backward_kernel(
    own_ref,
    other_ref,
    out_weight_ref,
    projected_ref,
    probs_ref,
    attention_ref,
    query_gain_ref,
    key_gain_ref,
    gate_ref,
    grad_ref,
    gate_grad_ref,
    scaled_ref,
):
    step = pl.program_id(0)
    local = own_ref.shape[0]
    width = query_gain_ref.shape[1]
    heads = probs_ref.shape[0]
    columns = attention_ref.shape[1]

    @pl.when(step == 0)
    def _():
        gate = gate_ref[...]
        scaled_ref[:local, :] = (own_ref[...].astype(F32) * gate).astype(BF16)
        scaled_ref[local:, :] = (other_ref[...].astype(F32) * gate).astype(BF16)

    part = pl.ds(pl.multiple_of(step * columns, columns), columns)
    gate_grad_ref[...] = jnp.sum(
        own_ref[:, part].astype(F32) * attention_ref[:local, :], axis=0, keepdims=True
    ) + jnp.sum(other_ref[:, part].astype(F32) * attention_ref[local:, :], axis=0, keepdims=True)

    attended_grad = dot_nt(scaled_ref[...], out_weight_ref[...]).astype(BF16)
    scale_factor = 1.0 / math.sqrt(width)
    for head in range(heads):
        left = head * 3 * width
        query = projected_ref[0, :, left : left + width]
        key = projected_ref[0, :, left + width : left + 2 * width]
        value = projected_ref[0, :, left + 2 * width : left + 3 * width].astype(BF16)
        query_inverse = lax.rsqrt(jnp.mean(query * query, axis=-1, keepdims=True) + EPSILON)
        key_inverse = lax.rsqrt(jnp.mean(key * key, axis=-1, keepdims=True) + EPSILON)
        query_unit = query * query_inverse
        key_unit = key * key_inverse
        queries = (query_unit * query_gain_ref[...]).astype(BF16)
        keys = (key_unit * key_gain_ref[...]).astype(BF16)
        grad = attended_grad[:, head * width : (head + 1) * width]
        probs = probs_ref[head]
        probs_wide = probs.astype(F32)
        value_grad = dot_tn(probs, grad)
        prob_grad = dot_nt(grad, value)
        row_delta = jnp.sum(probs_wide * prob_grad, axis=-1, keepdims=True)
        score_grad = (probs_wide * (prob_grad - row_delta) * scale_factor).astype(BF16)
        query_scaled = dot_nn(score_grad, keys) * query_gain_ref[...]
        key_scaled = dot_tn(score_grad, queries) * key_gain_ref[...]
        query_mean = jnp.mean(query_scaled * query_unit, axis=-1, keepdims=True)
        key_mean = jnp.mean(key_scaled * key_unit, axis=-1, keepdims=True)
        grad_ref[0, :, left : left + width] = (
            (query_scaled - query_unit * query_mean) * query_inverse
        ).astype(BF16)
        grad_ref[0, :, left + width : left + 2 * width] = (
            (key_scaled - key_unit * key_mean) * key_inverse
        ).astype(BF16)
        grad_ref[0, :, left + 2 * width : left + 3 * width] = value_grad.astype(BF16)


def backward(own, other, out_weight, projected, probs, attention, query_gain, key_gain, gate):
    local, model = own.shape
    pairs, tokens, wide = projected.shape
    head_dim = query_gain.shape[1]
    whole = lambda i: (0, 0)
    return pl.pallas_call(
        backward_kernel,
        grid=(pairs,),
        out_shape=(
            jax.ShapeDtypeStruct((pairs, tokens, wide), BF16),
            jax.ShapeDtypeStruct((1, model), F32),
        ),
        in_specs=[
            pl.BlockSpec((local, model), whole),
            pl.BlockSpec((local, model), whole),
            pl.BlockSpec((2 * head_dim, model), lambda i: (i, 0)),
            pl.BlockSpec((1, tokens, wide), lambda i: (i, 0, 0)),
            pl.BlockSpec((2, tokens, tokens), lambda i: (i, 0, 0)),
            pl.BlockSpec((tokens, model // pairs), lambda i: (0, i)),
            pl.BlockSpec((1, head_dim), whole),
            pl.BlockSpec((1, head_dim), whole),
            pl.BlockSpec((1, model), whole),
        ],
        out_specs=(
            pl.BlockSpec((1, tokens, wide), lambda i: (i, 0, 0)),
            pl.BlockSpec((1, model // pairs), lambda i: (0, i)),
        ),
        scratch_shapes=[pltpu.VMEM((tokens, model), BF16)],
        compiler_params=params(46),
        cost_estimate=pl.CostEstimate(
            flops=2 * tokens * model * pairs * 2 * head_dim,
            bytes_accessed=2 * model * pairs * 2 * head_dim,
            transcendentals=0,
        ),
        name="attention_backward",
    )(own, other, out_weight, projected, probs, attention, query_gain, key_gain, gate)


def input_grad_kernel(grad_ref, weight_ref, own_ref, kept_ref, sent_ref):
    local = own_ref.shape[0]
    total = dot_nt(weight_ref[0], grad_ref[0])
    for pair in range(1, grad_ref.shape[0]):
        total += dot_nt(weight_ref[pair], grad_ref[pair])
    total = total.T
    kept_ref[...] = (own_ref[...].astype(F32) + total[:local]).astype(BF16)
    sent_ref[...] = total[local:].astype(BF16)


def input_grad_part(grad, weight, own, part, parts, block):
    local, model = own.shape
    pairs, tokens, wide = grad.shape
    columns = model // parts
    first = part * columns // block
    out = jax.ShapeDtypeStruct((local, columns), BF16)
    out_spec = pl.BlockSpec((local, block), lambda i: (0, i))
    return pl.pallas_call(
        input_grad_kernel,
        grid=(columns // block,),
        out_shape=(out, out),
        in_specs=[
            pl.BlockSpec((pairs, tokens, wide), lambda i: (0, 0, 0)),
            pl.BlockSpec((pairs, block, wide), lambda i: (0, i + first, 0)),
            pl.BlockSpec((local, block), lambda i: (0, i + first)),
        ],
        out_specs=(out_spec, out_spec),
        compiler_params=params(46),
        cost_estimate=pl.CostEstimate(
            flops=2 * tokens * columns * pairs * wide,
            bytes_accessed=2 * columns * pairs * wide,
            transcendentals=0,
        ),
        name="input_grad",
    )(grad, weight, own)


def routed(block, seq_step, pipe_step):
    seq_size, pipe_size = lax.axis_size("seq"), lax.axis_size("pipe")
    route = []
    for i in range(seq_size):
        for j in range(pipe_size):
            target = (i + seq_step) % seq_size * pipe_size + (j + pipe_step) % pipe_size
            route.append((i * pipe_size + j, target))
    return lax.ppermute(block, ("seq", "pipe"), route)


def pair_body(
    segment_input,
    output_grad,
    qkv_weight,
    out_weight,
    query_gain,
    key_gain,
    gate_scale,
    neighbours,
    tile_slot,
):
    stream = segment_input[0]
    upstream = output_grad[0]
    out_local = out_weight[0]
    model = stream.shape[1]
    other_stream = routed(stream, 1, 0)
    weight = regroup(qkv_weight[0], 128)
    weight, upstream_after = lax.optimization_barrier((weight, upstream))
    other_upstream = routed(upstream_after, 1, 0)
    projected, probs, attention, kept, sent = forward(
        neighbours,
        tile_slot,
        stream,
        other_stream,
        weight,
        out_local,
        query_gain,
        key_gain,
        gate_scale,
    )
    kept = routed(kept, 0, 1)
    sent = routed(sent, 1, 1)
    grad, gate_share = backward(
        upstream,
        other_upstream,
        out_local,
        projected,
        probs,
        attention,
        query_gain,
        key_gain,
        gate_scale,
    )
    other_gate = routed(gate_share, 1, 0)
    first, second = input_grad_part(grad, weight, upstream, 0, 2, 512)
    pieces = [(routed(first, 0, -1), routed(second, 1, -1))]
    segment_output = (kept.astype(F32) + sent.astype(F32)).astype(BF16)
    half = model // lax.axis_size("seq")
    gate_total = lax.dynamic_slice_in_dim(
        gate_share + other_gate, lax.axis_index("seq") * half, half, 1
    )
    grad, segment_output, gate_total = lax.optimization_barrier((grad, segment_output, gate_total))
    first, second = input_grad_part(grad, weight, upstream, 1, 2, 512)
    pieces.append((routed(first, 0, -1), routed(second, 1, -1)))
    input_grad = jnp.concatenate(
        [(a.astype(F32) + b.astype(F32)).astype(BF16) for a, b in pieces], axis=1
    )
    return (segment_output[None], input_grad[None], gate_total)


def solution(mesh):
    in_specs = (
        P("pipe", ("dp", "seq"), None),
        P("pipe", ("dp", "seq"), None),
        P("pipe", None, "seq", None),
        P("pipe", "seq", None),
        P("pipe", None),
        P("pipe", None),
        P("pipe", None),
        P("dp", None),
        P("dp"),
    )
    out_specs = (
        P("pipe", ("dp", "seq"), None),
        P("pipe", ("dp", "seq"), None),
        P(("dp", "pipe"), "seq"),
    )

    def body(*args):
        one_tile_each = args[0].shape[1] == TILE and args[8].shape[0] == 2
        if mesh.shape["seq"] == 2 and one_tile_each and args[2].shape[2] % 2 == 0:
            return pair_body(*args)
        return general_body(*args)

    return jax.shard_map(body, mesh=mesh, in_specs=in_specs, out_specs=out_specs, check_vma=False)
```

```python
import functools
import math

import jax
import jax.numpy as jnp
from jax import lax
from jax.experimental import pallas as pl
from jax.experimental.pallas import tpu as pltpu
from jax.sharding import PartitionSpec as P

TILE = 64
EPSILON = 1e-06
F32 = jnp.float32
BF16 = jnp.bfloat16
MIB = 1024 * 1024


def passed_along(block, axis, distance):
    devices = range(lax.axis_size(axis))
    route = [((i - distance) % len(devices), i) for i in devices]
    return lax.ppermute(block, axis, route)


def slot_lists(neighbours, tile_slot):
    tile_count = tile_slot.shape[0]
    numbering = jnp.arange(tile_count, dtype=jnp.int32)
    placed = (tile_slot[:, None] == numbering[None, :]).astype(jnp.int32)
    tile_of_slot = jnp.sum(placed * numbering[:, None], axis=0)
    chosen = (tile_of_slot[:, None] == numbering[None, :]).astype(jnp.int32)
    listed_tiles = jnp.sum(chosen[:, :, None] * neighbours[None, :, :], axis=1)
    key_valid = listed_tiles >= 0
    safe_tiles = jnp.maximum(listed_tiles, 0)
    matches = (safe_tiles[:, :, None] == numbering[None, None, :]).astype(jnp.int32)
    key_slots = jnp.sum(matches * tile_slot[None, None, :], axis=2)
    return (key_slots, key_valid)


def block_tiles(tile_count):
    return math.gcd(tile_count, max(1, 512 // TILE))


def unit_norm(values):
    spread = jnp.sqrt(jnp.mean(values * values, axis=-1, keepdims=True) + EPSILON)
    return (values / spread, spread)


def probabilities(query_block, key_rows, block_valid):
    scores = jnp.einsum(
        "aihd,ajhd->ahij", query_block, key_rows, preferred_element_type=jnp.float32
    ) * (1.0 / math.sqrt(query_block.shape[-1]))
    key_mask = jnp.repeat(block_valid, TILE, axis=1)
    scores = jnp.where(key_mask[:, None, None, :], scores, -jnp.inf)
    row_max = jnp.max(scores, axis=-1, keepdims=True)
    weights = jnp.exp(scores - row_max)
    return (weights / jnp.sum(weights, axis=-1, keepdims=True)).astype(jnp.bfloat16)


def gathered(tiles_array, block_slots):
    picked = tiles_array[block_slots]
    return picked.reshape(block_slots.shape[0], -1, tiles_array.shape[2], tiles_array.shape[3])


def attend_both(query_tiles, key_tiles, value_tiles, grad_tiles, key_slots, key_valid):
    tile_count = query_tiles.shape[0]
    span = block_tiles(tile_count)
    scale_factor = 1.0 / math.sqrt(query_tiles.shape[-1])
    empty_grad = jnp.zeros(query_tiles.shape, jnp.float32)

    def per_block(accumulators, block_index):
        key_total, value_total = accumulators
        first_tile = block_index * span
        query_block = lax.dynamic_slice_in_dim(query_tiles, first_tile, span, 0)
        grad_block = lax.dynamic_slice_in_dim(grad_tiles, first_tile, span, 0)
        block_slots = lax.dynamic_slice_in_dim(key_slots, first_tile, span, 0)
        block_valid = lax.dynamic_slice_in_dim(key_valid, first_tile, span, 0)
        key_rows = gathered(key_tiles, block_slots)
        value_rows = gathered(value_tiles, block_slots)
        weights = probabilities(query_block, key_rows, block_valid)
        attended = jnp.einsum(
            "ahij,ajhd->aihd", weights, value_rows, preferred_element_type=jnp.float32
        )
        value_part = jnp.einsum(
            "ahij,aihd->ajhd", weights, grad_block, preferred_element_type=jnp.float32
        )
        prob_grad = jnp.einsum(
            "aihd,ajhd->ahij", grad_block, value_rows, preferred_element_type=jnp.float32
        )
        weights_wide = weights.astype(jnp.float32)
        row_delta = jnp.sum(weights_wide * prob_grad, axis=-1, keepdims=True)
        score_grad = (weights_wide * (prob_grad - row_delta) * scale_factor).astype(jnp.bfloat16)
        query_part = jnp.einsum(
            "ahij,ajhd->aihd", score_grad, key_rows, preferred_element_type=jnp.float32
        )
        key_part = jnp.einsum(
            "ahij,aihd->ajhd", score_grad, query_block, preferred_element_type=jnp.float32
        )
        block_shape = (span, block_slots.shape[1]) + query_tiles.shape[1:]
        key_total = key_total.at[block_slots].add(key_part.reshape(block_shape))
        value_total = value_total.at[block_slots].add(value_part.reshape(block_shape))
        return ((key_total, value_total), (attended, query_part))

    totals, parts = lax.scan(
        per_block, (empty_grad, empty_grad), jnp.arange(tile_count // span, dtype=jnp.int32)
    )
    flat_shape = (-1,) + query_tiles.shape[2:]
    return (
        parts[0].reshape(flat_shape),
        parts[1].reshape(flat_shape),
        totals[0].reshape(flat_shape),
        totals[1].reshape(flat_shape),
    )


def general_body(
    segment_input,
    output_grad,
    qkv_weight,
    out_weight,
    query_gain,
    key_gain,
    gate_scale,
    neighbours,
    tile_slot,
):
    key_slots, key_valid = slot_lists(neighbours, tile_slot)
    stream = segment_input[0]
    upstream = output_grad[0]
    model_width = stream.shape[1]
    head_dim = query_gain.shape[1]
    local_heads = qkv_weight.shape[2]
    local_width = local_heads * head_dim
    proj_weight = qkv_weight[0].reshape(model_width, local_heads * 3 * head_dim)
    out_local = out_weight[0]
    gate_row = gate_scale[0]
    query_weights = query_gain[0]
    key_weights = key_gain[0]
    projected = jnp.dot(
        lax.all_gather(stream, "seq", axis=0, tiled=True),
        proj_weight,
        preferred_element_type=jnp.float32,
    )
    all_tokens = projected.shape[0]
    projected = projected.reshape(all_tokens, local_heads, 3, head_dim)
    query_unit, query_spread = unit_norm(projected[:, :, 0])
    key_unit, key_spread = unit_norm(projected[:, :, 1])
    queries = (query_unit * query_weights).astype(jnp.bfloat16)
    keys_normed = (key_unit * key_weights).astype(jnp.bfloat16)
    value_rows = projected[:, :, 2].astype(jnp.bfloat16)
    scaled = (upstream.astype(jnp.float32) * gate_row).astype(jnp.bfloat16)
    attended_grad = jnp.einsum(
        "td,cd->tc",
        lax.all_gather(scaled, "seq", axis=0, tiled=True),
        out_local,
        preferred_element_type=jnp.float32,
    ).astype(jnp.bfloat16)

    def as_tiles(values):
        return values.reshape(-1, TILE, local_heads, head_dim)

    attended, query_grad, key_grad, value_grad = attend_both(
        as_tiles(queries),
        as_tiles(keys_normed),
        as_tiles(value_rows),
        as_tiles(attended_grad),
        key_slots,
        key_valid,
    )
    attended_low = attended.astype(jnp.bfloat16).reshape(all_tokens, local_width)
    rows = attended_low
    attention_out = lax.psum_scatter(
        jnp.dot(rows, out_local, preferred_element_type=jnp.float32),
        "seq",
        scatter_dimension=0,
        tiled=True,
    )
    section_out = (stream.astype(jnp.float32) + gate_row * attention_out).astype(jnp.bfloat16)
    segment_output = passed_along(section_out, "pipe", 1)
    gate_local = lax.psum_scatter(
        jnp.sum(upstream.astype(jnp.float32) * attention_out, axis=0),
        "seq",
        scatter_dimension=0,
        tiled=True,
    )
    query_scaled = query_grad * query_weights
    query_part_grad = (
        query_scaled - query_unit * jnp.mean(query_scaled * query_unit, axis=-1, keepdims=True)
    ) / query_spread
    key_scaled = key_grad * key_weights
    key_part_grad = (
        key_scaled - key_unit * jnp.mean(key_scaled * key_unit, axis=-1, keepdims=True)
    ) / key_spread
    projected_grad = (
        jnp.stack([query_part_grad, key_part_grad, value_grad], axis=2)
        .astype(jnp.bfloat16)
        .reshape(all_tokens, local_heads * 3 * head_dim)
    )
    rows = projected_grad
    stream_grad = lax.psum_scatter(
        jnp.einsum("tc,dc->td", rows, proj_weight, preferred_element_type=jnp.float32).astype(
            jnp.bfloat16
        ),
        "seq",
        scatter_dimension=0,
        tiled=True,
    ).astype(jnp.float32)
    token_grad = (upstream.astype(jnp.float32) + stream_grad).astype(jnp.bfloat16)
    input_grad = passed_along(token_grad, "pipe", -1)
    return (segment_output[None], input_grad[None], gate_local[None])


def dot_nn(a, b):
    return lax.dot_general(a, b, (((1,), (0,)), ((), ())), preferred_element_type=F32)


def dot_nt(a, b):
    return lax.dot_general(a, b, (((1,), (1,)), ((), ())), preferred_element_type=F32)


def dot_tn(a, b):
    return lax.dot_general(a, b, (((0,), (0,)), ((), ())), preferred_element_type=F32)


def params(mebibytes):
    return pltpu.CompilerParams(vmem_limit_bytes=mebibytes * MIB)


def regroup_kernel(weight_ref, out_ref):
    rows, heads, width = weight_ref.shape
    first = pl.multiple_of(pl.program_id(0) * rows, rows)
    by_head = jnp.swapaxes(weight_ref[...], 0, 1)
    for head in range(heads):
        left = (head % 2) * width
        out_ref[head // 2, pl.ds(first, rows), left : left + width] = by_head[head]


def regroup(weight, rows):
    depth, heads, width = weight.shape
    pairs = heads // 2
    return pl.pallas_call(
        regroup_kernel,
        grid=(depth // rows,),
        out_shape=pltpu.VMEM((pairs, depth, 2 * width), weight.dtype),
        in_specs=[pl.BlockSpec((rows, heads, width), lambda i: (i, 0, 0))],
        out_specs=pl.BlockSpec(memory_space=pltpu.VMEM),
        compiler_params=params(8),
        cost_estimate=pl.CostEstimate(
            flops=0, bytes_accessed=4 * depth * heads * width, transcendentals=0
        ),
        name="regroup",
    )(pltpu.with_memory_space_constraint(weight, pltpu.HBM))


def listed_slots(neighbours_ref, tile_slot_ref):
    tiles, places = neighbours_ref.shape
    one, zero = jnp.int32(1), jnp.int32(0)
    allowed = [[zero] * tiles for _ in range(tiles)]
    for t in range(tiles):
        for u in range(tiles):
            listed = zero
            for k in range(places):
                listed = jnp.where(neighbours_ref[t, k] == u, one, listed)
            for r in range(tiles):
                for c in range(tiles):
                    here = (tile_slot_ref[t] == r) & (tile_slot_ref[u] == c)
                    allowed[r][c] = jnp.where(here, listed, allowed[r][c])
    return allowed


def forward_kernel(
    neighbours_ref,
    tile_slot_ref,
    own_ref,
    other_ref,
    weight_ref,
    out_weight_ref,
    query_gain_ref,
    key_gain_ref,
    gate_ref,
    projected_ref,
    probs_ref,
    attention_ref,
    kept_ref,
    sent_ref,
    tokens_ref,
    bias_ref,
):
    step = pl.program_id(0)
    local = own_ref.shape[0]
    tokens = 2 * local
    width = query_gain_ref.shape[1]
    heads = probs_ref.shape[0]

    @pl.when(step == 0)
    def _():
        tokens_ref[:local, :] = own_ref[...]
        tokens_ref[local:, :] = other_ref[...]
        allowed = listed_slots(neighbours_ref, tile_slot_ref)
        mine = lax.axis_index("seq")
        row_half = lax.broadcasted_iota(jnp.int32, (tokens, tokens), 0) // local
        column_half = lax.broadcasted_iota(jnp.int32, (tokens, tokens), 1) // local
        row_slot = jnp.where(row_half == 0, mine, 1 - mine)
        column_slot = jnp.where(column_half == 0, mine, 1 - mine)
        table = jnp.zeros((tokens, tokens), jnp.int32)
        for r in range(2):
            for c in range(2):
                table = jnp.where((row_slot == r) & (column_slot == c), allowed[r][c], table)
        bias_ref[...] = jnp.where(table > 0, 0.0, -jnp.inf).astype(F32)

    projected = dot_nn(tokens_ref[...], weight_ref[step])
    projected_ref[0] = projected
    scale_factor = 1.0 / math.sqrt(width)
    bias = bias_ref[...]
    attended = []
    for head in range(heads):
        left = head * 3 * width
        query = projected[:, left : left + width]
        key = projected[:, left + width : left + 2 * width]
        value = projected[:, left + 2 * width : left + 3 * width].astype(BF16)
        query_inverse = lax.rsqrt(jnp.mean(query * query, axis=-1, keepdims=True) + EPSILON)
        key_inverse = lax.rsqrt(jnp.mean(key * key, axis=-1, keepdims=True) + EPSILON)
        queries = (query * query_inverse * query_gain_ref[...]).astype(BF16)
        keys = (key * key_inverse * key_gain_ref[...]).astype(BF16)
        scores = dot_nt(queries, keys) * scale_factor + bias
        row_max = jnp.max(scores, axis=-1, keepdims=True)
        weights = jnp.exp(scores - row_max)
        probs = (weights / jnp.sum(weights, axis=-1, keepdims=True)).astype(BF16)
        probs_ref[head] = probs
        attended.append(dot_nn(probs, value).astype(BF16))
    share = dot_nn(jnp.concatenate(attended, axis=1), out_weight_ref[...])

    @pl.when(step == 0)
    def _():
        attention_ref[...] = share

    @pl.when(step > 0)
    def _():
        attention_ref[...] += share

    @pl.when(step == pl.num_programs(0) - 1)
    def _():
        gate = gate_ref[...]
        kept_ref[...] = (own_ref[...].astype(F32) + gate * attention_ref[:local, :]).astype(BF16)
        sent_ref[...] = (gate * attention_ref[local:, :]).astype(BF16)


def forward(neighbours, tile_slot, own, other, weight, out_weight, query_gain, key_gain, gate):
    local, model = own.shape
    pairs, _, wide = weight.shape
    head_dim = query_gain.shape[1]
    tokens = 2 * local
    whole = lambda i: (0, 0)
    weight = pltpu.with_memory_space_constraint(weight, pltpu.VMEM)
    smem = pl.BlockSpec(memory_space=pltpu.SMEM)
    return pl.pallas_call(
        forward_kernel,
        grid=(pairs,),
        out_shape=(
            jax.ShapeDtypeStruct((pairs, tokens, wide), F32),
            jax.ShapeDtypeStruct((2 * pairs, tokens, tokens), BF16),
            jax.ShapeDtypeStruct((tokens, model), F32),
            jax.ShapeDtypeStruct((local, model), BF16),
            jax.ShapeDtypeStruct((local, model), BF16),
        ),
        in_specs=[
            smem,
            smem,
            pl.BlockSpec((local, model), whole),
            pl.BlockSpec((local, model), whole),
            pl.BlockSpec(memory_space=pltpu.VMEM),
            pl.BlockSpec((2 * head_dim, model), lambda i: (i, 0)),
            pl.BlockSpec((1, head_dim), whole),
            pl.BlockSpec((1, head_dim), whole),
            pl.BlockSpec((1, model), whole),
        ],
        out_specs=(
            pl.BlockSpec((1, tokens, wide), lambda i: (i, 0, 0)),
            pl.BlockSpec((2, tokens, tokens), lambda i: (i, 0, 0)),
            pl.BlockSpec((tokens, model), whole),
            pl.BlockSpec((local, model), whole),
            pl.BlockSpec((local, model), whole),
        ),
        scratch_shapes=[pltpu.VMEM((tokens, model), BF16), pltpu.VMEM((tokens, tokens), F32)],
        compiler_params=params(16),
        cost_estimate=pl.CostEstimate(
            flops=2 * tokens * model * pairs * (wide + 2 * head_dim),
            bytes_accessed=2 * model * pairs * (wide + 2 * head_dim),
            transcendentals=0,
        ),
        name="attention_forward",
    )(neighbours, tile_slot, own, other, weight, out_weight, query_gain, key_gain, gate)


def backward_kernel(
    own_ref,
    other_ref,
    out_weight_ref,
    projected_ref,
    probs_ref,
    attention_ref,
    query_gain_ref,
    key_gain_ref,
    gate_ref,
    grad_ref,
    gate_grad_ref,
    scaled_ref,
):
    step = pl.program_id(0)
    local = own_ref.shape[0]
    width = query_gain_ref.shape[1]
    heads = probs_ref.shape[0]
    columns = attention_ref.shape[1]

    @pl.when(step == 0)
    def _():
        gate = gate_ref[...]
        scaled_ref[:local, :] = (own_ref[...].astype(F32) * gate).astype(BF16)
        scaled_ref[local:, :] = (other_ref[...].astype(F32) * gate).astype(BF16)

    part = pl.ds(pl.multiple_of(step * columns, columns), columns)
    gate_grad_ref[...] = jnp.sum(
        own_ref[:, part].astype(F32) * attention_ref[:local, :], axis=0, keepdims=True
    ) + jnp.sum(other_ref[:, part].astype(F32) * attention_ref[local:, :], axis=0, keepdims=True)

    attended_grad = dot_nt(scaled_ref[...], out_weight_ref[...]).astype(BF16)
    scale_factor = 1.0 / math.sqrt(width)
    for head in range(heads):
        left = head * 3 * width
        query = projected_ref[0, :, left : left + width]
        key = projected_ref[0, :, left + width : left + 2 * width]
        value = projected_ref[0, :, left + 2 * width : left + 3 * width].astype(BF16)
        query_inverse = lax.rsqrt(jnp.mean(query * query, axis=-1, keepdims=True) + EPSILON)
        key_inverse = lax.rsqrt(jnp.mean(key * key, axis=-1, keepdims=True) + EPSILON)
        query_unit = query * query_inverse
        key_unit = key * key_inverse
        queries = (query_unit * query_gain_ref[...]).astype(BF16)
        keys = (key_unit * key_gain_ref[...]).astype(BF16)
        grad = attended_grad[:, head * width : (head + 1) * width]
        probs = probs_ref[head]
        probs_wide = probs.astype(F32)
        value_grad = dot_tn(probs, grad)
        prob_grad = dot_nt(grad, value)
        row_delta = jnp.sum(probs_wide * prob_grad, axis=-1, keepdims=True)
        score_grad = (probs_wide * (prob_grad - row_delta) * scale_factor).astype(BF16)
        query_scaled = dot_nn(score_grad, keys) * query_gain_ref[...]
        key_scaled = dot_tn(score_grad, queries) * key_gain_ref[...]
        query_mean = jnp.mean(query_scaled * query_unit, axis=-1, keepdims=True)
        key_mean = jnp.mean(key_scaled * key_unit, axis=-1, keepdims=True)
        grad_ref[0, :, left : left + width] = (
            (query_scaled - query_unit * query_mean) * query_inverse
        ).astype(BF16)
        grad_ref[0, :, left + width : left + 2 * width] = (
            (key_scaled - key_unit * key_mean) * key_inverse
        ).astype(BF16)
        grad_ref[0, :, left + 2 * width : left + 3 * width] = value_grad.astype(BF16)


def backward(own, other, out_weight, projected, probs, attention, query_gain, key_gain, gate):
    local, model = own.shape
    pairs, tokens, wide = projected.shape
    head_dim = query_gain.shape[1]
    whole = lambda i: (0, 0)
    return pl.pallas_call(
        backward_kernel,
        grid=(pairs,),
        out_shape=(
            jax.ShapeDtypeStruct((pairs, tokens, wide), BF16),
            jax.ShapeDtypeStruct((1, model), F32),
        ),
        in_specs=[
            pl.BlockSpec((local, model), whole),
            pl.BlockSpec((local, model), whole),
            pl.BlockSpec((2 * head_dim, model), lambda i: (i, 0)),
            pl.BlockSpec((1, tokens, wide), lambda i: (i, 0, 0)),
            pl.BlockSpec((2, tokens, tokens), lambda i: (i, 0, 0)),
            pl.BlockSpec((tokens, model // pairs), lambda i: (0, i)),
            pl.BlockSpec((1, head_dim), whole),
            pl.BlockSpec((1, head_dim), whole),
            pl.BlockSpec((1, model), whole),
        ],
        out_specs=(
            pl.BlockSpec((1, tokens, wide), lambda i: (i, 0, 0)),
            pl.BlockSpec((1, model // pairs), lambda i: (0, i)),
        ),
        scratch_shapes=[pltpu.VMEM((tokens, model), BF16)],
        compiler_params=params(16),
        cost_estimate=pl.CostEstimate(
            flops=2 * tokens * model * pairs * 2 * head_dim,
            bytes_accessed=2 * model * pairs * 2 * head_dim,
            transcendentals=0,
        ),
        name="attention_backward",
    )(own, other, out_weight, projected, probs, attention, query_gain, key_gain, gate)


def input_grad_kernel(first, grad_ref, weight_ref, own_ref, kept_ref, sent_ref):
    local, block = own_ref.shape
    rows = pl.ds(pl.multiple_of((pl.program_id(0) + first) * block, block), block)
    total = dot_nt(grad_ref[0], weight_ref[0, rows, :])
    for pair in range(1, grad_ref.shape[0]):
        total += dot_nt(grad_ref[pair], weight_ref[pair, rows, :])
    kept_ref[...] = (own_ref[...].astype(F32) + total[:local]).astype(BF16)
    sent_ref[...] = total[local:].astype(BF16)


def input_grad_part(grad, weight, own, part, parts, block):
    local, model = own.shape
    pairs, tokens, wide = grad.shape
    columns = model // parts
    first = part * columns // block
    out = jax.ShapeDtypeStruct((local, columns), BF16)
    out_spec = pl.BlockSpec((local, block), lambda i: (0, i))
    weight = pltpu.with_memory_space_constraint(weight, pltpu.VMEM)
    return pl.pallas_call(
        functools.partial(input_grad_kernel, first),
        grid=(columns // block,),
        out_shape=(out, out),
        in_specs=[
            pl.BlockSpec((pairs, tokens, wide), lambda i: (0, 0, 0)),
            pl.BlockSpec(memory_space=pltpu.VMEM),
            pl.BlockSpec((local, block), lambda i: (0, i + first)),
        ],
        out_specs=(out_spec, out_spec),
        compiler_params=params(12),
        cost_estimate=pl.CostEstimate(
            flops=2 * tokens * columns * pairs * wide,
            bytes_accessed=2 * columns * pairs * wide,
            transcendentals=0,
        ),
        name="input_grad",
    )(grad, weight, own)


def routed(block, seq_step, pipe_step):
    seq_size, pipe_size = lax.axis_size("seq"), lax.axis_size("pipe")
    route = []
    for i in range(seq_size):
        for j in range(pipe_size):
            target = (i + seq_step) % seq_size * pipe_size + (j + pipe_step) % pipe_size
            route.append((i * pipe_size + j, target))
    return lax.ppermute(block, ("seq", "pipe"), route)


def pair_body(
    segment_input,
    output_grad,
    qkv_weight,
    out_weight,
    query_gain,
    key_gain,
    gate_scale,
    neighbours,
    tile_slot,
):
    stream = segment_input[0]
    upstream = output_grad[0]
    out_local = out_weight[0]
    model = stream.shape[1]
    other_stream = routed(stream, 1, 0)
    weight = regroup(qkv_weight[0], 128)
    weight, upstream_after = lax.optimization_barrier((weight, upstream))
    other_upstream = routed(upstream_after, 1, 0)
    projected, probs, attention, kept, sent = forward(
        neighbours,
        tile_slot,
        stream,
        other_stream,
        weight,
        out_local,
        query_gain,
        key_gain,
        gate_scale,
    )
    kept = routed(kept, 0, 1)
    sent = routed(sent, 1, 1)
    grad, gate_share = backward(
        upstream,
        other_upstream,
        out_local,
        projected,
        probs,
        attention,
        query_gain,
        key_gain,
        gate_scale,
    )
    other_gate = routed(gate_share, 1, 0)
    first, second = input_grad_part(grad, weight, upstream, 0, 2, 512)
    pieces = [(routed(first, 0, -1), routed(second, 1, -1))]
    segment_output = (kept.astype(F32) + sent.astype(F32)).astype(BF16)
    half = model // lax.axis_size("seq")
    gate_total = lax.dynamic_slice_in_dim(
        gate_share + other_gate, lax.axis_index("seq") * half, half, 1
    )
    grad, segment_output, gate_total = lax.optimization_barrier((grad, segment_output, gate_total))
    first, second = input_grad_part(grad, weight, upstream, 1, 2, 512)
    pieces.append((routed(first, 0, -1), routed(second, 1, -1)))
    input_grad = jnp.concatenate(
        [(a.astype(F32) + b.astype(F32)).astype(BF16) for a, b in pieces], axis=1
    )
    return (segment_output[None], input_grad[None], gate_total)


def solution(mesh):
    in_specs = (
        P("pipe", ("dp", "seq"), None),
        P("pipe", ("dp", "seq"), None),
        P("pipe", None, "seq", None),
        P("pipe", "seq", None),
        P("pipe", None),
        P("pipe", None),
        P("pipe", None),
        P("dp", None),
        P("dp"),
    )
    out_specs = (
        P("pipe", ("dp", "seq"), None),
        P("pipe", ("dp", "seq"), None),
        P(("dp", "pipe"), "seq"),
    )

    def body(*args):
        one_tile_each = args[0].shape[1] == TILE and args[8].shape[0] == 2
        if mesh.shape["seq"] == 2 and one_tile_each and args[2].shape[2] % 2 == 0:
            return pair_body(*args)
        return general_body(*args)

    return jax.shard_map(body, mesh=mesh, in_specs=in_specs, out_specs=out_specs, check_vma=False)
```

```python
import functools
import math

import jax
import jax.numpy as jnp
from jax import lax
from jax.experimental import pallas as pl
from jax.experimental.pallas import tpu as pltpu
from jax.sharding import PartitionSpec as P

TILE = 64
EPSILON = 1e-06
F32 = jnp.float32
BF16 = jnp.bfloat16
MIB = 1024 * 1024


def passed_along(block, axis, distance):
    devices = range(lax.axis_size(axis))
    route = [((i - distance) % len(devices), i) for i in devices]
    return lax.ppermute(block, axis, route)


def slot_lists(neighbours, tile_slot):
    tile_count = tile_slot.shape[0]
    numbering = jnp.arange(tile_count, dtype=jnp.int32)
    placed = (tile_slot[:, None] == numbering[None, :]).astype(jnp.int32)
    tile_of_slot = jnp.sum(placed * numbering[:, None], axis=0)
    chosen = (tile_of_slot[:, None] == numbering[None, :]).astype(jnp.int32)
    listed_tiles = jnp.sum(chosen[:, :, None] * neighbours[None, :, :], axis=1)
    key_valid = listed_tiles >= 0
    safe_tiles = jnp.maximum(listed_tiles, 0)
    matches = (safe_tiles[:, :, None] == numbering[None, None, :]).astype(jnp.int32)
    key_slots = jnp.sum(matches * tile_slot[None, None, :], axis=2)
    return (key_slots, key_valid)


def block_tiles(tile_count):
    return math.gcd(tile_count, max(1, 512 // TILE))


def unit_norm(values):
    spread = jnp.sqrt(jnp.mean(values * values, axis=-1, keepdims=True) + EPSILON)
    return (values / spread, spread)


def probabilities(query_block, key_rows, block_valid):
    scores = jnp.einsum(
        "aihd,ajhd->ahij", query_block, key_rows, preferred_element_type=jnp.float32
    ) * (1.0 / math.sqrt(query_block.shape[-1]))
    key_mask = jnp.repeat(block_valid, TILE, axis=1)
    scores = jnp.where(key_mask[:, None, None, :], scores, -jnp.inf)
    row_max = jnp.max(scores, axis=-1, keepdims=True)
    weights = jnp.exp(scores - row_max)
    return (weights / jnp.sum(weights, axis=-1, keepdims=True)).astype(jnp.bfloat16)


def gathered(tiles_array, block_slots):
    picked = tiles_array[block_slots]
    return picked.reshape(block_slots.shape[0], -1, tiles_array.shape[2], tiles_array.shape[3])


def attend_both(query_tiles, key_tiles, value_tiles, grad_tiles, key_slots, key_valid):
    tile_count = query_tiles.shape[0]
    span = block_tiles(tile_count)
    scale_factor = 1.0 / math.sqrt(query_tiles.shape[-1])
    empty_grad = jnp.zeros(query_tiles.shape, jnp.float32)

    def per_block(accumulators, block_index):
        key_total, value_total = accumulators
        first_tile = block_index * span
        query_block = lax.dynamic_slice_in_dim(query_tiles, first_tile, span, 0)
        grad_block = lax.dynamic_slice_in_dim(grad_tiles, first_tile, span, 0)
        block_slots = lax.dynamic_slice_in_dim(key_slots, first_tile, span, 0)
        block_valid = lax.dynamic_slice_in_dim(key_valid, first_tile, span, 0)
        key_rows = gathered(key_tiles, block_slots)
        value_rows = gathered(value_tiles, block_slots)
        weights = probabilities(query_block, key_rows, block_valid)
        attended = jnp.einsum(
            "ahij,ajhd->aihd", weights, value_rows, preferred_element_type=jnp.float32
        )
        value_part = jnp.einsum(
            "ahij,aihd->ajhd", weights, grad_block, preferred_element_type=jnp.float32
        )
        prob_grad = jnp.einsum(
            "aihd,ajhd->ahij", grad_block, value_rows, preferred_element_type=jnp.float32
        )
        weights_wide = weights.astype(jnp.float32)
        row_delta = jnp.sum(weights_wide * prob_grad, axis=-1, keepdims=True)
        score_grad = (weights_wide * (prob_grad - row_delta) * scale_factor).astype(jnp.bfloat16)
        query_part = jnp.einsum(
            "ahij,ajhd->aihd", score_grad, key_rows, preferred_element_type=jnp.float32
        )
        key_part = jnp.einsum(
            "ahij,aihd->ajhd", score_grad, query_block, preferred_element_type=jnp.float32
        )
        block_shape = (span, block_slots.shape[1]) + query_tiles.shape[1:]
        key_total = key_total.at[block_slots].add(key_part.reshape(block_shape))
        value_total = value_total.at[block_slots].add(value_part.reshape(block_shape))
        return ((key_total, value_total), (attended, query_part))

    totals, parts = lax.scan(
        per_block, (empty_grad, empty_grad), jnp.arange(tile_count // span, dtype=jnp.int32)
    )
    flat_shape = (-1,) + query_tiles.shape[2:]
    return (
        parts[0].reshape(flat_shape),
        parts[1].reshape(flat_shape),
        totals[0].reshape(flat_shape),
        totals[1].reshape(flat_shape),
    )


def general_body(
    segment_input,
    output_grad,
    qkv_weight,
    out_weight,
    query_gain,
    key_gain,
    gate_scale,
    neighbours,
    tile_slot,
):
    key_slots, key_valid = slot_lists(neighbours, tile_slot)
    stream = segment_input[0]
    upstream = output_grad[0]
    model_width = stream.shape[1]
    head_dim = query_gain.shape[1]
    local_heads = qkv_weight.shape[2]
    local_width = local_heads * head_dim
    proj_weight = qkv_weight[0].reshape(model_width, local_heads * 3 * head_dim)
    out_local = out_weight[0]
    gate_row = gate_scale[0]
    query_weights = query_gain[0]
    key_weights = key_gain[0]
    projected = jnp.dot(
        lax.all_gather(stream, "seq", axis=0, tiled=True),
        proj_weight,
        preferred_element_type=jnp.float32,
    )
    all_tokens = projected.shape[0]
    projected = projected.reshape(all_tokens, local_heads, 3, head_dim)
    query_unit, query_spread = unit_norm(projected[:, :, 0])
    key_unit, key_spread = unit_norm(projected[:, :, 1])
    queries = (query_unit * query_weights).astype(jnp.bfloat16)
    keys_normed = (key_unit * key_weights).astype(jnp.bfloat16)
    value_rows = projected[:, :, 2].astype(jnp.bfloat16)
    scaled = (upstream.astype(jnp.float32) * gate_row).astype(jnp.bfloat16)
    attended_grad = jnp.einsum(
        "td,cd->tc",
        lax.all_gather(scaled, "seq", axis=0, tiled=True),
        out_local,
        preferred_element_type=jnp.float32,
    ).astype(jnp.bfloat16)

    def as_tiles(values):
        return values.reshape(-1, TILE, local_heads, head_dim)

    attended, query_grad, key_grad, value_grad = attend_both(
        as_tiles(queries),
        as_tiles(keys_normed),
        as_tiles(value_rows),
        as_tiles(attended_grad),
        key_slots,
        key_valid,
    )
    attended_low = attended.astype(jnp.bfloat16).reshape(all_tokens, local_width)
    rows = attended_low
    attention_out = lax.psum_scatter(
        jnp.dot(rows, out_local, preferred_element_type=jnp.float32),
        "seq",
        scatter_dimension=0,
        tiled=True,
    )
    section_out = (stream.astype(jnp.float32) + gate_row * attention_out).astype(jnp.bfloat16)
    segment_output = passed_along(section_out, "pipe", 1)
    gate_local = lax.psum_scatter(
        jnp.sum(upstream.astype(jnp.float32) * attention_out, axis=0),
        "seq",
        scatter_dimension=0,
        tiled=True,
    )
    query_scaled = query_grad * query_weights
    query_part_grad = (
        query_scaled - query_unit * jnp.mean(query_scaled * query_unit, axis=-1, keepdims=True)
    ) / query_spread
    key_scaled = key_grad * key_weights
    key_part_grad = (
        key_scaled - key_unit * jnp.mean(key_scaled * key_unit, axis=-1, keepdims=True)
    ) / key_spread
    projected_grad = (
        jnp.stack([query_part_grad, key_part_grad, value_grad], axis=2)
        .astype(jnp.bfloat16)
        .reshape(all_tokens, local_heads * 3 * head_dim)
    )
    rows = projected_grad
    stream_grad = lax.psum_scatter(
        jnp.einsum("tc,dc->td", rows, proj_weight, preferred_element_type=jnp.float32).astype(
            jnp.bfloat16
        ),
        "seq",
        scatter_dimension=0,
        tiled=True,
    ).astype(jnp.float32)
    token_grad = (upstream.astype(jnp.float32) + stream_grad).astype(jnp.bfloat16)
    input_grad = passed_along(token_grad, "pipe", -1)
    return (segment_output[None], input_grad[None], gate_local[None])


def dot_nn(a, b):
    return lax.dot_general(a, b, (((1,), (0,)), ((), ())), preferred_element_type=F32)


def dot_nt(a, b):
    return lax.dot_general(a, b, (((1,), (1,)), ((), ())), preferred_element_type=F32)


def dot_tn(a, b):
    return lax.dot_general(a, b, (((0,), (0,)), ((), ())), preferred_element_type=F32)


def params(mebibytes):
    return pltpu.CompilerParams(vmem_limit_bytes=mebibytes * MIB)


def regroup_kernel(weight_ref, out_ref, token_ref):
    token_ref[...] = jnp.zeros_like(token_ref)
    rows, heads, width = weight_ref.shape
    first = pl.multiple_of(pl.program_id(0) * rows, rows)
    by_head = jnp.swapaxes(weight_ref[...], 0, 1)
    for head in range(heads):
        left = (head % 2) * width
        out_ref[head // 2, pl.ds(first, rows), left : left + width] = by_head[head]


def regroup(weight, rows):
    depth, heads, width = weight.shape
    pairs = heads // 2
    return pl.pallas_call(
        regroup_kernel,
        grid=(depth // rows,),
        out_shape=(
            pltpu.VMEM((pairs, depth, 2 * width), weight.dtype),
            jax.ShapeDtypeStruct((8, 128), F32),
        ),
        in_specs=[pl.BlockSpec((rows, heads, width), lambda i: (i, 0, 0))],
        out_specs=(
            pl.BlockSpec(memory_space=pltpu.VMEM),
            pl.BlockSpec((8, 128), lambda i: (0, 0)),
        ),
        compiler_params=params(8),
        cost_estimate=pl.CostEstimate(
            flops=0, bytes_accessed=4 * depth * heads * width, transcendentals=0
        ),
        name="regroup",
    )(pltpu.with_memory_space_constraint(weight, pltpu.HBM))


def listed_slots(neighbours_ref, tile_slot_ref):
    tiles, places = neighbours_ref.shape
    one, zero = jnp.int32(1), jnp.int32(0)
    allowed = [[zero] * tiles for _ in range(tiles)]
    for t in range(tiles):
        for u in range(tiles):
            listed = zero
            for k in range(places):
                listed = jnp.where(neighbours_ref[t, k] == u, one, listed)
            for r in range(tiles):
                for c in range(tiles):
                    here = (tile_slot_ref[t] == r) & (tile_slot_ref[u] == c)
                    allowed[r][c] = jnp.where(here, listed, allowed[r][c])
    return allowed


def forward_kernel(
    neighbours_ref,
    tile_slot_ref,
    own_ref,
    other_ref,
    weight_ref,
    out_weight_ref,
    query_gain_ref,
    key_gain_ref,
    gate_ref,
    projected_ref,
    probs_ref,
    attention_ref,
    kept_ref,
    sent_ref,
    tokens_ref,
    bias_ref,
):
    step = pl.program_id(0)
    local = own_ref.shape[0]
    tokens = 2 * local
    width = query_gain_ref.shape[1]
    heads = probs_ref.shape[0]

    @pl.when(step == 0)
    def _():
        tokens_ref[:local, :] = own_ref[...]
        tokens_ref[local:, :] = other_ref[...]
        allowed = listed_slots(neighbours_ref, tile_slot_ref)
        mine = lax.axis_index("seq")
        row_half = lax.broadcasted_iota(jnp.int32, (tokens, tokens), 0) // local
        column_half = lax.broadcasted_iota(jnp.int32, (tokens, tokens), 1) // local
        row_slot = jnp.where(row_half == 0, mine, 1 - mine)
        column_slot = jnp.where(column_half == 0, mine, 1 - mine)
        table = jnp.zeros((tokens, tokens), jnp.int32)
        for r in range(2):
            for c in range(2):
                table = jnp.where((row_slot == r) & (column_slot == c), allowed[r][c], table)
        bias_ref[...] = jnp.where(table > 0, 0.0, -jnp.inf).astype(F32)

    projected = dot_nn(tokens_ref[...], weight_ref[step])
    projected_ref[0] = projected
    scale_factor = 1.0 / math.sqrt(width)
    bias = bias_ref[...]
    attended = []
    for head in range(heads):
        left = head * 3 * width
        query = projected[:, left : left + width]
        key = projected[:, left + width : left + 2 * width]
        value = projected[:, left + 2 * width : left + 3 * width].astype(BF16)
        query_inverse = lax.rsqrt(jnp.mean(query * query, axis=-1, keepdims=True) + EPSILON)
        key_inverse = lax.rsqrt(jnp.mean(key * key, axis=-1, keepdims=True) + EPSILON)
        queries = (query * query_inverse * query_gain_ref[...]).astype(BF16)
        keys = (key * key_inverse * key_gain_ref[...]).astype(BF16)
        scores = dot_nt(queries, keys) * scale_factor + bias
        row_max = jnp.max(scores, axis=-1, keepdims=True)
        weights = jnp.exp(scores - row_max)
        probs = (weights / jnp.sum(weights, axis=-1, keepdims=True)).astype(BF16)
        probs_ref[head] = probs
        attended.append(dot_nn(probs, value).astype(BF16))
    share = dot_nn(jnp.concatenate(attended, axis=1), out_weight_ref[...])

    @pl.when(step == 0)
    def _():
        attention_ref[...] = share

    @pl.when(step > 0)
    def _():
        attention_ref[...] += share

    @pl.when(step == pl.num_programs(0) - 1)
    def _():
        gate = gate_ref[...]
        kept_ref[...] = (own_ref[...].astype(F32) + gate * attention_ref[:local, :]).astype(BF16)
        sent_ref[...] = (gate * attention_ref[local:, :]).astype(BF16)


def forward(neighbours, tile_slot, own, other, weight, out_weight, query_gain, key_gain, gate):
    local, model = own.shape
    pairs, _, wide = weight.shape
    head_dim = query_gain.shape[1]
    tokens = 2 * local
    whole = lambda i: (0, 0)
    weight = pltpu.with_memory_space_constraint(weight, pltpu.VMEM)
    smem = pl.BlockSpec(memory_space=pltpu.SMEM)
    return pl.pallas_call(
        forward_kernel,
        grid=(pairs,),
        out_shape=(
            jax.ShapeDtypeStruct((pairs, tokens, wide), F32),
            jax.ShapeDtypeStruct((2 * pairs, tokens, tokens), BF16),
            jax.ShapeDtypeStruct((tokens, model), F32),
            jax.ShapeDtypeStruct((local, model), BF16),
            jax.ShapeDtypeStruct((local, model), BF16),
        ),
        in_specs=[
            smem,
            smem,
            pl.BlockSpec((local, model), whole),
            pl.BlockSpec((local, model), whole),
            pl.BlockSpec(memory_space=pltpu.VMEM),
            pl.BlockSpec((2 * head_dim, model), lambda i: (i, 0)),
            pl.BlockSpec((1, head_dim), whole),
            pl.BlockSpec((1, head_dim), whole),
            pl.BlockSpec((1, model), whole),
        ],
        out_specs=(
            pl.BlockSpec((1, tokens, wide), lambda i: (i, 0, 0)),
            pl.BlockSpec((2, tokens, tokens), lambda i: (i, 0, 0)),
            pl.BlockSpec((tokens, model), whole),
            pl.BlockSpec((local, model), whole),
            pl.BlockSpec((local, model), whole),
        ),
        scratch_shapes=[pltpu.VMEM((tokens, model), BF16), pltpu.VMEM((tokens, tokens), F32)],
        compiler_params=params(16),
        cost_estimate=pl.CostEstimate(
            flops=2 * tokens * model * pairs * (wide + 2 * head_dim),
            bytes_accessed=2 * model * pairs * (wide + 2 * head_dim),
            transcendentals=0,
        ),
        name="attention_forward",
    )(neighbours, tile_slot, own, other, weight, out_weight, query_gain, key_gain, gate)


def backward_kernel(
    own_ref,
    other_ref,
    out_weight_ref,
    projected_ref,
    probs_ref,
    attention_ref,
    query_gain_ref,
    key_gain_ref,
    gate_ref,
    grad_ref,
    gate_grad_ref,
    scaled_ref,
):
    step = pl.program_id(0)
    local = own_ref.shape[0]
    width = query_gain_ref.shape[1]
    heads = probs_ref.shape[0]
    columns = attention_ref.shape[1]

    @pl.when(step == 0)
    def _():
        gate = gate_ref[...]
        scaled_ref[:local, :] = (own_ref[...].astype(F32) * gate).astype(BF16)
        scaled_ref[local:, :] = (other_ref[...].astype(F32) * gate).astype(BF16)

    part = pl.ds(pl.multiple_of(step * columns, columns), columns)
    gate_grad_ref[...] = jnp.sum(
        own_ref[:, part].astype(F32) * attention_ref[:local, :], axis=0, keepdims=True
    ) + jnp.sum(other_ref[:, part].astype(F32) * attention_ref[local:, :], axis=0, keepdims=True)

    attended_grad = dot_nt(scaled_ref[...], out_weight_ref[...]).astype(BF16)
    scale_factor = 1.0 / math.sqrt(width)
    for head in range(heads):
        left = head * 3 * width
        query = projected_ref[0, :, left : left + width]
        key = projected_ref[0, :, left + width : left + 2 * width]
        value = projected_ref[0, :, left + 2 * width : left + 3 * width].astype(BF16)
        query_inverse = lax.rsqrt(jnp.mean(query * query, axis=-1, keepdims=True) + EPSILON)
        key_inverse = lax.rsqrt(jnp.mean(key * key, axis=-1, keepdims=True) + EPSILON)
        query_unit = query * query_inverse
        key_unit = key * key_inverse
        queries = (query_unit * query_gain_ref[...]).astype(BF16)
        keys = (key_unit * key_gain_ref[...]).astype(BF16)
        grad = attended_grad[:, head * width : (head + 1) * width]
        probs = probs_ref[head]
        probs_wide = probs.astype(F32)
        value_grad = dot_tn(probs, grad)
        prob_grad = dot_nt(grad, value)
        row_delta = jnp.sum(probs_wide * prob_grad, axis=-1, keepdims=True)
        score_grad = (probs_wide * (prob_grad - row_delta) * scale_factor).astype(BF16)
        query_scaled = dot_nn(score_grad, keys) * query_gain_ref[...]
        key_scaled = dot_tn(score_grad, queries) * key_gain_ref[...]
        query_mean = jnp.mean(query_scaled * query_unit, axis=-1, keepdims=True)
        key_mean = jnp.mean(key_scaled * key_unit, axis=-1, keepdims=True)
        grad_ref[0, :, left : left + width] = (
            (query_scaled - query_unit * query_mean) * query_inverse
        ).astype(BF16)
        grad_ref[0, :, left + width : left + 2 * width] = (
            (key_scaled - key_unit * key_mean) * key_inverse
        ).astype(BF16)
        grad_ref[0, :, left + 2 * width : left + 3 * width] = value_grad.astype(BF16)


def backward(own, other, out_weight, projected, probs, attention, query_gain, key_gain, gate):
    local, model = own.shape
    pairs, tokens, wide = projected.shape
    head_dim = query_gain.shape[1]
    whole = lambda i: (0, 0)
    return pl.pallas_call(
        backward_kernel,
        grid=(pairs,),
        out_shape=(
            jax.ShapeDtypeStruct((pairs, tokens, wide), BF16),
            jax.ShapeDtypeStruct((1, model), F32),
        ),
        in_specs=[
            pl.BlockSpec((local, model), whole),
            pl.BlockSpec((local, model), whole),
            pl.BlockSpec((2 * head_dim, model), lambda i: (i, 0)),
            pl.BlockSpec((1, tokens, wide), lambda i: (i, 0, 0)),
            pl.BlockSpec((2, tokens, tokens), lambda i: (i, 0, 0)),
            pl.BlockSpec((tokens, model // pairs), lambda i: (0, i)),
            pl.BlockSpec((1, head_dim), whole),
            pl.BlockSpec((1, head_dim), whole),
            pl.BlockSpec((1, model), whole),
        ],
        out_specs=(
            pl.BlockSpec((1, tokens, wide), lambda i: (i, 0, 0)),
            pl.BlockSpec((1, model // pairs), lambda i: (0, i)),
        ),
        scratch_shapes=[pltpu.VMEM((tokens, model), BF16)],
        compiler_params=params(16),
        cost_estimate=pl.CostEstimate(
            flops=2 * tokens * model * pairs * 2 * head_dim,
            bytes_accessed=2 * model * pairs * 2 * head_dim,
            transcendentals=0,
        ),
        name="attention_backward",
    )(own, other, out_weight, projected, probs, attention, query_gain, key_gain, gate)


def input_grad_kernel(first, grad_ref, weight_ref, own_ref, kept_ref, sent_ref):
    local, block = own_ref.shape
    rows = pl.ds(pl.multiple_of((pl.program_id(0) + first) * block, block), block)
    total = dot_nt(grad_ref[0], weight_ref[0, rows, :])
    for pair in range(1, grad_ref.shape[0]):
        total += dot_nt(grad_ref[pair], weight_ref[pair, rows, :])
    kept_ref[...] = (own_ref[...].astype(F32) + total[:local]).astype(BF16)
    sent_ref[...] = total[local:].astype(BF16)


def input_grad_part(grad, weight, own, part, parts, block):
    local, model = own.shape
    pairs, tokens, wide = grad.shape
    columns = model // parts
    first = part * columns // block
    out = jax.ShapeDtypeStruct((local, columns), BF16)
    out_spec = pl.BlockSpec((local, block), lambda i: (0, i))
    weight = pltpu.with_memory_space_constraint(weight, pltpu.VMEM)
    return pl.pallas_call(
        functools.partial(input_grad_kernel, first),
        grid=(columns // block,),
        out_shape=(out, out),
        in_specs=[
            pl.BlockSpec((pairs, tokens, wide), lambda i: (0, 0, 0)),
            pl.BlockSpec(memory_space=pltpu.VMEM),
            pl.BlockSpec((local, block), lambda i: (0, i + first)),
        ],
        out_specs=(out_spec, out_spec),
        compiler_params=params(12),
        cost_estimate=pl.CostEstimate(
            flops=2 * tokens * columns * pairs * wide,
            bytes_accessed=2 * columns * pairs * wide,
            transcendentals=0,
        ),
        name="input_grad",
    )(grad, weight, own)


def routed(block, seq_step, pipe_step):
    seq_size, pipe_size = lax.axis_size("seq"), lax.axis_size("pipe")
    route = []
    for i in range(seq_size):
        for j in range(pipe_size):
            target = (i + seq_step) % seq_size * pipe_size + (j + pipe_step) % pipe_size
            route.append((i * pipe_size + j, target))
    return lax.ppermute(block, ("seq", "pipe"), route)


def pair_body(
    segment_input,
    output_grad,
    qkv_weight,
    out_weight,
    query_gain,
    key_gain,
    gate_scale,
    neighbours,
    tile_slot,
):
    stream = segment_input[0]
    upstream = output_grad[0]
    out_local = out_weight[0]
    model = stream.shape[1]
    other_stream = routed(stream, 1, 0)
    weight, regrouped = regroup(qkv_weight[0], 128)
    regrouped, upstream_after = lax.optimization_barrier((regrouped, upstream))
    other_upstream = routed(upstream_after, 1, 0)
    projected, probs, attention, kept, sent = forward(
        neighbours,
        tile_slot,
        stream,
        other_stream,
        weight,
        out_local,
        query_gain,
        key_gain,
        gate_scale,
    )
    kept = routed(kept, 0, 1)
    sent = routed(sent, 1, 1)
    grad, gate_share = backward(
        upstream,
        other_upstream,
        out_local,
        projected,
        probs,
        attention,
        query_gain,
        key_gain,
        gate_scale,
    )
    other_gate = routed(gate_share, 1, 0)
    first, second = input_grad_part(grad, weight, upstream, 0, 2, 512)
    pieces = [(routed(first, 0, -1), routed(second, 1, -1))]
    segment_output = (kept.astype(F32) + sent.astype(F32)).astype(BF16)
    half = model // lax.axis_size("seq")
    gate_total = lax.dynamic_slice_in_dim(
        gate_share + other_gate, lax.axis_index("seq") * half, half, 1
    )
    grad, segment_output, gate_total = lax.optimization_barrier((grad, segment_output, gate_total))
    first, second = input_grad_part(grad, weight, upstream, 1, 2, 512)
    pieces.append((routed(first, 0, -1), routed(second, 1, -1)))
    input_grad = jnp.concatenate(
        [(a.astype(F32) + b.astype(F32)).astype(BF16) for a, b in pieces], axis=1
    )
    return (segment_output[None], input_grad[None], gate_total)


def solution(mesh):
    in_specs = (
        P("pipe", ("dp", "seq"), None),
        P("pipe", ("dp", "seq"), None),
        P("pipe", None, "seq", None),
        P("pipe", "seq", None),
        P("pipe", None),
        P("pipe", None),
        P("pipe", None),
        P("dp", None),
        P("dp"),
    )
    out_specs = (
        P("pipe", ("dp", "seq"), None),
        P("pipe", ("dp", "seq"), None),
        P(("dp", "pipe"), "seq"),
    )

    def body(*args):
        one_tile_each = args[0].shape[1] == TILE and args[8].shape[0] == 2
        if mesh.shape["seq"] == 2 and one_tile_each and args[2].shape[2] % 2 == 0:
            return pair_body(*args)
        return general_body(*args)

    return jax.shard_map(body, mesh=mesh, in_specs=in_specs, out_specs=out_specs, check_vma=False)
```

```python
import functools
import math

import jax
import jax.numpy as jnp
from jax import lax
from jax.experimental import pallas as pl
from jax.experimental.pallas import tpu as pltpu
from jax.sharding import PartitionSpec as P

TILE = 64
EPSILON = 1e-06
F32 = jnp.float32
BF16 = jnp.bfloat16
MIB = 1024 * 1024


def passed_along(block, axis, distance):
    devices = range(lax.axis_size(axis))
    route = [((i - distance) % len(devices), i) for i in devices]
    return lax.ppermute(block, axis, route)


def slot_lists(neighbours, tile_slot):
    tile_count = tile_slot.shape[0]
    numbering = jnp.arange(tile_count, dtype=jnp.int32)
    placed = (tile_slot[:, None] == numbering[None, :]).astype(jnp.int32)
    tile_of_slot = jnp.sum(placed * numbering[:, None], axis=0)
    chosen = (tile_of_slot[:, None] == numbering[None, :]).astype(jnp.int32)
    listed_tiles = jnp.sum(chosen[:, :, None] * neighbours[None, :, :], axis=1)
    key_valid = listed_tiles >= 0
    safe_tiles = jnp.maximum(listed_tiles, 0)
    matches = (safe_tiles[:, :, None] == numbering[None, None, :]).astype(jnp.int32)
    key_slots = jnp.sum(matches * tile_slot[None, None, :], axis=2)
    return (key_slots, key_valid)


def block_tiles(tile_count):
    return math.gcd(tile_count, max(1, 512 // TILE))


def unit_norm(values):
    spread = jnp.sqrt(jnp.mean(values * values, axis=-1, keepdims=True) + EPSILON)
    return (values / spread, spread)


def probabilities(query_block, key_rows, block_valid):
    scores = jnp.einsum(
        "aihd,ajhd->ahij", query_block, key_rows, preferred_element_type=jnp.float32
    ) * (1.0 / math.sqrt(query_block.shape[-1]))
    key_mask = jnp.repeat(block_valid, TILE, axis=1)
    scores = jnp.where(key_mask[:, None, None, :], scores, -jnp.inf)
    row_max = jnp.max(scores, axis=-1, keepdims=True)
    weights = jnp.exp(scores - row_max)
    return (weights / jnp.sum(weights, axis=-1, keepdims=True)).astype(jnp.bfloat16)


def gathered(tiles_array, block_slots):
    picked = tiles_array[block_slots]
    return picked.reshape(block_slots.shape[0], -1, tiles_array.shape[2], tiles_array.shape[3])


def attend_both(query_tiles, key_tiles, value_tiles, grad_tiles, key_slots, key_valid):
    tile_count = query_tiles.shape[0]
    span = block_tiles(tile_count)
    scale_factor = 1.0 / math.sqrt(query_tiles.shape[-1])
    empty_grad = jnp.zeros(query_tiles.shape, jnp.float32)

    def per_block(accumulators, block_index):
        key_total, value_total = accumulators
        first_tile = block_index * span
        query_block = lax.dynamic_slice_in_dim(query_tiles, first_tile, span, 0)
        grad_block = lax.dynamic_slice_in_dim(grad_tiles, first_tile, span, 0)
        block_slots = lax.dynamic_slice_in_dim(key_slots, first_tile, span, 0)
        block_valid = lax.dynamic_slice_in_dim(key_valid, first_tile, span, 0)
        key_rows = gathered(key_tiles, block_slots)
        value_rows = gathered(value_tiles, block_slots)
        weights = probabilities(query_block, key_rows, block_valid)
        attended = jnp.einsum(
            "ahij,ajhd->aihd", weights, value_rows, preferred_element_type=jnp.float32
        )
        value_part = jnp.einsum(
            "ahij,aihd->ajhd", weights, grad_block, preferred_element_type=jnp.float32
        )
        prob_grad = jnp.einsum(
            "aihd,ajhd->ahij", grad_block, value_rows, preferred_element_type=jnp.float32
        )
        weights_wide = weights.astype(jnp.float32)
        row_delta = jnp.sum(weights_wide * prob_grad, axis=-1, keepdims=True)
        score_grad = (weights_wide * (prob_grad - row_delta) * scale_factor).astype(jnp.bfloat16)
        query_part = jnp.einsum(
            "ahij,ajhd->aihd", score_grad, key_rows, preferred_element_type=jnp.float32
        )
        key_part = jnp.einsum(
            "ahij,aihd->ajhd", score_grad, query_block, preferred_element_type=jnp.float32
        )
        block_shape = (span, block_slots.shape[1]) + query_tiles.shape[1:]
        key_total = key_total.at[block_slots].add(key_part.reshape(block_shape))
        value_total = value_total.at[block_slots].add(value_part.reshape(block_shape))
        return ((key_total, value_total), (attended, query_part))

    totals, parts = lax.scan(
        per_block, (empty_grad, empty_grad), jnp.arange(tile_count // span, dtype=jnp.int32)
    )
    flat_shape = (-1,) + query_tiles.shape[2:]
    return (
        parts[0].reshape(flat_shape),
        parts[1].reshape(flat_shape),
        totals[0].reshape(flat_shape),
        totals[1].reshape(flat_shape),
    )


def general_body(
    segment_input,
    output_grad,
    qkv_weight,
    out_weight,
    query_gain,
    key_gain,
    gate_scale,
    neighbours,
    tile_slot,
):
    key_slots, key_valid = slot_lists(neighbours, tile_slot)
    stream = segment_input[0]
    upstream = output_grad[0]
    model_width = stream.shape[1]
    head_dim = query_gain.shape[1]
    local_heads = qkv_weight.shape[2]
    local_width = local_heads * head_dim
    proj_weight = qkv_weight[0].reshape(model_width, local_heads * 3 * head_dim)
    out_local = out_weight[0]
    gate_row = gate_scale[0]
    query_weights = query_gain[0]
    key_weights = key_gain[0]
    projected = jnp.dot(
        lax.all_gather(stream, "seq", axis=0, tiled=True),
        proj_weight,
        preferred_element_type=jnp.float32,
    )
    all_tokens = projected.shape[0]
    projected = projected.reshape(all_tokens, local_heads, 3, head_dim)
    query_unit, query_spread = unit_norm(projected[:, :, 0])
    key_unit, key_spread = unit_norm(projected[:, :, 1])
    queries = (query_unit * query_weights).astype(jnp.bfloat16)
    keys_normed = (key_unit * key_weights).astype(jnp.bfloat16)
    value_rows = projected[:, :, 2].astype(jnp.bfloat16)
    scaled = (upstream.astype(jnp.float32) * gate_row).astype(jnp.bfloat16)
    attended_grad = jnp.einsum(
        "td,cd->tc",
        lax.all_gather(scaled, "seq", axis=0, tiled=True),
        out_local,
        preferred_element_type=jnp.float32,
    ).astype(jnp.bfloat16)

    def as_tiles(values):
        return values.reshape(-1, TILE, local_heads, head_dim)

    attended, query_grad, key_grad, value_grad = attend_both(
        as_tiles(queries),
        as_tiles(keys_normed),
        as_tiles(value_rows),
        as_tiles(attended_grad),
        key_slots,
        key_valid,
    )
    attended_low = attended.astype(jnp.bfloat16).reshape(all_tokens, local_width)
    rows = attended_low
    attention_out = lax.psum_scatter(
        jnp.dot(rows, out_local, preferred_element_type=jnp.float32),
        "seq",
        scatter_dimension=0,
        tiled=True,
    )
    section_out = (stream.astype(jnp.float32) + gate_row * attention_out).astype(jnp.bfloat16)
    segment_output = passed_along(section_out, "pipe", 1)
    gate_local = lax.psum_scatter(
        jnp.sum(upstream.astype(jnp.float32) * attention_out, axis=0),
        "seq",
        scatter_dimension=0,
        tiled=True,
    )
    query_scaled = query_grad * query_weights
    query_part_grad = (
        query_scaled - query_unit * jnp.mean(query_scaled * query_unit, axis=-1, keepdims=True)
    ) / query_spread
    key_scaled = key_grad * key_weights
    key_part_grad = (
        key_scaled - key_unit * jnp.mean(key_scaled * key_unit, axis=-1, keepdims=True)
    ) / key_spread
    projected_grad = (
        jnp.stack([query_part_grad, key_part_grad, value_grad], axis=2)
        .astype(jnp.bfloat16)
        .reshape(all_tokens, local_heads * 3 * head_dim)
    )
    rows = projected_grad
    stream_grad = lax.psum_scatter(
        jnp.einsum("tc,dc->td", rows, proj_weight, preferred_element_type=jnp.float32).astype(
            jnp.bfloat16
        ),
        "seq",
        scatter_dimension=0,
        tiled=True,
    ).astype(jnp.float32)
    token_grad = (upstream.astype(jnp.float32) + stream_grad).astype(jnp.bfloat16)
    input_grad = passed_along(token_grad, "pipe", -1)
    return (segment_output[None], input_grad[None], gate_local[None])


def dot_nn(a, b):
    return lax.dot_general(a, b, (((1,), (0,)), ((), ())), preferred_element_type=F32)


def dot_nt(a, b):
    return lax.dot_general(a, b, (((1,), (1,)), ((), ())), preferred_element_type=F32)


def dot_tn(a, b):
    return lax.dot_general(a, b, (((0,), (0,)), ((), ())), preferred_element_type=F32)


def params(mebibytes):
    return pltpu.CompilerParams(vmem_limit_bytes=mebibytes * MIB)


def regroup_kernel(weight_ref, out_ref, order_ref):
    rows, heads, width = weight_ref.shape
    size = order_ref.shape[0]
    span = size // heads

    @pl.when(pl.program_id(0) == 0)
    def _():
        row = lax.broadcasted_iota(jnp.int32, (size, size), 0)
        column = lax.broadcasted_iota(jnp.int32, (size, size), 1)
        chosen = column == (row % span) * heads + row // span
        order_ref[...] = jnp.where(chosen, 1.0, 0.0).astype(BF16)

    order = order_ref[...]
    for first in range(0, rows, span):
        piece = weight_ref[first : first + span].reshape(size, width)
        by_head = dot_nn(order, piece).astype(BF16)
        for head in range(heads):
            left = (head % 2) * width
            out_ref[head // 2, first : first + span, left : left + width] = by_head[
                head * span : (head + 1) * span
            ]


def regroup(weight, rows):
    depth, heads, width = weight.shape
    pairs = heads // 2
    return pl.pallas_call(
        regroup_kernel,
        grid=(depth // rows,),
        out_shape=jax.ShapeDtypeStruct((pairs, depth, 2 * width), weight.dtype),
        in_specs=[pl.BlockSpec((rows, heads, width), lambda i: (i, 0, 0))],
        out_specs=pl.BlockSpec((pairs, rows, 2 * width), lambda i: (0, i, 0)),
        scratch_shapes=[pltpu.VMEM((256, 256), BF16)],
        compiler_params=params(46),
        cost_estimate=pl.CostEstimate(
            flops=0, bytes_accessed=4 * depth * heads * width, transcendentals=0
        ),
        name="regroup",
    )(weight)


def listed_slots(neighbours_ref, tile_slot_ref):
    tiles, places = neighbours_ref.shape
    one, zero = jnp.int32(1), jnp.int32(0)
    allowed = [[zero] * tiles for _ in range(tiles)]
    for t in range(tiles):
        for u in range(tiles):
            listed = zero
            for k in range(places):
                listed = jnp.where(neighbours_ref[t, k] == u, one, listed)
            for r in range(tiles):
                for c in range(tiles):
                    here = (tile_slot_ref[t] == r) & (tile_slot_ref[u] == c)
                    allowed[r][c] = jnp.where(here, listed, allowed[r][c])
    return allowed


def forward_kernel(
    neighbours_ref,
    tile_slot_ref,
    own_ref,
    other_ref,
    weight_ref,
    out_weight_ref,
    query_gain_ref,
    key_gain_ref,
    gate_ref,
    projected_ref,
    probs_ref,
    attention_ref,
    kept_ref,
    sent_ref,
    tokens_ref,
    bias_ref,
    total_ref,
):
    step = pl.program_id(0)
    part = pl.program_id(1)
    last_part = pl.num_programs(1) - 1
    depth = weight_ref.shape[1]
    local = own_ref.shape[0]
    tokens = 2 * local
    width = query_gain_ref.shape[1]
    heads = probs_ref.shape[0]

    @pl.when((step == 0) & (part == 0))
    def _():
        tokens_ref[:local, :] = own_ref[...]
        tokens_ref[local:, :] = other_ref[...]
        allowed = listed_slots(neighbours_ref, tile_slot_ref)
        mine = lax.axis_index("seq")
        row_half = lax.broadcasted_iota(jnp.int32, (tokens, tokens), 0) // local
        column_half = lax.broadcasted_iota(jnp.int32, (tokens, tokens), 1) // local
        row_slot = jnp.where(row_half == 0, mine, 1 - mine)
        column_slot = jnp.where(column_half == 0, mine, 1 - mine)
        table = jnp.zeros((tokens, tokens), jnp.int32)
        for r in range(2):
            for c in range(2):
                table = jnp.where((row_slot == r) & (column_slot == c), allowed[r][c], table)
        bias_ref[...] = jnp.where(table > 0, 0.0, -jnp.inf).astype(F32)

    def attend(product):
        projected = total_ref[...] + product
        projected_ref[0] = projected
        scale_factor = 1.0 / math.sqrt(width)
        bias = bias_ref[...]
        attended = []
        for head in range(heads):
            left = head * 3 * width
            query = projected[:, left : left + width]
            key = projected[:, left + width : left + 2 * width]
            value = projected[:, left + 2 * width : left + 3 * width].astype(BF16)
            query_inverse = lax.rsqrt(jnp.mean(query * query, axis=-1, keepdims=True) + EPSILON)
            key_inverse = lax.rsqrt(jnp.mean(key * key, axis=-1, keepdims=True) + EPSILON)
            queries = (query * query_inverse * query_gain_ref[...]).astype(BF16)
            keys = (key * key_inverse * key_gain_ref[...]).astype(BF16)
            scores = dot_nt(queries, keys) * scale_factor + bias
            row_max = jnp.max(scores, axis=-1, keepdims=True)
            weights = jnp.exp(scores - row_max)
            probs = (weights / jnp.sum(weights, axis=-1, keepdims=True)).astype(BF16)
            probs_ref[head] = probs
            attended.append(dot_nn(probs, value).astype(BF16))
        share = dot_nn(jnp.concatenate(attended, axis=1), out_weight_ref[...])

        @pl.when(step == 0)
        def _():
            attention_ref[...] = share

        @pl.when(step > 0)
        def _():
            attention_ref[...] += share

        @pl.when(step == pl.num_programs(0) - 1)
        def _():
            gate = gate_ref[...]
            kept_ref[...] = (own_ref[...].astype(F32) + gate * attention_ref[:local, :]).astype(BF16)
            sent_ref[...] = (gate * attention_ref[local:, :]).astype(BF16)

    columns = pl.ds(pl.multiple_of(part * depth, depth), depth)
    product = dot_nn(tokens_ref[:, columns], weight_ref[0])

    @pl.when(part == 0)
    def _():
        total_ref[...] = product

    @pl.when((part > 0) & (part < last_part))
    def _():
        total_ref[...] += product

    @pl.when(part == last_part)
    def _():
        attend(product)


def forward(neighbours, tile_slot, own, other, weight, out_weight, query_gain, key_gain, gate):
    local, model = own.shape
    pairs, _, wide = weight.shape
    head_dim = query_gain.shape[1]
    tokens = 2 * local
    whole = lambda i, k: (0, 0)
    parts = 4
    smem = pl.BlockSpec(memory_space=pltpu.SMEM)
    return pl.pallas_call(
        forward_kernel,
        grid=(pairs, parts),
        out_shape=(
            jax.ShapeDtypeStruct((pairs, tokens, wide), F32),
            jax.ShapeDtypeStruct((2 * pairs, tokens, tokens), BF16),
            jax.ShapeDtypeStruct((tokens, model), F32),
            jax.ShapeDtypeStruct((local, model), BF16),
            jax.ShapeDtypeStruct((local, model), BF16),
        ),
        in_specs=[
            smem,
            smem,
            pl.BlockSpec((local, model), whole),
            pl.BlockSpec((local, model), whole),
            pl.BlockSpec((1, model // parts, wide), lambda i, k: (i, k, 0)),
            pl.BlockSpec((2 * head_dim, model), lambda i, k: (i, 0)),
            pl.BlockSpec((1, head_dim), whole),
            pl.BlockSpec((1, head_dim), whole),
            pl.BlockSpec((1, model), whole),
        ],
        out_specs=(
            pl.BlockSpec((1, tokens, wide), lambda i, k: (i, 0, 0)),
            pl.BlockSpec((2, tokens, tokens), lambda i, k: (i, 0, 0)),
            pl.BlockSpec((tokens, model), whole),
            pl.BlockSpec((local, model), whole),
            pl.BlockSpec((local, model), whole),
        ),
        scratch_shapes=[
            pltpu.VMEM((tokens, model), BF16),
            pltpu.VMEM((tokens, tokens), F32),
            pltpu.VMEM((tokens, wide), F32),
        ],
        compiler_params=params(46),
        cost_estimate=pl.CostEstimate(
            flops=2 * tokens * model * pairs * (wide + 2 * head_dim),
            bytes_accessed=2 * model * pairs * (wide + 2 * head_dim),
            transcendentals=0,
        ),
        name="attention_forward",
    )(neighbours, tile_slot, own, other, weight, out_weight, query_gain, key_gain, gate)


def backward_kernel(
    own_ref,
    other_ref,
    out_weight_ref,
    projected_ref,
    probs_ref,
    attention_ref,
    query_gain_ref,
    key_gain_ref,
    gate_ref,
    grad_ref,
    gate_grad_ref,
    scaled_ref,
):
    step = pl.program_id(0)
    local = own_ref.shape[0]
    width = query_gain_ref.shape[1]
    heads = probs_ref.shape[0]
    columns = attention_ref.shape[1]

    @pl.when(step == 0)
    def _():
        gate = gate_ref[...]
        scaled_ref[:local, :] = (own_ref[...].astype(F32) * gate).astype(BF16)
        scaled_ref[local:, :] = (other_ref[...].astype(F32) * gate).astype(BF16)

    part = pl.ds(pl.multiple_of(step * columns, columns), columns)
    gate_grad_ref[...] = jnp.sum(
        own_ref[:, part].astype(F32) * attention_ref[:local, :], axis=0, keepdims=True
    ) + jnp.sum(other_ref[:, part].astype(F32) * attention_ref[local:, :], axis=0, keepdims=True)

    attended_grad = dot_nt(scaled_ref[...], out_weight_ref[...]).astype(BF16)
    scale_factor = 1.0 / math.sqrt(width)
    for head in range(heads):
        left = head * 3 * width
        query = projected_ref[0, :, left : left + width]
        key = projected_ref[0, :, left + width : left + 2 * width]
        value = projected_ref[0, :, left + 2 * width : left + 3 * width].astype(BF16)
        query_inverse = lax.rsqrt(jnp.mean(query * query, axis=-1, keepdims=True) + EPSILON)
        key_inverse = lax.rsqrt(jnp.mean(key * key, axis=-1, keepdims=True) + EPSILON)
        query_unit = query * query_inverse
        key_unit = key * key_inverse
        queries = (query_unit * query_gain_ref[...]).astype(BF16)
        keys = (key_unit * key_gain_ref[...]).astype(BF16)
        grad = attended_grad[:, head * width : (head + 1) * width]
        probs = probs_ref[head]
        probs_wide = probs.astype(F32)
        value_grad = dot_tn(probs, grad)
        prob_grad = dot_nt(grad, value)
        row_delta = jnp.sum(probs_wide * prob_grad, axis=-1, keepdims=True)
        score_grad = (probs_wide * (prob_grad - row_delta) * scale_factor).astype(BF16)
        query_scaled = dot_nn(score_grad, keys) * query_gain_ref[...]
        key_scaled = dot_tn(score_grad, queries) * key_gain_ref[...]
        query_mean = jnp.mean(query_scaled * query_unit, axis=-1, keepdims=True)
        key_mean = jnp.mean(key_scaled * key_unit, axis=-1, keepdims=True)
        grad_ref[0, :, left : left + width] = (
            (query_scaled - query_unit * query_mean) * query_inverse
        ).astype(BF16)
        grad_ref[0, :, left + width : left + 2 * width] = (
            (key_scaled - key_unit * key_mean) * key_inverse
        ).astype(BF16)
        grad_ref[0, :, left + 2 * width : left + 3 * width] = value_grad.astype(BF16)


def backward(own, other, out_weight, projected, probs, attention, query_gain, key_gain, gate):
    local, model = own.shape
    pairs, tokens, wide = projected.shape
    head_dim = query_gain.shape[1]
    whole = lambda i: (0, 0)
    return pl.pallas_call(
        backward_kernel,
        grid=(pairs,),
        out_shape=(
            jax.ShapeDtypeStruct((pairs, tokens, wide), BF16),
            jax.ShapeDtypeStruct((1, model), F32),
        ),
        in_specs=[
            pl.BlockSpec((local, model), whole),
            pl.BlockSpec((local, model), whole),
            pl.BlockSpec((2 * head_dim, model), lambda i: (i, 0)),
            pl.BlockSpec((1, tokens, wide), lambda i: (i, 0, 0)),
            pl.BlockSpec((2, tokens, tokens), lambda i: (i, 0, 0)),
            pl.BlockSpec((tokens, model // pairs), lambda i: (0, i)),
            pl.BlockSpec((1, head_dim), whole),
            pl.BlockSpec((1, head_dim), whole),
            pl.BlockSpec((1, model), whole),
        ],
        out_specs=(
            pl.BlockSpec((1, tokens, wide), lambda i: (i, 0, 0)),
            pl.BlockSpec((1, model // pairs), lambda i: (0, i)),
        ),
        scratch_shapes=[pltpu.VMEM((tokens, model), BF16)],
        compiler_params=params(46),
        cost_estimate=pl.CostEstimate(
            flops=2 * tokens * model * pairs * 2 * head_dim,
            bytes_accessed=2 * model * pairs * 2 * head_dim,
            transcendentals=0,
        ),
        name="attention_backward",
    )(own, other, out_weight, projected, probs, attention, query_gain, key_gain, gate)


def input_grad_kernel(grad_ref, weight_ref, own_ref, kept_ref, sent_ref):
    local = own_ref.shape[0]
    total = dot_nt(grad_ref[0], weight_ref[0])
    for pair in range(1, grad_ref.shape[0]):
        total += dot_nt(grad_ref[pair], weight_ref[pair])
    kept_ref[...] = (own_ref[...].astype(F32) + total[:local]).astype(BF16)
    sent_ref[...] = total[local:].astype(BF16)


def input_grad_part(grad, weight, own, part, parts, block):
    local, model = own.shape
    pairs, tokens, wide = grad.shape
    columns = model // parts
    first = part * columns // block
    out = jax.ShapeDtypeStruct((local, columns), BF16)
    out_spec = pl.BlockSpec((local, block), lambda i: (0, i))
    return pl.pallas_call(
        input_grad_kernel,
        grid=(columns // block,),
        out_shape=(out, out),
        in_specs=[
            pl.BlockSpec((pairs, tokens, wide), lambda i: (0, 0, 0)),
            pl.BlockSpec((pairs, block, wide), lambda i: (0, i + first, 0)),
            pl.BlockSpec((local, block), lambda i: (0, i + first)),
        ],
        out_specs=(out_spec, out_spec),
        compiler_params=params(46),
        cost_estimate=pl.CostEstimate(
            flops=2 * tokens * columns * pairs * wide,
            bytes_accessed=2 * columns * pairs * wide,
            transcendentals=0,
        ),
        name="input_grad",
    )(grad, weight, own)


def routed(block, seq_step, pipe_step):
    seq_size, pipe_size = lax.axis_size("seq"), lax.axis_size("pipe")
    route = []
    for i in range(seq_size):
        for j in range(pipe_size):
            target = (i + seq_step) % seq_size * pipe_size + (j + pipe_step) % pipe_size
            route.append((i * pipe_size + j, target))
    return lax.ppermute(block, ("seq", "pipe"), route)


def pair_body(
    segment_input,
    output_grad,
    qkv_weight,
    out_weight,
    query_gain,
    key_gain,
    gate_scale,
    neighbours,
    tile_slot,
):
    stream = segment_input[0]
    upstream = output_grad[0]
    out_local = out_weight[0]
    model = stream.shape[1]
    other_stream = routed(stream, 1, 0)
    weight = regroup(qkv_weight[0], 128)
    weight, upstream_after = lax.optimization_barrier((weight, upstream))
    other_upstream = routed(upstream_after, 1, 0)
    projected, probs, attention, kept, sent = forward(
        neighbours,
        tile_slot,
        stream,
        other_stream,
        weight,
        out_local,
        query_gain,
        key_gain,
        gate_scale,
    )
    kept = routed(kept, 0, 1)
    sent = routed(sent, 1, 1)
    grad, gate_share = backward(
        upstream,
        other_upstream,
        out_local,
        projected,
        probs,
        attention,
        query_gain,
        key_gain,
        gate_scale,
    )
    other_gate = routed(gate_share, 1, 0)
    first, second = input_grad_part(grad, weight, upstream, 0, 2, 256)
    pieces = [(routed(first, 0, -1), routed(second, 1, -1))]
    segment_output = (kept.astype(F32) + sent.astype(F32)).astype(BF16)
    half = model // lax.axis_size("seq")
    gate_total = lax.dynamic_slice_in_dim(
        gate_share + other_gate, lax.axis_index("seq") * half, half, 1
    )
    grad, segment_output, gate_total = lax.optimization_barrier((grad, segment_output, gate_total))
    first, second = input_grad_part(grad, weight, upstream, 1, 2, 256)
    pieces.append((routed(first, 0, -1), routed(second, 1, -1)))
    input_grad = jnp.concatenate(
        [(a.astype(F32) + b.astype(F32)).astype(BF16) for a, b in pieces], axis=1
    )
    return (segment_output[None], input_grad[None], gate_total)


def solution(mesh):
    in_specs = (
        P("pipe", ("dp", "seq"), None),
        P("pipe", ("dp", "seq"), None),
        P("pipe", None, "seq", None),
        P("pipe", "seq", None),
        P("pipe", None),
        P("pipe", None),
        P("pipe", None),
        P("dp", None),
        P("dp"),
    )
    out_specs = (
        P("pipe", ("dp", "seq"), None),
        P("pipe", ("dp", "seq"), None),
        P(("dp", "pipe"), "seq"),
    )

    def body(*args):
        one_tile_each = args[0].shape[1] == TILE and args[8].shape[0] == 2
        if mesh.shape["seq"] == 2 and one_tile_each and args[2].shape[2] % 2 == 0:
            return pair_body(*args)
        return general_body(*args)

    return jax.shard_map(body, mesh=mesh, in_specs=in_specs, out_specs=out_specs, check_vma=False)
```

```python
import functools
import math

import jax
import jax.numpy as jnp
from jax import lax
from jax.experimental import pallas as pl
from jax.experimental.pallas import tpu as pltpu
from jax.sharding import PartitionSpec as P

TILE = 64
EPSILON = 1e-06
F32 = jnp.float32
BF16 = jnp.bfloat16
MIB = 1024 * 1024


def passed_along(block, axis, distance):
    devices = range(lax.axis_size(axis))
    route = [((i - distance) % len(devices), i) for i in devices]
    return lax.ppermute(block, axis, route)


def slot_lists(neighbours, tile_slot):
    tile_count = tile_slot.shape[0]
    numbering = jnp.arange(tile_count, dtype=jnp.int32)
    placed = (tile_slot[:, None] == numbering[None, :]).astype(jnp.int32)
    tile_of_slot = jnp.sum(placed * numbering[:, None], axis=0)
    chosen = (tile_of_slot[:, None] == numbering[None, :]).astype(jnp.int32)
    listed_tiles = jnp.sum(chosen[:, :, None] * neighbours[None, :, :], axis=1)
    key_valid = listed_tiles >= 0
    safe_tiles = jnp.maximum(listed_tiles, 0)
    matches = (safe_tiles[:, :, None] == numbering[None, None, :]).astype(jnp.int32)
    key_slots = jnp.sum(matches * tile_slot[None, None, :], axis=2)
    return (key_slots, key_valid)


def block_tiles(tile_count):
    return math.gcd(tile_count, max(1, 512 // TILE))


def unit_norm(values):
    spread = jnp.sqrt(jnp.mean(values * values, axis=-1, keepdims=True) + EPSILON)
    return (values / spread, spread)


def probabilities(query_block, key_rows, block_valid):
    scores = jnp.einsum(
        "aihd,ajhd->ahij", query_block, key_rows, preferred_element_type=jnp.float32
    ) * (1.0 / math.sqrt(query_block.shape[-1]))
    key_mask = jnp.repeat(block_valid, TILE, axis=1)
    scores = jnp.where(key_mask[:, None, None, :], scores, -jnp.inf)
    row_max = jnp.max(scores, axis=-1, keepdims=True)
    weights = jnp.exp(scores - row_max)
    return (weights / jnp.sum(weights, axis=-1, keepdims=True)).astype(jnp.bfloat16)


def gathered(tiles_array, block_slots):
    picked = tiles_array[block_slots]
    return picked.reshape(block_slots.shape[0], -1, tiles_array.shape[2], tiles_array.shape[3])


def attend_both(query_tiles, key_tiles, value_tiles, grad_tiles, key_slots, key_valid):
    tile_count = query_tiles.shape[0]
    span = block_tiles(tile_count)
    scale_factor = 1.0 / math.sqrt(query_tiles.shape[-1])
    empty_grad = jnp.zeros(query_tiles.shape, jnp.float32)

    def per_block(accumulators, block_index):
        key_total, value_total = accumulators
        first_tile = block_index * span
        query_block = lax.dynamic_slice_in_dim(query_tiles, first_tile, span, 0)
        grad_block = lax.dynamic_slice_in_dim(grad_tiles, first_tile, span, 0)
        block_slots = lax.dynamic_slice_in_dim(key_slots, first_tile, span, 0)
        block_valid = lax.dynamic_slice_in_dim(key_valid, first_tile, span, 0)
        key_rows = gathered(key_tiles, block_slots)
        value_rows = gathered(value_tiles, block_slots)
        weights = probabilities(query_block, key_rows, block_valid)
        attended = jnp.einsum(
            "ahij,ajhd->aihd", weights, value_rows, preferred_element_type=jnp.float32
        )
        value_part = jnp.einsum(
            "ahij,aihd->ajhd", weights, grad_block, preferred_element_type=jnp.float32
        )
        prob_grad = jnp.einsum(
            "aihd,ajhd->ahij", grad_block, value_rows, preferred_element_type=jnp.float32
        )
        weights_wide = weights.astype(jnp.float32)
        row_delta = jnp.sum(weights_wide * prob_grad, axis=-1, keepdims=True)
        score_grad = (weights_wide * (prob_grad - row_delta) * scale_factor).astype(jnp.bfloat16)
        query_part = jnp.einsum(
            "ahij,ajhd->aihd", score_grad, key_rows, preferred_element_type=jnp.float32
        )
        key_part = jnp.einsum(
            "ahij,aihd->ajhd", score_grad, query_block, preferred_element_type=jnp.float32
        )
        block_shape = (span, block_slots.shape[1]) + query_tiles.shape[1:]
        key_total = key_total.at[block_slots].add(key_part.reshape(block_shape))
        value_total = value_total.at[block_slots].add(value_part.reshape(block_shape))
        return ((key_total, value_total), (attended, query_part))

    totals, parts = lax.scan(
        per_block, (empty_grad, empty_grad), jnp.arange(tile_count // span, dtype=jnp.int32)
    )
    flat_shape = (-1,) + query_tiles.shape[2:]
    return (
        parts[0].reshape(flat_shape),
        parts[1].reshape(flat_shape),
        totals[0].reshape(flat_shape),
        totals[1].reshape(flat_shape),
    )


def general_body(
    segment_input,
    output_grad,
    qkv_weight,
    out_weight,
    query_gain,
    key_gain,
    gate_scale,
    neighbours,
    tile_slot,
):
    key_slots, key_valid = slot_lists(neighbours, tile_slot)
    stream = segment_input[0]
    upstream = output_grad[0]
    model_width = stream.shape[1]
    head_dim = query_gain.shape[1]
    local_heads = qkv_weight.shape[2]
    local_width = local_heads * head_dim
    proj_weight = qkv_weight[0].reshape(model_width, local_heads * 3 * head_dim)
    out_local = out_weight[0]
    gate_row = gate_scale[0]
    query_weights = query_gain[0]
    key_weights = key_gain[0]
    projected = jnp.dot(
        lax.all_gather(stream, "seq", axis=0, tiled=True),
        proj_weight,
        preferred_element_type=jnp.float32,
    )
    all_tokens = projected.shape[0]
    projected = projected.reshape(all_tokens, local_heads, 3, head_dim)
    query_unit, query_spread = unit_norm(projected[:, :, 0])
    key_unit, key_spread = unit_norm(projected[:, :, 1])
    queries = (query_unit * query_weights).astype(jnp.bfloat16)
    keys_normed = (key_unit * key_weights).astype(jnp.bfloat16)
    value_rows = projected[:, :, 2].astype(jnp.bfloat16)
    scaled = (upstream.astype(jnp.float32) * gate_row).astype(jnp.bfloat16)
    attended_grad = jnp.einsum(
        "td,cd->tc",
        lax.all_gather(scaled, "seq", axis=0, tiled=True),
        out_local,
        preferred_element_type=jnp.float32,
    ).astype(jnp.bfloat16)

    def as_tiles(values):
        return values.reshape(-1, TILE, local_heads, head_dim)

    attended, query_grad, key_grad, value_grad = attend_both(
        as_tiles(queries),
        as_tiles(keys_normed),
        as_tiles(value_rows),
        as_tiles(attended_grad),
        key_slots,
        key_valid,
    )
    attended_low = attended.astype(jnp.bfloat16).reshape(all_tokens, local_width)
    rows = attended_low
    attention_out = lax.psum_scatter(
        jnp.dot(rows, out_local, preferred_element_type=jnp.float32),
        "seq",
        scatter_dimension=0,
        tiled=True,
    )
    section_out = (stream.astype(jnp.float32) + gate_row * attention_out).astype(jnp.bfloat16)
    segment_output = passed_along(section_out, "pipe", 1)
    gate_local = lax.psum_scatter(
        jnp.sum(upstream.astype(jnp.float32) * attention_out, axis=0),
        "seq",
        scatter_dimension=0,
        tiled=True,
    )
    query_scaled = query_grad * query_weights
    query_part_grad = (
        query_scaled - query_unit * jnp.mean(query_scaled * query_unit, axis=-1, keepdims=True)
    ) / query_spread
    key_scaled = key_grad * key_weights
    key_part_grad = (
        key_scaled - key_unit * jnp.mean(key_scaled * key_unit, axis=-1, keepdims=True)
    ) / key_spread
    projected_grad = (
        jnp.stack([query_part_grad, key_part_grad, value_grad], axis=2)
        .astype(jnp.bfloat16)
        .reshape(all_tokens, local_heads * 3 * head_dim)
    )
    rows = projected_grad
    stream_grad = lax.psum_scatter(
        jnp.einsum("tc,dc->td", rows, proj_weight, preferred_element_type=jnp.float32).astype(
            jnp.bfloat16
        ),
        "seq",
        scatter_dimension=0,
        tiled=True,
    ).astype(jnp.float32)
    token_grad = (upstream.astype(jnp.float32) + stream_grad).astype(jnp.bfloat16)
    input_grad = passed_along(token_grad, "pipe", -1)
    return (segment_output[None], input_grad[None], gate_local[None])


def dot_nn(a, b):
    return lax.dot_general(a, b, (((1,), (0,)), ((), ())), preferred_element_type=F32)


def dot_nt(a, b):
    return lax.dot_general(a, b, (((1,), (1,)), ((), ())), preferred_element_type=F32)


def dot_tn(a, b):
    return lax.dot_general(a, b, (((0,), (0,)), ((), ())), preferred_element_type=F32)


def params(mebibytes):
    return pltpu.CompilerParams(vmem_limit_bytes=mebibytes * MIB)


class Copies:
    def __init__(self, pairs, semaphores, ahead):
        self.copies = [
            pltpu.make_async_copy(source, target, semaphores.at[i])
            for i, (source, target) in enumerate(pairs)
        ]
        self.ahead = ahead
        self.waited = 0
        for copy in self.copies[:ahead]:
            copy.start()

    def wait(self, count=1):
        for _ in range(count):
            self.copies[self.waited].wait()
            following = self.waited + self.ahead
            if following < len(self.copies):
                self.copies[following].start()
            self.waited += 1


def regroup_kernel(rows, ahead, weight_ref, out_ref, read_ref, written_ref, reads, writes):
    depth, heads, width = weight_ref.shape
    steps = depth // rows

    def part(step):
        return pl.ds(pl.multiple_of(step * rows, rows), rows)

    def read(step):
        return pltpu.make_async_copy(
            weight_ref.at[part(step)], read_ref.at[part(step)], reads.at[step]
        )

    def write(step):
        return pltpu.make_async_copy(
            written_ref.at[:, part(step)], out_ref.at[:, part(step)], writes.at[step]
        )

    for step in range(ahead):
        read(step).start()

    @pl.loop(0, steps)
    def _(step):
        read(step).wait()

        @pl.when(step + ahead < steps)
        def _():
            read(step + ahead).start()

        by_head = jnp.swapaxes(read_ref[part(step)], 0, 1)
        for head in range(heads):
            left = (head % 2) * width
            written_ref[head // 2, part(step), left : left + width] = by_head[head]
        write(step).start()

    @pl.loop(0, steps)
    def _(step):
        write(step).wait()


def regroup(weight, rows, ahead):
    depth, heads, width = weight.shape
    out = (heads // 2, depth, 2 * width)
    return pl.pallas_call(
        functools.partial(regroup_kernel, rows, ahead),
        out_shape=jax.ShapeDtypeStruct(out, weight.dtype),
        in_specs=[pl.BlockSpec(memory_space=pl.ANY)],
        out_specs=pl.BlockSpec(memory_space=pl.ANY),
        scratch_shapes=[
            pltpu.VMEM(weight.shape, weight.dtype),
            pltpu.VMEM(out, weight.dtype),
            pltpu.SemaphoreType.DMA((depth // rows,)),
            pltpu.SemaphoreType.DMA((depth // rows,)),
        ],
        compiler_params=params(46),
        cost_estimate=pl.CostEstimate(
            flops=0, bytes_accessed=4 * depth * heads * width, transcendentals=0
        ),
        name="regroup",
    )(weight)


def listed_slots(neighbours_ref, tile_slot_ref):
    tiles, places = neighbours_ref.shape
    one, zero = jnp.int32(1), jnp.int32(0)
    allowed = [[zero] * tiles for _ in range(tiles)]
    for t in range(tiles):
        for u in range(tiles):
            listed = zero
            for k in range(places):
                listed = jnp.where(neighbours_ref[t, k] == u, one, listed)
            for r in range(tiles):
                for c in range(tiles):
                    here = (tile_slot_ref[t] == r) & (tile_slot_ref[u] == c)
                    allowed[r][c] = jnp.where(here, listed, allowed[r][c])
    return allowed


def normed(rows, gain):
    inverse = lax.rsqrt(jnp.mean(rows * rows, axis=-1, keepdims=True) + EPSILON)
    unit = rows * inverse
    return unit, inverse, (unit * gain).astype(BF16)


def forward_kernel(
    neighbours_ref,
    tile_slot_ref,
    own_ref,
    other_ref,
    weight_ref,
    out_weight_ref,
    query_gain_ref,
    key_gain_ref,
    gate_ref,
    projected_ref,
    probs_ref,
    attention_ref,
    kept_ref,
    sent_ref,
    tokens_ref,
    weight_buffer,
    out_weight_buffer,
    semaphores,
):
    local, model = own_ref.shape
    tokens = 2 * local
    width = query_gain_ref.shape[1]
    pairs = weight_ref.shape[0]
    halves = 2
    half = model // halves

    def weight_part(pair, index):
        place = (pair, pl.ds(index * half, half))
        return weight_ref.at[place], weight_buffer.at[place]

    def out_weight_part(pair):
        place = pl.ds(pair * 2 * width, 2 * width)
        return out_weight_ref.at[place], out_weight_buffer.at[place]

    order = [weight_part(0, 0), weight_part(0, 1)]
    for pair in range(1, pairs):
        order += [weight_part(pair, 0), weight_part(pair, 1), out_weight_part(pair - 1)]
    order.append(out_weight_part(pairs - 1))
    copies = Copies(order, semaphores, 3)

    tokens_ref[:local, :] = own_ref[...]
    tokens_ref[local:, :] = other_ref[...]
    allowed = listed_slots(neighbours_ref, tile_slot_ref)
    mine = lax.axis_index("seq")
    row_half = lax.broadcasted_iota(jnp.int32, (tokens, tokens), 0) // local
    column_half = lax.broadcasted_iota(jnp.int32, (tokens, tokens), 1) // local
    row_slot = jnp.where(row_half == 0, mine, 1 - mine)
    column_slot = jnp.where(column_half == 0, mine, 1 - mine)
    table = jnp.zeros((tokens, tokens), jnp.int32)
    for r in range(2):
        for c in range(2):
            table = jnp.where((row_slot == r) & (column_slot == c), allowed[r][c], table)
    bias = jnp.where(table > 0, 0.0, -jnp.inf).astype(F32)

    def project(pair):
        total = None
        for index in range(halves):
            part = slice(index * half, (index + 1) * half)
            product = dot_nn(tokens_ref[:, part], weight_buffer[pair, part, :])
            total = product if total is None else total + product
        projected_ref[pair] = total

    def attend(pair):
        attended = []
        for head in range(2):
            left = head * 3 * width
            _, _, queries = normed(projected_ref[pair, :, left : left + width], query_gain_ref[...])
            left += width
            _, _, keys = normed(projected_ref[pair, :, left : left + width], key_gain_ref[...])
            left += width
            value = projected_ref[pair, :, left : left + width].astype(BF16)
            scores = dot_nt(queries, keys) * (1.0 / math.sqrt(width)) + bias
            row_max = jnp.max(scores, axis=-1, keepdims=True)
            weights = jnp.exp(scores - row_max)
            probs = (weights / jnp.sum(weights, axis=-1, keepdims=True)).astype(BF16)
            probs_ref[2 * pair + head] = probs
            attended.append(dot_nn(probs, value).astype(BF16))
        return jnp.concatenate(attended, axis=1)

    copies.wait(halves)
    project(0)
    for pair in range(pairs):
        if pair + 1 < pairs:
            copies.wait(halves + 1)
            project(pair + 1)
        else:
            copies.wait()
        part = slice(pair * 2 * width, (pair + 1) * 2 * width)
        share = dot_nn(attend(pair), out_weight_buffer[part, :])
        if pair == 0:
            attention_ref[...] = share
        elif pair + 1 < pairs:
            attention_ref[...] += share
        else:
            total = attention_ref[...] + share
            attention_ref[...] = total
            gate = gate_ref[...]
            kept_ref[...] = (own_ref[...].astype(F32) + gate * total[:local]).astype(BF16)
            sent_ref[...] = (gate * total[local:]).astype(BF16)


def forward(neighbours, tile_slot, own, other, weight, out_weight, query_gain, key_gain, gate):
    local, model = own.shape
    pairs, _, wide = weight.shape
    tokens = 2 * local
    smem = pl.BlockSpec(memory_space=pltpu.SMEM)
    vmem = pl.BlockSpec(memory_space=pltpu.VMEM)
    hbm = pl.BlockSpec(memory_space=pl.ANY)
    return pl.pallas_call(
        forward_kernel,
        out_shape=(
            jax.ShapeDtypeStruct((pairs, tokens, wide), F32),
            jax.ShapeDtypeStruct((2 * pairs, tokens, tokens), BF16),
            jax.ShapeDtypeStruct((tokens, model), F32),
            jax.ShapeDtypeStruct((local, model), BF16),
            jax.ShapeDtypeStruct((local, model), BF16),
        ),
        in_specs=[smem, smem, vmem, vmem, hbm, hbm, vmem, vmem, vmem],
        out_specs=(vmem,) * 5,
        scratch_shapes=[
            pltpu.VMEM((tokens, model), BF16),
            pltpu.VMEM(weight.shape, BF16),
            pltpu.VMEM(out_weight.shape, BF16),
            pltpu.SemaphoreType.DMA((3 * pairs,)),
        ],
        compiler_params=params(46),
        cost_estimate=pl.CostEstimate(
            flops=2 * tokens * (weight.size + out_weight.size),
            bytes_accessed=2 * (weight.size + out_weight.size),
            transcendentals=0,
        ),
        name="attention_forward",
    )(neighbours, tile_slot, own, other, weight, out_weight, query_gain, key_gain, gate)


def input_grad_parts(weight_ref, buffer, first, block):
    return [
        (
            weight_ref.at[:, pl.ds(first + start, block)],
            buffer.at[:, pl.ds(start, block)],
        )
        for start in range(0, buffer.shape[1], block)
    ]


def input_grad_blocks(copies, grad_ref, buffer, own_ref, first, block, kept_ref, sent_ref):
    local = own_ref.shape[0]
    for start in range(0, buffer.shape[1], block):
        copies.wait()
        part = slice(start, start + block)
        total = dot_nt(grad_ref[0], buffer[0, part, :])
        for pair in range(1, grad_ref.shape[0]):
            total += dot_nt(grad_ref[pair], buffer[pair, part, :])
        own = own_ref[:, first + start : first + start + block].astype(F32)
        kept_ref[:, part] = (own + total[:local]).astype(BF16)
        sent_ref[:, part] = total[local:].astype(BF16)


def backward_kernel(
    block,
    own_ref,
    other_ref,
    out_weight_ref,
    weight_ref,
    projected_ref,
    probs_ref,
    attention_ref,
    query_gain_ref,
    key_gain_ref,
    gate_ref,
    grad_ref,
    gate_grad_ref,
    kept_ref,
    sent_ref,
    scaled_ref,
    attended_grad_ref,
    out_weight_buffer,
    weight_buffer,
    semaphores,
):
    local = own_ref.shape[0]
    width = query_gain_ref.shape[1]
    pairs = grad_ref.shape[0]
    order = []
    for pair in range(pairs):
        place = pl.ds(pair * 2 * width, 2 * width)
        order.append((out_weight_ref.at[place], out_weight_buffer.at[place]))
    order += input_grad_parts(weight_ref, weight_buffer, 0, block)
    copies = Copies(order, semaphores, 4)

    gate = gate_ref[...]
    own, other = own_ref[...].astype(F32), other_ref[...].astype(F32)
    scaled_ref[:local, :] = (own * gate).astype(BF16)
    scaled_ref[local:, :] = (other * gate).astype(BF16)
    gate_grad_ref[...] = jnp.sum(
        own * attention_ref[:local, :] + other * attention_ref[local:, :], axis=0, keepdims=True
    )

    def attended_grad(pair):
        part = slice(pair * 2 * width, (pair + 1) * 2 * width)
        product = dot_nt(scaled_ref[...], out_weight_buffer[part, :])
        attended_grad_ref[pair] = product.astype(BF16)

    def attend_backward(pair, head):
        left = head * 3 * width
        query_part = slice(left, left + width)
        key_part = slice(left + width, left + 2 * width)
        value_part = slice(left + 2 * width, left + 3 * width)
        query_gain, key_gain = query_gain_ref[...], key_gain_ref[...]
        query_unit, query_inverse, queries = normed(projected_ref[pair, :, query_part], query_gain)
        key_unit, key_inverse, keys = normed(projected_ref[pair, :, key_part], key_gain)
        value = projected_ref[pair, :, value_part].astype(BF16)
        grad = attended_grad_ref[pair, :, head * width : (head + 1) * width]
        probs = probs_ref[2 * pair + head]
        probs_wide = probs.astype(F32)
        grad_ref[pair, :, value_part] = dot_tn(probs, grad).astype(BF16)
        prob_grad = dot_nt(grad, value)
        row_delta = jnp.sum(probs_wide * prob_grad, axis=-1, keepdims=True)
        scale_factor = 1.0 / math.sqrt(width)
        score_grad = (probs_wide * (prob_grad - row_delta) * scale_factor).astype(BF16)
        query_scaled = dot_nn(score_grad, keys) * query_gain
        key_scaled = dot_tn(score_grad, queries) * key_gain
        query_mean = jnp.mean(query_scaled * query_unit, axis=-1, keepdims=True)
        key_mean = jnp.mean(key_scaled * key_unit, axis=-1, keepdims=True)
        grad_ref[pair, :, query_part] = (
            (query_scaled - query_unit * query_mean) * query_inverse
        ).astype(BF16)
        grad_ref[pair, :, key_part] = ((key_scaled - key_unit * key_mean) * key_inverse).astype(BF16)

    copies.wait()
    attended_grad(0)
    for pair in range(pairs):
        if pair + 1 < pairs:
            copies.wait()
            attended_grad(pair + 1)
        for head in range(2):
            attend_backward(pair, head)
    input_grad_blocks(copies, grad_ref, weight_buffer, own_ref, 0, block, kept_ref, sent_ref)


def backward(
    own, other, out_weight, weight, projected, probs, attention, query_gain, key_gain, gate, columns
):
    local, model = own.shape
    pairs, tokens, wide = projected.shape
    head_dim = query_gain.shape[1]
    block = 256
    vmem = pl.BlockSpec(memory_space=pltpu.VMEM)
    hbm = pl.BlockSpec(memory_space=pl.ANY)
    return pl.pallas_call(
        functools.partial(backward_kernel, block),
        out_shape=(
            jax.ShapeDtypeStruct((pairs, tokens, wide), BF16),
            jax.ShapeDtypeStruct((1, model), F32),
            jax.ShapeDtypeStruct((local, columns), BF16),
            jax.ShapeDtypeStruct((local, columns), BF16),
        ),
        in_specs=[vmem, vmem, hbm, hbm] + [vmem] * 6,
        out_specs=(vmem,) * 4,
        scratch_shapes=[
            pltpu.VMEM((tokens, model), BF16),
            pltpu.VMEM((pairs, tokens, 2 * head_dim), BF16),
            pltpu.VMEM(out_weight.shape, BF16),
            pltpu.VMEM((pairs, columns, wide), BF16),
            pltpu.SemaphoreType.DMA((pairs + columns // block,)),
        ],
        compiler_params=params(46),
        cost_estimate=pl.CostEstimate(
            flops=2 * tokens * (out_weight.size + pairs * columns * wide),
            bytes_accessed=2 * (out_weight.size + pairs * columns * wide),
            transcendentals=0,
        ),
        name="attention_backward",
    )(own, other, out_weight, weight, projected, probs, attention, query_gain, key_gain, gate)


def input_grad_kernel(first, block, grad_ref, weight_ref, own_ref, kept_ref, sent_ref, buffer, sems):
    copies = Copies(input_grad_parts(weight_ref, buffer, first, block), sems, 4)
    input_grad_blocks(copies, grad_ref, buffer, own_ref, first, block, kept_ref, sent_ref)


def input_grad_part(grad, weight, own, first, columns):
    local, model = own.shape
    pairs, tokens, wide = grad.shape
    block = 256
    out = jax.ShapeDtypeStruct((local, columns), BF16)
    vmem = pl.BlockSpec(memory_space=pltpu.VMEM)
    return pl.pallas_call(
        functools.partial(input_grad_kernel, first, block),
        out_shape=(out, out),
        in_specs=[vmem, pl.BlockSpec(memory_space=pl.ANY), vmem],
        out_specs=(vmem, vmem),
        scratch_shapes=[
            pltpu.VMEM((pairs, columns, wide), BF16),
            pltpu.SemaphoreType.DMA((columns // block,)),
        ],
        compiler_params=params(46),
        cost_estimate=pl.CostEstimate(
            flops=2 * tokens * columns * pairs * wide,
            bytes_accessed=2 * columns * pairs * wide,
            transcendentals=0,
        ),
        name="input_grad",
    )(grad, weight, own)


def routed(block, seq_step, pipe_step):
    seq_size, pipe_size = lax.axis_size("seq"), lax.axis_size("pipe")
    route = []
    for i in range(seq_size):
        for j in range(pipe_size):
            target = (i + seq_step) % seq_size * pipe_size + (j + pipe_step) % pipe_size
            route.append((i * pipe_size + j, target))
    return lax.ppermute(block, ("seq", "pipe"), route)


def pair_body(
    segment_input,
    output_grad,
    qkv_weight,
    out_weight,
    query_gain,
    key_gain,
    gate_scale,
    neighbours,
    tile_slot,
):
    stream = segment_input[0]
    upstream = output_grad[0]
    out_local = out_weight[0]
    model = stream.shape[1]
    other_stream = routed(stream, 1, 0)
    weight = regroup(qkv_weight[0], 128, 6)
    weight, upstream_after = lax.optimization_barrier((weight, upstream))
    other_upstream = routed(upstream_after, 1, 0)
    projected, probs, attention, kept, sent = forward(
        neighbours,
        tile_slot,
        stream,
        other_stream,
        weight,
        out_local,
        query_gain,
        key_gain,
        gate_scale,
    )
    kept = routed(kept, 0, 1)
    sent = routed(sent, 1, 1)
    columns = model // 2
    grad, gate_share, first, second = backward(
        upstream,
        other_upstream,
        out_local,
        weight,
        projected,
        probs,
        attention,
        query_gain,
        key_gain,
        gate_scale,
        columns,
    )
    other_gate = routed(gate_share, 1, 0)
    pieces = [(routed(first, 0, -1), routed(second, 1, -1))]
    segment_output = (kept.astype(F32) + sent.astype(F32)).astype(BF16)
    half = model // lax.axis_size("seq")
    gate_total = lax.dynamic_slice_in_dim(
        gate_share + other_gate, lax.axis_index("seq") * half, half, 1
    )
    grad, segment_output, gate_total = lax.optimization_barrier((grad, segment_output, gate_total))
    first, second = input_grad_part(grad, weight, upstream, columns, model - columns)
    pieces.append((routed(first, 0, -1), routed(second, 1, -1)))
    input_grad = jnp.concatenate(
        [(a.astype(F32) + b.astype(F32)).astype(BF16) for a, b in pieces], axis=1
    )
    return (segment_output[None], input_grad[None], gate_total)


def solution(mesh):
    in_specs = (
        P("pipe", ("dp", "seq"), None),
        P("pipe", ("dp", "seq"), None),
        P("pipe", None, "seq", None),
        P("pipe", "seq", None),
        P("pipe", None),
        P("pipe", None),
        P("pipe", None),
        P("dp", None),
        P("dp"),
    )
    out_specs = (
        P("pipe", ("dp", "seq"), None),
        P("pipe", ("dp", "seq"), None),
        P(("dp", "pipe"), "seq"),
    )

    def body(*args):
        one_tile_each = args[0].shape[1] == TILE and args[8].shape[0] == 2
        if mesh.shape["seq"] == 2 and one_tile_each and args[2].shape[2] % 2 == 0:
            return pair_body(*args)
        return general_body(*args)

    return jax.shard_map(body, mesh=mesh, in_specs=in_specs, out_specs=out_specs, check_vma=False)
```

```python
import functools
import math

import jax
import jax.numpy as jnp
from jax import lax
from jax.experimental import pallas as pl
from jax.experimental.pallas import tpu as pltpu
from jax.sharding import PartitionSpec as P

TILE = 64
EPSILON = 1e-06
F32 = jnp.float32
BF16 = jnp.bfloat16
MIB = 1024 * 1024
GROUP = 4


def passed_along(block, axis, distance):
    devices = range(lax.axis_size(axis))
    route = [((i - distance) % len(devices), i) for i in devices]
    return lax.ppermute(block, axis, route)


def slot_lists(neighbours, tile_slot):
    tile_count = tile_slot.shape[0]
    numbering = jnp.arange(tile_count, dtype=jnp.int32)
    placed = (tile_slot[:, None] == numbering[None, :]).astype(jnp.int32)
    tile_of_slot = jnp.sum(placed * numbering[:, None], axis=0)
    chosen = (tile_of_slot[:, None] == numbering[None, :]).astype(jnp.int32)
    listed_tiles = jnp.sum(chosen[:, :, None] * neighbours[None, :, :], axis=1)
    key_valid = listed_tiles >= 0
    safe_tiles = jnp.maximum(listed_tiles, 0)
    matches = (safe_tiles[:, :, None] == numbering[None, None, :]).astype(jnp.int32)
    key_slots = jnp.sum(matches * tile_slot[None, None, :], axis=2)
    return (key_slots, key_valid)


def block_tiles(tile_count):
    return math.gcd(tile_count, max(1, 512 // TILE))


def unit_norm(values):
    spread = jnp.sqrt(jnp.mean(values * values, axis=-1, keepdims=True) + EPSILON)
    return (values / spread, spread)


def probabilities(query_block, key_rows, block_valid):
    scores = jnp.einsum(
        "aihd,ajhd->ahij", query_block, key_rows, preferred_element_type=jnp.float32
    ) * (1.0 / math.sqrt(query_block.shape[-1]))
    key_mask = jnp.repeat(block_valid, TILE, axis=1)
    scores = jnp.where(key_mask[:, None, None, :], scores, -jnp.inf)
    row_max = jnp.max(scores, axis=-1, keepdims=True)
    weights = jnp.exp(scores - row_max)
    return (weights / jnp.sum(weights, axis=-1, keepdims=True)).astype(jnp.bfloat16)


def gathered(tiles_array, block_slots):
    picked = tiles_array[block_slots]
    return picked.reshape(block_slots.shape[0], -1, tiles_array.shape[2], tiles_array.shape[3])


def attend_both(query_tiles, key_tiles, value_tiles, grad_tiles, key_slots, key_valid):
    tile_count = query_tiles.shape[0]
    span = block_tiles(tile_count)
    scale_factor = 1.0 / math.sqrt(query_tiles.shape[-1])
    empty_grad = jnp.zeros(query_tiles.shape, jnp.float32)

    def per_block(accumulators, block_index):
        key_total, value_total = accumulators
        first_tile = block_index * span
        query_block = lax.dynamic_slice_in_dim(query_tiles, first_tile, span, 0)
        grad_block = lax.dynamic_slice_in_dim(grad_tiles, first_tile, span, 0)
        block_slots = lax.dynamic_slice_in_dim(key_slots, first_tile, span, 0)
        block_valid = lax.dynamic_slice_in_dim(key_valid, first_tile, span, 0)
        key_rows = gathered(key_tiles, block_slots)
        value_rows = gathered(value_tiles, block_slots)
        weights = probabilities(query_block, key_rows, block_valid)
        attended = jnp.einsum(
            "ahij,ajhd->aihd", weights, value_rows, preferred_element_type=jnp.float32
        )
        value_part = jnp.einsum(
            "ahij,aihd->ajhd", weights, grad_block, preferred_element_type=jnp.float32
        )
        prob_grad = jnp.einsum(
            "aihd,ajhd->ahij", grad_block, value_rows, preferred_element_type=jnp.float32
        )
        weights_wide = weights.astype(jnp.float32)
        row_delta = jnp.sum(weights_wide * prob_grad, axis=-1, keepdims=True)
        score_grad = (weights_wide * (prob_grad - row_delta) * scale_factor).astype(jnp.bfloat16)
        query_part = jnp.einsum(
            "ahij,ajhd->aihd", score_grad, key_rows, preferred_element_type=jnp.float32
        )
        key_part = jnp.einsum(
            "ahij,aihd->ajhd", score_grad, query_block, preferred_element_type=jnp.float32
        )
        block_shape = (span, block_slots.shape[1]) + query_tiles.shape[1:]
        key_total = key_total.at[block_slots].add(key_part.reshape(block_shape))
        value_total = value_total.at[block_slots].add(value_part.reshape(block_shape))
        return ((key_total, value_total), (attended, query_part))

    totals, parts = lax.scan(
        per_block, (empty_grad, empty_grad), jnp.arange(tile_count // span, dtype=jnp.int32)
    )
    flat_shape = (-1,) + query_tiles.shape[2:]
    return (
        parts[0].reshape(flat_shape),
        parts[1].reshape(flat_shape),
        totals[0].reshape(flat_shape),
        totals[1].reshape(flat_shape),
    )


def general_body(
    segment_input,
    output_grad,
    qkv_weight,
    out_weight,
    query_gain,
    key_gain,
    gate_scale,
    neighbours,
    tile_slot,
):
    key_slots, key_valid = slot_lists(neighbours, tile_slot)
    stream = segment_input[0]
    upstream = output_grad[0]
    model_width = stream.shape[1]
    head_dim = query_gain.shape[1]
    local_heads = qkv_weight.shape[2]
    local_width = local_heads * head_dim
    proj_weight = qkv_weight[0].reshape(model_width, local_heads * 3 * head_dim)
    out_local = out_weight[0]
    gate_row = gate_scale[0]
    query_weights = query_gain[0]
    key_weights = key_gain[0]
    projected = jnp.dot(
        lax.all_gather(stream, "seq", axis=0, tiled=True),
        proj_weight,
        preferred_element_type=jnp.float32,
    )
    all_tokens = projected.shape[0]
    projected = projected.reshape(all_tokens, local_heads, 3, head_dim)
    query_unit, query_spread = unit_norm(projected[:, :, 0])
    key_unit, key_spread = unit_norm(projected[:, :, 1])
    queries = (query_unit * query_weights).astype(jnp.bfloat16)
    keys_normed = (key_unit * key_weights).astype(jnp.bfloat16)
    value_rows = projected[:, :, 2].astype(jnp.bfloat16)
    scaled = (upstream.astype(jnp.float32) * gate_row).astype(jnp.bfloat16)
    attended_grad = jnp.einsum(
        "td,cd->tc",
        lax.all_gather(scaled, "seq", axis=0, tiled=True),
        out_local,
        preferred_element_type=jnp.float32,
    ).astype(jnp.bfloat16)

    def as_tiles(values):
        return values.reshape(-1, TILE, local_heads, head_dim)

    attended, query_grad, key_grad, value_grad = attend_both(
        as_tiles(queries),
        as_tiles(keys_normed),
        as_tiles(value_rows),
        as_tiles(attended_grad),
        key_slots,
        key_valid,
    )
    attended_low = attended.astype(jnp.bfloat16).reshape(all_tokens, local_width)
    rows = attended_low
    attention_out = lax.psum_scatter(
        jnp.dot(rows, out_local, preferred_element_type=jnp.float32),
        "seq",
        scatter_dimension=0,
        tiled=True,
    )
    section_out = (stream.astype(jnp.float32) + gate_row * attention_out).astype(jnp.bfloat16)
    segment_output = passed_along(section_out, "pipe", 1)
    gate_local = lax.psum_scatter(
        jnp.sum(upstream.astype(jnp.float32) * attention_out, axis=0),
        "seq",
        scatter_dimension=0,
        tiled=True,
    )
    query_scaled = query_grad * query_weights
    query_part_grad = (
        query_scaled - query_unit * jnp.mean(query_scaled * query_unit, axis=-1, keepdims=True)
    ) / query_spread
    key_scaled = key_grad * key_weights
    key_part_grad = (
        key_scaled - key_unit * jnp.mean(key_scaled * key_unit, axis=-1, keepdims=True)
    ) / key_spread
    projected_grad = (
        jnp.stack([query_part_grad, key_part_grad, value_grad], axis=2)
        .astype(jnp.bfloat16)
        .reshape(all_tokens, local_heads * 3 * head_dim)
    )
    rows = projected_grad
    stream_grad = lax.psum_scatter(
        jnp.einsum("tc,dc->td", rows, proj_weight, preferred_element_type=jnp.float32).astype(
            jnp.bfloat16
        ),
        "seq",
        scatter_dimension=0,
        tiled=True,
    ).astype(jnp.float32)
    token_grad = (upstream.astype(jnp.float32) + stream_grad).astype(jnp.bfloat16)
    input_grad = passed_along(token_grad, "pipe", -1)
    return (segment_output[None], input_grad[None], gate_local[None])


def dot_nn(a, b):
    return lax.dot_general(a, b, (((1,), (0,)), ((), ())), preferred_element_type=F32)


def dot_nt(a, b):
    return lax.dot_general(a, b, (((1,), (1,)), ((), ())), preferred_element_type=F32)


def dot_tn(a, b):
    return lax.dot_general(a, b, (((0,), (0,)), ((), ())), preferred_element_type=F32)


def params(mebibytes):
    return pltpu.CompilerParams(vmem_limit_bytes=mebibytes * MIB)


class Copies:
    def __init__(self, pairs, semaphores, ahead):
        self.copies = [
            pltpu.make_async_copy(source, target, semaphores.at[i])
            for i, (source, target) in enumerate(pairs)
        ]
        self.ahead = ahead
        self.waited = 0
        for copy in self.copies[:ahead]:
            copy.start()

    def wait(self, count=1):
        for _ in range(count):
            self.copies[self.waited].wait()
            following = self.waited + self.ahead
            if following < len(self.copies):
                self.copies[following].start()
            self.waited += 1


def regroup_kernel(rows, ahead, weight_ref, out_ref, read_ref, written_ref, reads, writes):
    depth, heads, width = weight_ref.shape
    steps = depth // rows

    def part(step):
        return pl.ds(pl.multiple_of(step * rows, rows), rows)

    def read(step):
        return pltpu.make_async_copy(
            weight_ref.at[part(step)], read_ref.at[part(step)], reads.at[step]
        )

    def write(step):
        return pltpu.make_async_copy(
            written_ref.at[:, part(step)], out_ref.at[:, part(step)], writes.at[step]
        )

    for step in range(ahead):
        read(step).start()

    @pl.loop(0, steps)
    def _(step):
        read(step).wait()

        @pl.when(step + ahead < steps)
        def _():
            read(step + ahead).start()

        by_head = jnp.swapaxes(read_ref[part(step)], 0, 1)
        for head in range(heads):
            left = (head % GROUP) * width
            written_ref[head // GROUP, part(step), left : left + width] = by_head[head]
        write(step).start()

    @pl.loop(0, steps)
    def _(step):
        write(step).wait()


def regroup(weight, rows, ahead):
    depth, heads, width = weight.shape
    out = (heads // GROUP, depth, GROUP * width)
    return pl.pallas_call(
        functools.partial(regroup_kernel, rows, ahead),
        out_shape=jax.ShapeDtypeStruct(out, weight.dtype),
        in_specs=[pl.BlockSpec(memory_space=pl.ANY)],
        out_specs=pl.BlockSpec(memory_space=pl.ANY),
        scratch_shapes=[
            pltpu.VMEM(weight.shape, weight.dtype),
            pltpu.VMEM(out, weight.dtype),
            pltpu.SemaphoreType.DMA((depth // rows,)),
            pltpu.SemaphoreType.DMA((depth // rows,)),
        ],
        compiler_params=params(46),
        cost_estimate=pl.CostEstimate(
            flops=0, bytes_accessed=4 * depth * heads * width, transcendentals=0
        ),
        name="regroup",
    )(weight)


def listed_slots(neighbours_ref, tile_slot_ref):
    tiles, places = neighbours_ref.shape
    one, zero = jnp.int32(1), jnp.int32(0)
    allowed = [[zero] * tiles for _ in range(tiles)]
    for t in range(tiles):
        for u in range(tiles):
            listed = zero
            for k in range(places):
                listed = jnp.where(neighbours_ref[t, k] == u, one, listed)
            for r in range(tiles):
                for c in range(tiles):
                    here = (tile_slot_ref[t] == r) & (tile_slot_ref[u] == c)
                    allowed[r][c] = jnp.where(here, listed, allowed[r][c])
    return allowed


def normed(rows, gain):
    inverse = lax.rsqrt(jnp.mean(rows * rows, axis=-1, keepdims=True) + EPSILON)
    unit = rows * inverse
    return unit, inverse, (unit * gain).astype(BF16)


def forward_kernel(
    neighbours_ref,
    tile_slot_ref,
    own_ref,
    other_ref,
    weight_ref,
    out_weight_ref,
    query_gain_ref,
    key_gain_ref,
    gate_ref,
    projected_ref,
    probs_ref,
    attention_ref,
    kept_ref,
    sent_ref,
    tokens_ref,
    weight_buffer,
    out_weight_buffer,
    semaphores,
):
    local, model = own_ref.shape
    tokens = 2 * local
    width = query_gain_ref.shape[1]
    groups = weight_ref.shape[0]
    parts = 4
    depth = model // parts
    rows = GROUP * width

    def weight_part(group, index):
        place = (group, pl.ds(index * depth, depth))
        return weight_ref.at[place], weight_buffer.at[place]

    def out_weight_part(group):
        place = pl.ds(group * rows, rows)
        return out_weight_ref.at[place], out_weight_buffer.at[place]

    order = []
    for group in range(groups):
        order += [weight_part(group, index) for index in range(parts)]
    order += [out_weight_part(group) for group in range(groups)]
    copies = Copies(order, semaphores, 4)

    tokens_ref[:local, :] = own_ref[...]
    tokens_ref[local:, :] = other_ref[...]
    allowed = listed_slots(neighbours_ref, tile_slot_ref)
    mine = lax.axis_index("seq")
    row_half = lax.broadcasted_iota(jnp.int32, (tokens, tokens), 0) // local
    column_half = lax.broadcasted_iota(jnp.int32, (tokens, tokens), 1) // local
    row_slot = jnp.where(row_half == 0, mine, 1 - mine)
    column_slot = jnp.where(column_half == 0, mine, 1 - mine)
    table = jnp.zeros((tokens, tokens), jnp.int32)
    for r in range(2):
        for c in range(2):
            table = jnp.where((row_slot == r) & (column_slot == c), allowed[r][c], table)
    bias = jnp.where(table > 0, 0.0, -jnp.inf).astype(F32)

    def project(group):
        total = None
        for index in range(parts):
            copies.wait()
            part = slice(index * depth, (index + 1) * depth)
            product = dot_nn(tokens_ref[:, part], weight_buffer[group, part, :])
            total = product if total is None else total + product
        projected_ref[group] = total

    def attend(group):
        attended = []
        for head in range(GROUP):
            left = head * 3 * width
            _, _, queries = normed(projected_ref[group, :, left : left + width], query_gain_ref[...])
            left += width
            _, _, keys = normed(projected_ref[group, :, left : left + width], key_gain_ref[...])
            left += width
            value = projected_ref[group, :, left : left + width].astype(BF16)
            scores = dot_nt(queries, keys) * (1.0 / math.sqrt(width)) + bias
            row_max = jnp.max(scores, axis=-1, keepdims=True)
            weights = jnp.exp(scores - row_max)
            probs = (weights / jnp.sum(weights, axis=-1, keepdims=True)).astype(BF16)
            probs_ref[GROUP * group + head] = probs
            attended.append(dot_nn(probs, value).astype(BF16))
        return jnp.concatenate(attended, axis=1)

    def share(group, attended):
        return dot_nn(attended, out_weight_buffer[group * rows : (group + 1) * rows, :])

    project(0)
    attended = attend(0)
    for group in range(1, groups):
        project(group)
        copies.wait()
        following = attend(group)
        if group == 1:
            attention_ref[...] = share(0, attended)
        else:
            attention_ref[...] += share(group - 1, attended)
        attended = following
    copies.wait()
    total = share(groups - 1, attended)
    if groups > 1:
        total += attention_ref[...]
    attention_ref[...] = total
    gate = gate_ref[...]
    kept_ref[...] = (own_ref[...].astype(F32) + gate * total[:local]).astype(BF16)
    sent_ref[...] = (gate * total[local:]).astype(BF16)


def forward(neighbours, tile_slot, own, other, weight, out_weight, query_gain, key_gain, gate):
    local, model = own.shape
    groups, _, wide = weight.shape
    tokens = 2 * local
    smem = pl.BlockSpec(memory_space=pltpu.SMEM)
    vmem = pl.BlockSpec(memory_space=pltpu.VMEM)
    hbm = pl.BlockSpec(memory_space=pl.ANY)
    return pl.pallas_call(
        forward_kernel,
        out_shape=(
            jax.ShapeDtypeStruct((groups, tokens, wide), F32),
            jax.ShapeDtypeStruct((GROUP * groups, tokens, tokens), BF16),
            jax.ShapeDtypeStruct((tokens, model), F32),
            jax.ShapeDtypeStruct((local, model), BF16),
            jax.ShapeDtypeStruct((local, model), BF16),
        ),
        in_specs=[smem, smem, vmem, vmem, hbm, hbm, vmem, vmem, vmem],
        out_specs=(vmem,) * 5,
        scratch_shapes=[
            pltpu.VMEM((tokens, model), BF16),
            pltpu.VMEM(weight.shape, BF16),
            pltpu.VMEM(out_weight.shape, BF16),
            pltpu.SemaphoreType.DMA((5 * groups,)),
        ],
        compiler_params=params(46),
        cost_estimate=pl.CostEstimate(
            flops=2 * tokens * (weight.size + out_weight.size),
            bytes_accessed=2 * (weight.size + out_weight.size),
            transcendentals=0,
        ),
        name="attention_forward",
    )(neighbours, tile_slot, own, other, weight, out_weight, query_gain, key_gain, gate)


def input_grad_parts(weight_ref, buffer, first, block):
    return [
        (
            weight_ref.at[:, pl.ds(first + start, block)],
            buffer.at[:, pl.ds(start, block)],
        )
        for start in range(0, buffer.shape[1], block)
    ]


def input_grad_blocks(copies, grad_ref, buffer, own_ref, first, block, kept_ref, sent_ref):
    local = own_ref.shape[0]
    for start in range(0, buffer.shape[1], block):
        copies.wait()
        part = slice(start, start + block)
        total = dot_nt(grad_ref[0], buffer[0, part, :])
        for pair in range(1, grad_ref.shape[0]):
            total += dot_nt(grad_ref[pair], buffer[pair, part, :])
        own = own_ref[:, first + start : first + start + block].astype(F32)
        kept_ref[:, part] = (own + total[:local]).astype(BF16)
        sent_ref[:, part] = total[local:].astype(BF16)


def backward_kernel(
    block,
    own_ref,
    other_ref,
    out_weight_ref,
    weight_ref,
    projected_ref,
    probs_ref,
    attention_ref,
    query_gain_ref,
    key_gain_ref,
    gate_ref,
    grad_ref,
    gate_grad_ref,
    kept_ref,
    sent_ref,
    scaled_ref,
    attended_grad_ref,
    out_weight_buffer,
    weight_buffer,
    semaphores,
):
    local = own_ref.shape[0]
    width = query_gain_ref.shape[1]
    groups = grad_ref.shape[0]
    rows = GROUP * width
    order = []
    for start in range(0, groups * rows, rows // 2):
        place = pl.ds(start, rows // 2)
        order.append((out_weight_ref.at[place], out_weight_buffer.at[place]))
    order += input_grad_parts(weight_ref, weight_buffer, 0, block)
    copies = Copies(order, semaphores, 4)

    gate = gate_ref[...]
    own, other = own_ref[...].astype(F32), other_ref[...].astype(F32)
    scaled_ref[:local, :] = (own * gate).astype(BF16)
    scaled_ref[local:, :] = (other * gate).astype(BF16)
    gate_grad_ref[...] = jnp.sum(
        own * attention_ref[:local, :] + other * attention_ref[local:, :], axis=0, keepdims=True
    )

    def attended_grad(group):
        copies.wait(2)
        part = slice(group * rows, (group + 1) * rows)
        product = dot_nt(scaled_ref[...], out_weight_buffer[part, :])
        attended_grad_ref[group] = product.astype(BF16)

    def attend_backward(group, head):
        left = head * 3 * width
        query_part = slice(left, left + width)
        key_part = slice(left + width, left + 2 * width)
        value_part = slice(left + 2 * width, left + 3 * width)
        query_gain, key_gain = query_gain_ref[...], key_gain_ref[...]
        query_unit, query_inverse, queries = normed(projected_ref[group, :, query_part], query_gain)
        key_unit, key_inverse, keys = normed(projected_ref[group, :, key_part], key_gain)
        value = projected_ref[group, :, value_part].astype(BF16)
        grad = attended_grad_ref[group, :, head * width : (head + 1) * width]
        probs = probs_ref[GROUP * group + head]
        probs_wide = probs.astype(F32)
        grad_ref[group, :, value_part] = dot_tn(probs, grad).astype(BF16)
        prob_grad = dot_nt(grad, value)
        row_delta = jnp.sum(probs_wide * prob_grad, axis=-1, keepdims=True)
        scale_factor = 1.0 / math.sqrt(width)
        score_grad = (probs_wide * (prob_grad - row_delta) * scale_factor).astype(BF16)
        query_scaled = dot_nn(score_grad, keys) * query_gain
        key_scaled = dot_tn(score_grad, queries) * key_gain
        query_mean = jnp.mean(query_scaled * query_unit, axis=-1, keepdims=True)
        key_mean = jnp.mean(key_scaled * key_unit, axis=-1, keepdims=True)
        grad_ref[group, :, query_part] = (
            (query_scaled - query_unit * query_mean) * query_inverse
        ).astype(BF16)
        grad_ref[group, :, key_part] = ((key_scaled - key_unit * key_mean) * key_inverse).astype(BF16)

    attended_grad(0)
    for group in range(groups):
        if group + 1 < groups:
            attended_grad(group + 1)
        for head in range(GROUP):
            attend_backward(group, head)
    input_grad_blocks(copies, grad_ref, weight_buffer, own_ref, 0, block, kept_ref, sent_ref)


def backward(
    own, other, out_weight, weight, projected, probs, attention, query_gain, key_gain, gate, columns
):
    local, model = own.shape
    groups, tokens, wide = projected.shape
    head_dim = query_gain.shape[1]
    block = 512
    vmem = pl.BlockSpec(memory_space=pltpu.VMEM)
    hbm = pl.BlockSpec(memory_space=pl.ANY)
    return pl.pallas_call(
        functools.partial(backward_kernel, block),
        out_shape=(
            jax.ShapeDtypeStruct((groups, tokens, wide), BF16),
            jax.ShapeDtypeStruct((1, model), F32),
            jax.ShapeDtypeStruct((local, columns), BF16),
            jax.ShapeDtypeStruct((local, columns), BF16),
        ),
        in_specs=[vmem, vmem, hbm, hbm] + [vmem] * 6,
        out_specs=(vmem,) * 4,
        scratch_shapes=[
            pltpu.VMEM((tokens, model), BF16),
            pltpu.VMEM((groups, tokens, GROUP * head_dim), BF16),
            pltpu.VMEM(out_weight.shape, BF16),
            pltpu.VMEM((groups, columns, wide), BF16),
            pltpu.SemaphoreType.DMA((2 * groups + columns // block,)),
        ],
        compiler_params=params(46),
        cost_estimate=pl.CostEstimate(
            flops=2 * tokens * (out_weight.size + groups * columns * wide),
            bytes_accessed=2 * (out_weight.size + groups * columns * wide),
            transcendentals=0,
        ),
        name="attention_backward",
    )(own, other, out_weight, weight, projected, probs, attention, query_gain, key_gain, gate)


def input_grad_kernel(first, block, grad_ref, weight_ref, own_ref, kept_ref, sent_ref, buffer, sems):
    copies = Copies(input_grad_parts(weight_ref, buffer, first, block), sems, 4)
    input_grad_blocks(copies, grad_ref, buffer, own_ref, first, block, kept_ref, sent_ref)


def input_grad_part(grad, weight, own, first, columns):
    local, model = own.shape
    pairs, tokens, wide = grad.shape
    block = 512
    out = jax.ShapeDtypeStruct((local, columns), BF16)
    vmem = pl.BlockSpec(memory_space=pltpu.VMEM)
    return pl.pallas_call(
        functools.partial(input_grad_kernel, first, block),
        out_shape=(out, out),
        in_specs=[vmem, pl.BlockSpec(memory_space=pl.ANY), vmem],
        out_specs=(vmem, vmem),
        scratch_shapes=[
            pltpu.VMEM((pairs, columns, wide), BF16),
            pltpu.SemaphoreType.DMA((columns // block,)),
        ],
        compiler_params=params(46),
        cost_estimate=pl.CostEstimate(
            flops=2 * tokens * columns * pairs * wide,
            bytes_accessed=2 * columns * pairs * wide,
            transcendentals=0,
        ),
        name="input_grad",
    )(grad, weight, own)


def routed(block, seq_step, pipe_step):
    seq_size, pipe_size = lax.axis_size("seq"), lax.axis_size("pipe")
    route = []
    for i in range(seq_size):
        for j in range(pipe_size):
            target = (i + seq_step) % seq_size * pipe_size + (j + pipe_step) % pipe_size
            route.append((i * pipe_size + j, target))
    return lax.ppermute(block, ("seq", "pipe"), route)


def pair_body(
    segment_input,
    output_grad,
    qkv_weight,
    out_weight,
    query_gain,
    key_gain,
    gate_scale,
    neighbours,
    tile_slot,
):
    stream = segment_input[0]
    upstream = output_grad[0]
    out_local = out_weight[0]
    model = stream.shape[1]
    other_stream = routed(stream, 1, 0)
    weight = regroup(qkv_weight[0], 128, 6)
    weight, upstream_after = lax.optimization_barrier((weight, upstream))
    other_upstream = routed(upstream_after, 1, 0)
    projected, probs, attention, kept, sent = forward(
        neighbours,
        tile_slot,
        stream,
        other_stream,
        weight,
        out_local,
        query_gain,
        key_gain,
        gate_scale,
    )
    kept = routed(kept, 0, 1)
    sent = routed(sent, 1, 1)
    columns = model // 2
    grad, gate_share, first, second = backward(
        upstream,
        other_upstream,
        out_local,
        weight,
        projected,
        probs,
        attention,
        query_gain,
        key_gain,
        gate_scale,
        columns,
    )
    other_gate = routed(gate_share, 1, 0)
    pieces = [(routed(first, 0, -1), routed(second, 1, -1))]
    grad, kept, sent = lax.optimization_barrier((grad, kept, sent))
    first, second = input_grad_part(grad, weight, upstream, columns, model - columns)
    first, second, kept, sent, gate_share, other_gate = lax.optimization_barrier(
        (first, second, kept, sent, gate_share, other_gate)
    )
    pieces.append((routed(first, 0, -1), routed(second, 1, -1)))
    segment_output = (kept.astype(F32) + sent.astype(F32)).astype(BF16)
    half = model // lax.axis_size("seq")
    gate_total = lax.dynamic_slice_in_dim(
        gate_share + other_gate, lax.axis_index("seq") * half, half, 1
    )
    input_grad = jnp.concatenate(
        [(a.astype(F32) + b.astype(F32)).astype(BF16) for a, b in pieces], axis=1
    )
    return (segment_output[None], input_grad[None], gate_total)


def solution(mesh):
    in_specs = (
        P("pipe", ("dp", "seq"), None),
        P("pipe", ("dp", "seq"), None),
        P("pipe", None, "seq", None),
        P("pipe", "seq", None),
        P("pipe", None),
        P("pipe", None),
        P("pipe", None),
        P("dp", None),
        P("dp"),
    )
    out_specs = (
        P("pipe", ("dp", "seq"), None),
        P("pipe", ("dp", "seq"), None),
        P(("dp", "pipe"), "seq"),
    )

    def body(*args):
        one_tile_each = args[0].shape[1] == TILE and args[8].shape[0] == 2
        if mesh.shape["seq"] == 2 and one_tile_each and args[2].shape[2] % GROUP == 0:
            return pair_body(*args)
        return general_body(*args)

    return jax.shard_map(body, mesh=mesh, in_specs=in_specs, out_specs=out_specs, check_vma=False)
```

```python
import functools
import math

import jax
import jax.numpy as jnp
from jax import lax
from jax.experimental import pallas as pl
from jax.experimental.pallas import tpu as pltpu
from jax.sharding import PartitionSpec as P

TILE = 64
EPSILON = 1e-06
F32 = jnp.float32
BF16 = jnp.bfloat16
MIB = 1024 * 1024
GROUP = 4


def passed_along(block, axis, distance):
    devices = range(lax.axis_size(axis))
    route = [((i - distance) % len(devices), i) for i in devices]
    return lax.ppermute(block, axis, route)


def slot_lists(neighbours, tile_slot):
    tile_count = tile_slot.shape[0]
    numbering = jnp.arange(tile_count, dtype=jnp.int32)
    placed = (tile_slot[:, None] == numbering[None, :]).astype(jnp.int32)
    tile_of_slot = jnp.sum(placed * numbering[:, None], axis=0)
    chosen = (tile_of_slot[:, None] == numbering[None, :]).astype(jnp.int32)
    listed_tiles = jnp.sum(chosen[:, :, None] * neighbours[None, :, :], axis=1)
    key_valid = listed_tiles >= 0
    safe_tiles = jnp.maximum(listed_tiles, 0)
    matches = (safe_tiles[:, :, None] == numbering[None, None, :]).astype(jnp.int32)
    key_slots = jnp.sum(matches * tile_slot[None, None, :], axis=2)
    return (key_slots, key_valid)


def block_tiles(tile_count):
    return math.gcd(tile_count, max(1, 512 // TILE))


def unit_norm(values):
    spread = jnp.sqrt(jnp.mean(values * values, axis=-1, keepdims=True) + EPSILON)
    return (values / spread, spread)


def probabilities(query_block, key_rows, block_valid):
    scores = jnp.einsum(
        "aihd,ajhd->ahij", query_block, key_rows, preferred_element_type=jnp.float32
    ) * (1.0 / math.sqrt(query_block.shape[-1]))
    key_mask = jnp.repeat(block_valid, TILE, axis=1)
    scores = jnp.where(key_mask[:, None, None, :], scores, -jnp.inf)
    row_max = jnp.max(scores, axis=-1, keepdims=True)
    weights = jnp.exp(scores - row_max)
    return (weights / jnp.sum(weights, axis=-1, keepdims=True)).astype(jnp.bfloat16)


def gathered(tiles_array, block_slots):
    picked = tiles_array[block_slots]
    return picked.reshape(block_slots.shape[0], -1, tiles_array.shape[2], tiles_array.shape[3])


def attend_both(query_tiles, key_tiles, value_tiles, grad_tiles, key_slots, key_valid):
    tile_count = query_tiles.shape[0]
    span = block_tiles(tile_count)
    scale_factor = 1.0 / math.sqrt(query_tiles.shape[-1])
    empty_grad = jnp.zeros(query_tiles.shape, jnp.float32)

    def per_block(accumulators, block_index):
        key_total, value_total = accumulators
        first_tile = block_index * span
        query_block = lax.dynamic_slice_in_dim(query_tiles, first_tile, span, 0)
        grad_block = lax.dynamic_slice_in_dim(grad_tiles, first_tile, span, 0)
        block_slots = lax.dynamic_slice_in_dim(key_slots, first_tile, span, 0)
        block_valid = lax.dynamic_slice_in_dim(key_valid, first_tile, span, 0)
        key_rows = gathered(key_tiles, block_slots)
        value_rows = gathered(value_tiles, block_slots)
        weights = probabilities(query_block, key_rows, block_valid)
        attended = jnp.einsum(
            "ahij,ajhd->aihd", weights, value_rows, preferred_element_type=jnp.float32
        )
        value_part = jnp.einsum(
            "ahij,aihd->ajhd", weights, grad_block, preferred_element_type=jnp.float32
        )
        prob_grad = jnp.einsum(
            "aihd,ajhd->ahij", grad_block, value_rows, preferred_element_type=jnp.float32
        )
        weights_wide = weights.astype(jnp.float32)
        row_delta = jnp.sum(weights_wide * prob_grad, axis=-1, keepdims=True)
        score_grad = (weights_wide * (prob_grad - row_delta) * scale_factor).astype(jnp.bfloat16)
        query_part = jnp.einsum(
            "ahij,ajhd->aihd", score_grad, key_rows, preferred_element_type=jnp.float32
        )
        key_part = jnp.einsum(
            "ahij,aihd->ajhd", score_grad, query_block, preferred_element_type=jnp.float32
        )
        block_shape = (span, block_slots.shape[1]) + query_tiles.shape[1:]
        key_total = key_total.at[block_slots].add(key_part.reshape(block_shape))
        value_total = value_total.at[block_slots].add(value_part.reshape(block_shape))
        return ((key_total, value_total), (attended, query_part))

    totals, parts = lax.scan(
        per_block, (empty_grad, empty_grad), jnp.arange(tile_count // span, dtype=jnp.int32)
    )
    flat_shape = (-1,) + query_tiles.shape[2:]
    return (
        parts[0].reshape(flat_shape),
        parts[1].reshape(flat_shape),
        totals[0].reshape(flat_shape),
        totals[1].reshape(flat_shape),
    )


def general_body(
    segment_input,
    output_grad,
    qkv_weight,
    out_weight,
    query_gain,
    key_gain,
    gate_scale,
    neighbours,
    tile_slot,
):
    key_slots, key_valid = slot_lists(neighbours, tile_slot)
    stream = segment_input[0]
    upstream = output_grad[0]
    model_width = stream.shape[1]
    head_dim = query_gain.shape[1]
    local_heads = qkv_weight.shape[2]
    local_width = local_heads * head_dim
    proj_weight = qkv_weight[0].reshape(model_width, local_heads * 3 * head_dim)
    out_local = out_weight[0]
    gate_row = gate_scale[0]
    query_weights = query_gain[0]
    key_weights = key_gain[0]
    projected = jnp.dot(
        lax.all_gather(stream, "seq", axis=0, tiled=True),
        proj_weight,
        preferred_element_type=jnp.float32,
    )
    all_tokens = projected.shape[0]
    projected = projected.reshape(all_tokens, local_heads, 3, head_dim)
    query_unit, query_spread = unit_norm(projected[:, :, 0])
    key_unit, key_spread = unit_norm(projected[:, :, 1])
    queries = (query_unit * query_weights).astype(jnp.bfloat16)
    keys_normed = (key_unit * key_weights).astype(jnp.bfloat16)
    value_rows = projected[:, :, 2].astype(jnp.bfloat16)
    scaled = (upstream.astype(jnp.float32) * gate_row).astype(jnp.bfloat16)
    attended_grad = jnp.einsum(
        "td,cd->tc",
        lax.all_gather(scaled, "seq", axis=0, tiled=True),
        out_local,
        preferred_element_type=jnp.float32,
    ).astype(jnp.bfloat16)

    def as_tiles(values):
        return values.reshape(-1, TILE, local_heads, head_dim)

    attended, query_grad, key_grad, value_grad = attend_both(
        as_tiles(queries),
        as_tiles(keys_normed),
        as_tiles(value_rows),
        as_tiles(attended_grad),
        key_slots,
        key_valid,
    )
    attended_low = attended.astype(jnp.bfloat16).reshape(all_tokens, local_width)
    rows = attended_low
    attention_out = lax.psum_scatter(
        jnp.dot(rows, out_local, preferred_element_type=jnp.float32),
        "seq",
        scatter_dimension=0,
        tiled=True,
    )
    section_out = (stream.astype(jnp.float32) + gate_row * attention_out).astype(jnp.bfloat16)
    segment_output = passed_along(section_out, "pipe", 1)
    gate_local = lax.psum_scatter(
        jnp.sum(upstream.astype(jnp.float32) * attention_out, axis=0),
        "seq",
        scatter_dimension=0,
        tiled=True,
    )
    query_scaled = query_grad * query_weights
    query_part_grad = (
        query_scaled - query_unit * jnp.mean(query_scaled * query_unit, axis=-1, keepdims=True)
    ) / query_spread
    key_scaled = key_grad * key_weights
    key_part_grad = (
        key_scaled - key_unit * jnp.mean(key_scaled * key_unit, axis=-1, keepdims=True)
    ) / key_spread
    projected_grad = (
        jnp.stack([query_part_grad, key_part_grad, value_grad], axis=2)
        .astype(jnp.bfloat16)
        .reshape(all_tokens, local_heads * 3 * head_dim)
    )
    rows = projected_grad
    stream_grad = lax.psum_scatter(
        jnp.einsum("tc,dc->td", rows, proj_weight, preferred_element_type=jnp.float32).astype(
            jnp.bfloat16
        ),
        "seq",
        scatter_dimension=0,
        tiled=True,
    ).astype(jnp.float32)
    token_grad = (upstream.astype(jnp.float32) + stream_grad).astype(jnp.bfloat16)
    input_grad = passed_along(token_grad, "pipe", -1)
    return (segment_output[None], input_grad[None], gate_local[None])


def dot_nn(a, b):
    return lax.dot_general(a, b, (((1,), (0,)), ((), ())), preferred_element_type=F32)


def dot_nt(a, b):
    return lax.dot_general(a, b, (((1,), (1,)), ((), ())), preferred_element_type=F32)


def dot_tn(a, b):
    return lax.dot_general(a, b, (((0,), (0,)), ((), ())), preferred_element_type=F32)


def params(mebibytes):
    return pltpu.CompilerParams(vmem_limit_bytes=mebibytes * MIB)


class Copies:
    def __init__(self, pairs, semaphores, ahead):
        self.copies = [
            pltpu.make_async_copy(source, target, semaphores.at[i])
            for i, (source, target) in enumerate(pairs)
        ]
        self.ahead = ahead
        self.waited = 0
        for copy in self.copies[:ahead]:
            copy.start()

    def wait(self, count=1):
        for _ in range(count):
            self.copies[self.waited].wait()
            following = self.waited + self.ahead
            if following < len(self.copies):
                self.copies[following].start()
            self.waited += 1


def regroup_kernel(weight_ref, out_ref, read_ref, reads):
    depth, heads, width = weight_ref.shape
    slots, rows = read_ref.shape[:2]
    steps = depth // rows

    def part(step):
        return pl.ds(pl.multiple_of(step * rows, rows), rows)

    def read(step, slot):
        return pltpu.make_async_copy(
            weight_ref.at[part(step)], read_ref.at[slot], reads.at[slot]
        )

    for slot in range(slots):
        read(slot, slot).start()

    @pl.loop(0, steps)
    def _(step):
        slot = lax.rem(step, slots)
        read(step, slot).wait()
        by_head = jnp.swapaxes(read_ref[slot], 0, 1)
        for head in range(heads):
            left = (head % GROUP) * width
            out_ref[head // GROUP, part(step), left : left + width] = by_head[head]

        @pl.when(step + slots < steps)
        def _():
            read(step + slots, slot).start()


def regroup(weight, rows, slots):
    depth, heads, width = weight.shape
    out = (heads // GROUP, depth, GROUP * width)
    return pl.pallas_call(
        regroup_kernel,
        out_shape=pltpu.VMEM(out, weight.dtype),
        in_specs=[pl.BlockSpec(memory_space=pl.ANY)],
        out_specs=pl.BlockSpec(memory_space=pltpu.VMEM),
        scratch_shapes=[
            pltpu.VMEM((slots, rows, heads, width), weight.dtype),
            pltpu.SemaphoreType.DMA((slots,)),
        ],
        compiler_params=params(12),
        cost_estimate=pl.CostEstimate(
            flops=0, bytes_accessed=4 * depth * heads * width, transcendentals=0
        ),
        name="regroup",
    )(pltpu.with_memory_space_constraint(weight, pltpu.HBM))


def listed_slots(neighbours_ref, tile_slot_ref):
    tiles, places = neighbours_ref.shape
    one, zero = jnp.int32(1), jnp.int32(0)
    allowed = [[zero] * tiles for _ in range(tiles)]
    for t in range(tiles):
        for u in range(tiles):
            listed = zero
            for k in range(places):
                listed = jnp.where(neighbours_ref[t, k] == u, one, listed)
            for r in range(tiles):
                for c in range(tiles):
                    here = (tile_slot_ref[t] == r) & (tile_slot_ref[u] == c)
                    allowed[r][c] = jnp.where(here, listed, allowed[r][c])
    return allowed


def normed(rows, gain):
    inverse = lax.rsqrt(jnp.mean(rows * rows, axis=-1, keepdims=True) + EPSILON)
    unit = rows * inverse
    return unit, inverse, (unit * gain).astype(BF16)


def forward_kernel(
    neighbours_ref,
    tile_slot_ref,
    own_ref,
    other_ref,
    weight_ref,
    out_weight_ref,
    query_gain_ref,
    key_gain_ref,
    gate_ref,
    projected_ref,
    probs_ref,
    attention_ref,
    kept_ref,
    sent_ref,
    out_weight_buffer,
    tokens_ref,
    semaphores,
):
    local, model = own_ref.shape
    tokens = 2 * local
    width = query_gain_ref.shape[1]
    groups = weight_ref.shape[0]
    rows = GROUP * width

    def out_weight_part(group):
        place = pl.ds(group * rows, rows)
        return out_weight_ref.at[place], out_weight_buffer.at[place]

    copies = Copies([out_weight_part(group) for group in range(groups)], semaphores, groups)

    tokens_ref[:local, :] = own_ref[...]
    tokens_ref[local:, :] = other_ref[...]
    allowed = listed_slots(neighbours_ref, tile_slot_ref)
    mine = lax.axis_index("seq")
    row_half = lax.broadcasted_iota(jnp.int32, (tokens, tokens), 0) // local
    column_half = lax.broadcasted_iota(jnp.int32, (tokens, tokens), 1) // local
    row_slot = jnp.where(row_half == 0, mine, 1 - mine)
    column_slot = jnp.where(column_half == 0, mine, 1 - mine)
    table = jnp.zeros((tokens, tokens), jnp.int32)
    for r in range(2):
        for c in range(2):
            table = jnp.where((row_slot == r) & (column_slot == c), allowed[r][c], table)
    bias = jnp.where(table > 0, 0.0, -jnp.inf).astype(F32)

    def project(group):
        projected_ref[group] = dot_nn(tokens_ref[...], weight_ref[group])

    def attend(group):
        attended = []
        for head in range(GROUP):
            left = head * 3 * width
            _, _, queries = normed(projected_ref[group, :, left : left + width], query_gain_ref[...])
            left += width
            _, _, keys = normed(projected_ref[group, :, left : left + width], key_gain_ref[...])
            left += width
            value = projected_ref[group, :, left : left + width].astype(BF16)
            scores = dot_nt(queries, keys) * (1.0 / math.sqrt(width)) + bias
            row_max = jnp.max(scores, axis=-1, keepdims=True)
            weights = jnp.exp(scores - row_max)
            probs = (weights / jnp.sum(weights, axis=-1, keepdims=True)).astype(BF16)
            probs_ref[GROUP * group + head] = probs
            attended.append(dot_nn(probs, value).astype(BF16))
        return jnp.concatenate(attended, axis=1)

    def share(group, attended):
        return dot_nn(attended, out_weight_buffer[group * rows : (group + 1) * rows, :])

    project(0)
    attended = attend(0)
    for group in range(1, groups):
        project(group)
        copies.wait()
        following = attend(group)
        if group == 1:
            attention_ref[...] = share(0, attended)
        else:
            attention_ref[...] += share(group - 1, attended)
        attended = following
    copies.wait()
    total = share(groups - 1, attended)
    if groups > 1:
        total += attention_ref[...]
    attention_ref[...] = total
    gate = gate_ref[...]
    kept_ref[...] = (own_ref[...].astype(F32) + gate * total[:local]).astype(BF16)
    sent_ref[...] = (gate * total[local:]).astype(BF16)


def forward(neighbours, tile_slot, own, other, weight, out_weight, query_gain, key_gain, gate):
    local, model = own.shape
    groups, _, wide = weight.shape
    tokens = 2 * local
    weight = pltpu.with_memory_space_constraint(weight, pltpu.VMEM)
    out_weight = pltpu.with_memory_space_constraint(out_weight, pltpu.HBM)
    smem = pl.BlockSpec(memory_space=pltpu.SMEM)
    vmem = pl.BlockSpec(memory_space=pltpu.VMEM)
    hbm = pl.BlockSpec(memory_space=pl.ANY)
    return pl.pallas_call(
        forward_kernel,
        out_shape=(
            jax.ShapeDtypeStruct((groups, tokens, wide), F32),
            jax.ShapeDtypeStruct((GROUP * groups, tokens, tokens), BF16),
            jax.ShapeDtypeStruct((tokens, model), F32),
            jax.ShapeDtypeStruct((local, model), BF16),
            jax.ShapeDtypeStruct((local, model), BF16),
            pltpu.VMEM(out_weight.shape, BF16),
        ),
        in_specs=[smem, smem, vmem, vmem, vmem, hbm, vmem, vmem, vmem],
        out_specs=(vmem,) * 6,
        scratch_shapes=[
            pltpu.VMEM((tokens, model), BF16),
            pltpu.SemaphoreType.DMA((groups,)),
        ],
        compiler_params=params(12),
        cost_estimate=pl.CostEstimate(
            flops=2 * tokens * (weight.size + out_weight.size),
            bytes_accessed=2 * (weight.size + out_weight.size),
            transcendentals=0,
        ),
        name="attention_forward",
    )(neighbours, tile_slot, own, other, weight, out_weight, query_gain, key_gain, gate)


def input_grad_blocks(grad_ref, weight_ref, own_ref, first, kept_ref, sent_ref):
    local, columns = kept_ref.shape
    block = math.gcd(columns, 512)
    for start in range(0, columns, block):
        rows = slice(first + start, first + start + block)
        total = dot_nt(grad_ref[0], weight_ref[0, rows, :])
        for group in range(1, grad_ref.shape[0]):
            total += dot_nt(grad_ref[group], weight_ref[group, rows, :])
        part = slice(start, start + block)
        kept_ref[:, part] = (own_ref[:, rows].astype(F32) + total[:local]).astype(BF16)
        sent_ref[:, part] = total[local:].astype(BF16)


def backward_kernel(
    own_ref,
    other_ref,
    out_weight_ref,
    weight_ref,
    projected_ref,
    probs_ref,
    attention_ref,
    query_gain_ref,
    key_gain_ref,
    gate_ref,
    grad_ref,
    gate_kept_ref,
    gate_sent_ref,
    kept_ref,
    sent_ref,
    scaled_ref,
    attended_grad_ref,
    gate_grad_ref,
):
    local = own_ref.shape[0]
    width = query_gain_ref.shape[1]
    groups = grad_ref.shape[0]
    rows = GROUP * width

    gate = gate_ref[...]
    own, other = own_ref[...].astype(F32), other_ref[...].astype(F32)
    scaled_ref[:local, :] = (own * gate).astype(BF16)
    scaled_ref[local:, :] = (other * gate).astype(BF16)
    gate_grad_ref[...] = jnp.sum(
        own * attention_ref[:local, :] + other * attention_ref[local:, :], axis=0, keepdims=True
    )
    half = gate_kept_ref.shape[1]
    mine = lax.axis_index("seq")
    gate_kept_ref[...] = gate_grad_ref[:, pl.ds(pl.multiple_of(mine * half, half), half)]
    gate_sent_ref[...] = gate_grad_ref[:, pl.ds(pl.multiple_of((1 - mine) * half, half), half)]

    def attended_grad(group):
        part = slice(group * rows, (group + 1) * rows)
        product = dot_nt(scaled_ref[...], out_weight_ref[part, :])
        attended_grad_ref[group] = product.astype(BF16)

    def attend_backward(group, head):
        left = head * 3 * width
        query_part = slice(left, left + width)
        key_part = slice(left + width, left + 2 * width)
        value_part = slice(left + 2 * width, left + 3 * width)
        query_gain, key_gain = query_gain_ref[...], key_gain_ref[...]
        query_unit, query_inverse, queries = normed(projected_ref[group, :, query_part], query_gain)
        key_unit, key_inverse, keys = normed(projected_ref[group, :, key_part], key_gain)
        value = projected_ref[group, :, value_part].astype(BF16)
        grad = attended_grad_ref[group, :, head * width : (head + 1) * width]
        probs = probs_ref[GROUP * group + head]
        probs_wide = probs.astype(F32)
        grad_ref[group, :, value_part] = dot_tn(probs, grad).astype(BF16)
        prob_grad = dot_nt(grad, value)
        row_delta = jnp.sum(probs_wide * prob_grad, axis=-1, keepdims=True)
        scale_factor = 1.0 / math.sqrt(width)
        score_grad = (probs_wide * (prob_grad - row_delta) * scale_factor).astype(BF16)
        query_scaled = dot_nn(score_grad, keys) * query_gain
        key_scaled = dot_tn(score_grad, queries) * key_gain
        query_mean = jnp.mean(query_scaled * query_unit, axis=-1, keepdims=True)
        key_mean = jnp.mean(key_scaled * key_unit, axis=-1, keepdims=True)
        grad_ref[group, :, query_part] = (
            (query_scaled - query_unit * query_mean) * query_inverse
        ).astype(BF16)
        grad_ref[group, :, key_part] = ((key_scaled - key_unit * key_mean) * key_inverse).astype(BF16)

    attended_grad(0)
    for group in range(groups):
        if group + 1 < groups:
            attended_grad(group + 1)
        for head in range(GROUP):
            attend_backward(group, head)
    input_grad_blocks(grad_ref, weight_ref, own_ref, 0, kept_ref, sent_ref)


def backward(
    own, other, out_weight, weight, projected, probs, attention, query_gain, key_gain, gate, columns
):
    local, model = own.shape
    groups, tokens, wide = projected.shape
    head_dim = query_gain.shape[1]
    out_weight = pltpu.with_memory_space_constraint(out_weight, pltpu.VMEM)
    weight = pltpu.with_memory_space_constraint(weight, pltpu.VMEM)
    vmem = pl.BlockSpec(memory_space=pltpu.VMEM)
    return pl.pallas_call(
        backward_kernel,
        out_shape=(
            jax.ShapeDtypeStruct((groups, tokens, wide), BF16),
            jax.ShapeDtypeStruct((1, model // 2), F32),
            jax.ShapeDtypeStruct((1, model // 2), F32),
            jax.ShapeDtypeStruct((local, columns), BF16),
            jax.ShapeDtypeStruct((local, columns), BF16),
        ),
        in_specs=[vmem] * 10,
        out_specs=(vmem,) * 5,
        scratch_shapes=[
            pltpu.VMEM((tokens, model), BF16),
            pltpu.VMEM((groups, tokens, GROUP * head_dim), BF16),
            pltpu.VMEM((1, model), F32),
        ],
        compiler_params=params(12),
        cost_estimate=pl.CostEstimate(
            flops=2 * tokens * (out_weight.size + groups * columns * wide),
            bytes_accessed=2 * (out_weight.size + groups * columns * wide),
            transcendentals=0,
        ),
        name="attention_backward",
    )(own, other, out_weight, weight, projected, probs, attention, query_gain, key_gain, gate)


def input_grad_kernel(first, grad_ref, weight_ref, own_ref, kept_ref, sent_ref):
    input_grad_blocks(grad_ref, weight_ref, own_ref, first, kept_ref, sent_ref)


def input_grad_part(grad, weight, own, first, columns):
    local, model = own.shape
    groups, tokens, wide = grad.shape
    out = jax.ShapeDtypeStruct((local, columns), BF16)
    vmem = pl.BlockSpec(memory_space=pltpu.VMEM)
    return pl.pallas_call(
        functools.partial(input_grad_kernel, first),
        out_shape=(out, out),
        in_specs=[vmem, vmem, vmem],
        out_specs=(vmem, vmem),
        compiler_params=params(8),
        cost_estimate=pl.CostEstimate(
            flops=2 * tokens * columns * groups * wide,
            bytes_accessed=2 * columns * groups * wide,
            transcendentals=0,
        ),
        name="input_grad",
    )(grad, pltpu.with_memory_space_constraint(weight, pltpu.VMEM), own)


def routed(block, seq_step, pipe_step):
    seq_size, pipe_size = lax.axis_size("seq"), lax.axis_size("pipe")
    route = []
    for i in range(seq_size):
        for j in range(pipe_size):
            target = (i + seq_step) % seq_size * pipe_size + (j + pipe_step) % pipe_size
            route.append((i * pipe_size + j, target))
    return lax.ppermute(block, ("seq", "pipe"), route)


def pair_body(
    segment_input,
    output_grad,
    qkv_weight,
    out_weight,
    query_gain,
    key_gain,
    gate_scale,
    neighbours,
    tile_slot,
):
    stream = segment_input[0]
    upstream = output_grad[0]
    out_local = out_weight[0]
    model = stream.shape[1]
    other_stream = routed(stream, 1, 0)
    weight = regroup(qkv_weight[0], 128, 8)
    weight, upstream = lax.optimization_barrier((weight, upstream))
    other_upstream = routed(upstream, 1, 0)
    projected, probs, attention, kept, sent, out_local = forward(
        neighbours,
        tile_slot,
        stream,
        other_stream,
        weight,
        out_local,
        query_gain,
        key_gain,
        gate_scale,
    )
    kept = routed(kept, 0, 1)
    sent = routed(sent, 1, 1)
    columns = model // 2
    grad, gate_kept, gate_sent, first, second = backward(
        upstream,
        other_upstream,
        out_local,
        weight,
        projected,
        probs,
        attention,
        query_gain,
        key_gain,
        gate_scale,
        columns,
    )
    grad, first, second, kept, sent = lax.optimization_barrier((grad, first, second, kept, sent))
    gate_sent = routed(gate_sent, 1, 0)
    early = (routed(first, 0, -1), routed(second, 1, -1))
    late = input_grad_part(grad, weight, upstream, columns, model - columns)
    late, early, kept, sent, gate_sent = lax.optimization_barrier(
        (late, early, kept, sent, gate_sent)
    )
    pieces = [early, (routed(late[0], 0, -1), routed(late[1], 1, -1))]
    segment_output = (kept.astype(F32) + sent.astype(F32)).astype(BF16)
    input_grad = jnp.concatenate(
        [(a.astype(F32) + b.astype(F32)).astype(BF16) for a, b in pieces], axis=1
    )
    return (segment_output[None], input_grad[None], gate_kept + gate_sent)


def solution(mesh):
    in_specs = (
        P("pipe", ("dp", "seq"), None),
        P("pipe", ("dp", "seq"), None),
        P("pipe", None, "seq", None),
        P("pipe", "seq", None),
        P("pipe", None),
        P("pipe", None),
        P("pipe", None),
        P("dp", None),
        P("dp"),
    )
    out_specs = (
        P("pipe", ("dp", "seq"), None),
        P("pipe", ("dp", "seq"), None),
        P(("dp", "pipe"), "seq"),
    )

    def body(*args):
        one_tile_each = args[0].shape[1] == TILE and args[8].shape[0] == 2
        if mesh.shape["seq"] == 2 and one_tile_each and args[2].shape[2] % GROUP == 0:
            return pair_body(*args)
        return general_body(*args)

    return jax.shard_map(body, mesh=mesh, in_specs=in_specs, out_specs=out_specs, check_vma=False)
```

```python
import functools
import math

import jax
import jax.numpy as jnp
from jax import lax
from jax.experimental import pallas as pl
from jax.experimental.pallas import tpu as pltpu
from jax.sharding import PartitionSpec as P

TILE = 64
EPSILON = 1e-06
F32 = jnp.float32
BF16 = jnp.bfloat16
MIB = 1024 * 1024
GROUP = 4


def passed_along(block, axis, distance):
    devices = range(lax.axis_size(axis))
    route = [((i - distance) % len(devices), i) for i in devices]
    return lax.ppermute(block, axis, route)


def slot_lists(neighbours, tile_slot):
    tile_count = tile_slot.shape[0]
    numbering = jnp.arange(tile_count, dtype=jnp.int32)
    placed = (tile_slot[:, None] == numbering[None, :]).astype(jnp.int32)
    tile_of_slot = jnp.sum(placed * numbering[:, None], axis=0)
    chosen = (tile_of_slot[:, None] == numbering[None, :]).astype(jnp.int32)
    listed_tiles = jnp.sum(chosen[:, :, None] * neighbours[None, :, :], axis=1)
    key_valid = listed_tiles >= 0
    safe_tiles = jnp.maximum(listed_tiles, 0)
    matches = (safe_tiles[:, :, None] == numbering[None, None, :]).astype(jnp.int32)
    key_slots = jnp.sum(matches * tile_slot[None, None, :], axis=2)
    return (key_slots, key_valid)


def block_tiles(tile_count):
    return math.gcd(tile_count, max(1, 512 // TILE))


def unit_norm(values):
    spread = jnp.sqrt(jnp.mean(values * values, axis=-1, keepdims=True) + EPSILON)
    return (values / spread, spread)


def probabilities(query_block, key_rows, block_valid):
    scores = jnp.einsum(
        "aihd,ajhd->ahij", query_block, key_rows, preferred_element_type=jnp.float32
    ) * (1.0 / math.sqrt(query_block.shape[-1]))
    key_mask = jnp.repeat(block_valid, TILE, axis=1)
    scores = jnp.where(key_mask[:, None, None, :], scores, -jnp.inf)
    row_max = jnp.max(scores, axis=-1, keepdims=True)
    weights = jnp.exp(scores - row_max)
    return (weights / jnp.sum(weights, axis=-1, keepdims=True)).astype(jnp.bfloat16)


def gathered(tiles_array, block_slots):
    picked = tiles_array[block_slots]
    return picked.reshape(block_slots.shape[0], -1, tiles_array.shape[2], tiles_array.shape[3])


def attend_both(query_tiles, key_tiles, value_tiles, grad_tiles, key_slots, key_valid):
    tile_count = query_tiles.shape[0]
    span = block_tiles(tile_count)
    scale_factor = 1.0 / math.sqrt(query_tiles.shape[-1])
    empty_grad = jnp.zeros(query_tiles.shape, jnp.float32)

    def per_block(accumulators, block_index):
        key_total, value_total = accumulators
        first_tile = block_index * span
        query_block = lax.dynamic_slice_in_dim(query_tiles, first_tile, span, 0)
        grad_block = lax.dynamic_slice_in_dim(grad_tiles, first_tile, span, 0)
        block_slots = lax.dynamic_slice_in_dim(key_slots, first_tile, span, 0)
        block_valid = lax.dynamic_slice_in_dim(key_valid, first_tile, span, 0)
        key_rows = gathered(key_tiles, block_slots)
        value_rows = gathered(value_tiles, block_slots)
        weights = probabilities(query_block, key_rows, block_valid)
        attended = jnp.einsum(
            "ahij,ajhd->aihd", weights, value_rows, preferred_element_type=jnp.float32
        )
        value_part = jnp.einsum(
            "ahij,aihd->ajhd", weights, grad_block, preferred_element_type=jnp.float32
        )
        prob_grad = jnp.einsum(
            "aihd,ajhd->ahij", grad_block, value_rows, preferred_element_type=jnp.float32
        )
        weights_wide = weights.astype(jnp.float32)
        row_delta = jnp.sum(weights_wide * prob_grad, axis=-1, keepdims=True)
        score_grad = (weights_wide * (prob_grad - row_delta) * scale_factor).astype(jnp.bfloat16)
        query_part = jnp.einsum(
            "ahij,ajhd->aihd", score_grad, key_rows, preferred_element_type=jnp.float32
        )
        key_part = jnp.einsum(
            "ahij,aihd->ajhd", score_grad, query_block, preferred_element_type=jnp.float32
        )
        block_shape = (span, block_slots.shape[1]) + query_tiles.shape[1:]
        key_total = key_total.at[block_slots].add(key_part.reshape(block_shape))
        value_total = value_total.at[block_slots].add(value_part.reshape(block_shape))
        return ((key_total, value_total), (attended, query_part))

    totals, parts = lax.scan(
        per_block, (empty_grad, empty_grad), jnp.arange(tile_count // span, dtype=jnp.int32)
    )
    flat_shape = (-1,) + query_tiles.shape[2:]
    return (
        parts[0].reshape(flat_shape),
        parts[1].reshape(flat_shape),
        totals[0].reshape(flat_shape),
        totals[1].reshape(flat_shape),
    )


def general_body(
    segment_input,
    output_grad,
    qkv_weight,
    out_weight,
    query_gain,
    key_gain,
    gate_scale,
    neighbours,
    tile_slot,
):
    key_slots, key_valid = slot_lists(neighbours, tile_slot)
    stream = segment_input[0]
    upstream = output_grad[0]
    model_width = stream.shape[1]
    head_dim = query_gain.shape[1]
    local_heads = qkv_weight.shape[2]
    local_width = local_heads * head_dim
    proj_weight = qkv_weight[0].reshape(model_width, local_heads * 3 * head_dim)
    out_local = out_weight[0]
    gate_row = gate_scale[0]
    query_weights = query_gain[0]
    key_weights = key_gain[0]
    projected = jnp.dot(
        lax.all_gather(stream, "seq", axis=0, tiled=True),
        proj_weight,
        preferred_element_type=jnp.float32,
    )
    all_tokens = projected.shape[0]
    projected = projected.reshape(all_tokens, local_heads, 3, head_dim)
    query_unit, query_spread = unit_norm(projected[:, :, 0])
    key_unit, key_spread = unit_norm(projected[:, :, 1])
    queries = (query_unit * query_weights).astype(jnp.bfloat16)
    keys_normed = (key_unit * key_weights).astype(jnp.bfloat16)
    value_rows = projected[:, :, 2].astype(jnp.bfloat16)
    scaled = (upstream.astype(jnp.float32) * gate_row).astype(jnp.bfloat16)
    attended_grad = jnp.einsum(
        "td,cd->tc",
        lax.all_gather(scaled, "seq", axis=0, tiled=True),
        out_local,
        preferred_element_type=jnp.float32,
    ).astype(jnp.bfloat16)

    def as_tiles(values):
        return values.reshape(-1, TILE, local_heads, head_dim)

    attended, query_grad, key_grad, value_grad = attend_both(
        as_tiles(queries),
        as_tiles(keys_normed),
        as_tiles(value_rows),
        as_tiles(attended_grad),
        key_slots,
        key_valid,
    )
    attended_low = attended.astype(jnp.bfloat16).reshape(all_tokens, local_width)
    rows = attended_low
    attention_out = lax.psum_scatter(
        jnp.dot(rows, out_local, preferred_element_type=jnp.float32),
        "seq",
        scatter_dimension=0,
        tiled=True,
    )
    section_out = (stream.astype(jnp.float32) + gate_row * attention_out).astype(jnp.bfloat16)
    segment_output = passed_along(section_out, "pipe", 1)
    gate_local = lax.psum_scatter(
        jnp.sum(upstream.astype(jnp.float32) * attention_out, axis=0),
        "seq",
        scatter_dimension=0,
        tiled=True,
    )
    query_scaled = query_grad * query_weights
    query_part_grad = (
        query_scaled - query_unit * jnp.mean(query_scaled * query_unit, axis=-1, keepdims=True)
    ) / query_spread
    key_scaled = key_grad * key_weights
    key_part_grad = (
        key_scaled - key_unit * jnp.mean(key_scaled * key_unit, axis=-1, keepdims=True)
    ) / key_spread
    projected_grad = (
        jnp.stack([query_part_grad, key_part_grad, value_grad], axis=2)
        .astype(jnp.bfloat16)
        .reshape(all_tokens, local_heads * 3 * head_dim)
    )
    rows = projected_grad
    stream_grad = lax.psum_scatter(
        jnp.einsum("tc,dc->td", rows, proj_weight, preferred_element_type=jnp.float32).astype(
            jnp.bfloat16
        ),
        "seq",
        scatter_dimension=0,
        tiled=True,
    ).astype(jnp.float32)
    token_grad = (upstream.astype(jnp.float32) + stream_grad).astype(jnp.bfloat16)
    input_grad = passed_along(token_grad, "pipe", -1)
    return (segment_output[None], input_grad[None], gate_local[None])


def dot_nn(a, b):
    return lax.dot_general(a, b, (((1,), (0,)), ((), ())), preferred_element_type=F32)


def dot_nt(a, b):
    return lax.dot_general(a, b, (((1,), (1,)), ((), ())), preferred_element_type=F32)


def dot_tn(a, b):
    return lax.dot_general(a, b, (((0,), (0,)), ((), ())), preferred_element_type=F32)


def params(mebibytes):
    return pltpu.CompilerParams(vmem_limit_bytes=mebibytes * MIB)


class Copies:
    def __init__(self, pairs, semaphores, ahead):
        self.copies = [
            pltpu.make_async_copy(source, target, semaphores.at[i])
            for i, (source, target) in enumerate(pairs)
        ]
        self.ahead = ahead
        self.waited = 0
        for copy in self.copies[:ahead]:
            copy.start()

    def wait(self, count=1):
        for _ in range(count):
            self.copies[self.waited].wait()
            following = self.waited + self.ahead
            if following < len(self.copies):
                self.copies[following].start()
            self.waited += 1


def regroup_kernel(weight_ref, out_ref, read_ref, reads):
    depth, heads, width = weight_ref.shape
    slots, rows = read_ref.shape[:2]
    steps = depth // rows

    def part(step):
        return pl.ds(pl.multiple_of(step * rows, rows), rows)

    def read(step, slot):
        return pltpu.make_async_copy(
            weight_ref.at[part(step)], read_ref.at[slot], reads.at[slot]
        )

    for slot in range(slots):
        read(slot, slot).start()

    @pl.loop(0, steps)
    def _(step):
        slot = lax.rem(step, slots)
        read(step, slot).wait()
        by_head = jnp.swapaxes(read_ref[slot], 0, 1)
        for head in range(heads):
            left = (head % GROUP) * width
            out_ref[head // GROUP, part(step), left : left + width] = by_head[head]

        @pl.when(step + slots < steps)
        def _():
            read(step + slots, slot).start()


def regroup(weight, rows, slots):
    depth, heads, width = weight.shape
    out = (heads // GROUP, depth, GROUP * width)
    return pl.pallas_call(
        regroup_kernel,
        out_shape=pltpu.VMEM(out, weight.dtype),
        in_specs=[pl.BlockSpec(memory_space=pl.ANY)],
        out_specs=pl.BlockSpec(memory_space=pltpu.VMEM),
        scratch_shapes=[
            pltpu.VMEM((slots, rows, heads, width), weight.dtype),
            pltpu.SemaphoreType.DMA((slots,)),
        ],
        compiler_params=params(12),
        cost_estimate=pl.CostEstimate(
            flops=0, bytes_accessed=4 * depth * heads * width, transcendentals=0
        ),
        name="regroup",
    )(pltpu.with_memory_space_constraint(weight, pltpu.HBM))


def listed_slots(neighbours_ref, tile_slot_ref):
    tiles, places = neighbours_ref.shape
    one, zero = jnp.int32(1), jnp.int32(0)
    allowed = [[zero] * tiles for _ in range(tiles)]
    for t in range(tiles):
        for u in range(tiles):
            listed = zero
            for k in range(places):
                listed = jnp.where(neighbours_ref[t, k] == u, one, listed)
            for r in range(tiles):
                for c in range(tiles):
                    here = (tile_slot_ref[t] == r) & (tile_slot_ref[u] == c)
                    allowed[r][c] = jnp.where(here, listed, allowed[r][c])
    return allowed


def normed(rows, gain):
    inverse = lax.rsqrt(jnp.mean(rows * rows, axis=-1, keepdims=True) + EPSILON)
    unit = rows * inverse
    return unit, inverse, (unit * gain).astype(BF16)


def forward_kernel(
    neighbours_ref,
    tile_slot_ref,
    own_ref,
    other_ref,
    weight_ref,
    out_weight_ref,
    query_gain_ref,
    key_gain_ref,
    gate_ref,
    projected_ref,
    probs_ref,
    attention_ref,
    kept_ref,
    sent_ref,
    out_weight_buffer,
    tokens_ref,
    semaphores,
):
    local, model = own_ref.shape
    tokens = 2 * local
    width = query_gain_ref.shape[1]
    groups = weight_ref.shape[0]
    rows = GROUP * width

    def out_weight_part(group):
        place = pl.ds(group * rows, rows)
        return out_weight_ref.at[place], out_weight_buffer.at[place]

    copies = Copies([out_weight_part(group) for group in range(groups)], semaphores, groups)

    tokens_ref[:local, :] = own_ref[...]
    tokens_ref[local:, :] = other_ref[...]
    allowed = listed_slots(neighbours_ref, tile_slot_ref)
    mine = lax.axis_index("seq")
    row_half = lax.broadcasted_iota(jnp.int32, (tokens, tokens), 0) // local
    column_half = lax.broadcasted_iota(jnp.int32, (tokens, tokens), 1) // local
    row_slot = jnp.where(row_half == 0, mine, 1 - mine)
    column_slot = jnp.where(column_half == 0, mine, 1 - mine)
    table = jnp.zeros((tokens, tokens), jnp.int32)
    for r in range(2):
        for c in range(2):
            table = jnp.where((row_slot == r) & (column_slot == c), allowed[r][c], table)
    bias = jnp.where(table > 0, 0.0, -jnp.inf).astype(F32)

    def project(group):
        projected_ref[group] = dot_nn(tokens_ref[...], weight_ref[group])

    def attend(group):
        attended = []
        for head in range(GROUP):
            left = head * 3 * width
            _, _, queries = normed(projected_ref[group, :, left : left + width], query_gain_ref[...])
            left += width
            _, _, keys = normed(projected_ref[group, :, left : left + width], key_gain_ref[...])
            left += width
            value = projected_ref[group, :, left : left + width].astype(BF16)
            scores = dot_nt(queries, keys) * (1.0 / math.sqrt(width)) + bias
            row_max = jnp.max(scores, axis=-1, keepdims=True)
            weights = jnp.exp(scores - row_max)
            probs = (weights / jnp.sum(weights, axis=-1, keepdims=True)).astype(BF16)
            probs_ref[GROUP * group + head] = probs
            attended.append(dot_nn(probs, value).astype(BF16))
        return jnp.concatenate(attended, axis=1)

    def share(group, attended):
        return dot_nn(attended, out_weight_buffer[group * rows : (group + 1) * rows, :])

    project(0)
    attended = attend(0)
    for group in range(1, groups):
        project(group)
        copies.wait()
        following = attend(group)
        if group == 1:
            attention_ref[...] = share(0, attended)
        else:
            attention_ref[...] += share(group - 1, attended)
        attended = following
    copies.wait()
    total = share(groups - 1, attended)
    if groups > 1:
        total += attention_ref[...]
    attention_ref[...] = total
    gate = gate_ref[...]
    kept_ref[...] = (own_ref[...].astype(F32) + gate * total[:local]).astype(BF16)
    sent_ref[...] = (gate * total[local:]).astype(BF16)


def forward(neighbours, tile_slot, own, other, weight, out_weight, query_gain, key_gain, gate):
    local, model = own.shape
    groups, _, wide = weight.shape
    tokens = 2 * local
    weight = pltpu.with_memory_space_constraint(weight, pltpu.VMEM)
    out_weight = pltpu.with_memory_space_constraint(out_weight, pltpu.HBM)
    smem = pl.BlockSpec(memory_space=pltpu.SMEM)
    vmem = pl.BlockSpec(memory_space=pltpu.VMEM)
    hbm = pl.BlockSpec(memory_space=pl.ANY)
    return pl.pallas_call(
        forward_kernel,
        out_shape=(
            jax.ShapeDtypeStruct((groups, tokens, wide), F32),
            jax.ShapeDtypeStruct((GROUP * groups, tokens, tokens), BF16),
            jax.ShapeDtypeStruct((tokens, model), F32),
            jax.ShapeDtypeStruct((local, model), BF16),
            jax.ShapeDtypeStruct((local, model), BF16),
            pltpu.VMEM(out_weight.shape, BF16),
        ),
        in_specs=[smem, smem, vmem, vmem, vmem, hbm, vmem, vmem, vmem],
        out_specs=(vmem,) * 6,
        scratch_shapes=[
            pltpu.VMEM((tokens, model), BF16),
            pltpu.SemaphoreType.DMA((groups,)),
        ],
        compiler_params=params(12),
        cost_estimate=pl.CostEstimate(
            flops=2 * tokens * (weight.size + out_weight.size),
            bytes_accessed=2 * (weight.size + out_weight.size),
            transcendentals=0,
        ),
        name="attention_forward",
    )(neighbours, tile_slot, own, other, weight, out_weight, query_gain, key_gain, gate)


def input_grad(grad_ref, weight_ref, own_ref, kept_ref, sent_ref):
    local, model = own_ref.shape
    block = 512
    for start in range(0, model, block):
        part = slice(start, start + block)
        total = dot_nt(grad_ref[0], weight_ref[0, part, :])
        for group in range(1, grad_ref.shape[0]):
            total += dot_nt(grad_ref[group], weight_ref[group, part, :])
        kept_ref[:, part] = (own_ref[:, part].astype(F32) + total[:local]).astype(BF16)
        sent_ref[:, part] = total[local:].astype(BF16)


def backward_kernel(
    own_ref,
    other_ref,
    out_weight_ref,
    weight_ref,
    projected_ref,
    probs_ref,
    attention_ref,
    query_gain_ref,
    key_gain_ref,
    gate_ref,
    gate_kept_ref,
    gate_sent_ref,
    kept_ref,
    sent_ref,
    grad_ref,
    scaled_ref,
    attended_grad_ref,
    gate_grad_ref,
):
    local = own_ref.shape[0]
    width = query_gain_ref.shape[1]
    groups = grad_ref.shape[0]
    rows = GROUP * width

    gate = gate_ref[...]
    own, other = own_ref[...].astype(F32), other_ref[...].astype(F32)
    scaled_ref[:local, :] = (own * gate).astype(BF16)
    scaled_ref[local:, :] = (other * gate).astype(BF16)
    gate_grad_ref[...] = jnp.sum(
        own * attention_ref[:local, :] + other * attention_ref[local:, :], axis=0, keepdims=True
    )
    half = gate_kept_ref.shape[1]
    mine = lax.axis_index("seq")
    gate_kept_ref[...] = gate_grad_ref[:, pl.ds(pl.multiple_of(mine * half, half), half)]
    gate_sent_ref[...] = gate_grad_ref[:, pl.ds(pl.multiple_of((1 - mine) * half, half), half)]

    def attended_grad(group):
        part = slice(group * rows, (group + 1) * rows)
        product = dot_nt(scaled_ref[...], out_weight_ref[part, :])
        attended_grad_ref[group] = product.astype(BF16)

    def attend_backward(group, head):
        left = head * 3 * width
        query_part = slice(left, left + width)
        key_part = slice(left + width, left + 2 * width)
        value_part = slice(left + 2 * width, left + 3 * width)
        query_gain, key_gain = query_gain_ref[...], key_gain_ref[...]
        query_unit, query_inverse, queries = normed(projected_ref[group, :, query_part], query_gain)
        key_unit, key_inverse, keys = normed(projected_ref[group, :, key_part], key_gain)
        value = projected_ref[group, :, value_part].astype(BF16)
        grad = attended_grad_ref[group, :, head * width : (head + 1) * width]
        probs = probs_ref[GROUP * group + head]
        probs_wide = probs.astype(F32)
        grad_ref[group, :, value_part] = dot_tn(probs, grad).astype(BF16)
        prob_grad = dot_nt(grad, value)
        row_delta = jnp.sum(probs_wide * prob_grad, axis=-1, keepdims=True)
        scale_factor = 1.0 / math.sqrt(width)
        score_grad = (probs_wide * (prob_grad - row_delta) * scale_factor).astype(BF16)
        query_scaled = dot_nn(score_grad, keys) * query_gain
        key_scaled = dot_tn(score_grad, queries) * key_gain
        query_mean = jnp.mean(query_scaled * query_unit, axis=-1, keepdims=True)
        key_mean = jnp.mean(key_scaled * key_unit, axis=-1, keepdims=True)
        grad_ref[group, :, query_part] = (
            (query_scaled - query_unit * query_mean) * query_inverse
        ).astype(BF16)
        grad_ref[group, :, key_part] = ((key_scaled - key_unit * key_mean) * key_inverse).astype(BF16)

    attended_grad(0)
    for group in range(groups):
        if group + 1 < groups:
            attended_grad(group + 1)
        for head in range(GROUP):
            attend_backward(group, head)
    input_grad(grad_ref, weight_ref, own_ref, kept_ref, sent_ref)


def backward(
    own, other, out_weight, weight, projected, probs, attention, query_gain, key_gain, gate
):
    local, model = own.shape
    groups, tokens, wide = projected.shape
    head_dim = query_gain.shape[1]
    out_weight = pltpu.with_memory_space_constraint(out_weight, pltpu.VMEM)
    weight = pltpu.with_memory_space_constraint(weight, pltpu.VMEM)
    vmem = pl.BlockSpec(memory_space=pltpu.VMEM)
    return pl.pallas_call(
        backward_kernel,
        out_shape=(
            jax.ShapeDtypeStruct((1, model // 2), F32),
            jax.ShapeDtypeStruct((1, model // 2), F32),
            jax.ShapeDtypeStruct((local, model), BF16),
            jax.ShapeDtypeStruct((local, model), BF16),
        ),
        in_specs=[vmem] * 10,
        out_specs=(vmem,) * 4,
        scratch_shapes=[
            pltpu.VMEM((groups, tokens, wide), BF16),
            pltpu.VMEM((tokens, model), BF16),
            pltpu.VMEM((groups, tokens, GROUP * head_dim), BF16),
            pltpu.VMEM((1, model), F32),
        ],
        compiler_params=params(12),
        cost_estimate=pl.CostEstimate(
            flops=2 * tokens * (out_weight.size + weight.size),
            bytes_accessed=2 * (out_weight.size + weight.size),
            transcendentals=0,
        ),
        name="attention_backward",
    )(own, other, out_weight, weight, projected, probs, attention, query_gain, key_gain, gate)


def routed(block, seq_step, pipe_step):
    seq_size, pipe_size = lax.axis_size("seq"), lax.axis_size("pipe")
    route = []
    for i in range(seq_size):
        for j in range(pipe_size):
            target = (i + seq_step) % seq_size * pipe_size + (j + pipe_step) % pipe_size
            route.append((i * pipe_size + j, target))
    return lax.ppermute(block, ("seq", "pipe"), route)


def pair_body(
    segment_input,
    output_grad,
    qkv_weight,
    out_weight,
    query_gain,
    key_gain,
    gate_scale,
    neighbours,
    tile_slot,
):
    stream = segment_input[0]
    upstream = output_grad[0]
    out_local = out_weight[0]
    other_stream = routed(stream, 1, 0)
    weight = regroup(qkv_weight[0], 128, 8)
    weight, upstream = lax.optimization_barrier((weight, upstream))
    other_upstream = routed(upstream, 1, 0)
    projected, probs, attention, kept, sent, out_local = forward(
        neighbours,
        tile_slot,
        stream,
        other_stream,
        weight,
        out_local,
        query_gain,
        key_gain,
        gate_scale,
    )
    kept = routed(kept, 0, 1)
    sent = routed(sent, 1, 1)
    gate_kept, gate_sent, grad_kept, grad_sent = backward(
        upstream,
        other_upstream,
        out_local,
        weight,
        projected,
        probs,
        attention,
        query_gain,
        key_gain,
        gate_scale,
    )
    grad_kept, grad_sent, kept, sent = lax.optimization_barrier((grad_kept, grad_sent, kept, sent))
    grad_sent = routed(grad_sent, 1, -1)
    grad_kept = routed(grad_kept, 0, -1)
    gate_sent = routed(gate_sent, 1, 0)
    segment_output = (kept.astype(F32) + sent.astype(F32)).astype(BF16)
    input_grad = (grad_kept.astype(F32) + grad_sent.astype(F32)).astype(BF16)
    return (segment_output[None], input_grad[None], gate_kept + gate_sent)


def solution(mesh):
    in_specs = (
        P("pipe", ("dp", "seq"), None),
        P("pipe", ("dp", "seq"), None),
        P("pipe", None, "seq", None),
        P("pipe", "seq", None),
        P("pipe", None),
        P("pipe", None),
        P("pipe", None),
        P("dp", None),
        P("dp"),
    )
    out_specs = (
        P("pipe", ("dp", "seq"), None),
        P("pipe", ("dp", "seq"), None),
        P(("dp", "pipe"), "seq"),
    )

    def body(*args):
        one_tile_each = args[0].shape[1] == TILE and args[8].shape[0] == 2
        if mesh.shape["seq"] == 2 and one_tile_each and args[2].shape[2] % GROUP == 0:
            return pair_body(*args)
        return general_body(*args)

    return jax.shard_map(body, mesh=mesh, in_specs=in_specs, out_specs=out_specs, check_vma=False)
```

```python
import functools
import math

import jax
import jax.numpy as jnp
from jax import lax
from jax.experimental import pallas as pl
from jax.experimental.pallas import tpu as pltpu
from jax.sharding import PartitionSpec as P

TILE = 64
EPSILON = 1e-06
F32 = jnp.float32
BF16 = jnp.bfloat16
MIB = 1024 * 1024
GROUP = 4


def passed_along(block, axis, distance):
    devices = range(lax.axis_size(axis))
    route = [((i - distance) % len(devices), i) for i in devices]
    return lax.ppermute(block, axis, route)


def slot_lists(neighbours, tile_slot):
    tile_count = tile_slot.shape[0]
    numbering = jnp.arange(tile_count, dtype=jnp.int32)
    placed = (tile_slot[:, None] == numbering[None, :]).astype(jnp.int32)
    tile_of_slot = jnp.sum(placed * numbering[:, None], axis=0)
    chosen = (tile_of_slot[:, None] == numbering[None, :]).astype(jnp.int32)
    listed_tiles = jnp.sum(chosen[:, :, None] * neighbours[None, :, :], axis=1)
    key_valid = listed_tiles >= 0
    safe_tiles = jnp.maximum(listed_tiles, 0)
    matches = (safe_tiles[:, :, None] == numbering[None, None, :]).astype(jnp.int32)
    key_slots = jnp.sum(matches * tile_slot[None, None, :], axis=2)
    return (key_slots, key_valid)


def block_tiles(tile_count):
    return math.gcd(tile_count, max(1, 512 // TILE))


def unit_norm(values):
    spread = jnp.sqrt(jnp.mean(values * values, axis=-1, keepdims=True) + EPSILON)
    return (values / spread, spread)


def probabilities(query_block, key_rows, block_valid):
    scores = jnp.einsum(
        "aihd,ajhd->ahij", query_block, key_rows, preferred_element_type=jnp.float32
    ) * (1.0 / math.sqrt(query_block.shape[-1]))
    key_mask = jnp.repeat(block_valid, TILE, axis=1)
    scores = jnp.where(key_mask[:, None, None, :], scores, -jnp.inf)
    row_max = jnp.max(scores, axis=-1, keepdims=True)
    weights = jnp.exp(scores - row_max)
    return (weights / jnp.sum(weights, axis=-1, keepdims=True)).astype(jnp.bfloat16)


def gathered(tiles_array, block_slots):
    picked = tiles_array[block_slots]
    return picked.reshape(block_slots.shape[0], -1, tiles_array.shape[2], tiles_array.shape[3])


def attend_both(query_tiles, key_tiles, value_tiles, grad_tiles, key_slots, key_valid):
    tile_count = query_tiles.shape[0]
    span = block_tiles(tile_count)
    scale_factor = 1.0 / math.sqrt(query_tiles.shape[-1])
    empty_grad = jnp.zeros(query_tiles.shape, jnp.float32)

    def per_block(accumulators, block_index):
        key_total, value_total = accumulators
        first_tile = block_index * span
        query_block = lax.dynamic_slice_in_dim(query_tiles, first_tile, span, 0)
        grad_block = lax.dynamic_slice_in_dim(grad_tiles, first_tile, span, 0)
        block_slots = lax.dynamic_slice_in_dim(key_slots, first_tile, span, 0)
        block_valid = lax.dynamic_slice_in_dim(key_valid, first_tile, span, 0)
        key_rows = gathered(key_tiles, block_slots)
        value_rows = gathered(value_tiles, block_slots)
        weights = probabilities(query_block, key_rows, block_valid)
        attended = jnp.einsum(
            "ahij,ajhd->aihd", weights, value_rows, preferred_element_type=jnp.float32
        )
        value_part = jnp.einsum(
            "ahij,aihd->ajhd", weights, grad_block, preferred_element_type=jnp.float32
        )
        prob_grad = jnp.einsum(
            "aihd,ajhd->ahij", grad_block, value_rows, preferred_element_type=jnp.float32
        )
        weights_wide = weights.astype(jnp.float32)
        row_delta = jnp.sum(weights_wide * prob_grad, axis=-1, keepdims=True)
        score_grad = (weights_wide * (prob_grad - row_delta) * scale_factor).astype(jnp.bfloat16)
        query_part = jnp.einsum(
            "ahij,ajhd->aihd", score_grad, key_rows, preferred_element_type=jnp.float32
        )
        key_part = jnp.einsum(
            "ahij,aihd->ajhd", score_grad, query_block, preferred_element_type=jnp.float32
        )
        block_shape = (span, block_slots.shape[1]) + query_tiles.shape[1:]
        key_total = key_total.at[block_slots].add(key_part.reshape(block_shape))
        value_total = value_total.at[block_slots].add(value_part.reshape(block_shape))
        return ((key_total, value_total), (attended, query_part))

    totals, parts = lax.scan(
        per_block, (empty_grad, empty_grad), jnp.arange(tile_count // span, dtype=jnp.int32)
    )
    flat_shape = (-1,) + query_tiles.shape[2:]
    return (
        parts[0].reshape(flat_shape),
        parts[1].reshape(flat_shape),
        totals[0].reshape(flat_shape),
        totals[1].reshape(flat_shape),
    )


def general_body(
    segment_input,
    output_grad,
    qkv_weight,
    out_weight,
    query_gain,
    key_gain,
    gate_scale,
    neighbours,
    tile_slot,
):
    key_slots, key_valid = slot_lists(neighbours, tile_slot)
    stream = segment_input[0]
    upstream = output_grad[0]
    model_width = stream.shape[1]
    head_dim = query_gain.shape[1]
    local_heads = qkv_weight.shape[2]
    local_width = local_heads * head_dim
    proj_weight = qkv_weight[0].reshape(model_width, local_heads * 3 * head_dim)
    out_local = out_weight[0]
    gate_row = gate_scale[0]
    query_weights = query_gain[0]
    key_weights = key_gain[0]
    projected = jnp.dot(
        lax.all_gather(stream, "seq", axis=0, tiled=True),
        proj_weight,
        preferred_element_type=jnp.float32,
    )
    all_tokens = projected.shape[0]
    projected = projected.reshape(all_tokens, local_heads, 3, head_dim)
    query_unit, query_spread = unit_norm(projected[:, :, 0])
    key_unit, key_spread = unit_norm(projected[:, :, 1])
    queries = (query_unit * query_weights).astype(jnp.bfloat16)
    keys_normed = (key_unit * key_weights).astype(jnp.bfloat16)
    value_rows = projected[:, :, 2].astype(jnp.bfloat16)
    scaled = (upstream.astype(jnp.float32) * gate_row).astype(jnp.bfloat16)
    attended_grad = jnp.einsum(
        "td,cd->tc",
        lax.all_gather(scaled, "seq", axis=0, tiled=True),
        out_local,
        preferred_element_type=jnp.float32,
    ).astype(jnp.bfloat16)

    def as_tiles(values):
        return values.reshape(-1, TILE, local_heads, head_dim)

    attended, query_grad, key_grad, value_grad = attend_both(
        as_tiles(queries),
        as_tiles(keys_normed),
        as_tiles(value_rows),
        as_tiles(attended_grad),
        key_slots,
        key_valid,
    )
    attended_low = attended.astype(jnp.bfloat16).reshape(all_tokens, local_width)
    rows = attended_low
    attention_out = lax.psum_scatter(
        jnp.dot(rows, out_local, preferred_element_type=jnp.float32),
        "seq",
        scatter_dimension=0,
        tiled=True,
    )
    section_out = (stream.astype(jnp.float32) + gate_row * attention_out).astype(jnp.bfloat16)
    segment_output = passed_along(section_out, "pipe", 1)
    gate_local = lax.psum_scatter(
        jnp.sum(upstream.astype(jnp.float32) * attention_out, axis=0),
        "seq",
        scatter_dimension=0,
        tiled=True,
    )
    query_scaled = query_grad * query_weights
    query_part_grad = (
        query_scaled - query_unit * jnp.mean(query_scaled * query_unit, axis=-1, keepdims=True)
    ) / query_spread
    key_scaled = key_grad * key_weights
    key_part_grad = (
        key_scaled - key_unit * jnp.mean(key_scaled * key_unit, axis=-1, keepdims=True)
    ) / key_spread
    projected_grad = (
        jnp.stack([query_part_grad, key_part_grad, value_grad], axis=2)
        .astype(jnp.bfloat16)
        .reshape(all_tokens, local_heads * 3 * head_dim)
    )
    rows = projected_grad
    stream_grad = lax.psum_scatter(
        jnp.einsum("tc,dc->td", rows, proj_weight, preferred_element_type=jnp.float32).astype(
            jnp.bfloat16
        ),
        "seq",
        scatter_dimension=0,
        tiled=True,
    ).astype(jnp.float32)
    token_grad = (upstream.astype(jnp.float32) + stream_grad).astype(jnp.bfloat16)
    input_grad = passed_along(token_grad, "pipe", -1)
    return (segment_output[None], input_grad[None], gate_local[None])


def dot_nn(a, b):
    return lax.dot_general(a, b, (((1,), (0,)), ((), ())), preferred_element_type=F32)


def dot_nt(a, b):
    return lax.dot_general(a, b, (((1,), (1,)), ((), ())), preferred_element_type=F32)


def dot_tn(a, b):
    return lax.dot_general(a, b, (((0,), (0,)), ((), ())), preferred_element_type=F32)


def params(mebibytes):
    return pltpu.CompilerParams(vmem_limit_bytes=mebibytes * MIB)


class Copies:
    def __init__(self, pairs, semaphores, ahead):
        self.copies = [
            pltpu.make_async_copy(source, target, semaphores.at[i])
            for i, (source, target) in enumerate(pairs)
        ]
        self.ahead = ahead
        self.waited = 0
        for copy in self.copies[:ahead]:
            copy.start()

    def wait(self, count=1):
        for _ in range(count):
            self.copies[self.waited].wait()
            following = self.waited + self.ahead
            if following < len(self.copies):
                self.copies[following].start()
            self.waited += 1


def regroup_kernel(weight_ref, out_ref, read_ref, reads):
    depth, heads, width = weight_ref.shape
    slots, rows = read_ref.shape[:2]
    steps = depth // rows

    def part(step):
        return pl.ds(pl.multiple_of(step * rows, rows), rows)

    def read(step, slot):
        return pltpu.make_async_copy(
            weight_ref.at[part(step)], read_ref.at[slot], reads.at[slot]
        )

    for slot in range(slots):
        read(slot, slot).start()

    @pl.loop(0, steps)
    def _(step):
        slot = lax.rem(step, slots)
        read(step, slot).wait()
        by_head = jnp.swapaxes(read_ref[slot], 0, 1)
        for head in range(heads):
            left = (head % GROUP) * width
            out_ref[head // GROUP, part(step), left : left + width] = by_head[head]

        @pl.when(step + slots < steps)
        def _():
            read(step + slots, slot).start()


def regroup(weight, rows, slots):
    depth, heads, width = weight.shape
    out = (heads // GROUP, depth, GROUP * width)
    return pl.pallas_call(
        regroup_kernel,
        out_shape=pltpu.VMEM(out, weight.dtype),
        in_specs=[pl.BlockSpec(memory_space=pl.ANY)],
        out_specs=pl.BlockSpec(memory_space=pltpu.VMEM),
        scratch_shapes=[
            pltpu.VMEM((slots, rows, heads, width), weight.dtype),
            pltpu.SemaphoreType.DMA((slots,)),
        ],
        compiler_params=params(12),
        cost_estimate=pl.CostEstimate(
            flops=0, bytes_accessed=4 * depth * heads * width, transcendentals=0
        ),
        name="regroup",
    )(pltpu.with_memory_space_constraint(weight, pltpu.HBM))


def listed_slots(neighbours_ref, tile_slot_ref):
    tiles, places = neighbours_ref.shape
    one, zero = jnp.int32(1), jnp.int32(0)
    allowed = [[zero] * tiles for _ in range(tiles)]
    for t in range(tiles):
        for u in range(tiles):
            listed = zero
            for k in range(places):
                listed = jnp.where(neighbours_ref[t, k] == u, one, listed)
            for r in range(tiles):
                for c in range(tiles):
                    here = (tile_slot_ref[t] == r) & (tile_slot_ref[u] == c)
                    allowed[r][c] = jnp.where(here, listed, allowed[r][c])
    return allowed


def normed(rows, gain):
    inverse = lax.rsqrt(jnp.mean(rows * rows, axis=-1, keepdims=True) + EPSILON)
    unit = rows * inverse
    return unit, inverse, (unit * gain).astype(BF16)


def forward_kernel(
    neighbours_ref,
    tile_slot_ref,
    own_ref,
    other_ref,
    weight_ref,
    out_weight_ref,
    query_gain_ref,
    key_gain_ref,
    gate_ref,
    projected_ref,
    probs_ref,
    attention_ref,
    kept_ref,
    sent_ref,
    out_weight_buffer,
    tokens_ref,
    semaphores,
):
    local, model = own_ref.shape
    tokens = 2 * local
    width = query_gain_ref.shape[1]
    groups = weight_ref.shape[0]
    rows = GROUP * width

    def out_weight_part(group):
        place = pl.ds(group * rows, rows)
        return out_weight_ref.at[place], out_weight_buffer.at[place]

    copies = Copies([out_weight_part(group) for group in range(groups)], semaphores, groups)

    tokens_ref[:local, :] = own_ref[...]
    tokens_ref[local:, :] = other_ref[...]
    allowed = listed_slots(neighbours_ref, tile_slot_ref)
    mine = lax.axis_index("seq")
    row_half = lax.broadcasted_iota(jnp.int32, (tokens, tokens), 0) // local
    column_half = lax.broadcasted_iota(jnp.int32, (tokens, tokens), 1) // local
    row_slot = jnp.where(row_half == 0, mine, 1 - mine)
    column_slot = jnp.where(column_half == 0, mine, 1 - mine)
    table = jnp.zeros((tokens, tokens), jnp.int32)
    for r in range(2):
        for c in range(2):
            table = jnp.where((row_slot == r) & (column_slot == c), allowed[r][c], table)
    bias = jnp.where(table > 0, 0.0, -jnp.inf).astype(F32)

    def project(group):
        projected_ref[group] = dot_nn(tokens_ref[...], weight_ref[group])

    def attend(group):
        attended = []
        for head in range(GROUP):
            left = head * 3 * width
            _, _, queries = normed(projected_ref[group, :, left : left + width], query_gain_ref[...])
            left += width
            _, _, keys = normed(projected_ref[group, :, left : left + width], key_gain_ref[...])
            left += width
            value = projected_ref[group, :, left : left + width].astype(BF16)
            scores = dot_nt(queries, keys) * (1.0 / math.sqrt(width)) + bias
            row_max = jnp.max(scores, axis=-1, keepdims=True)
            weights = jnp.exp(scores - row_max)
            probs = (weights / jnp.sum(weights, axis=-1, keepdims=True)).astype(BF16)
            probs_ref[GROUP * group + head] = probs
            attended.append(dot_nn(probs, value).astype(BF16))
        return jnp.concatenate(attended, axis=1)

    def share(group, attended):
        return dot_nn(attended, out_weight_buffer[group * rows : (group + 1) * rows, :])

    project(0)
    attended = attend(0)
    for group in range(1, groups):
        project(group)
        copies.wait()
        following = attend(group)
        if group == 1:
            attention_ref[...] = share(0, attended)
        else:
            attention_ref[...] += share(group - 1, attended)
        attended = following
    copies.wait()
    total = share(groups - 1, attended)
    if groups > 1:
        total += attention_ref[...]
    attention_ref[...] = total
    gate = gate_ref[...]
    kept_ref[...] = (own_ref[...].astype(F32) + gate * total[:local]).astype(BF16)
    sent_ref[...] = (gate * total[local:]).astype(BF16)


def forward(neighbours, tile_slot, own, other, weight, out_weight, query_gain, key_gain, gate):
    local, model = own.shape
    groups, _, wide = weight.shape
    tokens = 2 * local
    weight = pltpu.with_memory_space_constraint(weight, pltpu.VMEM)
    out_weight = pltpu.with_memory_space_constraint(out_weight, pltpu.HBM)
    smem = pl.BlockSpec(memory_space=pltpu.SMEM)
    vmem = pl.BlockSpec(memory_space=pltpu.VMEM)
    hbm = pl.BlockSpec(memory_space=pl.ANY)
    return pl.pallas_call(
        forward_kernel,
        out_shape=(
            jax.ShapeDtypeStruct((groups, tokens, wide), F32),
            jax.ShapeDtypeStruct((GROUP * groups, tokens, tokens), BF16),
            jax.ShapeDtypeStruct((tokens, model), F32),
            jax.ShapeDtypeStruct((local, model), BF16),
            jax.ShapeDtypeStruct((local, model), BF16),
            pltpu.VMEM(out_weight.shape, BF16),
        ),
        in_specs=[smem, smem, vmem, vmem, vmem, hbm, vmem, vmem, vmem],
        out_specs=(vmem,) * 6,
        scratch_shapes=[
            pltpu.VMEM((tokens, model), BF16),
            pltpu.SemaphoreType.DMA((groups,)),
        ],
        compiler_params=params(12),
        cost_estimate=pl.CostEstimate(
            flops=2 * tokens * (weight.size + out_weight.size),
            bytes_accessed=2 * (weight.size + out_weight.size),
            transcendentals=0,
        ),
        name="attention_forward",
    )(neighbours, tile_slot, own, other, weight, out_weight, query_gain, key_gain, gate)


def input_grad(grad_ref, weight_ref, own_ref, kept_ref, sent_ref):
    local, model = own_ref.shape
    block = 512
    for start in range(0, model, block):
        part = slice(start, start + block)
        total = dot_nt(weight_ref[0, part, :], grad_ref[0])
        for group in range(1, grad_ref.shape[0]):
            total += dot_nt(weight_ref[group, part, :], grad_ref[group])
        total = total.T
        kept_ref[:, part] = (own_ref[:, part].astype(F32) + total[:local]).astype(BF16)
        sent_ref[:, part] = total[local:].astype(BF16)


def backward_kernel(
    own_ref,
    other_ref,
    out_weight_ref,
    weight_ref,
    projected_ref,
    probs_ref,
    attention_ref,
    query_gain_ref,
    key_gain_ref,
    gate_ref,
    gate_kept_ref,
    gate_sent_ref,
    kept_ref,
    sent_ref,
    grad_ref,
    scaled_ref,
    attended_grad_ref,
    gate_grad_ref,
):
    local = own_ref.shape[0]
    width = query_gain_ref.shape[1]
    groups = grad_ref.shape[0]
    rows = GROUP * width

    gate = gate_ref[...]
    own, other = own_ref[...].astype(F32), other_ref[...].astype(F32)
    scaled_ref[:local, :] = (own * gate).astype(BF16)
    scaled_ref[local:, :] = (other * gate).astype(BF16)
    gate_grad_ref[...] = jnp.sum(
        own * attention_ref[:local, :] + other * attention_ref[local:, :], axis=0, keepdims=True
    )
    half = gate_kept_ref.shape[1]
    mine = lax.axis_index("seq")
    gate_kept_ref[...] = gate_grad_ref[:, pl.ds(pl.multiple_of(mine * half, half), half)]
    gate_sent_ref[...] = gate_grad_ref[:, pl.ds(pl.multiple_of((1 - mine) * half, half), half)]

    def attended_grad(group):
        part = slice(group * rows, (group + 1) * rows)
        product = dot_nt(scaled_ref[...], out_weight_ref[part, :])
        attended_grad_ref[group] = product.astype(BF16)

    def attend_backward(group, head):
        left = head * 3 * width
        query_part = slice(left, left + width)
        key_part = slice(left + width, left + 2 * width)
        value_part = slice(left + 2 * width, left + 3 * width)
        query_gain, key_gain = query_gain_ref[...], key_gain_ref[...]
        query_unit, query_inverse, queries = normed(projected_ref[group, :, query_part], query_gain)
        key_unit, key_inverse, keys = normed(projected_ref[group, :, key_part], key_gain)
        value = projected_ref[group, :, value_part].astype(BF16)
        grad = attended_grad_ref[group, :, head * width : (head + 1) * width]
        probs = probs_ref[GROUP * group + head]
        probs_wide = probs.astype(F32)
        grad_ref[group, :, value_part] = dot_tn(probs, grad).astype(BF16)
        prob_grad = dot_nt(grad, value)
        row_delta = jnp.sum(probs_wide * prob_grad, axis=-1, keepdims=True)
        scale_factor = 1.0 / math.sqrt(width)
        score_grad = (probs_wide * (prob_grad - row_delta) * scale_factor).astype(BF16)
        query_scaled = dot_nn(score_grad, keys) * query_gain
        key_scaled = dot_tn(score_grad, queries) * key_gain
        query_mean = jnp.mean(query_scaled * query_unit, axis=-1, keepdims=True)
        key_mean = jnp.mean(key_scaled * key_unit, axis=-1, keepdims=True)
        grad_ref[group, :, query_part] = (
            (query_scaled - query_unit * query_mean) * query_inverse
        ).astype(BF16)
        grad_ref[group, :, key_part] = ((key_scaled - key_unit * key_mean) * key_inverse).astype(BF16)

    attended_grad(0)
    for group in range(groups):
        if group + 1 < groups:
            attended_grad(group + 1)
        for head in range(GROUP):
            attend_backward(group, head)
    input_grad(grad_ref, weight_ref, own_ref, kept_ref, sent_ref)


def backward(
    own, other, out_weight, weight, projected, probs, attention, query_gain, key_gain, gate
):
    local, model = own.shape
    groups, tokens, wide = projected.shape
    head_dim = query_gain.shape[1]
    out_weight = pltpu.with_memory_space_constraint(out_weight, pltpu.VMEM)
    weight = pltpu.with_memory_space_constraint(weight, pltpu.VMEM)
    vmem = pl.BlockSpec(memory_space=pltpu.VMEM)
    return pl.pallas_call(
        backward_kernel,
        out_shape=(
            jax.ShapeDtypeStruct((1, model // 2), F32),
            jax.ShapeDtypeStruct((1, model // 2), F32),
            jax.ShapeDtypeStruct((local, model), BF16),
            jax.ShapeDtypeStruct((local, model), BF16),
        ),
        in_specs=[vmem] * 10,
        out_specs=(vmem,) * 4,
        scratch_shapes=[
            pltpu.VMEM((groups, tokens, wide), BF16),
            pltpu.VMEM((tokens, model), BF16),
            pltpu.VMEM((groups, tokens, GROUP * head_dim), BF16),
            pltpu.VMEM((1, model), F32),
        ],
        compiler_params=params(12),
        cost_estimate=pl.CostEstimate(
            flops=2 * tokens * (out_weight.size + weight.size),
            bytes_accessed=2 * (out_weight.size + weight.size),
            transcendentals=0,
        ),
        name="attention_backward",
    )(own, other, out_weight, weight, projected, probs, attention, query_gain, key_gain, gate)


def routed(block, seq_step, pipe_step):
    seq_size, pipe_size = lax.axis_size("seq"), lax.axis_size("pipe")
    route = []
    for i in range(seq_size):
        for j in range(pipe_size):
            target = (i + seq_step) % seq_size * pipe_size + (j + pipe_step) % pipe_size
            route.append((i * pipe_size + j, target))
    return lax.ppermute(block, ("seq", "pipe"), route)


def pair_body(
    segment_input,
    output_grad,
    qkv_weight,
    out_weight,
    query_gain,
    key_gain,
    gate_scale,
    neighbours,
    tile_slot,
):
    stream = segment_input[0]
    upstream = output_grad[0]
    out_local = out_weight[0]
    other_stream = routed(stream, 1, 0)
    weight = regroup(qkv_weight[0], 128, 8)
    weight, upstream = lax.optimization_barrier((weight, upstream))
    other_upstream = routed(upstream, 1, 0)
    projected, probs, attention, kept, sent, out_local = forward(
        neighbours,
        tile_slot,
        stream,
        other_stream,
        weight,
        out_local,
        query_gain,
        key_gain,
        gate_scale,
    )
    kept = routed(kept, 0, 1)
    sent = routed(sent, 1, 1)
    gate_kept, gate_sent, grad_kept, grad_sent = backward(
        upstream,
        other_upstream,
        out_local,
        weight,
        projected,
        probs,
        attention,
        query_gain,
        key_gain,
        gate_scale,
    )
    grad_kept, grad_sent, kept, sent = lax.optimization_barrier((grad_kept, grad_sent, kept, sent))
    grad_sent = routed(grad_sent, 1, -1)
    grad_kept = routed(grad_kept, 0, -1)
    segment_output = (kept.astype(F32) + sent.astype(F32)).astype(BF16)
    segment_output, gate_sent = lax.optimization_barrier((segment_output, gate_sent))
    gate_sent = routed(gate_sent, 1, 0)
    input_grad = (grad_kept.astype(F32) + grad_sent.astype(F32)).astype(BF16)
    return (segment_output[None], input_grad[None], gate_kept + gate_sent)


def solution(mesh):
    in_specs = (
        P("pipe", ("dp", "seq"), None),
        P("pipe", ("dp", "seq"), None),
        P("pipe", None, "seq", None),
        P("pipe", "seq", None),
        P("pipe", None),
        P("pipe", None),
        P("pipe", None),
        P("dp", None),
        P("dp"),
    )
    out_specs = (
        P("pipe", ("dp", "seq"), None),
        P("pipe", ("dp", "seq"), None),
        P(("dp", "pipe"), "seq"),
    )

    def body(*args):
        one_tile_each = args[0].shape[1] == TILE and args[8].shape[0] == 2
        if mesh.shape["seq"] == 2 and one_tile_each and args[2].shape[2] % GROUP == 0:
            return pair_body(*args)
        return general_body(*args)

    return jax.shard_map(body, mesh=mesh, in_specs=in_specs, out_specs=out_specs, check_vma=False)
```

```python
import functools
import math

import jax
import jax.numpy as jnp
from jax import lax
from jax.experimental import pallas as pl
from jax.experimental.pallas import tpu as pltpu
from jax.sharding import PartitionSpec as P

TILE = 64
EPSILON = 1e-06
F32 = jnp.float32
BF16 = jnp.bfloat16
MIB = 1024 * 1024
GROUP = 4


def passed_along(block, axis, distance):
    devices = range(lax.axis_size(axis))
    route = [((i - distance) % len(devices), i) for i in devices]
    return lax.ppermute(block, axis, route)


def slot_lists(neighbours, tile_slot):
    tile_count = tile_slot.shape[0]
    numbering = jnp.arange(tile_count, dtype=jnp.int32)
    placed = (tile_slot[:, None] == numbering[None, :]).astype(jnp.int32)
    tile_of_slot = jnp.sum(placed * numbering[:, None], axis=0)
    chosen = (tile_of_slot[:, None] == numbering[None, :]).astype(jnp.int32)
    listed_tiles = jnp.sum(chosen[:, :, None] * neighbours[None, :, :], axis=1)
    key_valid = listed_tiles >= 0
    safe_tiles = jnp.maximum(listed_tiles, 0)
    matches = (safe_tiles[:, :, None] == numbering[None, None, :]).astype(jnp.int32)
    key_slots = jnp.sum(matches * tile_slot[None, None, :], axis=2)
    return (key_slots, key_valid)


def block_tiles(tile_count):
    return math.gcd(tile_count, max(1, 512 // TILE))


def unit_norm(values):
    spread = jnp.sqrt(jnp.mean(values * values, axis=-1, keepdims=True) + EPSILON)
    return (values / spread, spread)


def probabilities(query_block, key_rows, block_valid):
    scores = jnp.einsum(
        "aihd,ajhd->ahij", query_block, key_rows, preferred_element_type=jnp.float32
    ) * (1.0 / math.sqrt(query_block.shape[-1]))
    key_mask = jnp.repeat(block_valid, TILE, axis=1)
    scores = jnp.where(key_mask[:, None, None, :], scores, -jnp.inf)
    row_max = jnp.max(scores, axis=-1, keepdims=True)
    weights = jnp.exp(scores - row_max)
    return (weights / jnp.sum(weights, axis=-1, keepdims=True)).astype(jnp.bfloat16)


def gathered(tiles_array, block_slots):
    picked = tiles_array[block_slots]
    return picked.reshape(block_slots.shape[0], -1, tiles_array.shape[2], tiles_array.shape[3])


def attend_both(query_tiles, key_tiles, value_tiles, grad_tiles, key_slots, key_valid):
    tile_count = query_tiles.shape[0]
    span = block_tiles(tile_count)
    scale_factor = 1.0 / math.sqrt(query_tiles.shape[-1])
    empty_grad = jnp.zeros(query_tiles.shape, jnp.float32)

    def per_block(accumulators, block_index):
        key_total, value_total = accumulators
        first_tile = block_index * span
        query_block = lax.dynamic_slice_in_dim(query_tiles, first_tile, span, 0)
        grad_block = lax.dynamic_slice_in_dim(grad_tiles, first_tile, span, 0)
        block_slots = lax.dynamic_slice_in_dim(key_slots, first_tile, span, 0)
        block_valid = lax.dynamic_slice_in_dim(key_valid, first_tile, span, 0)
        key_rows = gathered(key_tiles, block_slots)
        value_rows = gathered(value_tiles, block_slots)
        weights = probabilities(query_block, key_rows, block_valid)
        attended = jnp.einsum(
            "ahij,ajhd->aihd", weights, value_rows, preferred_element_type=jnp.float32
        )
        value_part = jnp.einsum(
            "ahij,aihd->ajhd", weights, grad_block, preferred_element_type=jnp.float32
        )
        prob_grad = jnp.einsum(
            "aihd,ajhd->ahij", grad_block, value_rows, preferred_element_type=jnp.float32
        )
        weights_wide = weights.astype(jnp.float32)
        row_delta = jnp.sum(weights_wide * prob_grad, axis=-1, keepdims=True)
        score_grad = (weights_wide * (prob_grad - row_delta) * scale_factor).astype(jnp.bfloat16)
        query_part = jnp.einsum(
            "ahij,ajhd->aihd", score_grad, key_rows, preferred_element_type=jnp.float32
        )
        key_part = jnp.einsum(
            "ahij,aihd->ajhd", score_grad, query_block, preferred_element_type=jnp.float32
        )
        block_shape = (span, block_slots.shape[1]) + query_tiles.shape[1:]
        key_total = key_total.at[block_slots].add(key_part.reshape(block_shape))
        value_total = value_total.at[block_slots].add(value_part.reshape(block_shape))
        return ((key_total, value_total), (attended, query_part))

    totals, parts = lax.scan(
        per_block, (empty_grad, empty_grad), jnp.arange(tile_count // span, dtype=jnp.int32)
    )
    flat_shape = (-1,) + query_tiles.shape[2:]
    return (
        parts[0].reshape(flat_shape),
        parts[1].reshape(flat_shape),
        totals[0].reshape(flat_shape),
        totals[1].reshape(flat_shape),
    )


def general_body(
    segment_input,
    output_grad,
    qkv_weight,
    out_weight,
    query_gain,
    key_gain,
    gate_scale,
    neighbours,
    tile_slot,
):
    key_slots, key_valid = slot_lists(neighbours, tile_slot)
    stream = segment_input[0]
    upstream = output_grad[0]
    model_width = stream.shape[1]
    head_dim = query_gain.shape[1]
    local_heads = qkv_weight.shape[2]
    local_width = local_heads * head_dim
    proj_weight = qkv_weight[0].reshape(model_width, local_heads * 3 * head_dim)
    out_local = out_weight[0]
    gate_row = gate_scale[0]
    query_weights = query_gain[0]
    key_weights = key_gain[0]
    projected = jnp.dot(
        lax.all_gather(stream, "seq", axis=0, tiled=True),
        proj_weight,
        preferred_element_type=jnp.float32,
    )
    all_tokens = projected.shape[0]
    projected = projected.reshape(all_tokens, local_heads, 3, head_dim)
    query_unit, query_spread = unit_norm(projected[:, :, 0])
    key_unit, key_spread = unit_norm(projected[:, :, 1])
    queries = (query_unit * query_weights).astype(jnp.bfloat16)
    keys_normed = (key_unit * key_weights).astype(jnp.bfloat16)
    value_rows = projected[:, :, 2].astype(jnp.bfloat16)
    scaled = (upstream.astype(jnp.float32) * gate_row).astype(jnp.bfloat16)
    attended_grad = jnp.einsum(
        "td,cd->tc",
        lax.all_gather(scaled, "seq", axis=0, tiled=True),
        out_local,
        preferred_element_type=jnp.float32,
    ).astype(jnp.bfloat16)

    def as_tiles(values):
        return values.reshape(-1, TILE, local_heads, head_dim)

    attended, query_grad, key_grad, value_grad = attend_both(
        as_tiles(queries),
        as_tiles(keys_normed),
        as_tiles(value_rows),
        as_tiles(attended_grad),
        key_slots,
        key_valid,
    )
    attended_low = attended.astype(jnp.bfloat16).reshape(all_tokens, local_width)
    rows = attended_low
    attention_out = lax.psum_scatter(
        jnp.dot(rows, out_local, preferred_element_type=jnp.float32),
        "seq",
        scatter_dimension=0,
        tiled=True,
    )
    section_out = (stream.astype(jnp.float32) + gate_row * attention_out).astype(jnp.bfloat16)
    segment_output = passed_along(section_out, "pipe", 1)
    gate_local = lax.psum_scatter(
        jnp.sum(upstream.astype(jnp.float32) * attention_out, axis=0),
        "seq",
        scatter_dimension=0,
        tiled=True,
    )
    query_scaled = query_grad * query_weights
    query_part_grad = (
        query_scaled - query_unit * jnp.mean(query_scaled * query_unit, axis=-1, keepdims=True)
    ) / query_spread
    key_scaled = key_grad * key_weights
    key_part_grad = (
        key_scaled - key_unit * jnp.mean(key_scaled * key_unit, axis=-1, keepdims=True)
    ) / key_spread
    projected_grad = (
        jnp.stack([query_part_grad, key_part_grad, value_grad], axis=2)
        .astype(jnp.bfloat16)
        .reshape(all_tokens, local_heads * 3 * head_dim)
    )
    rows = projected_grad
    stream_grad = lax.psum_scatter(
        jnp.einsum("tc,dc->td", rows, proj_weight, preferred_element_type=jnp.float32).astype(
            jnp.bfloat16
        ),
        "seq",
        scatter_dimension=0,
        tiled=True,
    ).astype(jnp.float32)
    token_grad = (upstream.astype(jnp.float32) + stream_grad).astype(jnp.bfloat16)
    input_grad = passed_along(token_grad, "pipe", -1)
    return (segment_output[None], input_grad[None], gate_local[None])


def dot_nn(a, b):
    return lax.dot_general(a, b, (((1,), (0,)), ((), ())), preferred_element_type=F32)


def dot_nt(a, b):
    return lax.dot_general(a, b, (((1,), (1,)), ((), ())), preferred_element_type=F32)


def dot_tn(a, b):
    return lax.dot_general(a, b, (((0,), (0,)), ((), ())), preferred_element_type=F32)


def params(mebibytes):
    return pltpu.CompilerParams(vmem_limit_bytes=mebibytes * MIB)


class Copies:
    def __init__(self, pairs, semaphores, ahead):
        self.copies = [
            pltpu.make_async_copy(source, target, semaphores.at[i])
            for i, (source, target) in enumerate(pairs)
        ]
        self.ahead = ahead
        self.waited = 0
        for copy in self.copies[:ahead]:
            copy.start()

    def wait(self, count=1):
        for _ in range(count):
            self.copies[self.waited].wait()
            following = self.waited + self.ahead
            if following < len(self.copies):
                self.copies[following].start()
            self.waited += 1


def regroup_kernel(weight_ref, out_ref, read_ref, reads):
    depth, heads, width = weight_ref.shape
    slots, rows = read_ref.shape[:2]
    steps = depth // rows

    def part(step):
        return pl.ds(pl.multiple_of(step * rows, rows), rows)

    def read(step, slot):
        return pltpu.make_async_copy(
            weight_ref.at[part(step)], read_ref.at[slot], reads.at[slot]
        )

    for slot in range(slots):
        read(slot, slot).start()

    @pl.loop(0, steps)
    def _(step):
        slot = lax.rem(step, slots)
        read(step, slot).wait()
        by_head = jnp.swapaxes(read_ref[slot], 0, 1)
        for head in range(heads):
            left = (head % GROUP) * width
            out_ref[head // GROUP, part(step), left : left + width] = by_head[head]

        @pl.when(step + slots < steps)
        def _():
            read(step + slots, slot).start()


def regroup(weight, rows, slots):
    depth, heads, width = weight.shape
    out = (heads // GROUP, depth, GROUP * width)
    return pl.pallas_call(
        regroup_kernel,
        out_shape=pltpu.VMEM(out, weight.dtype),
        in_specs=[pl.BlockSpec(memory_space=pl.ANY)],
        out_specs=pl.BlockSpec(memory_space=pltpu.VMEM),
        scratch_shapes=[
            pltpu.VMEM((slots, rows, heads, width), weight.dtype),
            pltpu.SemaphoreType.DMA((slots,)),
        ],
        compiler_params=params(12),
        cost_estimate=pl.CostEstimate(
            flops=0, bytes_accessed=4 * depth * heads * width, transcendentals=0
        ),
        name="regroup",
    )(pltpu.with_memory_space_constraint(weight, pltpu.HBM))


def listed_slots(neighbours_ref, tile_slot_ref):
    tiles, places = neighbours_ref.shape
    one, zero = jnp.int32(1), jnp.int32(0)
    allowed = [[zero] * tiles for _ in range(tiles)]
    for t in range(tiles):
        for u in range(tiles):
            listed = zero
            for k in range(places):
                listed = jnp.where(neighbours_ref[t, k] == u, one, listed)
            for r in range(tiles):
                for c in range(tiles):
                    here = (tile_slot_ref[t] == r) & (tile_slot_ref[u] == c)
                    allowed[r][c] = jnp.where(here, listed, allowed[r][c])
    return allowed


def normed(rows, gain):
    inverse = lax.rsqrt(jnp.mean(rows * rows, axis=-1, keepdims=True) + EPSILON)
    unit = rows * inverse
    return unit, inverse, (unit * gain).astype(BF16)


def forward_kernel(
    neighbours_ref,
    tile_slot_ref,
    own_ref,
    other_ref,
    weight_ref,
    out_weight_ref,
    query_gain_ref,
    key_gain_ref,
    gate_ref,
    projected_ref,
    probs_ref,
    attention_ref,
    kept_ref,
    sent_ref,
    out_weight_buffer,
    tokens_ref,
    semaphores,
):
    local, model = own_ref.shape
    tokens = 2 * local
    width = query_gain_ref.shape[1]
    groups = weight_ref.shape[0]
    rows = GROUP * width

    def out_weight_part(group):
        place = pl.ds(group * rows, rows)
        return out_weight_ref.at[place], out_weight_buffer.at[place]

    copies = Copies([out_weight_part(group) for group in range(groups)], semaphores, groups)

    tokens_ref[:local, :] = own_ref[...]
    tokens_ref[local:, :] = other_ref[...]
    allowed = listed_slots(neighbours_ref, tile_slot_ref)
    mine = lax.axis_index("seq")
    row_half = lax.broadcasted_iota(jnp.int32, (tokens, tokens), 0) // local
    column_half = lax.broadcasted_iota(jnp.int32, (tokens, tokens), 1) // local
    row_slot = jnp.where(row_half == 0, mine, 1 - mine)
    column_slot = jnp.where(column_half == 0, mine, 1 - mine)
    table = jnp.zeros((tokens, tokens), jnp.int32)
    for r in range(2):
        for c in range(2):
            table = jnp.where((row_slot == r) & (column_slot == c), allowed[r][c], table)
    bias = jnp.where(table > 0, 0.0, -jnp.inf).astype(F32)

    def project(group):
        projected_ref[group] = dot_nn(tokens_ref[...], weight_ref[group])

    def attend(group):
        attended = []
        for head in range(GROUP):
            left = head * 3 * width
            _, _, queries = normed(projected_ref[group, :, left : left + width], query_gain_ref[...])
            left += width
            _, _, keys = normed(projected_ref[group, :, left : left + width], key_gain_ref[...])
            left += width
            value = projected_ref[group, :, left : left + width].astype(BF16)
            scores = dot_nt(queries, keys) * (1.0 / math.sqrt(width)) + bias
            row_max = jnp.max(scores, axis=-1, keepdims=True)
            weights = jnp.exp(scores - row_max)
            probs = (weights / jnp.sum(weights, axis=-1, keepdims=True)).astype(BF16)
            probs_ref[GROUP * group + head] = probs
            attended.append(dot_nn(probs, value).astype(BF16))
        return jnp.concatenate(attended, axis=1)

    def share(group, attended):
        return dot_nn(attended, out_weight_buffer[group * rows : (group + 1) * rows, :])

    project(0)
    attended = attend(0)
    for group in range(1, groups):
        project(group)
        copies.wait()
        following = attend(group)
        if group == 1:
            attention_ref[...] = share(0, attended)
        else:
            attention_ref[...] += share(group - 1, attended)
        attended = following
    copies.wait()
    total = share(groups - 1, attended)
    if groups > 1:
        total += attention_ref[...]
    attention_ref[...] = total
    gate = gate_ref[...]
    kept_ref[...] = (own_ref[...].astype(F32) + gate * total[:local]).astype(BF16)
    sent_ref[...] = (gate * total[local:]).astype(BF16)


def forward(neighbours, tile_slot, own, other, weight, out_weight, query_gain, key_gain, gate):
    local, model = own.shape
    groups, _, wide = weight.shape
    tokens = 2 * local
    weight = pltpu.with_memory_space_constraint(weight, pltpu.VMEM)
    out_weight = pltpu.with_memory_space_constraint(out_weight, pltpu.HBM)
    smem = pl.BlockSpec(memory_space=pltpu.SMEM)
    vmem = pl.BlockSpec(memory_space=pltpu.VMEM)
    hbm = pl.BlockSpec(memory_space=pl.ANY)
    return pl.pallas_call(
        forward_kernel,
        out_shape=(
            jax.ShapeDtypeStruct((groups, tokens, wide), F32),
            jax.ShapeDtypeStruct((GROUP * groups, tokens, tokens), BF16),
            jax.ShapeDtypeStruct((tokens, model), F32),
            jax.ShapeDtypeStruct((local, model), BF16),
            jax.ShapeDtypeStruct((local, model), BF16),
            pltpu.VMEM(out_weight.shape, BF16),
        ),
        in_specs=[smem, smem, vmem, vmem, vmem, hbm, vmem, vmem, vmem],
        out_specs=(vmem,) * 6,
        scratch_shapes=[
            pltpu.VMEM((tokens, model), BF16),
            pltpu.SemaphoreType.DMA((groups,)),
        ],
        compiler_params=params(12),
        cost_estimate=pl.CostEstimate(
            flops=2 * tokens * (weight.size + out_weight.size),
            bytes_accessed=2 * (weight.size + out_weight.size),
            transcendentals=0,
        ),
        name="attention_forward",
    )(neighbours, tile_slot, own, other, weight, out_weight, query_gain, key_gain, gate)


def input_grad(grad_ref, weight_ref, own_ref, kept_ref, sent_ref):
    local, model = own_ref.shape
    block = 512
    for start in range(0, model, block):
        part = slice(start, start + block)
        total = dot_nt(weight_ref[0, part, :], grad_ref[0])
        for group in range(1, grad_ref.shape[0]):
            total += dot_nt(weight_ref[group, part, :], grad_ref[group])
        total = total.T
        kept_ref[:, part] = (own_ref[:, part].astype(F32) + total[:local]).astype(BF16)
        sent_ref[:, part] = total[local:].astype(BF16)


def backward_kernel(
    own_ref,
    other_ref,
    out_weight_ref,
    weight_ref,
    projected_ref,
    probs_ref,
    attention_ref,
    query_gain_ref,
    key_gain_ref,
    gate_ref,
    gate_kept_ref,
    gate_sent_ref,
    kept_ref,
    sent_ref,
    grad_ref,
    scaled_ref,
    attended_grad_ref,
    gate_grad_ref,
):
    local = own_ref.shape[0]
    width = query_gain_ref.shape[1]
    groups = grad_ref.shape[0]
    rows = GROUP * width

    gate = gate_ref[...]
    own, other = own_ref[...].astype(F32), other_ref[...].astype(F32)
    scaled_ref[:local, :] = (own * gate).astype(BF16)
    scaled_ref[local:, :] = (other * gate).astype(BF16)
    gate_grad_ref[...] = jnp.sum(
        own * attention_ref[:local, :] + other * attention_ref[local:, :], axis=0, keepdims=True
    )
    half = gate_kept_ref.shape[1]
    mine = lax.axis_index("seq")
    gate_kept_ref[...] = gate_grad_ref[:, pl.ds(pl.multiple_of(mine * half, half), half)]
    gate_sent_ref[...] = gate_grad_ref[:, pl.ds(pl.multiple_of((1 - mine) * half, half), half)]

    def attended_grad(group):
        part = slice(group * rows, (group + 1) * rows)
        product = dot_nt(scaled_ref[...], out_weight_ref[part, :])
        attended_grad_ref[group] = product.astype(BF16)

    def attend_backward(group, head):
        left = head * 3 * width
        query_part = slice(left, left + width)
        key_part = slice(left + width, left + 2 * width)
        value_part = slice(left + 2 * width, left + 3 * width)
        query_gain, key_gain = query_gain_ref[...], key_gain_ref[...]
        query_unit, query_inverse, queries = normed(projected_ref[group, :, query_part], query_gain)
        key_unit, key_inverse, keys = normed(projected_ref[group, :, key_part], key_gain)
        value = projected_ref[group, :, value_part].astype(BF16)
        grad = attended_grad_ref[group, :, head * width : (head + 1) * width]
        probs = probs_ref[GROUP * group + head]
        probs_wide = probs.astype(F32)
        grad_ref[group, :, value_part] = dot_tn(probs, grad).astype(BF16)
        prob_grad = dot_nt(grad, value)
        row_delta = jnp.sum(probs_wide * prob_grad, axis=-1, keepdims=True)
        scale_factor = 1.0 / math.sqrt(width)
        score_grad = (probs_wide * (prob_grad - row_delta) * scale_factor).astype(BF16)
        query_scaled = dot_nn(score_grad, keys) * query_gain
        key_scaled = dot_tn(score_grad, queries) * key_gain
        query_mean = jnp.mean(query_scaled * query_unit, axis=-1, keepdims=True)
        key_mean = jnp.mean(key_scaled * key_unit, axis=-1, keepdims=True)
        grad_ref[group, :, query_part] = (
            (query_scaled - query_unit * query_mean) * query_inverse
        ).astype(BF16)
        grad_ref[group, :, key_part] = ((key_scaled - key_unit * key_mean) * key_inverse).astype(BF16)

    attended_grad(0)
    for group in range(groups):
        if group + 1 < groups:
            attended_grad(group + 1)
        for head in range(GROUP):
            attend_backward(group, head)
    input_grad(grad_ref, weight_ref, own_ref, kept_ref, sent_ref)


def backward(
    own, other, out_weight, weight, projected, probs, attention, query_gain, key_gain, gate
):
    local, model = own.shape
    groups, tokens, wide = projected.shape
    head_dim = query_gain.shape[1]
    out_weight = pltpu.with_memory_space_constraint(out_weight, pltpu.VMEM)
    weight = pltpu.with_memory_space_constraint(weight, pltpu.VMEM)
    vmem = pl.BlockSpec(memory_space=pltpu.VMEM)
    return pl.pallas_call(
        backward_kernel,
        out_shape=(
            jax.ShapeDtypeStruct((1, model // 2), F32),
            jax.ShapeDtypeStruct((1, model // 2), F32),
            jax.ShapeDtypeStruct((local, model), BF16),
            jax.ShapeDtypeStruct((local, model), BF16),
        ),
        in_specs=[vmem] * 10,
        out_specs=(vmem,) * 4,
        scratch_shapes=[
            pltpu.VMEM((groups, tokens, wide), BF16),
            pltpu.VMEM((tokens, model), BF16),
            pltpu.VMEM((groups, tokens, GROUP * head_dim), BF16),
            pltpu.VMEM((1, model), F32),
        ],
        compiler_params=params(12),
        cost_estimate=pl.CostEstimate(
            flops=2 * tokens * (out_weight.size + weight.size),
            bytes_accessed=2 * (out_weight.size + weight.size),
            transcendentals=0,
        ),
        name="attention_backward",
    )(own, other, out_weight, weight, projected, probs, attention, query_gain, key_gain, gate)


def routed(block, seq_step, pipe_step):
    seq_size, pipe_size = lax.axis_size("seq"), lax.axis_size("pipe")
    route = []
    for i in range(seq_size):
        for j in range(pipe_size):
            target = (i + seq_step) % seq_size * pipe_size + (j + pipe_step) % pipe_size
            route.append((i * pipe_size + j, target))
    return lax.ppermute(block, ("seq", "pipe"), route)


def pair_body(
    segment_input,
    output_grad,
    qkv_weight,
    out_weight,
    query_gain,
    key_gain,
    gate_scale,
    neighbours,
    tile_slot,
):
    stream = segment_input[0]
    upstream = output_grad[0]
    out_local = out_weight[0]
    other_stream = routed(stream, 1, 0)
    weight = regroup(qkv_weight[0], 128, 8)
    weight, upstream = lax.optimization_barrier((weight, upstream))
    other_upstream = routed(upstream, 1, 0)
    projected, probs, attention, kept, sent, out_local = forward(
        neighbours,
        tile_slot,
        stream,
        other_stream,
        weight,
        out_local,
        query_gain,
        key_gain,
        gate_scale,
    )
    kept = routed(kept, 0, 1)
    sent = routed(sent, 1, 1)
    gate_kept, gate_sent, grad_kept, grad_sent = backward(
        upstream,
        other_upstream,
        out_local,
        weight,
        projected,
        probs,
        attention,
        query_gain,
        key_gain,
        gate_scale,
    )
    grad_sent = routed(grad_sent, 1, -1)
    grad_kept = routed(grad_kept, 0, -1)
    segment_output = (kept.astype(F32) + sent.astype(F32)).astype(BF16)
    segment_output, gate_sent = lax.optimization_barrier((segment_output, gate_sent))
    gate_sent = routed(gate_sent, 1, 0)
    input_grad = (grad_kept.astype(F32) + grad_sent.astype(F32)).astype(BF16)
    input_grad, gate_sent = lax.optimization_barrier((input_grad, gate_sent))
    return (segment_output[None], input_grad[None], gate_kept + gate_sent)


def solution(mesh):
    in_specs = (
        P("pipe", ("dp", "seq"), None),
        P("pipe", ("dp", "seq"), None),
        P("pipe", None, "seq", None),
        P("pipe", "seq", None),
        P("pipe", None),
        P("pipe", None),
        P("pipe", None),
        P("dp", None),
        P("dp"),
    )
    out_specs = (
        P("pipe", ("dp", "seq"), None),
        P("pipe", ("dp", "seq"), None),
        P(("dp", "pipe"), "seq"),
    )

    def body(*args):
        one_tile_each = args[0].shape[1] == TILE and args[8].shape[0] == 2
        if mesh.shape["seq"] == 2 and one_tile_each and args[2].shape[2] % GROUP == 0:
            return pair_body(*args)
        return general_body(*args)

    return jax.shard_map(body, mesh=mesh, in_specs=in_specs, out_specs=out_specs, check_vma=False)
```

```python
import functools
import math

import jax
import jax.numpy as jnp
from jax import lax
from jax.experimental import pallas as pl
from jax.experimental.pallas import tpu as pltpu
from jax.sharding import PartitionSpec as P

TILE = 64
EPSILON = 1e-06
F32 = jnp.float32
BF16 = jnp.bfloat16
MIB = 1024 * 1024
GROUP = 4


def passed_along(block, axis, distance):
    devices = range(lax.axis_size(axis))
    route = [((i - distance) % len(devices), i) for i in devices]
    return lax.ppermute(block, axis, route)


def slot_lists(neighbours, tile_slot):
    tile_count = tile_slot.shape[0]
    numbering = jnp.arange(tile_count, dtype=jnp.int32)
    placed = (tile_slot[:, None] == numbering[None, :]).astype(jnp.int32)
    tile_of_slot = jnp.sum(placed * numbering[:, None], axis=0)
    chosen = (tile_of_slot[:, None] == numbering[None, :]).astype(jnp.int32)
    listed_tiles = jnp.sum(chosen[:, :, None] * neighbours[None, :, :], axis=1)
    key_valid = listed_tiles >= 0
    safe_tiles = jnp.maximum(listed_tiles, 0)
    matches = (safe_tiles[:, :, None] == numbering[None, None, :]).astype(jnp.int32)
    key_slots = jnp.sum(matches * tile_slot[None, None, :], axis=2)
    return (key_slots, key_valid)


def block_tiles(tile_count):
    return math.gcd(tile_count, max(1, 512 // TILE))


def unit_norm(values):
    spread = jnp.sqrt(jnp.mean(values * values, axis=-1, keepdims=True) + EPSILON)
    return (values / spread, spread)


def probabilities(query_block, key_rows, block_valid):
    scores = jnp.einsum(
        "aihd,ajhd->ahij", query_block, key_rows, preferred_element_type=jnp.float32
    ) * (1.0 / math.sqrt(query_block.shape[-1]))
    key_mask = jnp.repeat(block_valid, TILE, axis=1)
    scores = jnp.where(key_mask[:, None, None, :], scores, -jnp.inf)
    row_max = jnp.max(scores, axis=-1, keepdims=True)
    weights = jnp.exp(scores - row_max)
    return (weights / jnp.sum(weights, axis=-1, keepdims=True)).astype(jnp.bfloat16)


def gathered(tiles_array, block_slots):
    picked = tiles_array[block_slots]
    return picked.reshape(block_slots.shape[0], -1, tiles_array.shape[2], tiles_array.shape[3])


def attend_both(query_tiles, key_tiles, value_tiles, grad_tiles, key_slots, key_valid):
    tile_count = query_tiles.shape[0]
    span = block_tiles(tile_count)
    scale_factor = 1.0 / math.sqrt(query_tiles.shape[-1])
    empty_grad = jnp.zeros(query_tiles.shape, jnp.float32)

    def per_block(accumulators, block_index):
        key_total, value_total = accumulators
        first_tile = block_index * span
        query_block = lax.dynamic_slice_in_dim(query_tiles, first_tile, span, 0)
        grad_block = lax.dynamic_slice_in_dim(grad_tiles, first_tile, span, 0)
        block_slots = lax.dynamic_slice_in_dim(key_slots, first_tile, span, 0)
        block_valid = lax.dynamic_slice_in_dim(key_valid, first_tile, span, 0)
        key_rows = gathered(key_tiles, block_slots)
        value_rows = gathered(value_tiles, block_slots)
        weights = probabilities(query_block, key_rows, block_valid)
        attended = jnp.einsum(
            "ahij,ajhd->aihd", weights, value_rows, preferred_element_type=jnp.float32
        )
        value_part = jnp.einsum(
            "ahij,aihd->ajhd", weights, grad_block, preferred_element_type=jnp.float32
        )
        prob_grad = jnp.einsum(
            "aihd,ajhd->ahij", grad_block, value_rows, preferred_element_type=jnp.float32
        )
        weights_wide = weights.astype(jnp.float32)
        row_delta = jnp.sum(weights_wide * prob_grad, axis=-1, keepdims=True)
        score_grad = (weights_wide * (prob_grad - row_delta) * scale_factor).astype(jnp.bfloat16)
        query_part = jnp.einsum(
            "ahij,ajhd->aihd", score_grad, key_rows, preferred_element_type=jnp.float32
        )
        key_part = jnp.einsum(
            "ahij,aihd->ajhd", score_grad, query_block, preferred_element_type=jnp.float32
        )
        block_shape = (span, block_slots.shape[1]) + query_tiles.shape[1:]
        key_total = key_total.at[block_slots].add(key_part.reshape(block_shape))
        value_total = value_total.at[block_slots].add(value_part.reshape(block_shape))
        return ((key_total, value_total), (attended, query_part))

    totals, parts = lax.scan(
        per_block, (empty_grad, empty_grad), jnp.arange(tile_count // span, dtype=jnp.int32)
    )
    flat_shape = (-1,) + query_tiles.shape[2:]
    return (
        parts[0].reshape(flat_shape),
        parts[1].reshape(flat_shape),
        totals[0].reshape(flat_shape),
        totals[1].reshape(flat_shape),
    )


def general_body(
    segment_input,
    output_grad,
    qkv_weight,
    out_weight,
    query_gain,
    key_gain,
    gate_scale,
    neighbours,
    tile_slot,
):
    key_slots, key_valid = slot_lists(neighbours, tile_slot)
    stream = segment_input[0]
    upstream = output_grad[0]
    model_width = stream.shape[1]
    head_dim = query_gain.shape[1]
    local_heads = qkv_weight.shape[2]
    local_width = local_heads * head_dim
    proj_weight = qkv_weight[0].reshape(model_width, local_heads * 3 * head_dim)
    out_local = out_weight[0]
    gate_row = gate_scale[0]
    query_weights = query_gain[0]
    key_weights = key_gain[0]
    projected = jnp.dot(
        lax.all_gather(stream, "seq", axis=0, tiled=True),
        proj_weight,
        preferred_element_type=jnp.float32,
    )
    all_tokens = projected.shape[0]
    projected = projected.reshape(all_tokens, local_heads, 3, head_dim)
    query_unit, query_spread = unit_norm(projected[:, :, 0])
    key_unit, key_spread = unit_norm(projected[:, :, 1])
    queries = (query_unit * query_weights).astype(jnp.bfloat16)
    keys_normed = (key_unit * key_weights).astype(jnp.bfloat16)
    value_rows = projected[:, :, 2].astype(jnp.bfloat16)
    scaled = (upstream.astype(jnp.float32) * gate_row).astype(jnp.bfloat16)
    attended_grad = jnp.einsum(
        "td,cd->tc",
        lax.all_gather(scaled, "seq", axis=0, tiled=True),
        out_local,
        preferred_element_type=jnp.float32,
    ).astype(jnp.bfloat16)

    def as_tiles(values):
        return values.reshape(-1, TILE, local_heads, head_dim)

    attended, query_grad, key_grad, value_grad = attend_both(
        as_tiles(queries),
        as_tiles(keys_normed),
        as_tiles(value_rows),
        as_tiles(attended_grad),
        key_slots,
        key_valid,
    )
    attended_low = attended.astype(jnp.bfloat16).reshape(all_tokens, local_width)
    rows = attended_low
    attention_out = lax.psum_scatter(
        jnp.dot(rows, out_local, preferred_element_type=jnp.float32),
        "seq",
        scatter_dimension=0,
        tiled=True,
    )
    section_out = (stream.astype(jnp.float32) + gate_row * attention_out).astype(jnp.bfloat16)
    segment_output = passed_along(section_out, "pipe", 1)
    gate_local = lax.psum_scatter(
        jnp.sum(upstream.astype(jnp.float32) * attention_out, axis=0),
        "seq",
        scatter_dimension=0,
        tiled=True,
    )
    query_scaled = query_grad * query_weights
    query_part_grad = (
        query_scaled - query_unit * jnp.mean(query_scaled * query_unit, axis=-1, keepdims=True)
    ) / query_spread
    key_scaled = key_grad * key_weights
    key_part_grad = (
        key_scaled - key_unit * jnp.mean(key_scaled * key_unit, axis=-1, keepdims=True)
    ) / key_spread
    projected_grad = (
        jnp.stack([query_part_grad, key_part_grad, value_grad], axis=2)
        .astype(jnp.bfloat16)
        .reshape(all_tokens, local_heads * 3 * head_dim)
    )
    rows = projected_grad
    stream_grad = lax.psum_scatter(
        jnp.einsum("tc,dc->td", rows, proj_weight, preferred_element_type=jnp.float32).astype(
            jnp.bfloat16
        ),
        "seq",
        scatter_dimension=0,
        tiled=True,
    ).astype(jnp.float32)
    token_grad = (upstream.astype(jnp.float32) + stream_grad).astype(jnp.bfloat16)
    input_grad = passed_along(token_grad, "pipe", -1)
    return (segment_output[None], input_grad[None], gate_local[None])


def dot_nn(a, b):
    return lax.dot_general(a, b, (((1,), (0,)), ((), ())), preferred_element_type=F32)


def dot_nt(a, b):
    return lax.dot_general(a, b, (((1,), (1,)), ((), ())), preferred_element_type=F32)


def dot_tn(a, b):
    return lax.dot_general(a, b, (((0,), (0,)), ((), ())), preferred_element_type=F32)


def params(mebibytes):
    return pltpu.CompilerParams(vmem_limit_bytes=mebibytes * MIB)


class Copies:
    def __init__(self, pairs, semaphores, ahead):
        self.copies = [
            pltpu.make_async_copy(source, target, semaphores.at[i])
            for i, (source, target) in enumerate(pairs)
        ]
        self.ahead = ahead
        self.waited = 0
        for copy in self.copies[:ahead]:
            copy.start()

    def wait(self, count=1):
        for _ in range(count):
            self.copies[self.waited].wait()
            following = self.waited + self.ahead
            if following < len(self.copies):
                self.copies[following].start()
            self.waited += 1


def regroup_kernel(weight_ref, out_ref, read_ref, reads):
    depth, heads, width = weight_ref.shape
    slots, rows = read_ref.shape[:2]
    steps = depth // rows

    def part(step):
        return pl.ds(pl.multiple_of(step * rows, rows), rows)

    def read(step, slot):
        return pltpu.make_async_copy(
            weight_ref.at[part(step)], read_ref.at[slot], reads.at[slot]
        )

    for slot in range(slots):
        read(slot, slot).start()

    @pl.loop(0, steps)
    def _(step):
        slot = lax.rem(step, slots)
        read(step, slot).wait()
        by_head = jnp.swapaxes(read_ref[slot], 0, 1)
        for head in range(heads):
            left = (head % GROUP) * width
            out_ref[head // GROUP, part(step), left : left + width] = by_head[head]

        @pl.when(step + slots < steps)
        def _():
            read(step + slots, slot).start()


def regroup(weight, rows, slots):
    depth, heads, width = weight.shape
    out = (heads // GROUP, depth, GROUP * width)
    return pl.pallas_call(
        regroup_kernel,
        out_shape=pltpu.VMEM(out, weight.dtype),
        in_specs=[pl.BlockSpec(memory_space=pl.ANY)],
        out_specs=pl.BlockSpec(memory_space=pltpu.VMEM),
        scratch_shapes=[
            pltpu.VMEM((slots, rows, heads, width), weight.dtype),
            pltpu.SemaphoreType.DMA((slots,)),
        ],
        compiler_params=params(12),
        cost_estimate=pl.CostEstimate(
            flops=0, bytes_accessed=4 * depth * heads * width, transcendentals=0
        ),
        name="regroup",
    )(pltpu.with_memory_space_constraint(weight, pltpu.HBM))


def listed_slots(neighbours_ref, tile_slot_ref):
    tiles, places = neighbours_ref.shape
    one, zero = jnp.int32(1), jnp.int32(0)
    allowed = [[zero] * tiles for _ in range(tiles)]
    for t in range(tiles):
        for u in range(tiles):
            listed = zero
            for k in range(places):
                listed = jnp.where(neighbours_ref[t, k] == u, one, listed)
            for r in range(tiles):
                for c in range(tiles):
                    here = (tile_slot_ref[t] == r) & (tile_slot_ref[u] == c)
                    allowed[r][c] = jnp.where(here, listed, allowed[r][c])
    return allowed


def normed(rows, gain):
    inverse = lax.rsqrt(jnp.mean(rows * rows, axis=-1, keepdims=True) + EPSILON)
    unit = rows * inverse
    return unit, inverse, (unit * gain).astype(BF16)


def forward_kernel(
    neighbours_ref,
    tile_slot_ref,
    own_ref,
    other_ref,
    weight_ref,
    out_weight_ref,
    query_gain_ref,
    key_gain_ref,
    gate_ref,
    projected_ref,
    probs_ref,
    attention_ref,
    kept_ref,
    sent_ref,
    out_weight_buffer,
    tokens_ref,
    semaphores,
):
    local, model = own_ref.shape
    tokens = 2 * local
    width = query_gain_ref.shape[1]
    groups = weight_ref.shape[0]
    rows = GROUP * width

    def out_weight_part(group):
        place = pl.ds(group * rows, rows)
        return out_weight_ref.at[place], out_weight_buffer.at[place]

    copies = Copies([out_weight_part(group) for group in range(groups)], semaphores, groups)

    tokens_ref[:local, :] = own_ref[...]
    tokens_ref[local:, :] = other_ref[...]
    allowed = listed_slots(neighbours_ref, tile_slot_ref)
    mine = lax.axis_index("seq")
    row_half = lax.broadcasted_iota(jnp.int32, (tokens, tokens), 0) // local
    column_half = lax.broadcasted_iota(jnp.int32, (tokens, tokens), 1) // local
    row_slot = jnp.where(row_half == 0, mine, 1 - mine)
    column_slot = jnp.where(column_half == 0, mine, 1 - mine)
    table = jnp.zeros((tokens, tokens), jnp.int32)
    for r in range(2):
        for c in range(2):
            table = jnp.where((row_slot == r) & (column_slot == c), allowed[r][c], table)
    bias = jnp.where(table > 0, 0.0, -jnp.inf).astype(F32)

    def project(group):
        projected_ref[group] = dot_nn(tokens_ref[...], weight_ref[group])

    def attend(group):
        attended = []
        for head in range(GROUP):
            left = head * 3 * width
            _, _, queries = normed(projected_ref[group, :, left : left + width], query_gain_ref[...])
            left += width
            _, _, keys = normed(projected_ref[group, :, left : left + width], key_gain_ref[...])
            left += width
            value = projected_ref[group, :, left : left + width].astype(BF16)
            scores = dot_nt(queries, keys) * (1.0 / math.sqrt(width)) + bias
            row_max = jnp.max(scores, axis=-1, keepdims=True)
            weights = jnp.exp(scores - row_max)
            probs = (weights / jnp.sum(weights, axis=-1, keepdims=True)).astype(BF16)
            probs_ref[GROUP * group + head] = probs
            attended.append(dot_nn(probs, value).astype(BF16))
        return jnp.concatenate(attended, axis=1)

    def share(group, attended):
        return dot_nn(attended, out_weight_buffer[group * rows : (group + 1) * rows, :])

    project(0)
    attended = attend(0)
    for group in range(1, groups):
        project(group)
        copies.wait()
        following = attend(group)
        if group == 1:
            attention_ref[...] = share(0, attended)
        else:
            attention_ref[...] += share(group - 1, attended)
        attended = following
    copies.wait()
    total = share(groups - 1, attended)
    if groups > 1:
        total += attention_ref[...]
    attention_ref[...] = total
    gate = gate_ref[...]
    kept_ref[...] = (own_ref[...].astype(F32) + gate * total[:local]).astype(BF16)
    sent_ref[...] = (gate * total[local:]).astype(BF16)


def forward(neighbours, tile_slot, own, other, weight, out_weight, query_gain, key_gain, gate):
    local, model = own.shape
    groups, _, wide = weight.shape
    tokens = 2 * local
    weight = pltpu.with_memory_space_constraint(weight, pltpu.VMEM)
    out_weight = pltpu.with_memory_space_constraint(out_weight, pltpu.HBM)
    smem = pl.BlockSpec(memory_space=pltpu.SMEM)
    vmem = pl.BlockSpec(memory_space=pltpu.VMEM)
    hbm = pl.BlockSpec(memory_space=pl.ANY)
    return pl.pallas_call(
        forward_kernel,
        out_shape=(
            jax.ShapeDtypeStruct((groups, tokens, wide), F32),
            jax.ShapeDtypeStruct((GROUP * groups, tokens, tokens), BF16),
            jax.ShapeDtypeStruct((tokens, model), F32),
            jax.ShapeDtypeStruct((local, model), BF16),
            jax.ShapeDtypeStruct((local, model), BF16),
            pltpu.VMEM(out_weight.shape, BF16),
        ),
        in_specs=[smem, smem, vmem, vmem, vmem, hbm, vmem, vmem, vmem],
        out_specs=(vmem,) * 6,
        scratch_shapes=[
            pltpu.VMEM((tokens, model), BF16),
            pltpu.SemaphoreType.DMA((groups,)),
        ],
        compiler_params=params(12),
        cost_estimate=pl.CostEstimate(
            flops=2 * tokens * (weight.size + out_weight.size),
            bytes_accessed=2 * (weight.size + out_weight.size),
            transcendentals=0,
        ),
        name="attention_forward",
    )(neighbours, tile_slot, own, other, weight, out_weight, query_gain, key_gain, gate)


def backward_kernel(
    own_ref,
    other_ref,
    out_weight_ref,
    weight_ref,
    projected_ref,
    probs_ref,
    attention_ref,
    query_gain_ref,
    key_gain_ref,
    gate_ref,
    gate_kept_ref,
    gate_sent_ref,
    kept_ref,
    sent_ref,
    grad_ref,
    scaled_ref,
    attended_grad_ref,
    gate_grad_ref,
    partial_ref,
):
    local = own_ref.shape[0]
    width = query_gain_ref.shape[1]
    groups = grad_ref.shape[0]
    rows = GROUP * width

    model = own_ref.shape[1]
    gate = gate_ref[...]
    scaled_ref[:local, :] = (own_ref[...].astype(F32) * gate).astype(BF16)
    scaled_ref[local:, :] = (other_ref[...].astype(F32) * gate).astype(BF16)

    def attended_grad(group):
        part = slice(group * rows, (group + 1) * rows)
        product = dot_nt(scaled_ref[...], out_weight_ref[part, :])
        attended_grad_ref[group] = product.astype(BF16)

    def attend_backward(group, head):
        left = head * 3 * width
        query_part = slice(left, left + width)
        key_part = slice(left + width, left + 2 * width)
        value_part = slice(left + 2 * width, left + 3 * width)
        query_gain, key_gain = query_gain_ref[...], key_gain_ref[...]
        query_unit, query_inverse, queries = normed(projected_ref[group, :, query_part], query_gain)
        key_unit, key_inverse, keys = normed(projected_ref[group, :, key_part], key_gain)
        value = projected_ref[group, :, value_part].astype(BF16)
        grad = attended_grad_ref[group, :, head * width : (head + 1) * width]
        probs = probs_ref[GROUP * group + head]
        probs_wide = probs.astype(F32)
        grad_ref[group, :, value_part] = dot_tn(probs, grad).astype(BF16)
        prob_grad = dot_nt(grad, value)
        row_delta = jnp.sum(probs_wide * prob_grad, axis=-1, keepdims=True)
        scale_factor = 1.0 / math.sqrt(width)
        score_grad = (probs_wide * (prob_grad - row_delta) * scale_factor).astype(BF16)
        query_scaled = dot_nn(score_grad, keys) * query_gain
        key_scaled = dot_tn(score_grad, queries) * key_gain
        query_mean = jnp.mean(query_scaled * query_unit, axis=-1, keepdims=True)
        key_mean = jnp.mean(key_scaled * key_unit, axis=-1, keepdims=True)
        grad_ref[group, :, query_part] = (
            (query_scaled - query_unit * query_mean) * query_inverse
        ).astype(BF16)
        grad_ref[group, :, key_part] = ((key_scaled - key_unit * key_mean) * key_inverse).astype(BF16)

    def input_grad(group, part):
        return dot_nt(grad_ref[group], weight_ref[group, part, :])

    block = 512
    blocks = [slice(start, start + block) for start in range(0, model, block)]
    attended_grad(0)
    for group in range(groups):
        if group + 1 < groups:
            attended_grad(group + 1)
        for head in range(GROUP):
            attend_backward(group, head)
            if group > 0:
                for part in blocks[head::GROUP]:
                    product = input_grad(group - 1, part)
                    if group > 1:
                        product += partial_ref[:, part]
                    partial_ref[:, part] = product
    for part in blocks:
        total = input_grad(groups - 1, part)
        if groups > 1:
            total += partial_ref[:, part]
        own, other = own_ref[:, part].astype(F32), other_ref[:, part].astype(F32)
        kept_ref[:, part] = (own + total[:local]).astype(BF16)
        sent_ref[:, part] = total[local:].astype(BF16)
        gate_grad_ref[:, part] = jnp.sum(
            own * attention_ref[:local, part] + other * attention_ref[local:, part],
            axis=0,
            keepdims=True,
        )
    half = gate_kept_ref.shape[1]
    mine = lax.axis_index("seq")
    gate_kept_ref[...] = gate_grad_ref[:, pl.ds(pl.multiple_of(mine * half, half), half)]
    gate_sent_ref[...] = gate_grad_ref[:, pl.ds(pl.multiple_of((1 - mine) * half, half), half)]


def backward(
    own, other, out_weight, weight, projected, probs, attention, query_gain, key_gain, gate
):
    local, model = own.shape
    groups, tokens, wide = projected.shape
    head_dim = query_gain.shape[1]
    out_weight = pltpu.with_memory_space_constraint(out_weight, pltpu.VMEM)
    weight = pltpu.with_memory_space_constraint(weight, pltpu.VMEM)
    vmem = pl.BlockSpec(memory_space=pltpu.VMEM)
    return pl.pallas_call(
        backward_kernel,
        out_shape=(
            jax.ShapeDtypeStruct((1, model // 2), F32),
            jax.ShapeDtypeStruct((1, model // 2), F32),
            jax.ShapeDtypeStruct((local, model), BF16),
            jax.ShapeDtypeStruct((local, model), BF16),
        ),
        in_specs=[vmem] * 10,
        out_specs=(vmem,) * 4,
        scratch_shapes=[
            pltpu.VMEM((groups, tokens, wide), BF16),
            pltpu.VMEM((tokens, model), BF16),
            pltpu.VMEM((groups, tokens, GROUP * head_dim), BF16),
            pltpu.VMEM((1, model), F32),
            pltpu.VMEM((tokens, model), F32),
        ],
        compiler_params=params(12),
        cost_estimate=pl.CostEstimate(
            flops=2 * tokens * (out_weight.size + weight.size),
            bytes_accessed=2 * (out_weight.size + weight.size),
            transcendentals=0,
        ),
        name="attention_backward",
    )(own, other, out_weight, weight, projected, probs, attention, query_gain, key_gain, gate)


def sums_kernel(kept_ref, sent_ref, gate_kept_ref, gate_sent_ref, grad_ref, gate_ref):
    grad_ref[...] = (kept_ref[...].astype(F32) + sent_ref[...].astype(F32)).astype(BF16)
    gate_ref[...] = gate_kept_ref[...] + gate_sent_ref[...]


def sums(kept, sent, gate_kept, gate_sent):
    vmem = pl.BlockSpec(memory_space=pltpu.VMEM)
    return pl.pallas_call(
        sums_kernel,
        out_shape=(
            jax.ShapeDtypeStruct(kept.shape, BF16),
            jax.ShapeDtypeStruct(gate_kept.shape, F32),
        ),
        in_specs=[vmem] * 4,
        out_specs=(vmem, vmem),
        compiler_params=params(8),
        name="sums",
    )(kept, sent, gate_kept, gate_sent)


def routed(block, seq_step, pipe_step):
    seq_size, pipe_size = lax.axis_size("seq"), lax.axis_size("pipe")
    route = []
    for i in range(seq_size):
        for j in range(pipe_size):
            target = (i + seq_step) % seq_size * pipe_size + (j + pipe_step) % pipe_size
            route.append((i * pipe_size + j, target))
    return lax.ppermute(block, ("seq", "pipe"), route)


def pair_body(
    segment_input,
    output_grad,
    qkv_weight,
    out_weight,
    query_gain,
    key_gain,
    gate_scale,
    neighbours,
    tile_slot,
):
    stream = segment_input[0]
    upstream = output_grad[0]
    out_local = out_weight[0]
    other_stream = routed(stream, 1, 0)
    weight = regroup(qkv_weight[0], 128, 8)
    weight, upstream = lax.optimization_barrier((weight, upstream))
    other_upstream = routed(upstream, 1, 0)
    projected, probs, attention, kept, sent, out_local = forward(
        neighbours,
        tile_slot,
        stream,
        other_stream,
        weight,
        out_local,
        query_gain,
        key_gain,
        gate_scale,
    )
    kept = routed(kept, 0, 1)
    sent = routed(sent, 1, 1)
    gate_kept, gate_sent, grad_kept, grad_sent = backward(
        upstream,
        other_upstream,
        out_local,
        weight,
        projected,
        probs,
        attention,
        query_gain,
        key_gain,
        gate_scale,
    )
    grad_sent = routed(grad_sent, 1, -1)
    grad_kept = routed(grad_kept, 0, -1)
    segment_output = (kept.astype(F32) + sent.astype(F32)).astype(BF16)
    segment_output, gate_sent = lax.optimization_barrier((segment_output, gate_sent))
    gate_sent = routed(gate_sent, 1, 0)
    input_grad, gate_grad = sums(grad_sent, grad_kept, gate_kept, gate_sent)
    return (segment_output[None], input_grad[None], gate_grad)


def solution(mesh):
    in_specs = (
        P("pipe", ("dp", "seq"), None),
        P("pipe", ("dp", "seq"), None),
        P("pipe", None, "seq", None),
        P("pipe", "seq", None),
        P("pipe", None),
        P("pipe", None),
        P("pipe", None),
        P("dp", None),
        P("dp"),
    )
    out_specs = (
        P("pipe", ("dp", "seq"), None),
        P("pipe", ("dp", "seq"), None),
        P(("dp", "pipe"), "seq"),
    )

    def body(*args):
        one_tile_each = args[0].shape[1] == TILE and args[8].shape[0] == 2
        if mesh.shape["seq"] == 2 and one_tile_each and args[2].shape[2] % GROUP == 0:
            return pair_body(*args)
        return general_body(*args)

    return jax.shard_map(body, mesh=mesh, in_specs=in_specs, out_specs=out_specs, check_vma=False)
```

```python
import functools
import math

import jax
import jax.numpy as jnp
from jax import lax
from jax.experimental import pallas as pl
from jax.experimental.pallas import tpu as pltpu
from jax.sharding import PartitionSpec as P

TILE = 64
EPSILON = 1e-06
F32 = jnp.float32
BF16 = jnp.bfloat16
MIB = 1024 * 1024
GROUP = 4


def passed_along(block, axis, distance):
    devices = range(lax.axis_size(axis))
    route = [((i - distance) % len(devices), i) for i in devices]
    return lax.ppermute(block, axis, route)


def slot_lists(neighbours, tile_slot):
    tile_count = tile_slot.shape[0]
    numbering = jnp.arange(tile_count, dtype=jnp.int32)
    placed = (tile_slot[:, None] == numbering[None, :]).astype(jnp.int32)
    tile_of_slot = jnp.sum(placed * numbering[:, None], axis=0)
    chosen = (tile_of_slot[:, None] == numbering[None, :]).astype(jnp.int32)
    listed_tiles = jnp.sum(chosen[:, :, None] * neighbours[None, :, :], axis=1)
    key_valid = listed_tiles >= 0
    safe_tiles = jnp.maximum(listed_tiles, 0)
    matches = (safe_tiles[:, :, None] == numbering[None, None, :]).astype(jnp.int32)
    key_slots = jnp.sum(matches * tile_slot[None, None, :], axis=2)
    return (key_slots, key_valid)


def block_tiles(tile_count):
    return math.gcd(tile_count, max(1, 512 // TILE))


def unit_norm(values):
    spread = jnp.sqrt(jnp.mean(values * values, axis=-1, keepdims=True) + EPSILON)
    return (values / spread, spread)


def probabilities(query_block, key_rows, block_valid):
    scores = jnp.einsum(
        "aihd,ajhd->ahij", query_block, key_rows, preferred_element_type=jnp.float32
    ) * (1.0 / math.sqrt(query_block.shape[-1]))
    key_mask = jnp.repeat(block_valid, TILE, axis=1)
    scores = jnp.where(key_mask[:, None, None, :], scores, -jnp.inf)
    row_max = jnp.max(scores, axis=-1, keepdims=True)
    weights = jnp.exp(scores - row_max)
    return (weights / jnp.sum(weights, axis=-1, keepdims=True)).astype(jnp.bfloat16)


def gathered(tiles_array, block_slots):
    picked = tiles_array[block_slots]
    return picked.reshape(block_slots.shape[0], -1, tiles_array.shape[2], tiles_array.shape[3])


def attend_both(query_tiles, key_tiles, value_tiles, grad_tiles, key_slots, key_valid):
    tile_count = query_tiles.shape[0]
    span = block_tiles(tile_count)
    scale_factor = 1.0 / math.sqrt(query_tiles.shape[-1])
    empty_grad = jnp.zeros(query_tiles.shape, jnp.float32)

    def per_block(accumulators, block_index):
        key_total, value_total = accumulators
        first_tile = block_index * span
        query_block = lax.dynamic_slice_in_dim(query_tiles, first_tile, span, 0)
        grad_block = lax.dynamic_slice_in_dim(grad_tiles, first_tile, span, 0)
        block_slots = lax.dynamic_slice_in_dim(key_slots, first_tile, span, 0)
        block_valid = lax.dynamic_slice_in_dim(key_valid, first_tile, span, 0)
        key_rows = gathered(key_tiles, block_slots)
        value_rows = gathered(value_tiles, block_slots)
        weights = probabilities(query_block, key_rows, block_valid)
        attended = jnp.einsum(
            "ahij,ajhd->aihd", weights, value_rows, preferred_element_type=jnp.float32
        )
        value_part = jnp.einsum(
            "ahij,aihd->ajhd", weights, grad_block, preferred_element_type=jnp.float32
        )
        prob_grad = jnp.einsum(
            "aihd,ajhd->ahij", grad_block, value_rows, preferred_element_type=jnp.float32
        )
        weights_wide = weights.astype(jnp.float32)
        row_delta = jnp.sum(weights_wide * prob_grad, axis=-1, keepdims=True)
        score_grad = (weights_wide * (prob_grad - row_delta) * scale_factor).astype(jnp.bfloat16)
        query_part = jnp.einsum(
            "ahij,ajhd->aihd", score_grad, key_rows, preferred_element_type=jnp.float32
        )
        key_part = jnp.einsum(
            "ahij,aihd->ajhd", score_grad, query_block, preferred_element_type=jnp.float32
        )
        block_shape = (span, block_slots.shape[1]) + query_tiles.shape[1:]
        key_total = key_total.at[block_slots].add(key_part.reshape(block_shape))
        value_total = value_total.at[block_slots].add(value_part.reshape(block_shape))
        return ((key_total, value_total), (attended, query_part))

    totals, parts = lax.scan(
        per_block, (empty_grad, empty_grad), jnp.arange(tile_count // span, dtype=jnp.int32)
    )
    flat_shape = (-1,) + query_tiles.shape[2:]
    return (
        parts[0].reshape(flat_shape),
        parts[1].reshape(flat_shape),
        totals[0].reshape(flat_shape),
        totals[1].reshape(flat_shape),
    )


def general_body(
    segment_input,
    output_grad,
    qkv_weight,
    out_weight,
    query_gain,
    key_gain,
    gate_scale,
    neighbours,
    tile_slot,
):
    key_slots, key_valid = slot_lists(neighbours, tile_slot)
    stream = segment_input[0]
    upstream = output_grad[0]
    model_width = stream.shape[1]
    head_dim = query_gain.shape[1]
    local_heads = qkv_weight.shape[2]
    local_width = local_heads * head_dim
    proj_weight = qkv_weight[0].reshape(model_width, local_heads * 3 * head_dim)
    out_local = out_weight[0]
    gate_row = gate_scale[0]
    query_weights = query_gain[0]
    key_weights = key_gain[0]
    projected = jnp.dot(
        lax.all_gather(stream, "seq", axis=0, tiled=True),
        proj_weight,
        preferred_element_type=jnp.float32,
    )
    all_tokens = projected.shape[0]
    projected = projected.reshape(all_tokens, local_heads, 3, head_dim)
    query_unit, query_spread = unit_norm(projected[:, :, 0])
    key_unit, key_spread = unit_norm(projected[:, :, 1])
    queries = (query_unit * query_weights).astype(jnp.bfloat16)
    keys_normed = (key_unit * key_weights).astype(jnp.bfloat16)
    value_rows = projected[:, :, 2].astype(jnp.bfloat16)
    scaled = (upstream.astype(jnp.float32) * gate_row).astype(jnp.bfloat16)
    attended_grad = jnp.einsum(
        "td,cd->tc",
        lax.all_gather(scaled, "seq", axis=0, tiled=True),
        out_local,
        preferred_element_type=jnp.float32,
    ).astype(jnp.bfloat16)

    def as_tiles(values):
        return values.reshape(-1, TILE, local_heads, head_dim)

    attended, query_grad, key_grad, value_grad = attend_both(
        as_tiles(queries),
        as_tiles(keys_normed),
        as_tiles(value_rows),
        as_tiles(attended_grad),
        key_slots,
        key_valid,
    )
    attended_low = attended.astype(jnp.bfloat16).reshape(all_tokens, local_width)
    rows = attended_low
    attention_out = lax.psum_scatter(
        jnp.dot(rows, out_local, preferred_element_type=jnp.float32),
        "seq",
        scatter_dimension=0,
        tiled=True,
    )
    section_out = (stream.astype(jnp.float32) + gate_row * attention_out).astype(jnp.bfloat16)
    segment_output = passed_along(section_out, "pipe", 1)
    gate_local = lax.psum_scatter(
        jnp.sum(upstream.astype(jnp.float32) * attention_out, axis=0),
        "seq",
        scatter_dimension=0,
        tiled=True,
    )
    query_scaled = query_grad * query_weights
    query_part_grad = (
        query_scaled - query_unit * jnp.mean(query_scaled * query_unit, axis=-1, keepdims=True)
    ) / query_spread
    key_scaled = key_grad * key_weights
    key_part_grad = (
        key_scaled - key_unit * jnp.mean(key_scaled * key_unit, axis=-1, keepdims=True)
    ) / key_spread
    projected_grad = (
        jnp.stack([query_part_grad, key_part_grad, value_grad], axis=2)
        .astype(jnp.bfloat16)
        .reshape(all_tokens, local_heads * 3 * head_dim)
    )
    rows = projected_grad
    stream_grad = lax.psum_scatter(
        jnp.einsum("tc,dc->td", rows, proj_weight, preferred_element_type=jnp.float32).astype(
            jnp.bfloat16
        ),
        "seq",
        scatter_dimension=0,
        tiled=True,
    ).astype(jnp.float32)
    token_grad = (upstream.astype(jnp.float32) + stream_grad).astype(jnp.bfloat16)
    input_grad = passed_along(token_grad, "pipe", -1)
    return (segment_output[None], input_grad[None], gate_local[None])


def dot_nn(a, b):
    return lax.dot_general(a, b, (((1,), (0,)), ((), ())), preferred_element_type=F32)


def dot_nt(a, b):
    return lax.dot_general(a, b, (((1,), (1,)), ((), ())), preferred_element_type=F32)


def dot_tn(a, b):
    return lax.dot_general(a, b, (((0,), (0,)), ((), ())), preferred_element_type=F32)


def params(mebibytes):
    return pltpu.CompilerParams(vmem_limit_bytes=mebibytes * MIB)


class Copies:
    def __init__(self, pairs, semaphores, ahead):
        self.copies = [
            pltpu.make_async_copy(source, target, semaphores.at[i])
            for i, (source, target) in enumerate(pairs)
        ]
        self.ahead = ahead
        self.waited = 0
        for copy in self.copies[:ahead]:
            copy.start()

    def wait(self, count=1):
        for _ in range(count):
            self.copies[self.waited].wait()
            following = self.waited + self.ahead
            if following < len(self.copies):
                self.copies[following].start()
            self.waited += 1


def regroup_kernel(weight_ref, out_ref, read_ref, reads):
    depth, heads, width = weight_ref.shape
    slots, rows = read_ref.shape[:2]
    steps = depth // rows

    def part(step):
        return pl.ds(pl.multiple_of(step * rows, rows), rows)

    def read(step, slot):
        return pltpu.make_async_copy(
            weight_ref.at[part(step)], read_ref.at[slot], reads.at[slot]
        )

    for slot in range(slots):
        read(slot, slot).start()

    @pl.loop(0, steps)
    def _(step):
        slot = lax.rem(step, slots)
        read(step, slot).wait()
        by_head = jnp.swapaxes(read_ref[slot], 0, 1)
        for head in range(heads):
            left = (head % GROUP) * width
            out_ref[head // GROUP, part(step), left : left + width] = by_head[head]

        @pl.when(step + slots < steps)
        def _():
            read(step + slots, slot).start()


def regroup(weight, rows, slots):
    depth, heads, width = weight.shape
    out = (heads // GROUP, depth, GROUP * width)
    return pl.pallas_call(
        regroup_kernel,
        out_shape=pltpu.VMEM(out, weight.dtype),
        in_specs=[pl.BlockSpec(memory_space=pl.ANY)],
        out_specs=pl.BlockSpec(memory_space=pltpu.VMEM),
        scratch_shapes=[
            pltpu.VMEM((slots, rows, heads, width), weight.dtype),
            pltpu.SemaphoreType.DMA((slots,)),
        ],
        compiler_params=params(12),
        cost_estimate=pl.CostEstimate(
            flops=0, bytes_accessed=4 * depth * heads * width, transcendentals=0
        ),
        name="regroup",
    )(pltpu.with_memory_space_constraint(weight, pltpu.HBM))


def listed_slots(neighbours_ref, tile_slot_ref):
    tiles, places = neighbours_ref.shape
    one, zero = jnp.int32(1), jnp.int32(0)
    allowed = [[zero] * tiles for _ in range(tiles)]
    for t in range(tiles):
        for u in range(tiles):
            listed = zero
            for k in range(places):
                listed = jnp.where(neighbours_ref[t, k] == u, one, listed)
            for r in range(tiles):
                for c in range(tiles):
                    here = (tile_slot_ref[t] == r) & (tile_slot_ref[u] == c)
                    allowed[r][c] = jnp.where(here, listed, allowed[r][c])
    return allowed


def normed(rows, gain):
    inverse = lax.rsqrt(jnp.mean(rows * rows, axis=-1, keepdims=True) + EPSILON)
    unit = rows * inverse
    return unit, inverse, (unit * gain).astype(BF16)


def forward_kernel(
    neighbours_ref,
    tile_slot_ref,
    own_ref,
    other_ref,
    weight_ref,
    out_weight_ref,
    query_gain_ref,
    key_gain_ref,
    gate_ref,
    projected_ref,
    probs_ref,
    attention_ref,
    kept_ref,
    sent_ref,
    out_weight_buffer,
    tokens_ref,
    semaphores,
):
    local, model = own_ref.shape
    tokens = 2 * local
    width = query_gain_ref.shape[1]
    groups = weight_ref.shape[0]
    rows = GROUP * width

    def out_weight_part(group):
        place = pl.ds(group * rows, rows)
        return out_weight_ref.at[place], out_weight_buffer.at[place]

    copies = Copies([out_weight_part(group) for group in range(groups)], semaphores, groups)

    tokens_ref[:local, :] = own_ref[...]
    tokens_ref[local:, :] = other_ref[...]
    allowed = listed_slots(neighbours_ref, tile_slot_ref)
    mine = lax.axis_index("seq")
    row_half = lax.broadcasted_iota(jnp.int32, (tokens, tokens), 0) // local
    column_half = lax.broadcasted_iota(jnp.int32, (tokens, tokens), 1) // local
    row_slot = jnp.where(row_half == 0, mine, 1 - mine)
    column_slot = jnp.where(column_half == 0, mine, 1 - mine)
    table = jnp.zeros((tokens, tokens), jnp.int32)
    for r in range(2):
        for c in range(2):
            table = jnp.where((row_slot == r) & (column_slot == c), allowed[r][c], table)
    bias = jnp.where(table > 0, 0.0, -jnp.inf).astype(F32)

    def project(group):
        projected_ref[group] = dot_nn(tokens_ref[...], weight_ref[group])

    def attend(group):
        attended = []
        for head in range(GROUP):
            left = head * 3 * width
            _, _, queries = normed(projected_ref[group, :, left : left + width], query_gain_ref[...])
            left += width
            _, _, keys = normed(projected_ref[group, :, left : left + width], key_gain_ref[...])
            left += width
            value = projected_ref[group, :, left : left + width].astype(BF16)
            scores = dot_nt(queries, keys) * (1.0 / math.sqrt(width)) + bias
            row_max = jnp.max(scores, axis=-1, keepdims=True)
            weights = jnp.exp(scores - row_max)
            probs = (weights / jnp.sum(weights, axis=-1, keepdims=True)).astype(BF16)
            probs_ref[GROUP * group + head] = probs
            attended.append(dot_nn(probs, value).astype(BF16))
        return jnp.concatenate(attended, axis=1)

    def share(group, attended):
        return dot_nn(attended, out_weight_buffer[group * rows : (group + 1) * rows, :])

    project(0)
    attended = attend(0)
    for group in range(1, groups):
        project(group)
        copies.wait()
        following = attend(group)
        if group == 1:
            attention_ref[...] = share(0, attended)
        else:
            attention_ref[...] += share(group - 1, attended)
        attended = following
    copies.wait()
    total = share(groups - 1, attended)
    if groups > 1:
        total += attention_ref[...]
    attention_ref[...] = total
    gate = gate_ref[...]
    kept_ref[...] = (own_ref[...].astype(F32) + gate * total[:local]).astype(BF16)
    sent_ref[...] = (gate * total[local:]).astype(BF16)


def forward(neighbours, tile_slot, own, other, weight, out_weight, query_gain, key_gain, gate):
    local, model = own.shape
    groups, _, wide = weight.shape
    tokens = 2 * local
    weight = pltpu.with_memory_space_constraint(weight, pltpu.VMEM)
    out_weight = pltpu.with_memory_space_constraint(out_weight, pltpu.HBM)
    smem = pl.BlockSpec(memory_space=pltpu.SMEM)
    vmem = pl.BlockSpec(memory_space=pltpu.VMEM)
    hbm = pl.BlockSpec(memory_space=pl.ANY)
    return pl.pallas_call(
        forward_kernel,
        out_shape=(
            jax.ShapeDtypeStruct((groups, tokens, wide), F32),
            jax.ShapeDtypeStruct((GROUP * groups, tokens, tokens), BF16),
            jax.ShapeDtypeStruct((tokens, model), F32),
            jax.ShapeDtypeStruct((local, model), BF16),
            jax.ShapeDtypeStruct((local, model), BF16),
            pltpu.VMEM(out_weight.shape, BF16),
        ),
        in_specs=[smem, smem, vmem, vmem, vmem, hbm, vmem, vmem, vmem],
        out_specs=(vmem,) * 6,
        scratch_shapes=[
            pltpu.VMEM((tokens, model), BF16),
            pltpu.SemaphoreType.DMA((groups,)),
        ],
        compiler_params=params(12),
        cost_estimate=pl.CostEstimate(
            flops=2 * tokens * (weight.size + out_weight.size),
            bytes_accessed=2 * (weight.size + out_weight.size),
            transcendentals=0,
        ),
        name="attention_forward",
    )(neighbours, tile_slot, own, other, weight, out_weight, query_gain, key_gain, gate)


SIDE = 256


def tiled_products(accumulators, depth, columns, left, right, store):
    turn = 0
    for start in range(0, columns, 2 * SIDE):
        pair = accumulators[2 * turn : 2 * turn + 2]
        for step in range(depth // SIDE):
            for unit in range(2):
                tile = right(start + unit * SIDE, step)
                pltpu.matmul_push_rhs(tile, step % 2, unit, transpose=True)
            rows = left(step)
            for unit in range(2):
                pltpu.matmul_acc_lhs(pair[unit], rows, load_staged_rhs=step % 2)
        for unit in range(2):
            store(slice(start + unit * SIDE, start + (unit + 1) * SIDE), pltpu.matmul_pop(pair[unit]))
        turn = 1 - turn


def backward_kernel(
    own_ref,
    other_ref,
    out_weight_ref,
    projected_ref,
    probs_ref,
    query_gain_ref,
    key_gain_ref,
    gate_ref,
    grad_ref,
    scaled_ref,
    attended_grad_ref,
):
    local = own_ref.shape[0]
    width = query_gain_ref.shape[1]
    groups = grad_ref.shape[0]
    rows = GROUP * width

    model = own_ref.shape[1]
    gate = gate_ref[...]
    scaled_ref[:local, :] = (own_ref[...].astype(F32) * gate).astype(BF16)
    scaled_ref[local:, :] = (other_ref[...].astype(F32) * gate).astype(BF16)

    def attended_grad(group):
        part = slice(group * rows, (group + 1) * rows)
        product = dot_nt(scaled_ref[...], out_weight_ref[part, :])
        attended_grad_ref[group] = product.astype(BF16)

    def attend_backward(group, head):
        left = head * 3 * width
        query_part = slice(left, left + width)
        key_part = slice(left + width, left + 2 * width)
        value_part = slice(left + 2 * width, left + 3 * width)
        query_gain, key_gain = query_gain_ref[...], key_gain_ref[...]
        query_unit, query_inverse, queries = normed(projected_ref[group, :, query_part], query_gain)
        key_unit, key_inverse, keys = normed(projected_ref[group, :, key_part], key_gain)
        value = projected_ref[group, :, value_part].astype(BF16)
        grad = attended_grad_ref[group, :, head * width : (head + 1) * width]
        probs = probs_ref[GROUP * group + head]
        probs_wide = probs.astype(F32)
        grad_ref[group, :, value_part] = dot_tn(probs, grad).astype(BF16)
        prob_grad = dot_nt(grad, value)
        row_delta = jnp.sum(probs_wide * prob_grad, axis=-1, keepdims=True)
        scale_factor = 1.0 / math.sqrt(width)
        score_grad = (probs_wide * (prob_grad - row_delta) * scale_factor).astype(BF16)
        query_scaled = dot_nn(score_grad, keys) * query_gain
        key_scaled = dot_tn(score_grad, queries) * key_gain
        query_mean = jnp.mean(query_scaled * query_unit, axis=-1, keepdims=True)
        key_mean = jnp.mean(key_scaled * key_unit, axis=-1, keepdims=True)
        grad_ref[group, :, query_part] = (
            (query_scaled - query_unit * query_mean) * query_inverse
        ).astype(BF16)
        grad_ref[group, :, key_part] = ((key_scaled - key_unit * key_mean) * key_inverse).astype(BF16)

    attended_grad(0)
    for group in range(groups):
        if group + 1 < groups:
            attended_grad(group + 1)
        for head in range(GROUP):
            attend_backward(group, head)


def backward(own, other, out_weight, projected, probs, query_gain, key_gain, gate):
    local, model = own.shape
    groups, tokens, wide = projected.shape
    head_dim = query_gain.shape[1]
    out_weight = pltpu.with_memory_space_constraint(out_weight, pltpu.VMEM)
    vmem = pl.BlockSpec(memory_space=pltpu.VMEM)
    return pl.pallas_call(
        backward_kernel,
        out_shape=jax.ShapeDtypeStruct((groups, tokens, wide), BF16),
        in_specs=[vmem] * 8,
        out_specs=vmem,
        scratch_shapes=[
            pltpu.VMEM((tokens, model), BF16),
            pltpu.VMEM((groups, tokens, GROUP * head_dim), BF16),
        ],
        compiler_params=params(12),
        cost_estimate=pl.CostEstimate(
            flops=2 * tokens * out_weight.size,
            bytes_accessed=2 * out_weight.size,
            transcendentals=0,
        ),
        name="attention_backward",
    )(own, other, out_weight, projected, probs, query_gain, key_gain, gate)


def input_grad_kernel(
    grad_ref,
    weight_ref,
    own_ref,
    other_ref,
    attention_ref,
    gate_kept_ref,
    gate_sent_ref,
    kept_ref,
    sent_ref,
    gate_grad_ref,
):
    local, model = own_ref.shape
    groups, tokens, wide = grad_ref.shape
    steps = wide // SIDE

    def left(step):
        first = step % steps * SIDE
        return grad_ref[step // steps, :, first : first + SIDE]

    def right(row, step):
        first = step % steps * SIDE
        return weight_ref[step // steps, row : row + SIDE, first : first + SIDE]

    def store(part, total):
        own, other = own_ref[:, part].astype(F32), other_ref[:, part].astype(F32)
        kept_ref[:, part] = (own + total[:local]).astype(BF16)
        sent_ref[:, part] = total[local:].astype(BF16)
        gate_grad_ref[:, part] = jnp.sum(
            own * attention_ref[:local, part] + other * attention_ref[local:, part],
            axis=0,
            keepdims=True,
        )

    def products(*accumulators):
        tiled_products(accumulators, groups * wide, model, left, right, store)

    pl.run_scoped(
        products, *[pltpu.ACC(unit)((tokens, SIDE), F32) for _ in range(2) for unit in range(2)]
    )
    half = gate_kept_ref.shape[1]
    mine = lax.axis_index("seq")
    gate_kept_ref[...] = gate_grad_ref[:, pl.ds(pl.multiple_of(mine * half, half), half)]
    gate_sent_ref[...] = gate_grad_ref[:, pl.ds(pl.multiple_of((1 - mine) * half, half), half)]


def input_grad(grad, weight, own, other, attention):
    local, model = own.shape
    weight = pltpu.with_memory_space_constraint(weight, pltpu.VMEM)
    vmem = pl.BlockSpec(memory_space=pltpu.VMEM)
    return pl.pallas_call(
        input_grad_kernel,
        out_shape=(
            jax.ShapeDtypeStruct((1, model // 2), F32),
            jax.ShapeDtypeStruct((1, model // 2), F32),
            jax.ShapeDtypeStruct((local, model), BF16),
            jax.ShapeDtypeStruct((local, model), BF16),
        ),
        in_specs=[vmem] * 5,
        out_specs=(vmem,) * 4,
        scratch_shapes=[pltpu.VMEM((1, model), F32)],
        compiler_params=params(8),
        name="input_grad",
    )(grad, weight, own, other, attention)


def sums_kernel(kept_ref, sent_ref, gate_kept_ref, gate_sent_ref, grad_ref, gate_ref):
    grad_ref[...] = (kept_ref[...].astype(F32) + sent_ref[...].astype(F32)).astype(BF16)
    gate_ref[...] = gate_kept_ref[...] + gate_sent_ref[...]


def sums(kept, sent, gate_kept, gate_sent):
    vmem = pl.BlockSpec(memory_space=pltpu.VMEM)
    return pl.pallas_call(
        sums_kernel,
        out_shape=(
            jax.ShapeDtypeStruct(kept.shape, BF16),
            jax.ShapeDtypeStruct(gate_kept.shape, F32),
        ),
        in_specs=[vmem] * 4,
        out_specs=(vmem, vmem),
        compiler_params=params(8),
        name="sums",
    )(kept, sent, gate_kept, gate_sent)


def routed(block, seq_step, pipe_step):
    seq_size, pipe_size = lax.axis_size("seq"), lax.axis_size("pipe")
    route = []
    for i in range(seq_size):
        for j in range(pipe_size):
            target = (i + seq_step) % seq_size * pipe_size + (j + pipe_step) % pipe_size
            route.append((i * pipe_size + j, target))
    return lax.ppermute(block, ("seq", "pipe"), route)


def pair_body(
    segment_input,
    output_grad,
    qkv_weight,
    out_weight,
    query_gain,
    key_gain,
    gate_scale,
    neighbours,
    tile_slot,
):
    stream = segment_input[0]
    upstream = output_grad[0]
    out_local = out_weight[0]
    other_stream = routed(stream, 1, 0)
    weight = regroup(qkv_weight[0], 128, 8)
    weight, upstream = lax.optimization_barrier((weight, upstream))
    other_upstream = routed(upstream, 1, 0)
    projected, probs, attention, kept, sent, out_local = forward(
        neighbours,
        tile_slot,
        stream,
        other_stream,
        weight,
        out_local,
        query_gain,
        key_gain,
        gate_scale,
    )
    kept = routed(kept, 0, 1)
    sent = routed(sent, 1, 1)
    grad = backward(
        upstream, other_upstream, out_local, projected, probs, query_gain, key_gain, gate_scale
    )
    gate_kept, gate_sent, grad_kept, grad_sent = input_grad(
        grad, weight, upstream, other_upstream, attention
    )
    grad_sent = routed(grad_sent, 1, -1)
    grad_kept = routed(grad_kept, 0, -1)
    segment_output = (kept.astype(F32) + sent.astype(F32)).astype(BF16)
    segment_output, gate_sent = lax.optimization_barrier((segment_output, gate_sent))
    gate_sent = routed(gate_sent, 1, 0)
    token_grad, gate_grad = sums(grad_sent, grad_kept, gate_kept, gate_sent)
    return (segment_output[None], token_grad[None], gate_grad)


def solution(mesh):
    in_specs = (
        P("pipe", ("dp", "seq"), None),
        P("pipe", ("dp", "seq"), None),
        P("pipe", None, "seq", None),
        P("pipe", "seq", None),
        P("pipe", None),
        P("pipe", None),
        P("pipe", None),
        P("dp", None),
        P("dp"),
    )
    out_specs = (
        P("pipe", ("dp", "seq"), None),
        P("pipe", ("dp", "seq"), None),
        P(("dp", "pipe"), "seq"),
    )

    def body(*args):
        one_tile_each = args[0].shape[1] == TILE and args[8].shape[0] == 2
        if mesh.shape["seq"] == 2 and one_tile_each and args[2].shape[2] % GROUP == 0:
            return pair_body(*args)
        return general_body(*args)

    return jax.shard_map(body, mesh=mesh, in_specs=in_specs, out_specs=out_specs, check_vma=False)
```

```python
import functools
import math

import jax
import jax.numpy as jnp
from jax import lax
from jax.experimental import pallas as pl
from jax.experimental.pallas import tpu as pltpu
from jax.sharding import PartitionSpec as P

TILE = 64
EPSILON = 1e-06
F32 = jnp.float32
BF16 = jnp.bfloat16
MIB = 1024 * 1024
GROUP = 4


def passed_along(block, axis, distance):
    devices = range(lax.axis_size(axis))
    route = [((i - distance) % len(devices), i) for i in devices]
    return lax.ppermute(block, axis, route)


def slot_lists(neighbours, tile_slot):
    tile_count = tile_slot.shape[0]
    numbering = jnp.arange(tile_count, dtype=jnp.int32)
    placed = (tile_slot[:, None] == numbering[None, :]).astype(jnp.int32)
    tile_of_slot = jnp.sum(placed * numbering[:, None], axis=0)
    chosen = (tile_of_slot[:, None] == numbering[None, :]).astype(jnp.int32)
    listed_tiles = jnp.sum(chosen[:, :, None] * neighbours[None, :, :], axis=1)
    key_valid = listed_tiles >= 0
    safe_tiles = jnp.maximum(listed_tiles, 0)
    matches = (safe_tiles[:, :, None] == numbering[None, None, :]).astype(jnp.int32)
    key_slots = jnp.sum(matches * tile_slot[None, None, :], axis=2)
    return (key_slots, key_valid)


def block_tiles(tile_count):
    return math.gcd(tile_count, max(1, 512 // TILE))


def unit_norm(values):
    spread = jnp.sqrt(jnp.mean(values * values, axis=-1, keepdims=True) + EPSILON)
    return (values / spread, spread)


def probabilities(query_block, key_rows, block_valid):
    scores = jnp.einsum(
        "aihd,ajhd->ahij", query_block, key_rows, preferred_element_type=jnp.float32
    ) * (1.0 / math.sqrt(query_block.shape[-1]))
    key_mask = jnp.repeat(block_valid, TILE, axis=1)
    scores = jnp.where(key_mask[:, None, None, :], scores, -jnp.inf)
    row_max = jnp.max(scores, axis=-1, keepdims=True)
    weights = jnp.exp(scores - row_max)
    return (weights / jnp.sum(weights, axis=-1, keepdims=True)).astype(jnp.bfloat16)


def gathered(tiles_array, block_slots):
    picked = tiles_array[block_slots]
    return picked.reshape(block_slots.shape[0], -1, tiles_array.shape[2], tiles_array.shape[3])


def attend_both(query_tiles, key_tiles, value_tiles, grad_tiles, key_slots, key_valid):
    tile_count = query_tiles.shape[0]
    span = block_tiles(tile_count)
    scale_factor = 1.0 / math.sqrt(query_tiles.shape[-1])
    empty_grad = jnp.zeros(query_tiles.shape, jnp.float32)

    def per_block(accumulators, block_index):
        key_total, value_total = accumulators
        first_tile = block_index * span
        query_block = lax.dynamic_slice_in_dim(query_tiles, first_tile, span, 0)
        grad_block = lax.dynamic_slice_in_dim(grad_tiles, first_tile, span, 0)
        block_slots = lax.dynamic_slice_in_dim(key_slots, first_tile, span, 0)
        block_valid = lax.dynamic_slice_in_dim(key_valid, first_tile, span, 0)
        key_rows = gathered(key_tiles, block_slots)
        value_rows = gathered(value_tiles, block_slots)
        weights = probabilities(query_block, key_rows, block_valid)
        attended = jnp.einsum(
            "ahij,ajhd->aihd", weights, value_rows, preferred_element_type=jnp.float32
        )
        value_part = jnp.einsum(
            "ahij,aihd->ajhd", weights, grad_block, preferred_element_type=jnp.float32
        )
        prob_grad = jnp.einsum(
            "aihd,ajhd->ahij", grad_block, value_rows, preferred_element_type=jnp.float32
        )
        weights_wide = weights.astype(jnp.float32)
        row_delta = jnp.sum(weights_wide * prob_grad, axis=-1, keepdims=True)
        score_grad = (weights_wide * (prob_grad - row_delta) * scale_factor).astype(jnp.bfloat16)
        query_part = jnp.einsum(
            "ahij,ajhd->aihd", score_grad, key_rows, preferred_element_type=jnp.float32
        )
        key_part = jnp.einsum(
            "ahij,aihd->ajhd", score_grad, query_block, preferred_element_type=jnp.float32
        )
        block_shape = (span, block_slots.shape[1]) + query_tiles.shape[1:]
        key_total = key_total.at[block_slots].add(key_part.reshape(block_shape))
        value_total = value_total.at[block_slots].add(value_part.reshape(block_shape))
        return ((key_total, value_total), (attended, query_part))

    totals, parts = lax.scan(
        per_block, (empty_grad, empty_grad), jnp.arange(tile_count // span, dtype=jnp.int32)
    )
    flat_shape = (-1,) + query_tiles.shape[2:]
    return (
        parts[0].reshape(flat_shape),
        parts[1].reshape(flat_shape),
        totals[0].reshape(flat_shape),
        totals[1].reshape(flat_shape),
    )


def general_body(
    segment_input,
    output_grad,
    qkv_weight,
    out_weight,
    query_gain,
    key_gain,
    gate_scale,
    neighbours,
    tile_slot,
):
    key_slots, key_valid = slot_lists(neighbours, tile_slot)
    stream = segment_input[0]
    upstream = output_grad[0]
    model_width = stream.shape[1]
    head_dim = query_gain.shape[1]
    local_heads = qkv_weight.shape[2]
    local_width = local_heads * head_dim
    proj_weight = qkv_weight[0].reshape(model_width, local_heads * 3 * head_dim)
    out_local = out_weight[0]
    gate_row = gate_scale[0]
    query_weights = query_gain[0]
    key_weights = key_gain[0]
    projected = jnp.dot(
        lax.all_gather(stream, "seq", axis=0, tiled=True),
        proj_weight,
        preferred_element_type=jnp.float32,
    )
    all_tokens = projected.shape[0]
    projected = projected.reshape(all_tokens, local_heads, 3, head_dim)
    query_unit, query_spread = unit_norm(projected[:, :, 0])
    key_unit, key_spread = unit_norm(projected[:, :, 1])
    queries = (query_unit * query_weights).astype(jnp.bfloat16)
    keys_normed = (key_unit * key_weights).astype(jnp.bfloat16)
    value_rows = projected[:, :, 2].astype(jnp.bfloat16)
    scaled = (upstream.astype(jnp.float32) * gate_row).astype(jnp.bfloat16)
    attended_grad = jnp.einsum(
        "td,cd->tc",
        lax.all_gather(scaled, "seq", axis=0, tiled=True),
        out_local,
        preferred_element_type=jnp.float32,
    ).astype(jnp.bfloat16)

    def as_tiles(values):
        return values.reshape(-1, TILE, local_heads, head_dim)

    attended, query_grad, key_grad, value_grad = attend_both(
        as_tiles(queries),
        as_tiles(keys_normed),
        as_tiles(value_rows),
        as_tiles(attended_grad),
        key_slots,
        key_valid,
    )
    attended_low = attended.astype(jnp.bfloat16).reshape(all_tokens, local_width)
    rows = attended_low
    attention_out = lax.psum_scatter(
        jnp.dot(rows, out_local, preferred_element_type=jnp.float32),
        "seq",
        scatter_dimension=0,
        tiled=True,
    )
    section_out = (stream.astype(jnp.float32) + gate_row * attention_out).astype(jnp.bfloat16)
    segment_output = passed_along(section_out, "pipe", 1)
    gate_local = lax.psum_scatter(
        jnp.sum(upstream.astype(jnp.float32) * attention_out, axis=0),
        "seq",
        scatter_dimension=0,
        tiled=True,
    )
    query_scaled = query_grad * query_weights
    query_part_grad = (
        query_scaled - query_unit * jnp.mean(query_scaled * query_unit, axis=-1, keepdims=True)
    ) / query_spread
    key_scaled = key_grad * key_weights
    key_part_grad = (
        key_scaled - key_unit * jnp.mean(key_scaled * key_unit, axis=-1, keepdims=True)
    ) / key_spread
    projected_grad = (
        jnp.stack([query_part_grad, key_part_grad, value_grad], axis=2)
        .astype(jnp.bfloat16)
        .reshape(all_tokens, local_heads * 3 * head_dim)
    )
    rows = projected_grad
    stream_grad = lax.psum_scatter(
        jnp.einsum("tc,dc->td", rows, proj_weight, preferred_element_type=jnp.float32).astype(
            jnp.bfloat16
        ),
        "seq",
        scatter_dimension=0,
        tiled=True,
    ).astype(jnp.float32)
    token_grad = (upstream.astype(jnp.float32) + stream_grad).astype(jnp.bfloat16)
    input_grad = passed_along(token_grad, "pipe", -1)
    return (segment_output[None], input_grad[None], gate_local[None])


def dot_nn(a, b):
    return lax.dot_general(a, b, (((1,), (0,)), ((), ())), preferred_element_type=F32)


def dot_nt(a, b):
    return lax.dot_general(a, b, (((1,), (1,)), ((), ())), preferred_element_type=F32)


def dot_tn(a, b):
    return lax.dot_general(a, b, (((0,), (0,)), ((), ())), preferred_element_type=F32)


def params(mebibytes):
    return pltpu.CompilerParams(vmem_limit_bytes=mebibytes * MIB)


class Copies:
    def __init__(self, pairs, semaphores, ahead):
        self.copies = [
            pltpu.make_async_copy(source, target, semaphores.at[i])
            for i, (source, target) in enumerate(pairs)
        ]
        self.ahead = ahead
        self.waited = 0
        for copy in self.copies[:ahead]:
            copy.start()

    def wait(self, count=1):
        for _ in range(count):
            self.copies[self.waited].wait()
            following = self.waited + self.ahead
            if following < len(self.copies):
                self.copies[following].start()
            self.waited += 1


def regroup_kernel(weight_ref, out_ref, read_ref, reads):
    depth, heads, width = weight_ref.shape
    slots, rows = read_ref.shape[:2]
    steps = depth // rows

    def part(step):
        return pl.ds(pl.multiple_of(step * rows, rows), rows)

    def read(step, slot):
        return pltpu.make_async_copy(
            weight_ref.at[part(step)], read_ref.at[slot], reads.at[slot]
        )

    for slot in range(slots):
        read(slot, slot).start()

    @pl.loop(0, steps)
    def _(step):
        slot = lax.rem(step, slots)
        read(step, slot).wait()
        by_head = jnp.swapaxes(read_ref[slot], 0, 1)
        for head in range(heads):
            left = (head % GROUP) * width
            out_ref[head // GROUP, part(step), left : left + width] = by_head[head]

        @pl.when(step + slots < steps)
        def _():
            read(step + slots, slot).start()


def regroup(weight, rows, slots):
    depth, heads, width = weight.shape
    out = (heads // GROUP, depth, GROUP * width)
    return pl.pallas_call(
        regroup_kernel,
        out_shape=pltpu.VMEM(out, weight.dtype),
        in_specs=[pl.BlockSpec(memory_space=pl.ANY)],
        out_specs=pl.BlockSpec(memory_space=pltpu.VMEM),
        scratch_shapes=[
            pltpu.VMEM((slots, rows, heads, width), weight.dtype),
            pltpu.SemaphoreType.DMA((slots,)),
        ],
        compiler_params=params(12),
        cost_estimate=pl.CostEstimate(
            flops=0, bytes_accessed=4 * depth * heads * width, transcendentals=0
        ),
        name="regroup",
    )(pltpu.with_memory_space_constraint(weight, pltpu.HBM))


def listed_slots(neighbours_ref, tile_slot_ref):
    tiles, places = neighbours_ref.shape
    one, zero = jnp.int32(1), jnp.int32(0)
    allowed = [[zero] * tiles for _ in range(tiles)]
    for t in range(tiles):
        for u in range(tiles):
            listed = zero
            for k in range(places):
                listed = jnp.where(neighbours_ref[t, k] == u, one, listed)
            for r in range(tiles):
                for c in range(tiles):
                    here = (tile_slot_ref[t] == r) & (tile_slot_ref[u] == c)
                    allowed[r][c] = jnp.where(here, listed, allowed[r][c])
    return allowed


def normed(rows, gain):
    inverse = lax.rsqrt(jnp.mean(rows * rows, axis=-1, keepdims=True) + EPSILON)
    unit = rows * inverse
    return unit, inverse, (unit * gain).astype(BF16)


def forward_kernel(
    neighbours_ref,
    tile_slot_ref,
    own_ref,
    other_ref,
    weight_ref,
    out_weight_ref,
    query_gain_ref,
    key_gain_ref,
    gate_ref,
    projected_ref,
    probs_ref,
    attention_ref,
    kept_ref,
    sent_ref,
    out_weight_buffer,
    tokens_ref,
    semaphores,
):
    local, model = own_ref.shape
    tokens = 2 * local
    width = query_gain_ref.shape[1]
    groups = weight_ref.shape[0]
    rows = GROUP * width

    def out_weight_part(group):
        place = pl.ds(group * rows, rows)
        return out_weight_ref.at[place], out_weight_buffer.at[place]

    copies = Copies([out_weight_part(group) for group in range(groups)], semaphores, groups)

    tokens_ref[:local, :] = own_ref[...]
    tokens_ref[local:, :] = other_ref[...]
    allowed = listed_slots(neighbours_ref, tile_slot_ref)
    mine = lax.axis_index("seq")
    row_half = lax.broadcasted_iota(jnp.int32, (tokens, tokens), 0) // local
    column_half = lax.broadcasted_iota(jnp.int32, (tokens, tokens), 1) // local
    row_slot = jnp.where(row_half == 0, mine, 1 - mine)
    column_slot = jnp.where(column_half == 0, mine, 1 - mine)
    table = jnp.zeros((tokens, tokens), jnp.int32)
    for r in range(2):
        for c in range(2):
            table = jnp.where((row_slot == r) & (column_slot == c), allowed[r][c], table)
    bias = jnp.where(table > 0, 0.0, -jnp.inf).astype(F32)

    def project(group):
        projected_ref[group] = dot_nn(tokens_ref[...], weight_ref[group])

    def attend(group):
        attended = []
        for head in range(GROUP):
            left = head * 3 * width
            _, _, queries = normed(projected_ref[group, :, left : left + width], query_gain_ref[...])
            left += width
            _, _, keys = normed(projected_ref[group, :, left : left + width], key_gain_ref[...])
            left += width
            value = projected_ref[group, :, left : left + width].astype(BF16)
            scores = dot_nt(queries, keys) * (1.0 / math.sqrt(width)) + bias
            row_max = jnp.max(scores, axis=-1, keepdims=True)
            weights = jnp.exp(scores - row_max)
            probs = (weights / jnp.sum(weights, axis=-1, keepdims=True)).astype(BF16)
            probs_ref[GROUP * group + head] = probs
            attended.append(dot_nn(probs, value).astype(BF16))
        return jnp.concatenate(attended, axis=1)

    def share(group, attended):
        return dot_nn(attended, out_weight_buffer[group * rows : (group + 1) * rows, :])

    project(0)
    attended = attend(0)
    for group in range(1, groups):
        project(group)
        copies.wait()
        following = attend(group)
        if group == 1:
            attention_ref[...] = share(0, attended)
        else:
            attention_ref[...] += share(group - 1, attended)
        attended = following
    copies.wait()
    total = share(groups - 1, attended)
    if groups > 1:
        total += attention_ref[...]
    attention_ref[...] = total
    gate = gate_ref[...]
    kept_ref[...] = (own_ref[...].astype(F32) + gate * total[:local]).astype(BF16)
    sent_ref[...] = (gate * total[local:]).astype(BF16)


def forward(neighbours, tile_slot, own, other, weight, out_weight, query_gain, key_gain, gate):
    local, model = own.shape
    groups, _, wide = weight.shape
    tokens = 2 * local
    weight = pltpu.with_memory_space_constraint(weight, pltpu.VMEM)
    out_weight = pltpu.with_memory_space_constraint(out_weight, pltpu.HBM)
    smem = pl.BlockSpec(memory_space=pltpu.SMEM)
    vmem = pl.BlockSpec(memory_space=pltpu.VMEM)
    hbm = pl.BlockSpec(memory_space=pl.ANY)
    return pl.pallas_call(
        forward_kernel,
        out_shape=(
            jax.ShapeDtypeStruct((groups, tokens, wide), F32),
            jax.ShapeDtypeStruct((GROUP * groups, tokens, tokens), BF16),
            jax.ShapeDtypeStruct((tokens, model), F32),
            jax.ShapeDtypeStruct((local, model), BF16),
            jax.ShapeDtypeStruct((local, model), BF16),
            pltpu.VMEM(out_weight.shape, BF16),
        ),
        in_specs=[smem, smem, vmem, vmem, vmem, hbm, vmem, vmem, vmem],
        out_specs=(vmem,) * 6,
        scratch_shapes=[
            pltpu.VMEM((tokens, model), BF16),
            pltpu.SemaphoreType.DMA((groups,)),
        ],
        compiler_params=params(12),
        cost_estimate=pl.CostEstimate(
            flops=2 * tokens * (weight.size + out_weight.size),
            bytes_accessed=2 * (weight.size + out_weight.size),
            transcendentals=0,
        ),
        name="attention_forward",
    )(neighbours, tile_slot, own, other, weight, out_weight, query_gain, key_gain, gate)


def input_grad(grad_ref, weight_ref, own_ref, kept_ref, sent_ref):
    local, model = own_ref.shape
    block = 512
    for start in range(0, model, block):
        part = slice(start, start + block)
        total = dot_nt(weight_ref[0, part, :], grad_ref[0])
        for group in range(1, grad_ref.shape[0]):
            total += dot_nt(weight_ref[group, part, :], grad_ref[group])
        total = total.T
        kept_ref[:, part] = (own_ref[:, part].astype(F32) + total[:local]).astype(BF16)
        sent_ref[:, part] = total[local:].astype(BF16)


def backward_kernel(
    own_ref,
    other_ref,
    out_weight_ref,
    weight_ref,
    projected_ref,
    probs_ref,
    attention_ref,
    query_gain_ref,
    key_gain_ref,
    gate_ref,
    gate_kept_ref,
    gate_sent_ref,
    kept_ref,
    sent_ref,
    grad_ref,
    scaled_ref,
    attended_grad_ref,
    gate_grad_ref,
):
    local = own_ref.shape[0]
    width = query_gain_ref.shape[1]
    groups = grad_ref.shape[0]
    rows = GROUP * width

    gate = gate_ref[...]
    own, other = own_ref[...].astype(F32), other_ref[...].astype(F32)
    scaled_ref[:local, :] = (own * gate).astype(BF16)
    scaled_ref[local:, :] = (other * gate).astype(BF16)
    gate_grad_ref[...] = jnp.sum(
        own * attention_ref[:local, :] + other * attention_ref[local:, :], axis=0, keepdims=True
    )
    half = gate_kept_ref.shape[1]
    mine = lax.axis_index("seq")
    gate_kept_ref[...] = gate_grad_ref[:, pl.ds(pl.multiple_of(mine * half, half), half)]
    gate_sent_ref[...] = gate_grad_ref[:, pl.ds(pl.multiple_of((1 - mine) * half, half), half)]

    def attended_grad(group):
        part = slice(group * rows, (group + 1) * rows)
        product = dot_nt(scaled_ref[...], out_weight_ref[part, :])
        attended_grad_ref[group] = product.astype(BF16)

    def attend_backward(group, head):
        left = head * 3 * width
        query_part = slice(left, left + width)
        key_part = slice(left + width, left + 2 * width)
        value_part = slice(left + 2 * width, left + 3 * width)
        query_gain, key_gain = query_gain_ref[...], key_gain_ref[...]
        query_unit, query_inverse, queries = normed(projected_ref[group, :, query_part], query_gain)
        key_unit, key_inverse, keys = normed(projected_ref[group, :, key_part], key_gain)
        value = projected_ref[group, :, value_part].astype(BF16)
        grad = attended_grad_ref[group, :, head * width : (head + 1) * width]
        probs = probs_ref[GROUP * group + head]
        probs_wide = probs.astype(F32)
        grad_ref[group, :, value_part] = dot_tn(probs, grad).astype(BF16)
        prob_grad = dot_nt(grad, value)
        row_delta = jnp.sum(probs_wide * prob_grad, axis=-1, keepdims=True)
        scale_factor = 1.0 / math.sqrt(width)
        score_grad = (probs_wide * (prob_grad - row_delta) * scale_factor).astype(BF16)
        query_scaled = dot_nn(score_grad, keys) * query_gain
        key_scaled = dot_tn(score_grad, queries) * key_gain
        query_mean = jnp.mean(query_scaled * query_unit, axis=-1, keepdims=True)
        key_mean = jnp.mean(key_scaled * key_unit, axis=-1, keepdims=True)
        grad_ref[group, :, query_part] = (
            (query_scaled - query_unit * query_mean) * query_inverse
        ).astype(BF16)
        grad_ref[group, :, key_part] = ((key_scaled - key_unit * key_mean) * key_inverse).astype(BF16)

    attended_grad(0)
    for group in range(groups):
        if group + 1 < groups:
            attended_grad(group + 1)
        for head in range(GROUP):
            attend_backward(group, head)
    input_grad(grad_ref, weight_ref, own_ref, kept_ref, sent_ref)


def backward(
    own, other, out_weight, weight, projected, probs, attention, query_gain, key_gain, gate
):
    local, model = own.shape
    groups, tokens, wide = projected.shape
    head_dim = query_gain.shape[1]
    out_weight = pltpu.with_memory_space_constraint(out_weight, pltpu.VMEM)
    weight = pltpu.with_memory_space_constraint(weight, pltpu.VMEM)
    vmem = pl.BlockSpec(memory_space=pltpu.VMEM)
    return pl.pallas_call(
        backward_kernel,
        out_shape=(
            jax.ShapeDtypeStruct((1, model // 2), F32),
            jax.ShapeDtypeStruct((1, model // 2), F32),
            jax.ShapeDtypeStruct((local, model), BF16),
            jax.ShapeDtypeStruct((local, model), BF16),
        ),
        in_specs=[vmem] * 10,
        out_specs=(vmem,) * 4,
        scratch_shapes=[
            pltpu.VMEM((groups, tokens, wide), BF16),
            pltpu.VMEM((tokens, model), BF16),
            pltpu.VMEM((groups, tokens, GROUP * head_dim), BF16),
            pltpu.VMEM((1, model), F32),
        ],
        compiler_params=params(12),
        cost_estimate=pl.CostEstimate(
            flops=2 * tokens * (out_weight.size + weight.size),
            bytes_accessed=2 * (out_weight.size + weight.size),
            transcendentals=0,
        ),
        name="attention_backward",
    )(own, other, out_weight, weight, projected, probs, attention, query_gain, key_gain, gate)


def sums_kernel(sent_ref, kept_ref, gate_kept_ref, gate_sent_ref, grad_ref, gate_ref):
    grad_ref[...] = (kept_ref[...].astype(F32) + sent_ref[...].astype(F32)).astype(BF16)
    gate_ref[...] = gate_kept_ref[...] + gate_sent_ref[...]


def sums(sent, kept, gate_kept, gate_sent):
    vmem = pl.BlockSpec(memory_space=pltpu.VMEM)
    return pl.pallas_call(
        sums_kernel,
        out_shape=(
            jax.ShapeDtypeStruct(kept.shape, BF16),
            jax.ShapeDtypeStruct(gate_kept.shape, F32),
        ),
        in_specs=[vmem] * 4,
        out_specs=(vmem, vmem),
        compiler_params=params(8),
        name="sums",
    )(sent, kept, gate_kept, gate_sent)


def routed(block, seq_step, pipe_step):
    seq_size, pipe_size = lax.axis_size("seq"), lax.axis_size("pipe")
    route = []
    for i in range(seq_size):
        for j in range(pipe_size):
            target = (i + seq_step) % seq_size * pipe_size + (j + pipe_step) % pipe_size
            route.append((i * pipe_size + j, target))
    return lax.ppermute(block, ("seq", "pipe"), route)


def pair_body(
    segment_input,
    output_grad,
    qkv_weight,
    out_weight,
    query_gain,
    key_gain,
    gate_scale,
    neighbours,
    tile_slot,
):
    stream = segment_input[0]
    upstream = output_grad[0]
    out_local = out_weight[0]
    other_stream = routed(stream, 1, 0)
    weight = regroup(qkv_weight[0], 128, 8)
    other_upstream = routed(upstream, 1, 0)
    projected, probs, attention, kept, sent, out_local = forward(
        neighbours,
        tile_slot,
        stream,
        other_stream,
        weight,
        out_local,
        query_gain,
        key_gain,
        gate_scale,
    )
    kept = routed(kept, 0, 1)
    sent = routed(sent, 1, 1)
    gate_kept, gate_sent, grad_kept, grad_sent = backward(
        upstream,
        other_upstream,
        out_local,
        weight,
        projected,
        probs,
        attention,
        query_gain,
        key_gain,
        gate_scale,
    )
    grad_sent = routed(grad_sent, 1, -1)
    grad_kept = routed(grad_kept, 0, -1)
    segment_output = (kept.astype(F32) + sent.astype(F32)).astype(BF16)
    segment_output, gate_sent = lax.optimization_barrier((segment_output, gate_sent))
    gate_sent = routed(gate_sent, 1, 0)
    token_grad, gate_grad = sums(grad_sent, grad_kept, gate_kept, gate_sent)
    return (segment_output[None], token_grad[None], gate_grad)


def solution(mesh):
    in_specs = (
        P("pipe", ("dp", "seq"), None),
        P("pipe", ("dp", "seq"), None),
        P("pipe", None, "seq", None),
        P("pipe", "seq", None),
        P("pipe", None),
        P("pipe", None),
        P("pipe", None),
        P("dp", None),
        P("dp"),
    )
    out_specs = (
        P("pipe", ("dp", "seq"), None),
        P("pipe", ("dp", "seq"), None),
        P(("dp", "pipe"), "seq"),
    )

    def body(*args):
        one_tile_each = args[0].shape[1] == TILE and args[8].shape[0] == 2
        if mesh.shape["seq"] == 2 and one_tile_each and args[2].shape[2] % GROUP == 0:
            return pair_body(*args)
        return general_body(*args)

    return jax.shard_map(body, mesh=mesh, in_specs=in_specs, out_specs=out_specs, check_vma=False)
```

```python
import functools
import math

import jax
import jax.numpy as jnp
from jax import lax
from jax.experimental import pallas as pl
from jax.experimental.pallas import tpu as pltpu
from jax.sharding import PartitionSpec as P

TILE = 64
EPSILON = 1e-06
F32 = jnp.float32
BF16 = jnp.bfloat16
MIB = 1024 * 1024
GROUP = 4


def passed_along(block, axis, distance):
    devices = range(lax.axis_size(axis))
    route = [((i - distance) % len(devices), i) for i in devices]
    return lax.ppermute(block, axis, route)


def slot_lists(neighbours, tile_slot):
    tile_count = tile_slot.shape[0]
    numbering = jnp.arange(tile_count, dtype=jnp.int32)
    placed = (tile_slot[:, None] == numbering[None, :]).astype(jnp.int32)
    tile_of_slot = jnp.sum(placed * numbering[:, None], axis=0)
    chosen = (tile_of_slot[:, None] == numbering[None, :]).astype(jnp.int32)
    listed_tiles = jnp.sum(chosen[:, :, None] * neighbours[None, :, :], axis=1)
    key_valid = listed_tiles >= 0
    safe_tiles = jnp.maximum(listed_tiles, 0)
    matches = (safe_tiles[:, :, None] == numbering[None, None, :]).astype(jnp.int32)
    key_slots = jnp.sum(matches * tile_slot[None, None, :], axis=2)
    return (key_slots, key_valid)


def block_tiles(tile_count):
    return math.gcd(tile_count, max(1, 512 // TILE))


def unit_norm(values):
    spread = jnp.sqrt(jnp.mean(values * values, axis=-1, keepdims=True) + EPSILON)
    return (values / spread, spread)


def probabilities(query_block, key_rows, block_valid):
    scores = jnp.einsum(
        "aihd,ajhd->ahij", query_block, key_rows, preferred_element_type=jnp.float32
    ) * (1.0 / math.sqrt(query_block.shape[-1]))
    key_mask = jnp.repeat(block_valid, TILE, axis=1)
    scores = jnp.where(key_mask[:, None, None, :], scores, -jnp.inf)
    row_max = jnp.max(scores, axis=-1, keepdims=True)
    weights = jnp.exp(scores - row_max)
    return (weights / jnp.sum(weights, axis=-1, keepdims=True)).astype(jnp.bfloat16)


def gathered(tiles_array, block_slots):
    picked = tiles_array[block_slots]
    return picked.reshape(block_slots.shape[0], -1, tiles_array.shape[2], tiles_array.shape[3])


def attend_both(query_tiles, key_tiles, value_tiles, grad_tiles, key_slots, key_valid):
    tile_count = query_tiles.shape[0]
    span = block_tiles(tile_count)
    scale_factor = 1.0 / math.sqrt(query_tiles.shape[-1])
    empty_grad = jnp.zeros(query_tiles.shape, jnp.float32)

    def per_block(accumulators, block_index):
        key_total, value_total = accumulators
        first_tile = block_index * span
        query_block = lax.dynamic_slice_in_dim(query_tiles, first_tile, span, 0)
        grad_block = lax.dynamic_slice_in_dim(grad_tiles, first_tile, span, 0)
        block_slots = lax.dynamic_slice_in_dim(key_slots, first_tile, span, 0)
        block_valid = lax.dynamic_slice_in_dim(key_valid, first_tile, span, 0)
        key_rows = gathered(key_tiles, block_slots)
        value_rows = gathered(value_tiles, block_slots)
        weights = probabilities(query_block, key_rows, block_valid)
        attended = jnp.einsum(
            "ahij,ajhd->aihd", weights, value_rows, preferred_element_type=jnp.float32
        )
        value_part = jnp.einsum(
            "ahij,aihd->ajhd", weights, grad_block, preferred_element_type=jnp.float32
        )
        prob_grad = jnp.einsum(
            "aihd,ajhd->ahij", grad_block, value_rows, preferred_element_type=jnp.float32
        )
        weights_wide = weights.astype(jnp.float32)
        row_delta = jnp.sum(weights_wide * prob_grad, axis=-1, keepdims=True)
        score_grad = (weights_wide * (prob_grad - row_delta) * scale_factor).astype(jnp.bfloat16)
        query_part = jnp.einsum(
            "ahij,ajhd->aihd", score_grad, key_rows, preferred_element_type=jnp.float32
        )
        key_part = jnp.einsum(
            "ahij,aihd->ajhd", score_grad, query_block, preferred_element_type=jnp.float32
        )
        block_shape = (span, block_slots.shape[1]) + query_tiles.shape[1:]
        key_total = key_total.at[block_slots].add(key_part.reshape(block_shape))
        value_total = value_total.at[block_slots].add(value_part.reshape(block_shape))
        return ((key_total, value_total), (attended, query_part))

    totals, parts = lax.scan(
        per_block, (empty_grad, empty_grad), jnp.arange(tile_count // span, dtype=jnp.int32)
    )
    flat_shape = (-1,) + query_tiles.shape[2:]
    return (
        parts[0].reshape(flat_shape),
        parts[1].reshape(flat_shape),
        totals[0].reshape(flat_shape),
        totals[1].reshape(flat_shape),
    )


def general_body(
    segment_input,
    output_grad,
    qkv_weight,
    out_weight,
    query_gain,
    key_gain,
    gate_scale,
    neighbours,
    tile_slot,
):
    key_slots, key_valid = slot_lists(neighbours, tile_slot)
    stream = segment_input[0]
    upstream = output_grad[0]
    model_width = stream.shape[1]
    head_dim = query_gain.shape[1]
    local_heads = qkv_weight.shape[2]
    local_width = local_heads * head_dim
    proj_weight = qkv_weight[0].reshape(model_width, local_heads * 3 * head_dim)
    out_local = out_weight[0]
    gate_row = gate_scale[0]
    query_weights = query_gain[0]
    key_weights = key_gain[0]
    projected = jnp.dot(
        lax.all_gather(stream, "seq", axis=0, tiled=True),
        proj_weight,
        preferred_element_type=jnp.float32,
    )
    all_tokens = projected.shape[0]
    projected = projected.reshape(all_tokens, local_heads, 3, head_dim)
    query_unit, query_spread = unit_norm(projected[:, :, 0])
    key_unit, key_spread = unit_norm(projected[:, :, 1])
    queries = (query_unit * query_weights).astype(jnp.bfloat16)
    keys_normed = (key_unit * key_weights).astype(jnp.bfloat16)
    value_rows = projected[:, :, 2].astype(jnp.bfloat16)
    scaled = (upstream.astype(jnp.float32) * gate_row).astype(jnp.bfloat16)
    attended_grad = jnp.einsum(
        "td,cd->tc",
        lax.all_gather(scaled, "seq", axis=0, tiled=True),
        out_local,
        preferred_element_type=jnp.float32,
    ).astype(jnp.bfloat16)

    def as_tiles(values):
        return values.reshape(-1, TILE, local_heads, head_dim)

    attended, query_grad, key_grad, value_grad = attend_both(
        as_tiles(queries),
        as_tiles(keys_normed),
        as_tiles(value_rows),
        as_tiles(attended_grad),
        key_slots,
        key_valid,
    )
    attended_low = attended.astype(jnp.bfloat16).reshape(all_tokens, local_width)
    rows = attended_low
    attention_out = lax.psum_scatter(
        jnp.dot(rows, out_local, preferred_element_type=jnp.float32),
        "seq",
        scatter_dimension=0,
        tiled=True,
    )
    section_out = (stream.astype(jnp.float32) + gate_row * attention_out).astype(jnp.bfloat16)
    segment_output = passed_along(section_out, "pipe", 1)
    gate_local = lax.psum_scatter(
        jnp.sum(upstream.astype(jnp.float32) * attention_out, axis=0),
        "seq",
        scatter_dimension=0,
        tiled=True,
    )
    query_scaled = query_grad * query_weights
    query_part_grad = (
        query_scaled - query_unit * jnp.mean(query_scaled * query_unit, axis=-1, keepdims=True)
    ) / query_spread
    key_scaled = key_grad * key_weights
    key_part_grad = (
        key_scaled - key_unit * jnp.mean(key_scaled * key_unit, axis=-1, keepdims=True)
    ) / key_spread
    projected_grad = (
        jnp.stack([query_part_grad, key_part_grad, value_grad], axis=2)
        .astype(jnp.bfloat16)
        .reshape(all_tokens, local_heads * 3 * head_dim)
    )
    rows = projected_grad
    stream_grad = lax.psum_scatter(
        jnp.einsum("tc,dc->td", rows, proj_weight, preferred_element_type=jnp.float32).astype(
            jnp.bfloat16
        ),
        "seq",
        scatter_dimension=0,
        tiled=True,
    ).astype(jnp.float32)
    token_grad = (upstream.astype(jnp.float32) + stream_grad).astype(jnp.bfloat16)
    input_grad = passed_along(token_grad, "pipe", -1)
    return (segment_output[None], input_grad[None], gate_local[None])


def dot_nn(a, b):
    return lax.dot_general(a, b, (((1,), (0,)), ((), ())), preferred_element_type=F32)


def dot_nt(a, b):
    return lax.dot_general(a, b, (((1,), (1,)), ((), ())), preferred_element_type=F32)


def dot_tn(a, b):
    return lax.dot_general(a, b, (((0,), (0,)), ((), ())), preferred_element_type=F32)


def params(mebibytes):
    return pltpu.CompilerParams(vmem_limit_bytes=mebibytes * MIB)


class Copies:
    def __init__(self, pairs, semaphores, ahead):
        self.copies = [
            pltpu.make_async_copy(source, target, semaphores.at[i])
            for i, (source, target) in enumerate(pairs)
        ]
        self.ahead = ahead
        self.waited = 0
        for copy in self.copies[:ahead]:
            copy.start()

    def wait(self, count=1):
        for _ in range(count):
            self.copies[self.waited].wait()
            following = self.waited + self.ahead
            if following < len(self.copies):
                self.copies[following].start()
            self.waited += 1


def regroup_kernel(weight_ref, out_ref, turned_ref, read_ref, reads):
    depth, heads, width = weight_ref.shape
    slots, rows = read_ref.shape[:2]
    steps = depth // rows

    def part(step):
        return pl.ds(pl.multiple_of(step * rows, rows), rows)

    def read(step, slot):
        return pltpu.make_async_copy(
            weight_ref.at[part(step)], read_ref.at[slot], reads.at[slot]
        )

    for slot in range(slots):
        read(slot, slot).start()

    @pl.loop(0, steps)
    def _(step):
        slot = lax.rem(step, slots)
        read(step, slot).wait()
        by_head = jnp.swapaxes(read_ref[slot], 0, 1)
        for head in range(heads):
            left = (head % GROUP) * width
            out_ref[head // GROUP, part(step), left : left + width] = by_head[head]
            if head >= heads - GROUP:
                turned_ref[left : left + width, part(step)] = by_head[head].T

        @pl.when(step + slots < steps)
        def _():
            read(step + slots, slot).start()


def regroup(weight, rows, slots):
    depth, heads, width = weight.shape
    out = (heads // GROUP, depth, GROUP * width)
    return pl.pallas_call(
        regroup_kernel,
        out_shape=(
            pltpu.VMEM(out, weight.dtype),
            pltpu.VMEM((out[2], out[1]), weight.dtype),
        ),
        in_specs=[pl.BlockSpec(memory_space=pl.ANY)],
        out_specs=(pl.BlockSpec(memory_space=pltpu.VMEM),) * 2,
        scratch_shapes=[
            pltpu.VMEM((slots, rows, heads, width), weight.dtype),
            pltpu.SemaphoreType.DMA((slots,)),
        ],
        compiler_params=params(9),
        cost_estimate=pl.CostEstimate(
            flops=0, bytes_accessed=4 * depth * heads * width, transcendentals=0
        ),
        name="regroup",
    )(pltpu.with_memory_space_constraint(weight, pltpu.HBM))


def listed_slots(neighbours_ref, tile_slot_ref):
    tiles, places = neighbours_ref.shape
    one, zero = jnp.int32(1), jnp.int32(0)
    allowed = [[zero] * tiles for _ in range(tiles)]
    for t in range(tiles):
        for u in range(tiles):
            listed = zero
            for k in range(places):
                listed = jnp.where(neighbours_ref[t, k] == u, one, listed)
            for r in range(tiles):
                for c in range(tiles):
                    here = (tile_slot_ref[t] == r) & (tile_slot_ref[u] == c)
                    allowed[r][c] = jnp.where(here, listed, allowed[r][c])
    return allowed


def normed(rows, gain):
    inverse = lax.rsqrt(jnp.mean(rows * rows, axis=-1, keepdims=True) + EPSILON)
    unit = rows * inverse
    return unit, inverse, (unit * gain).astype(BF16)


def forward_kernel(
    neighbours_ref,
    tile_slot_ref,
    own_ref,
    other_ref,
    weight_ref,
    out_weight_ref,
    query_gain_ref,
    key_gain_ref,
    gate_ref,
    projected_ref,
    probs_ref,
    attention_ref,
    kept_ref,
    sent_ref,
    out_weight_buffer,
    tokens_ref,
    semaphores,
):
    local, model = own_ref.shape
    tokens = 2 * local
    width = query_gain_ref.shape[1]
    groups = weight_ref.shape[0]
    rows = GROUP * width

    def out_weight_part(group):
        place = pl.ds(group * rows, rows)
        return out_weight_ref.at[place], out_weight_buffer.at[place]

    copies = Copies([out_weight_part(group) for group in range(groups)], semaphores, groups)

    tokens_ref[:local, :] = own_ref[...]
    tokens_ref[local:, :] = other_ref[...]
    allowed = listed_slots(neighbours_ref, tile_slot_ref)
    mine = lax.axis_index("seq")
    row_half = lax.broadcasted_iota(jnp.int32, (tokens, tokens), 0) // local
    column_half = lax.broadcasted_iota(jnp.int32, (tokens, tokens), 1) // local
    row_slot = jnp.where(row_half == 0, mine, 1 - mine)
    column_slot = jnp.where(column_half == 0, mine, 1 - mine)
    table = jnp.zeros((tokens, tokens), jnp.int32)
    for r in range(2):
        for c in range(2):
            table = jnp.where((row_slot == r) & (column_slot == c), allowed[r][c], table)
    bias = jnp.where(table > 0, 0.0, -jnp.inf).astype(F32)

    def project(group):
        projected_ref[group] = dot_nn(tokens_ref[...], weight_ref[group])

    def attend(group):
        attended = []
        for head in range(GROUP):
            left = head * 3 * width
            _, _, queries = normed(projected_ref[group, :, left : left + width], query_gain_ref[...])
            left += width
            _, _, keys = normed(projected_ref[group, :, left : left + width], key_gain_ref[...])
            left += width
            value = projected_ref[group, :, left : left + width].astype(BF16)
            scores = dot_nt(queries, keys) * (1.0 / math.sqrt(width)) + bias
            row_max = jnp.max(scores, axis=-1, keepdims=True)
            weights = jnp.exp(scores - row_max)
            probs = (weights / jnp.sum(weights, axis=-1, keepdims=True)).astype(BF16)
            probs_ref[GROUP * group + head] = probs
            attended.append(dot_nn(probs, value).astype(BF16))
        return jnp.concatenate(attended, axis=1)

    def share(group, attended):
        return dot_nn(attended, out_weight_buffer[group * rows : (group + 1) * rows, :])

    project(0)
    attended = attend(0)
    for group in range(1, groups):
        project(group)
        copies.wait()
        following = attend(group)
        if group == 1:
            attention_ref[...] = share(0, attended)
        else:
            attention_ref[...] += share(group - 1, attended)
        attended = following
    copies.wait()
    total = share(groups - 1, attended)
    if groups > 1:
        total += attention_ref[...]
    attention_ref[...] = total
    gate = gate_ref[...]
    kept_ref[...] = (own_ref[...].astype(F32) + gate * total[:local]).astype(BF16)
    sent_ref[...] = (gate * total[local:]).astype(BF16)


def forward(neighbours, tile_slot, own, other, weight, out_weight, query_gain, key_gain, gate):
    local, model = own.shape
    groups, _, wide = weight.shape
    tokens = 2 * local
    weight = pltpu.with_memory_space_constraint(weight, pltpu.VMEM)
    out_weight = pltpu.with_memory_space_constraint(out_weight, pltpu.HBM)
    smem = pl.BlockSpec(memory_space=pltpu.SMEM)
    vmem = pl.BlockSpec(memory_space=pltpu.VMEM)
    hbm = pl.BlockSpec(memory_space=pl.ANY)
    return pl.pallas_call(
        forward_kernel,
        out_shape=(
            jax.ShapeDtypeStruct((groups, tokens, wide), F32),
            jax.ShapeDtypeStruct((GROUP * groups, tokens, tokens), BF16),
            jax.ShapeDtypeStruct((tokens, model), F32),
            jax.ShapeDtypeStruct((local, model), BF16),
            jax.ShapeDtypeStruct((local, model), BF16),
            pltpu.VMEM(out_weight.shape, BF16),
        ),
        in_specs=[smem, smem, vmem, vmem, vmem, hbm, vmem, vmem, vmem],
        out_specs=(vmem,) * 6,
        scratch_shapes=[
            pltpu.VMEM((tokens, model), BF16),
            pltpu.SemaphoreType.DMA((groups,)),
        ],
        compiler_params=params(8),
        cost_estimate=pl.CostEstimate(
            flops=2 * tokens * (weight.size + out_weight.size),
            bytes_accessed=2 * (weight.size + out_weight.size),
            transcendentals=0,
        ),
        name="attention_forward",
    )(neighbours, tile_slot, own, other, weight, out_weight, query_gain, key_gain, gate)


def input_grad(grad_ref, weight_ref, turned_ref, own_ref, kept_ref, sent_ref):
    local, model = own_ref.shape
    last = grad_ref.shape[0] - 1
    block = 512
    for start in range(0, model, block):
        part = slice(start, start + block)
        total = dot_nn(grad_ref[last], turned_ref[:, part])
        for group in range(last):
            total += dot_nt(weight_ref[group, part, :], grad_ref[group]).T
        kept_ref[:, part] = (own_ref[:, part].astype(F32) + total[:local]).astype(BF16)
        sent_ref[:, part] = total[local:].astype(BF16)


def backward_kernel(
    own_ref,
    other_ref,
    out_weight_ref,
    weight_ref,
    turned_ref,
    projected_ref,
    probs_ref,
    attention_ref,
    query_gain_ref,
    key_gain_ref,
    gate_ref,
    gate_kept_ref,
    gate_sent_ref,
    kept_ref,
    sent_ref,
    grad_ref,
    scaled_ref,
    attended_grad_ref,
    gate_grad_ref,
):
    local = own_ref.shape[0]
    width = query_gain_ref.shape[1]
    groups = grad_ref.shape[0]
    rows = GROUP * width

    gate = gate_ref[...]
    own, other = own_ref[...].astype(F32), other_ref[...].astype(F32)
    scaled_ref[:local, :] = (own * gate).astype(BF16)
    scaled_ref[local:, :] = (other * gate).astype(BF16)
    gate_grad_ref[...] = jnp.sum(
        own * attention_ref[:local, :] + other * attention_ref[local:, :], axis=0, keepdims=True
    )
    half = gate_kept_ref.shape[1]
    mine = lax.axis_index("seq")
    gate_kept_ref[...] = gate_grad_ref[:, pl.ds(pl.multiple_of(mine * half, half), half)]
    gate_sent_ref[...] = gate_grad_ref[:, pl.ds(pl.multiple_of((1 - mine) * half, half), half)]

    def attended_grad(group):
        part = slice(group * rows, (group + 1) * rows)
        product = dot_nt(scaled_ref[...], out_weight_ref[part, :])
        attended_grad_ref[group] = product.astype(BF16)

    def attend_backward(group, head):
        left = head * 3 * width
        query_part = slice(left, left + width)
        key_part = slice(left + width, left + 2 * width)
        value_part = slice(left + 2 * width, left + 3 * width)
        query_gain, key_gain = query_gain_ref[...], key_gain_ref[...]
        query_unit, query_inverse, queries = normed(projected_ref[group, :, query_part], query_gain)
        key_unit, key_inverse, keys = normed(projected_ref[group, :, key_part], key_gain)
        value = projected_ref[group, :, value_part].astype(BF16)
        grad = attended_grad_ref[group, :, head * width : (head + 1) * width]
        probs = probs_ref[GROUP * group + head]
        probs_wide = probs.astype(F32)
        grad_ref[group, :, value_part] = dot_tn(probs, grad).astype(BF16)
        prob_grad = dot_nt(grad, value)
        row_delta = jnp.sum(probs_wide * prob_grad, axis=-1, keepdims=True)
        scale_factor = 1.0 / math.sqrt(width)
        score_grad = (probs_wide * (prob_grad - row_delta) * scale_factor).astype(BF16)
        query_scaled = dot_nn(score_grad, keys) * query_gain
        key_scaled = dot_tn(score_grad, queries) * key_gain
        query_mean = jnp.mean(query_scaled * query_unit, axis=-1, keepdims=True)
        key_mean = jnp.mean(key_scaled * key_unit, axis=-1, keepdims=True)
        grad_ref[group, :, query_part] = (
            (query_scaled - query_unit * query_mean) * query_inverse
        ).astype(BF16)
        grad_ref[group, :, key_part] = ((key_scaled - key_unit * key_mean) * key_inverse).astype(BF16)

    attended_grad(0)
    for group in range(groups):
        if group + 1 < groups:
            attended_grad(group + 1)
        for head in range(GROUP):
            attend_backward(group, head)
    input_grad(grad_ref, weight_ref, turned_ref, own_ref, kept_ref, sent_ref)


def backward(
    own,
    other,
    out_weight,
    weight,
    turned,
    projected,
    probs,
    attention,
    query_gain,
    key_gain,
    gate,
):
    local, model = own.shape
    groups, tokens, wide = projected.shape
    head_dim = query_gain.shape[1]
    out_weight = pltpu.with_memory_space_constraint(out_weight, pltpu.VMEM)
    weight = pltpu.with_memory_space_constraint(weight, pltpu.VMEM)
    turned = pltpu.with_memory_space_constraint(turned, pltpu.VMEM)
    vmem = pl.BlockSpec(memory_space=pltpu.VMEM)
    return pl.pallas_call(
        backward_kernel,
        out_shape=(
            jax.ShapeDtypeStruct((1, model // 2), F32),
            jax.ShapeDtypeStruct((1, model // 2), F32),
            jax.ShapeDtypeStruct((local, model), BF16),
            jax.ShapeDtypeStruct((local, model), BF16),
        ),
        in_specs=[vmem] * 11,
        out_specs=(vmem,) * 4,
        scratch_shapes=[
            pltpu.VMEM((groups, tokens, wide), BF16),
            pltpu.VMEM((tokens, model), BF16),
            pltpu.VMEM((groups, tokens, GROUP * head_dim), BF16),
            pltpu.VMEM((1, model), F32),
        ],
        compiler_params=params(8),
        cost_estimate=pl.CostEstimate(
            flops=2 * tokens * (out_weight.size + weight.size),
            bytes_accessed=2 * (out_weight.size + weight.size),
            transcendentals=0,
        ),
        name="attention_backward",
    )(
        own,
        other,
        out_weight,
        weight,
        turned,
        projected,
        probs,
        attention,
        query_gain,
        key_gain,
        gate,
    )


def sums_kernel(sent_ref, kept_ref, gate_kept_ref, gate_sent_ref, grad_ref, gate_ref):
    grad_ref[...] = (kept_ref[...].astype(F32) + sent_ref[...].astype(F32)).astype(BF16)
    gate_ref[...] = gate_kept_ref[...] + gate_sent_ref[...]


def sums(sent, kept, gate_kept, gate_sent):
    vmem = pl.BlockSpec(memory_space=pltpu.VMEM)
    return pl.pallas_call(
        sums_kernel,
        out_shape=(
            jax.ShapeDtypeStruct(kept.shape, BF16),
            jax.ShapeDtypeStruct(gate_kept.shape, F32),
        ),
        in_specs=[vmem] * 4,
        out_specs=(vmem, vmem),
        compiler_params=params(8),
        name="sums",
    )(sent, kept, gate_kept, gate_sent)


def routed(block, seq_step, pipe_step):
    seq_size, pipe_size = lax.axis_size("seq"), lax.axis_size("pipe")
    route = []
    for i in range(seq_size):
        for j in range(pipe_size):
            target = (i + seq_step) % seq_size * pipe_size + (j + pipe_step) % pipe_size
            route.append((i * pipe_size + j, target))
    return lax.ppermute(block, ("seq", "pipe"), route)


def pair_body(
    segment_input,
    output_grad,
    qkv_weight,
    out_weight,
    query_gain,
    key_gain,
    gate_scale,
    neighbours,
    tile_slot,
):
    stream = segment_input[0]
    upstream = output_grad[0]
    out_local = out_weight[0]
    other_stream = routed(stream, 1, 0)
    weight, turned_weight = regroup(qkv_weight[0], 128, 6)
    other_upstream = routed(upstream, 1, 0)
    projected, probs, attention, kept, sent, out_local = forward(
        neighbours,
        tile_slot,
        stream,
        other_stream,
        weight,
        out_local,
        query_gain,
        key_gain,
        gate_scale,
    )
    kept = routed(kept, 0, 1)
    sent = routed(sent, 1, 1)
    gate_kept, gate_sent, grad_kept, grad_sent = backward(
        upstream,
        other_upstream,
        out_local,
        weight,
        turned_weight,
        projected,
        probs,
        attention,
        query_gain,
        key_gain,
        gate_scale,
    )
    grad_sent = routed(grad_sent, 1, -1)
    grad_kept = routed(grad_kept, 0, -1)
    segment_output = (kept.astype(F32) + sent.astype(F32)).astype(BF16)
    segment_output, gate_sent = lax.optimization_barrier((segment_output, gate_sent))
    gate_sent = routed(gate_sent, 1, 0)
    token_grad, gate_grad = sums(grad_sent, grad_kept, gate_kept, gate_sent)
    return (segment_output[None], token_grad[None], gate_grad)


def solution(mesh):
    in_specs = (
        P("pipe", ("dp", "seq"), None),
        P("pipe", ("dp", "seq"), None),
        P("pipe", None, "seq", None),
        P("pipe", "seq", None),
        P("pipe", None),
        P("pipe", None),
        P("pipe", None),
        P("dp", None),
        P("dp"),
    )
    out_specs = (
        P("pipe", ("dp", "seq"), None),
        P("pipe", ("dp", "seq"), None),
        P(("dp", "pipe"), "seq"),
    )

    def body(*args):
        one_tile_each = args[0].shape[1] == TILE and args[8].shape[0] == 2
        if mesh.shape["seq"] == 2 and one_tile_each and args[2].shape[2] % GROUP == 0:
            return pair_body(*args)
        return general_body(*args)

    return jax.shard_map(body, mesh=mesh, in_specs=in_specs, out_specs=out_specs, check_vma=False)
```

```python
import functools
import math

import jax
import jax.numpy as jnp
from jax import lax
from jax.experimental import pallas as pl
from jax.experimental.pallas import tpu as pltpu
from jax.sharding import PartitionSpec as P

TILE = 64
EPSILON = 1e-06
F32 = jnp.float32
BF16 = jnp.bfloat16
MIB = 1024 * 1024
GROUP = 4
TURNED = 6


def passed_along(block, axis, distance):
    devices = range(lax.axis_size(axis))
    route = [((i - distance) % len(devices), i) for i in devices]
    return lax.ppermute(block, axis, route)


def slot_lists(neighbours, tile_slot):
    tile_count = tile_slot.shape[0]
    numbering = jnp.arange(tile_count, dtype=jnp.int32)
    placed = (tile_slot[:, None] == numbering[None, :]).astype(jnp.int32)
    tile_of_slot = jnp.sum(placed * numbering[:, None], axis=0)
    chosen = (tile_of_slot[:, None] == numbering[None, :]).astype(jnp.int32)
    listed_tiles = jnp.sum(chosen[:, :, None] * neighbours[None, :, :], axis=1)
    key_valid = listed_tiles >= 0
    safe_tiles = jnp.maximum(listed_tiles, 0)
    matches = (safe_tiles[:, :, None] == numbering[None, None, :]).astype(jnp.int32)
    key_slots = jnp.sum(matches * tile_slot[None, None, :], axis=2)
    return (key_slots, key_valid)


def block_tiles(tile_count):
    return math.gcd(tile_count, max(1, 512 // TILE))


def unit_norm(values):
    spread = jnp.sqrt(jnp.mean(values * values, axis=-1, keepdims=True) + EPSILON)
    return (values / spread, spread)


def probabilities(query_block, key_rows, block_valid):
    scores = jnp.einsum(
        "aihd,ajhd->ahij", query_block, key_rows, preferred_element_type=jnp.float32
    ) * (1.0 / math.sqrt(query_block.shape[-1]))
    key_mask = jnp.repeat(block_valid, TILE, axis=1)
    scores = jnp.where(key_mask[:, None, None, :], scores, -jnp.inf)
    row_max = jnp.max(scores, axis=-1, keepdims=True)
    weights = jnp.exp(scores - row_max)
    return (weights / jnp.sum(weights, axis=-1, keepdims=True)).astype(jnp.bfloat16)


def gathered(tiles_array, block_slots):
    picked = tiles_array[block_slots]
    return picked.reshape(block_slots.shape[0], -1, tiles_array.shape[2], tiles_array.shape[3])


def attend_both(query_tiles, key_tiles, value_tiles, grad_tiles, key_slots, key_valid):
    tile_count = query_tiles.shape[0]
    span = block_tiles(tile_count)
    scale_factor = 1.0 / math.sqrt(query_tiles.shape[-1])
    empty_grad = jnp.zeros(query_tiles.shape, jnp.float32)

    def per_block(accumulators, block_index):
        key_total, value_total = accumulators
        first_tile = block_index * span
        query_block = lax.dynamic_slice_in_dim(query_tiles, first_tile, span, 0)
        grad_block = lax.dynamic_slice_in_dim(grad_tiles, first_tile, span, 0)
        block_slots = lax.dynamic_slice_in_dim(key_slots, first_tile, span, 0)
        block_valid = lax.dynamic_slice_in_dim(key_valid, first_tile, span, 0)
        key_rows = gathered(key_tiles, block_slots)
        value_rows = gathered(value_tiles, block_slots)
        weights = probabilities(query_block, key_rows, block_valid)
        attended = jnp.einsum(
            "ahij,ajhd->aihd", weights, value_rows, preferred_element_type=jnp.float32
        )
        value_part = jnp.einsum(
            "ahij,aihd->ajhd", weights, grad_block, preferred_element_type=jnp.float32
        )
        prob_grad = jnp.einsum(
            "aihd,ajhd->ahij", grad_block, value_rows, preferred_element_type=jnp.float32
        )
        weights_wide = weights.astype(jnp.float32)
        row_delta = jnp.sum(weights_wide * prob_grad, axis=-1, keepdims=True)
        score_grad = (weights_wide * (prob_grad - row_delta) * scale_factor).astype(jnp.bfloat16)
        query_part = jnp.einsum(
            "ahij,ajhd->aihd", score_grad, key_rows, preferred_element_type=jnp.float32
        )
        key_part = jnp.einsum(
            "ahij,aihd->ajhd", score_grad, query_block, preferred_element_type=jnp.float32
        )
        block_shape = (span, block_slots.shape[1]) + query_tiles.shape[1:]
        key_total = key_total.at[block_slots].add(key_part.reshape(block_shape))
        value_total = value_total.at[block_slots].add(value_part.reshape(block_shape))
        return ((key_total, value_total), (attended, query_part))

    totals, parts = lax.scan(
        per_block, (empty_grad, empty_grad), jnp.arange(tile_count // span, dtype=jnp.int32)
    )
    flat_shape = (-1,) + query_tiles.shape[2:]
    return (
        parts[0].reshape(flat_shape),
        parts[1].reshape(flat_shape),
        totals[0].reshape(flat_shape),
        totals[1].reshape(flat_shape),
    )


def general_body(
    segment_input,
    output_grad,
    qkv_weight,
    out_weight,
    query_gain,
    key_gain,
    gate_scale,
    neighbours,
    tile_slot,
):
    key_slots, key_valid = slot_lists(neighbours, tile_slot)
    stream = segment_input[0]
    upstream = output_grad[0]
    model_width = stream.shape[1]
    head_dim = query_gain.shape[1]
    local_heads = qkv_weight.shape[2]
    local_width = local_heads * head_dim
    proj_weight = qkv_weight[0].reshape(model_width, local_heads * 3 * head_dim)
    out_local = out_weight[0]
    gate_row = gate_scale[0]
    query_weights = query_gain[0]
    key_weights = key_gain[0]
    projected = jnp.dot(
        lax.all_gather(stream, "seq", axis=0, tiled=True),
        proj_weight,
        preferred_element_type=jnp.float32,
    )
    all_tokens = projected.shape[0]
    projected = projected.reshape(all_tokens, local_heads, 3, head_dim)
    query_unit, query_spread = unit_norm(projected[:, :, 0])
    key_unit, key_spread = unit_norm(projected[:, :, 1])
    queries = (query_unit * query_weights).astype(jnp.bfloat16)
    keys_normed = (key_unit * key_weights).astype(jnp.bfloat16)
    value_rows = projected[:, :, 2].astype(jnp.bfloat16)
    scaled = (upstream.astype(jnp.float32) * gate_row).astype(jnp.bfloat16)
    attended_grad = jnp.einsum(
        "td,cd->tc",
        lax.all_gather(scaled, "seq", axis=0, tiled=True),
        out_local,
        preferred_element_type=jnp.float32,
    ).astype(jnp.bfloat16)

    def as_tiles(values):
        return values.reshape(-1, TILE, local_heads, head_dim)

    attended, query_grad, key_grad, value_grad = attend_both(
        as_tiles(queries),
        as_tiles(keys_normed),
        as_tiles(value_rows),
        as_tiles(attended_grad),
        key_slots,
        key_valid,
    )
    attended_low = attended.astype(jnp.bfloat16).reshape(all_tokens, local_width)
    rows = attended_low
    attention_out = lax.psum_scatter(
        jnp.dot(rows, out_local, preferred_element_type=jnp.float32),
        "seq",
        scatter_dimension=0,
        tiled=True,
    )
    section_out = (stream.astype(jnp.float32) + gate_row * attention_out).astype(jnp.bfloat16)
    segment_output = passed_along(section_out, "pipe", 1)
    gate_local = lax.psum_scatter(
        jnp.sum(upstream.astype(jnp.float32) * attention_out, axis=0),
        "seq",
        scatter_dimension=0,
        tiled=True,
    )
    query_scaled = query_grad * query_weights
    query_part_grad = (
        query_scaled - query_unit * jnp.mean(query_scaled * query_unit, axis=-1, keepdims=True)
    ) / query_spread
    key_scaled = key_grad * key_weights
    key_part_grad = (
        key_scaled - key_unit * jnp.mean(key_scaled * key_unit, axis=-1, keepdims=True)
    ) / key_spread
    projected_grad = (
        jnp.stack([query_part_grad, key_part_grad, value_grad], axis=2)
        .astype(jnp.bfloat16)
        .reshape(all_tokens, local_heads * 3 * head_dim)
    )
    rows = projected_grad
    stream_grad = lax.psum_scatter(
        jnp.einsum("tc,dc->td", rows, proj_weight, preferred_element_type=jnp.float32).astype(
            jnp.bfloat16
        ),
        "seq",
        scatter_dimension=0,
        tiled=True,
    ).astype(jnp.float32)
    token_grad = (upstream.astype(jnp.float32) + stream_grad).astype(jnp.bfloat16)
    input_grad = passed_along(token_grad, "pipe", -1)
    return (segment_output[None], input_grad[None], gate_local[None])


def dot_nn(a, b):
    return lax.dot_general(a, b, (((1,), (0,)), ((), ())), preferred_element_type=F32)


def dot_nt(a, b):
    return lax.dot_general(a, b, (((1,), (1,)), ((), ())), preferred_element_type=F32)


def dot_tn(a, b):
    return lax.dot_general(a, b, (((0,), (0,)), ((), ())), preferred_element_type=F32)


def params(mebibytes):
    return pltpu.CompilerParams(vmem_limit_bytes=mebibytes * MIB)


class Copies:
    def __init__(self, pairs, semaphores, ahead):
        self.copies = [
            pltpu.make_async_copy(source, target, semaphores.at[i])
            for i, (source, target) in enumerate(pairs)
        ]
        self.ahead = ahead
        self.waited = 0
        for copy in self.copies[:ahead]:
            copy.start()

    def wait(self, count=1):
        for _ in range(count):
            self.copies[self.waited].wait()
            following = self.waited + self.ahead
            if following < len(self.copies):
                self.copies[following].start()
            self.waited += 1


def regroup_kernel(weight_ref, out_ref, turned_ref, read_ref, reads):
    depth, heads, width = weight_ref.shape
    slots, rows = read_ref.shape[:2]
    steps = depth // rows

    def part(step):
        return pl.ds(pl.multiple_of(step * rows, rows), rows)

    def read(step, slot):
        return pltpu.make_async_copy(
            weight_ref.at[part(step)], read_ref.at[slot], reads.at[slot]
        )

    for slot in range(slots):
        read(slot, slot).start()

    @pl.loop(0, steps)
    def _(step):
        slot = lax.rem(step, slots)
        read(step, slot).wait()
        by_head = jnp.swapaxes(read_ref[slot], 0, 1)
        for head in range(heads):
            left = (head % GROUP) * width
            out_ref[head // GROUP, part(step), left : left + width] = by_head[head]
            above = (head + 1) * width - (heads * width - turned_ref.shape[0])
            if above > 0:
                turned_ref[above - width : above, part(step)] = by_head[head].T

        @pl.when(step + slots < steps)
        def _():
            read(step + slots, slot).start()


def regroup(weight, rows, slots, turned):
    depth, heads, width = weight.shape
    out = (heads // GROUP, depth, GROUP * width)
    return pl.pallas_call(
        regroup_kernel,
        out_shape=(
            pltpu.VMEM(out, weight.dtype),
            pltpu.VMEM((turned * width, depth), weight.dtype),
        ),
        in_specs=[pl.BlockSpec(memory_space=pl.ANY)],
        out_specs=(pl.BlockSpec(memory_space=pltpu.VMEM),) * 2,
        scratch_shapes=[
            pltpu.VMEM((slots, rows, heads, width), weight.dtype),
            pltpu.SemaphoreType.DMA((slots,)),
        ],
        compiler_params=params(6),
        cost_estimate=pl.CostEstimate(
            flops=0, bytes_accessed=4 * depth * heads * width, transcendentals=0
        ),
        name="regroup",
    )(pltpu.with_memory_space_constraint(weight, pltpu.HBM))


def listed_slots(neighbours_ref, tile_slot_ref):
    tiles, places = neighbours_ref.shape
    one, zero = jnp.int32(1), jnp.int32(0)
    allowed = [[zero] * tiles for _ in range(tiles)]
    for t in range(tiles):
        for u in range(tiles):
            listed = zero
            for k in range(places):
                listed = jnp.where(neighbours_ref[t, k] == u, one, listed)
            for r in range(tiles):
                for c in range(tiles):
                    here = (tile_slot_ref[t] == r) & (tile_slot_ref[u] == c)
                    allowed[r][c] = jnp.where(here, listed, allowed[r][c])
    return allowed


def normed(rows, gain):
    inverse = lax.rsqrt(jnp.mean(rows * rows, axis=-1, keepdims=True) + EPSILON)
    unit = rows * inverse
    return unit, inverse, (unit * gain).astype(BF16)


def forward_kernel(
    neighbours_ref,
    tile_slot_ref,
    own_ref,
    other_ref,
    weight_ref,
    out_weight_ref,
    query_gain_ref,
    key_gain_ref,
    gate_ref,
    projected_ref,
    inverse_ref,
    probs_ref,
    attention_ref,
    kept_ref,
    sent_ref,
    out_weight_buffer,
    tokens_ref,
    semaphores,
):
    local, model = own_ref.shape
    tokens = 2 * local
    width = query_gain_ref.shape[1]
    groups = weight_ref.shape[0]
    rows = GROUP * width

    def out_weight_part(group):
        place = pl.ds(group * rows, rows)
        return out_weight_ref.at[place], out_weight_buffer.at[place]

    copies = Copies([out_weight_part(group) for group in range(groups)], semaphores, groups)

    tokens_ref[:local, :] = own_ref[...]
    tokens_ref[local:, :] = other_ref[...]
    allowed = listed_slots(neighbours_ref, tile_slot_ref)
    mine = lax.axis_index("seq")
    row_half = lax.broadcasted_iota(jnp.int32, (tokens, tokens), 0) // local
    column_half = lax.broadcasted_iota(jnp.int32, (tokens, tokens), 1) // local
    row_slot = jnp.where(row_half == 0, mine, 1 - mine)
    column_slot = jnp.where(column_half == 0, mine, 1 - mine)
    table = jnp.zeros((tokens, tokens), jnp.int32)
    for r in range(2):
        for c in range(2):
            table = jnp.where((row_slot == r) & (column_slot == c), allowed[r][c], table)
    bias = jnp.where(table > 0, 0.0, -jnp.inf).astype(F32)

    def project(group):
        projected_ref[group] = dot_nn(tokens_ref[...], weight_ref[group])

    def attend(group):
        attended = []
        for head in range(GROUP):
            left = head * 3 * width
            operands = []
            for index, gain_ref in enumerate((query_gain_ref, key_gain_ref)):
                part = slice(left, left + width)
                unit, inverse, operand = normed(projected_ref[group, :, part], gain_ref[...])
                projected_ref[group, :, part] = unit
                place = 2 * head + index
                inverse_ref[group, :, place : place + 1] = inverse
                operands.append(operand)
                left += width
            queries, keys = operands
            value = projected_ref[group, :, left : left + width].astype(BF16)
            scores = dot_nt(queries, keys) * (1.0 / math.sqrt(width)) + bias
            row_max = jnp.max(scores, axis=-1, keepdims=True)
            weights = jnp.exp(scores - row_max)
            probs = (weights / jnp.sum(weights, axis=-1, keepdims=True)).astype(BF16)
            probs_ref[GROUP * group + head] = probs
            attended.append(dot_nn(probs, value).astype(BF16))
        return jnp.concatenate(attended, axis=1)

    def share(group, attended):
        return dot_nn(attended, out_weight_buffer[group * rows : (group + 1) * rows, :])

    project(0)
    attended = attend(0)
    for group in range(1, groups):
        project(group)
        copies.wait()
        following = attend(group)
        if group == 1:
            attention_ref[...] = share(0, attended)
        else:
            attention_ref[...] += share(group - 1, attended)
        attended = following
    copies.wait()
    total = share(groups - 1, attended)
    if groups > 1:
        total += attention_ref[...]
    attention_ref[...] = total
    gate = gate_ref[...]
    kept_ref[...] = (own_ref[...].astype(F32) + gate * total[:local]).astype(BF16)
    sent_ref[...] = (gate * total[local:]).astype(BF16)


def forward(neighbours, tile_slot, own, other, weight, out_weight, query_gain, key_gain, gate):
    local, model = own.shape
    groups, _, wide = weight.shape
    tokens = 2 * local
    weight = pltpu.with_memory_space_constraint(weight, pltpu.VMEM)
    out_weight = pltpu.with_memory_space_constraint(out_weight, pltpu.HBM)
    smem = pl.BlockSpec(memory_space=pltpu.SMEM)
    vmem = pl.BlockSpec(memory_space=pltpu.VMEM)
    hbm = pl.BlockSpec(memory_space=pl.ANY)
    return pl.pallas_call(
        forward_kernel,
        out_shape=(
            jax.ShapeDtypeStruct((groups, tokens, wide), F32),
            jax.ShapeDtypeStruct((groups, tokens, 2 * GROUP), F32),
            jax.ShapeDtypeStruct((GROUP * groups, tokens, tokens), BF16),
            jax.ShapeDtypeStruct((tokens, model), F32),
            jax.ShapeDtypeStruct((local, model), BF16),
            jax.ShapeDtypeStruct((local, model), BF16),
            pltpu.VMEM(out_weight.shape, BF16),
        ),
        in_specs=[smem, smem, vmem, vmem, vmem, hbm, vmem, vmem, vmem],
        out_specs=(vmem,) * 7,
        scratch_shapes=[
            pltpu.VMEM((tokens, model), BF16),
            pltpu.SemaphoreType.DMA((groups,)),
        ],
        compiler_params=params(6),
        cost_estimate=pl.CostEstimate(
            flops=2 * tokens * (weight.size + out_weight.size),
            bytes_accessed=2 * (weight.size + out_weight.size),
            transcendentals=0,
        ),
        name="attention_forward",
    )(neighbours, tile_slot, own, other, weight, out_weight, query_gain, key_gain, gate)


def input_grad(grad_ref, weight_ref, turned_ref, own_ref, kept_ref, sent_ref):
    local, model = own_ref.shape
    groups, _, wide = grad_ref.shape
    streamed = groups * wide - turned_ref.shape[0]
    block = 512
    for start in range(0, model, block):
        part = slice(start, start + block)
        total = None
        for group in range(groups):
            first = group * wide
            cut = min(max(streamed - first, 0), wide)
            if cut < wide:
                rows = slice(first + cut - streamed, first + wide - streamed)
                product = dot_nn(grad_ref[group, :, cut:], turned_ref[rows, part])
                total = product if total is None else total + product
            if cut > 0:
                product = dot_nt(weight_ref[group, part, :cut], grad_ref[group, :, :cut]).T
                total = product if total is None else total + product
        kept_ref[:, part] = (own_ref[:, part].astype(F32) + total[:local]).astype(BF16)
        sent_ref[:, part] = total[local:].astype(BF16)


def backward_kernel(
    own_ref,
    other_ref,
    out_weight_ref,
    weight_ref,
    turned_ref,
    projected_ref,
    inverse_ref,
    probs_ref,
    attention_ref,
    query_gain_ref,
    key_gain_ref,
    gate_ref,
    gate_kept_ref,
    gate_sent_ref,
    kept_ref,
    sent_ref,
    grad_ref,
    scaled_ref,
    attended_grad_ref,
    gate_grad_ref,
):
    local = own_ref.shape[0]
    width = query_gain_ref.shape[1]
    groups = grad_ref.shape[0]
    rows = GROUP * width

    gate = gate_ref[...]
    own, other = own_ref[...].astype(F32), other_ref[...].astype(F32)
    scaled_ref[:local, :] = (own * gate).astype(BF16)
    scaled_ref[local:, :] = (other * gate).astype(BF16)
    gate_grad_ref[...] = jnp.sum(
        own * attention_ref[:local, :] + other * attention_ref[local:, :], axis=0, keepdims=True
    )
    half = gate_kept_ref.shape[1]
    mine = lax.axis_index("seq")
    gate_kept_ref[...] = gate_grad_ref[:, pl.ds(pl.multiple_of(mine * half, half), half)]
    gate_sent_ref[...] = gate_grad_ref[:, pl.ds(pl.multiple_of((1 - mine) * half, half), half)]

    def attended_grad(group):
        part = slice(group * rows, (group + 1) * rows)
        product = dot_nt(scaled_ref[...], out_weight_ref[part, :])
        attended_grad_ref[group] = product.astype(BF16)

    def attend_backward(group, head):
        left = head * 3 * width
        query_part = slice(left, left + width)
        key_part = slice(left + width, left + 2 * width)
        value_part = slice(left + 2 * width, left + 3 * width)
        query_gain, key_gain = query_gain_ref[...], key_gain_ref[...]
        query_unit, key_unit = projected_ref[group, :, query_part], projected_ref[group, :, key_part]
        query_inverse = inverse_ref[group, :, 2 * head : 2 * head + 1]
        key_inverse = inverse_ref[group, :, 2 * head + 1 : 2 * head + 2]
        queries = (query_unit * query_gain).astype(BF16)
        keys = (key_unit * key_gain).astype(BF16)
        value = projected_ref[group, :, value_part].astype(BF16)
        grad = attended_grad_ref[group, :, head * width : (head + 1) * width]
        probs = probs_ref[GROUP * group + head]
        probs_wide = probs.astype(F32)
        grad_ref[group, :, value_part] = dot_tn(probs, grad).astype(BF16)
        prob_grad = dot_nt(grad, value)
        row_delta = jnp.sum(probs_wide * prob_grad, axis=-1, keepdims=True)
        scale_factor = 1.0 / math.sqrt(width)
        score_grad = (probs_wide * (prob_grad - row_delta) * scale_factor).astype(BF16)
        query_scaled = dot_nn(score_grad, keys) * query_gain
        key_scaled = dot_tn(score_grad, queries) * key_gain
        query_mean = jnp.mean(query_scaled * query_unit, axis=-1, keepdims=True)
        key_mean = jnp.mean(key_scaled * key_unit, axis=-1, keepdims=True)
        grad_ref[group, :, query_part] = (
            (query_scaled - query_unit * query_mean) * query_inverse
        ).astype(BF16)
        grad_ref[group, :, key_part] = ((key_scaled - key_unit * key_mean) * key_inverse).astype(BF16)

    attended_grad(0)
    for group in range(groups):
        if group + 1 < groups:
            attended_grad(group + 1)
        for head in range(GROUP):
            attend_backward(group, head)
    input_grad(grad_ref, weight_ref, turned_ref, own_ref, kept_ref, sent_ref)


def backward(
    own,
    other,
    out_weight,
    weight,
    turned,
    projected,
    inverse,
    probs,
    attention,
    query_gain,
    key_gain,
    gate,
):
    local, model = own.shape
    groups, tokens, wide = projected.shape
    head_dim = query_gain.shape[1]
    out_weight = pltpu.with_memory_space_constraint(out_weight, pltpu.VMEM)
    weight = pltpu.with_memory_space_constraint(weight, pltpu.VMEM)
    turned = pltpu.with_memory_space_constraint(turned, pltpu.VMEM)
    vmem = pl.BlockSpec(memory_space=pltpu.VMEM)
    return pl.pallas_call(
        backward_kernel,
        out_shape=(
            jax.ShapeDtypeStruct((1, model // 2), F32),
            jax.ShapeDtypeStruct((1, model // 2), F32),
            jax.ShapeDtypeStruct((local, model), BF16),
            jax.ShapeDtypeStruct((local, model), BF16),
        ),
        in_specs=[vmem] * 12,
        out_specs=(vmem,) * 4,
        scratch_shapes=[
            pltpu.VMEM((groups, tokens, wide), BF16),
            pltpu.VMEM((tokens, model), BF16),
            pltpu.VMEM((groups, tokens, GROUP * head_dim), BF16),
            pltpu.VMEM((1, model), F32),
        ],
        compiler_params=params(6),
        cost_estimate=pl.CostEstimate(
            flops=2 * tokens * (out_weight.size + weight.size),
            bytes_accessed=2 * (out_weight.size + weight.size),
            transcendentals=0,
        ),
        name="attention_backward",
    )(
        own,
        other,
        out_weight,
        weight,
        turned,
        projected,
        inverse,
        probs,
        attention,
        query_gain,
        key_gain,
        gate,
    )


def sums_kernel(sent_ref, kept_ref, gate_kept_ref, gate_sent_ref, grad_ref, gate_ref):
    grad_ref[...] = (kept_ref[...].astype(F32) + sent_ref[...].astype(F32)).astype(BF16)
    gate_ref[...] = gate_kept_ref[...] + gate_sent_ref[...]


def sums(sent, kept, gate_kept, gate_sent):
    vmem = pl.BlockSpec(memory_space=pltpu.VMEM)
    return pl.pallas_call(
        sums_kernel,
        out_shape=(
            jax.ShapeDtypeStruct(kept.shape, BF16),
            jax.ShapeDtypeStruct(gate_kept.shape, F32),
        ),
        in_specs=[vmem] * 4,
        out_specs=(vmem, vmem),
        compiler_params=params(8),
        name="sums",
    )(sent, kept, gate_kept, gate_sent)


def routed(block, seq_step, pipe_step):
    seq_size, pipe_size = lax.axis_size("seq"), lax.axis_size("pipe")
    route = []
    for i in range(seq_size):
        for j in range(pipe_size):
            target = (i + seq_step) % seq_size * pipe_size + (j + pipe_step) % pipe_size
            route.append((i * pipe_size + j, target))
    return lax.ppermute(block, ("seq", "pipe"), route)


def pair_body(
    segment_input,
    output_grad,
    qkv_weight,
    out_weight,
    query_gain,
    key_gain,
    gate_scale,
    neighbours,
    tile_slot,
):
    stream = segment_input[0]
    upstream = output_grad[0]
    out_local = out_weight[0]
    other_stream = routed(stream, 1, 0)
    weight, turned_weight = regroup(qkv_weight[0], 128, 4, TURNED)
    other_upstream = routed(upstream, 1, 0)
    projected, inverse, probs, attention, kept, sent, out_local = forward(
        neighbours,
        tile_slot,
        stream,
        other_stream,
        weight,
        out_local,
        query_gain,
        key_gain,
        gate_scale,
    )
    kept = routed(kept, 0, 1)
    sent = routed(sent, 1, 1)
    gate_kept, gate_sent, grad_kept, grad_sent = backward(
        upstream,
        other_upstream,
        out_local,
        weight,
        turned_weight,
        projected,
        inverse,
        probs,
        attention,
        query_gain,
        key_gain,
        gate_scale,
    )
    grad_sent = routed(grad_sent, 1, -1)
    grad_kept = routed(grad_kept, 0, -1)
    segment_output = (kept.astype(F32) + sent.astype(F32)).astype(BF16)
    segment_output, gate_sent = lax.optimization_barrier((segment_output, gate_sent))
    gate_sent = routed(gate_sent, 1, 0)
    token_grad, gate_grad = sums(grad_sent, grad_kept, gate_kept, gate_sent)
    return (segment_output[None], token_grad[None], gate_grad)


def solution(mesh):
    in_specs = (
        P("pipe", ("dp", "seq"), None),
        P("pipe", ("dp", "seq"), None),
        P("pipe", None, "seq", None),
        P("pipe", "seq", None),
        P("pipe", None),
        P("pipe", None),
        P("pipe", None),
        P("dp", None),
        P("dp"),
    )
    out_specs = (
        P("pipe", ("dp", "seq"), None),
        P("pipe", ("dp", "seq"), None),
        P(("dp", "pipe"), "seq"),
    )

    def body(*args):
        one_tile_each = args[0].shape[1] == TILE and args[8].shape[0] == 2
        if mesh.shape["seq"] == 2 and one_tile_each and args[2].shape[2] % GROUP == 0:
            return pair_body(*args)
        return general_body(*args)

    return jax.shard_map(body, mesh=mesh, in_specs=in_specs, out_specs=out_specs, check_vma=False)
```

```python
import functools
import math

import jax
import jax.numpy as jnp
from jax import lax
from jax.experimental import pallas as pl
from jax.experimental.pallas import tpu as pltpu
from jax.sharding import PartitionSpec as P

TILE = 64
EPSILON = 1e-06
F32 = jnp.float32
BF16 = jnp.bfloat16
MIB = 1024 * 1024
GROUP = 4
TURNED = 6


def passed_along(block, axis, distance):
    devices = range(lax.axis_size(axis))
    route = [((i - distance) % len(devices), i) for i in devices]
    return lax.ppermute(block, axis, route)


def slot_lists(neighbours, tile_slot):
    tile_count = tile_slot.shape[0]
    numbering = jnp.arange(tile_count, dtype=jnp.int32)
    placed = (tile_slot[:, None] == numbering[None, :]).astype(jnp.int32)
    tile_of_slot = jnp.sum(placed * numbering[:, None], axis=0)
    chosen = (tile_of_slot[:, None] == numbering[None, :]).astype(jnp.int32)
    listed_tiles = jnp.sum(chosen[:, :, None] * neighbours[None, :, :], axis=1)
    key_valid = listed_tiles >= 0
    safe_tiles = jnp.maximum(listed_tiles, 0)
    matches = (safe_tiles[:, :, None] == numbering[None, None, :]).astype(jnp.int32)
    key_slots = jnp.sum(matches * tile_slot[None, None, :], axis=2)
    return (key_slots, key_valid)


def block_tiles(tile_count):
    return math.gcd(tile_count, max(1, 512 // TILE))


def unit_norm(values):
    spread = jnp.sqrt(jnp.mean(values * values, axis=-1, keepdims=True) + EPSILON)
    return (values / spread, spread)


def probabilities(query_block, key_rows, block_valid):
    scores = jnp.einsum(
        "aihd,ajhd->ahij", query_block, key_rows, preferred_element_type=jnp.float32
    ) * (1.0 / math.sqrt(query_block.shape[-1]))
    key_mask = jnp.repeat(block_valid, TILE, axis=1)
    scores = jnp.where(key_mask[:, None, None, :], scores, -jnp.inf)
    row_max = jnp.max(scores, axis=-1, keepdims=True)
    weights = jnp.exp(scores - row_max)
    return (weights / jnp.sum(weights, axis=-1, keepdims=True)).astype(jnp.bfloat16)


def gathered(tiles_array, block_slots):
    picked = tiles_array[block_slots]
    return picked.reshape(block_slots.shape[0], -1, tiles_array.shape[2], tiles_array.shape[3])


def attend_both(query_tiles, key_tiles, value_tiles, grad_tiles, key_slots, key_valid):
    tile_count = query_tiles.shape[0]
    span = block_tiles(tile_count)
    scale_factor = 1.0 / math.sqrt(query_tiles.shape[-1])
    empty_grad = jnp.zeros(query_tiles.shape, jnp.float32)

    def per_block(accumulators, block_index):
        key_total, value_total = accumulators
        first_tile = block_index * span
        query_block = lax.dynamic_slice_in_dim(query_tiles, first_tile, span, 0)
        grad_block = lax.dynamic_slice_in_dim(grad_tiles, first_tile, span, 0)
        block_slots = lax.dynamic_slice_in_dim(key_slots, first_tile, span, 0)
        block_valid = lax.dynamic_slice_in_dim(key_valid, first_tile, span, 0)
        key_rows = gathered(key_tiles, block_slots)
        value_rows = gathered(value_tiles, block_slots)
        weights = probabilities(query_block, key_rows, block_valid)
        attended = jnp.einsum(
            "ahij,ajhd->aihd", weights, value_rows, preferred_element_type=jnp.float32
        )
        value_part = jnp.einsum(
            "ahij,aihd->ajhd", weights, grad_block, preferred_element_type=jnp.float32
        )
        prob_grad = jnp.einsum(
            "aihd,ajhd->ahij", grad_block, value_rows, preferred_element_type=jnp.float32
        )
        weights_wide = weights.astype(jnp.float32)
        row_delta = jnp.sum(weights_wide * prob_grad, axis=-1, keepdims=True)
        score_grad = (weights_wide * (prob_grad - row_delta) * scale_factor).astype(jnp.bfloat16)
        query_part = jnp.einsum(
            "ahij,ajhd->aihd", score_grad, key_rows, preferred_element_type=jnp.float32
        )
        key_part = jnp.einsum(
            "ahij,aihd->ajhd", score_grad, query_block, preferred_element_type=jnp.float32
        )
        block_shape = (span, block_slots.shape[1]) + query_tiles.shape[1:]
        key_total = key_total.at[block_slots].add(key_part.reshape(block_shape))
        value_total = value_total.at[block_slots].add(value_part.reshape(block_shape))
        return ((key_total, value_total), (attended, query_part))

    totals, parts = lax.scan(
        per_block, (empty_grad, empty_grad), jnp.arange(tile_count // span, dtype=jnp.int32)
    )
    flat_shape = (-1,) + query_tiles.shape[2:]
    return (
        parts[0].reshape(flat_shape),
        parts[1].reshape(flat_shape),
        totals[0].reshape(flat_shape),
        totals[1].reshape(flat_shape),
    )


def general_body(
    segment_input,
    output_grad,
    qkv_weight,
    out_weight,
    query_gain,
    key_gain,
    gate_scale,
    neighbours,
    tile_slot,
):
    key_slots, key_valid = slot_lists(neighbours, tile_slot)
    stream = segment_input[0]
    upstream = output_grad[0]
    model_width = stream.shape[1]
    head_dim = query_gain.shape[1]
    local_heads = qkv_weight.shape[2]
    local_width = local_heads * head_dim
    proj_weight = qkv_weight[0].reshape(model_width, local_heads * 3 * head_dim)
    out_local = out_weight[0]
    gate_row = gate_scale[0]
    query_weights = query_gain[0]
    key_weights = key_gain[0]
    projected = jnp.dot(
        lax.all_gather(stream, "seq", axis=0, tiled=True),
        proj_weight,
        preferred_element_type=jnp.float32,
    )
    all_tokens = projected.shape[0]
    projected = projected.reshape(all_tokens, local_heads, 3, head_dim)
    query_unit, query_spread = unit_norm(projected[:, :, 0])
    key_unit, key_spread = unit_norm(projected[:, :, 1])
    queries = (query_unit * query_weights).astype(jnp.bfloat16)
    keys_normed = (key_unit * key_weights).astype(jnp.bfloat16)
    value_rows = projected[:, :, 2].astype(jnp.bfloat16)
    scaled = (upstream.astype(jnp.float32) * gate_row).astype(jnp.bfloat16)
    attended_grad = jnp.einsum(
        "td,cd->tc",
        lax.all_gather(scaled, "seq", axis=0, tiled=True),
        out_local,
        preferred_element_type=jnp.float32,
    ).astype(jnp.bfloat16)

    def as_tiles(values):
        return values.reshape(-1, TILE, local_heads, head_dim)

    attended, query_grad, key_grad, value_grad = attend_both(
        as_tiles(queries),
        as_tiles(keys_normed),
        as_tiles(value_rows),
        as_tiles(attended_grad),
        key_slots,
        key_valid,
    )
    attended_low = attended.astype(jnp.bfloat16).reshape(all_tokens, local_width)
    rows = attended_low
    attention_out = lax.psum_scatter(
        jnp.dot(rows, out_local, preferred_element_type=jnp.float32),
        "seq",
        scatter_dimension=0,
        tiled=True,
    )
    section_out = (stream.astype(jnp.float32) + gate_row * attention_out).astype(jnp.bfloat16)
    segment_output = passed_along(section_out, "pipe", 1)
    gate_local = lax.psum_scatter(
        jnp.sum(upstream.astype(jnp.float32) * attention_out, axis=0),
        "seq",
        scatter_dimension=0,
        tiled=True,
    )
    query_scaled = query_grad * query_weights
    query_part_grad = (
        query_scaled - query_unit * jnp.mean(query_scaled * query_unit, axis=-1, keepdims=True)
    ) / query_spread
    key_scaled = key_grad * key_weights
    key_part_grad = (
        key_scaled - key_unit * jnp.mean(key_scaled * key_unit, axis=-1, keepdims=True)
    ) / key_spread
    projected_grad = (
        jnp.stack([query_part_grad, key_part_grad, value_grad], axis=2)
        .astype(jnp.bfloat16)
        .reshape(all_tokens, local_heads * 3 * head_dim)
    )
    rows = projected_grad
    stream_grad = lax.psum_scatter(
        jnp.einsum("tc,dc->td", rows, proj_weight, preferred_element_type=jnp.float32).astype(
            jnp.bfloat16
        ),
        "seq",
        scatter_dimension=0,
        tiled=True,
    ).astype(jnp.float32)
    token_grad = (upstream.astype(jnp.float32) + stream_grad).astype(jnp.bfloat16)
    input_grad = passed_along(token_grad, "pipe", -1)
    return (segment_output[None], input_grad[None], gate_local[None])


def dot_nn(a, b):
    return lax.dot_general(a, b, (((1,), (0,)), ((), ())), preferred_element_type=F32)


def dot_nt(a, b):
    return lax.dot_general(a, b, (((1,), (1,)), ((), ())), preferred_element_type=F32)


def dot_tn(a, b):
    return lax.dot_general(a, b, (((0,), (0,)), ((), ())), preferred_element_type=F32)


def params(mebibytes):
    return pltpu.CompilerParams(vmem_limit_bytes=mebibytes * MIB)


class Copies:
    def __init__(self, pairs, semaphores, ahead):
        self.copies = [
            pltpu.make_async_copy(source, target, semaphores.at[i])
            for i, (source, target) in enumerate(pairs)
        ]
        self.ahead = ahead
        self.waited = 0
        for copy in self.copies[:ahead]:
            copy.start()

    def wait(self, count=1):
        for _ in range(count):
            self.copies[self.waited].wait()
            following = self.waited + self.ahead
            if following < len(self.copies):
                self.copies[following].start()
            self.waited += 1


def regroup_kernel(weight_ref, out_ref, turned_ref, read_ref, reads):
    depth, heads, width = weight_ref.shape
    slots, rows = read_ref.shape[:2]
    steps = depth // rows

    def part(step):
        return pl.ds(pl.multiple_of(step * rows, rows), rows)

    def read(step, slot):
        return pltpu.make_async_copy(
            weight_ref.at[part(step)], read_ref.at[slot], reads.at[slot]
        )

    for slot in range(slots):
        read(slot, slot).start()

    @pl.loop(0, steps)
    def _(step):
        slot = lax.rem(step, slots)
        read(step, slot).wait()
        by_head = jnp.swapaxes(read_ref[slot], 0, 1)
        for head in range(heads):
            left = (head % GROUP) * width
            out_ref[head // GROUP, part(step), left : left + width] = by_head[head]
            above = (head + 1) * width - (heads * width - turned_ref.shape[0])
            if above > 0:
                turned_ref[above - width : above, part(step)] = by_head[head].T

        @pl.when(step + slots < steps)
        def _():
            read(step + slots, slot).start()


def regroup(weight, rows, slots, turned):
    depth, heads, width = weight.shape
    out = (heads // GROUP, depth, GROUP * width)
    return pl.pallas_call(
        regroup_kernel,
        out_shape=(
            pltpu.VMEM(out, weight.dtype),
            pltpu.VMEM((turned * width, depth), weight.dtype),
        ),
        in_specs=[pl.BlockSpec(memory_space=pl.ANY)],
        out_specs=(pl.BlockSpec(memory_space=pltpu.VMEM),) * 2,
        scratch_shapes=[
            pltpu.VMEM((slots, rows, heads, width), weight.dtype),
            pltpu.SemaphoreType.DMA((slots,)),
        ],
        compiler_params=params(6),
        cost_estimate=pl.CostEstimate(
            flops=0, bytes_accessed=4 * depth * heads * width, transcendentals=0
        ),
        name="regroup",
    )(pltpu.with_memory_space_constraint(weight, pltpu.HBM))


def listed_slots(neighbours_ref, tile_slot_ref):
    tiles, places = neighbours_ref.shape
    one, zero = jnp.int32(1), jnp.int32(0)
    allowed = [[zero] * tiles for _ in range(tiles)]
    for t in range(tiles):
        for u in range(tiles):
            listed = zero
            for k in range(places):
                listed = jnp.where(neighbours_ref[t, k] == u, one, listed)
            for r in range(tiles):
                for c in range(tiles):
                    here = (tile_slot_ref[t] == r) & (tile_slot_ref[u] == c)
                    allowed[r][c] = jnp.where(here, listed, allowed[r][c])
    return allowed


def normed(rows, gain):
    inverse = lax.rsqrt(jnp.mean(rows * rows, axis=-1, keepdims=True) + EPSILON)
    unit = rows * inverse
    return unit, inverse, (unit * gain).astype(BF16)


def forward_kernel(
    neighbours_ref,
    tile_slot_ref,
    own_ref,
    other_ref,
    weight_ref,
    out_weight_ref,
    query_gain_ref,
    key_gain_ref,
    gate_ref,
    projected_ref,
    inverse_ref,
    probs_ref,
    attention_ref,
    kept_ref,
    sent_ref,
    out_weight_buffer,
    tokens_ref,
    semaphores,
):
    local, model = own_ref.shape
    tokens = 2 * local
    width = query_gain_ref.shape[1]
    groups = weight_ref.shape[0]
    rows = GROUP * width

    def out_weight_part(group):
        place = pl.ds(group * rows, rows)
        return out_weight_ref.at[place], out_weight_buffer.at[place]

    copies = Copies([out_weight_part(group) for group in range(groups)], semaphores, groups)

    tokens_ref[:local, :] = own_ref[...]
    tokens_ref[local:, :] = other_ref[...]
    allowed = listed_slots(neighbours_ref, tile_slot_ref)
    mine = lax.axis_index("seq")
    row_half = lax.broadcasted_iota(jnp.int32, (tokens, tokens), 0) // local
    column_half = lax.broadcasted_iota(jnp.int32, (tokens, tokens), 1) // local
    row_slot = jnp.where(row_half == 0, mine, 1 - mine)
    column_slot = jnp.where(column_half == 0, mine, 1 - mine)
    table = jnp.zeros((tokens, tokens), jnp.int32)
    for r in range(2):
        for c in range(2):
            table = jnp.where((row_slot == r) & (column_slot == c), allowed[r][c], table)
    bias = jnp.where(table > 0, 0.0, -jnp.inf).astype(F32)

    def project(group):
        projected_ref[group] = dot_nn(tokens_ref[...], weight_ref[group])

    def attend(group):
        heads = range(GROUP)
        operands = []
        for place in range(2 * GROUP):
            gain_ref = (query_gain_ref, key_gain_ref)[place % 2]
            left = (3 * (place // 2) + place % 2) * width
            part = slice(left, left + width)
            unit, inverse, operand = normed(projected_ref[group, :, part], gain_ref[...])
            projected_ref[group, :, part] = unit
            inverse_ref[group, :, place : place + 1] = inverse
            operands.append(operand)
        scale_factor = 1.0 / math.sqrt(width)
        scores = [dot_nt(operands[2 * h], operands[2 * h + 1]) * scale_factor + bias for h in heads]
        tops = [jnp.max(scores[h], axis=-1, keepdims=True) for h in heads]
        weights = [jnp.exp(scores[h] - tops[h]) for h in heads]
        sums = [jnp.sum(weights[h], axis=-1, keepdims=True) for h in heads]
        probs = [(weights[h] / sums[h]).astype(BF16) for h in heads]
        attended = []
        for h in heads:
            probs_ref[GROUP * group + h] = probs[h]
            left = (3 * h + 2) * width
            value = projected_ref[group, :, left : left + width].astype(BF16)
            attended.append(dot_nn(probs[h], value).astype(BF16))
        return jnp.concatenate(attended, axis=1)

    def share(group, attended):
        return dot_nn(attended, out_weight_buffer[group * rows : (group + 1) * rows, :])

    project(0)
    attended = attend(0)
    for group in range(1, groups):
        project(group)
        copies.wait()
        following = attend(group)
        if group == 1:
            attention_ref[...] = share(0, attended)
        else:
            attention_ref[...] += share(group - 1, attended)
        attended = following
    copies.wait()
    total = share(groups - 1, attended)
    if groups > 1:
        total += attention_ref[...]
    attention_ref[...] = total
    gate = gate_ref[...]
    kept_ref[...] = (own_ref[...].astype(F32) + gate * total[:local]).astype(BF16)
    sent_ref[...] = (gate * total[local:]).astype(BF16)


def forward(neighbours, tile_slot, own, other, weight, out_weight, query_gain, key_gain, gate):
    local, model = own.shape
    groups, _, wide = weight.shape
    tokens = 2 * local
    weight = pltpu.with_memory_space_constraint(weight, pltpu.VMEM)
    out_weight = pltpu.with_memory_space_constraint(out_weight, pltpu.HBM)
    smem = pl.BlockSpec(memory_space=pltpu.SMEM)
    vmem = pl.BlockSpec(memory_space=pltpu.VMEM)
    hbm = pl.BlockSpec(memory_space=pl.ANY)
    return pl.pallas_call(
        forward_kernel,
        out_shape=(
            jax.ShapeDtypeStruct((groups, tokens, wide), F32),
            jax.ShapeDtypeStruct((groups, tokens, 2 * GROUP), F32),
            jax.ShapeDtypeStruct((GROUP * groups, tokens, tokens), BF16),
            jax.ShapeDtypeStruct((tokens, model), F32),
            jax.ShapeDtypeStruct((local, model), BF16),
            jax.ShapeDtypeStruct((local, model), BF16),
            pltpu.VMEM(out_weight.shape, BF16),
        ),
        in_specs=[smem, smem, vmem, vmem, vmem, hbm, vmem, vmem, vmem],
        out_specs=(vmem,) * 7,
        scratch_shapes=[
            pltpu.VMEM((tokens, model), BF16),
            pltpu.SemaphoreType.DMA((groups,)),
        ],
        compiler_params=params(6),
        cost_estimate=pl.CostEstimate(
            flops=2 * tokens * (weight.size + out_weight.size),
            bytes_accessed=2 * (weight.size + out_weight.size),
            transcendentals=0,
        ),
        name="attention_forward",
    )(neighbours, tile_slot, own, other, weight, out_weight, query_gain, key_gain, gate)


def input_grad(grad_ref, weight_ref, turned_ref, own_ref, kept_ref, sent_ref):
    local, model = own_ref.shape
    groups, _, wide = grad_ref.shape
    streamed = groups * wide - turned_ref.shape[0]
    block = 512
    for start in range(0, model, block):
        part = slice(start, start + block)
        total = None
        for group in range(groups):
            first = group * wide
            cut = min(max(streamed - first, 0), wide)
            if cut < wide:
                rows = slice(first + cut - streamed, first + wide - streamed)
                product = dot_nn(grad_ref[group, :, cut:], turned_ref[rows, part])
                total = product if total is None else total + product
            if cut > 0:
                product = dot_nt(weight_ref[group, part, :cut], grad_ref[group, :, :cut]).T
                total = product if total is None else total + product
        kept_ref[:, part] = (own_ref[:, part].astype(F32) + total[:local]).astype(BF16)
        sent_ref[:, part] = total[local:].astype(BF16)


def backward_kernel(
    own_ref,
    other_ref,
    out_weight_ref,
    weight_ref,
    turned_ref,
    projected_ref,
    inverse_ref,
    probs_ref,
    attention_ref,
    query_gain_ref,
    key_gain_ref,
    gate_ref,
    gate_kept_ref,
    gate_sent_ref,
    kept_ref,
    sent_ref,
    grad_ref,
    scaled_ref,
    attended_grad_ref,
    gate_grad_ref,
):
    local = own_ref.shape[0]
    width = query_gain_ref.shape[1]
    groups = grad_ref.shape[0]
    rows = GROUP * width

    gate = gate_ref[...]
    own, other = own_ref[...].astype(F32), other_ref[...].astype(F32)
    scaled_ref[:local, :] = (own * gate).astype(BF16)
    scaled_ref[local:, :] = (other * gate).astype(BF16)
    gate_grad_ref[...] = jnp.sum(
        own * attention_ref[:local, :] + other * attention_ref[local:, :], axis=0, keepdims=True
    )
    half = gate_kept_ref.shape[1]
    mine = lax.axis_index("seq")
    gate_kept_ref[...] = gate_grad_ref[:, pl.ds(pl.multiple_of(mine * half, half), half)]
    gate_sent_ref[...] = gate_grad_ref[:, pl.ds(pl.multiple_of((1 - mine) * half, half), half)]

    def attended_grad(group):
        part = slice(group * rows, (group + 1) * rows)
        product = dot_nt(scaled_ref[...], out_weight_ref[part, :])
        attended_grad_ref[group] = product.astype(BF16)

    def attend_backward(group):
        heads = range(GROUP)
        query_gain, key_gain = query_gain_ref[...], key_gain_ref[...]
        scale_factor = 1.0 / math.sqrt(width)

        def part(head, index):
            left = (3 * head + index) * width
            return slice(left, left + width)

        def inverse(head, index):
            return inverse_ref[group, :, 2 * head + index : 2 * head + index + 1]

        grads = [attended_grad_ref[group, :, h * width : (h + 1) * width] for h in heads]
        values = [projected_ref[group, :, part(h, 2)].astype(BF16) for h in heads]
        prob_grads = [dot_nt(grads[h], values[h]) for h in heads]
        for h in heads:
            product = dot_tn(probs_ref[GROUP * group + h], grads[h])
            grad_ref[group, :, part(h, 2)] = product.astype(BF16)
        wide = [probs_ref[GROUP * group + h].astype(F32) for h in heads]
        deltas = [jnp.sum(wide[h] * prob_grads[h], axis=-1, keepdims=True) for h in heads]
        score_grads = [
            (wide[h] * (prob_grads[h] - deltas[h]) * scale_factor).astype(BF16) for h in heads
        ]
        units = [[projected_ref[group, :, part(h, index)] for index in range(2)] for h in heads]
        keys = [(units[h][1] * key_gain).astype(BF16) for h in heads]
        queries = [(units[h][0] * query_gain).astype(BF16) for h in heads]
        scaled = [
            [
                dot_nn(score_grads[h], keys[h]) * query_gain,
                dot_tn(score_grads[h], queries[h]) * key_gain,
            ]
            for h in heads
        ]
        means = [
            [jnp.mean(scaled[h][i] * units[h][i], axis=-1, keepdims=True) for i in range(2)]
            for h in heads
        ]
        for h in heads:
            for i in range(2):
                grad_ref[group, :, part(h, i)] = (
                    (scaled[h][i] - units[h][i] * means[h][i]) * inverse(h, i)
                ).astype(BF16)

    attended_grad(0)
    for group in range(groups):
        if group + 1 < groups:
            attended_grad(group + 1)
        attend_backward(group)
    input_grad(grad_ref, weight_ref, turned_ref, own_ref, kept_ref, sent_ref)


def backward(
    own,
    other,
    out_weight,
    weight,
    turned,
    projected,
    inverse,
    probs,
    attention,
    query_gain,
    key_gain,
    gate,
):
    local, model = own.shape
    groups, tokens, wide = projected.shape
    head_dim = query_gain.shape[1]
    out_weight = pltpu.with_memory_space_constraint(out_weight, pltpu.VMEM)
    weight = pltpu.with_memory_space_constraint(weight, pltpu.VMEM)
    turned = pltpu.with_memory_space_constraint(turned, pltpu.VMEM)
    vmem = pl.BlockSpec(memory_space=pltpu.VMEM)
    return pl.pallas_call(
        backward_kernel,
        out_shape=(
            jax.ShapeDtypeStruct((1, model // 2), F32),
            jax.ShapeDtypeStruct((1, model // 2), F32),
            jax.ShapeDtypeStruct((local, model), BF16),
            jax.ShapeDtypeStruct((local, model), BF16),
        ),
        in_specs=[vmem] * 12,
        out_specs=(vmem,) * 4,
        scratch_shapes=[
            pltpu.VMEM((groups, tokens, wide), BF16),
            pltpu.VMEM((tokens, model), BF16),
            pltpu.VMEM((groups, tokens, GROUP * head_dim), BF16),
            pltpu.VMEM((1, model), F32),
        ],
        compiler_params=params(6),
        cost_estimate=pl.CostEstimate(
            flops=2 * tokens * (out_weight.size + weight.size),
            bytes_accessed=2 * (out_weight.size + weight.size),
            transcendentals=0,
        ),
        name="attention_backward",
    )(
        own,
        other,
        out_weight,
        weight,
        turned,
        projected,
        inverse,
        probs,
        attention,
        query_gain,
        key_gain,
        gate,
    )


def sums_kernel(sent_ref, kept_ref, gate_kept_ref, gate_sent_ref, grad_ref, gate_ref):
    grad_ref[...] = (kept_ref[...].astype(F32) + sent_ref[...].astype(F32)).astype(BF16)
    gate_ref[...] = gate_kept_ref[...] + gate_sent_ref[...]


def sums(sent, kept, gate_kept, gate_sent):
    vmem = pl.BlockSpec(memory_space=pltpu.VMEM)
    return pl.pallas_call(
        sums_kernel,
        out_shape=(
            jax.ShapeDtypeStruct(kept.shape, BF16),
            jax.ShapeDtypeStruct(gate_kept.shape, F32),
        ),
        in_specs=[vmem] * 4,
        out_specs=(vmem, vmem),
        compiler_params=params(8),
        name="sums",
    )(sent, kept, gate_kept, gate_sent)


def routed(block, seq_step, pipe_step):
    seq_size, pipe_size = lax.axis_size("seq"), lax.axis_size("pipe")
    route = []
    for i in range(seq_size):
        for j in range(pipe_size):
            target = (i + seq_step) % seq_size * pipe_size + (j + pipe_step) % pipe_size
            route.append((i * pipe_size + j, target))
    return lax.ppermute(block, ("seq", "pipe"), route)


def pair_body(
    segment_input,
    output_grad,
    qkv_weight,
    out_weight,
    query_gain,
    key_gain,
    gate_scale,
    neighbours,
    tile_slot,
):
    stream = segment_input[0]
    upstream = output_grad[0]
    out_local = out_weight[0]
    other_stream = routed(stream, 1, 0)
    weight, turned_weight = regroup(qkv_weight[0], 128, 4, TURNED)
    other_upstream = routed(upstream, 1, 0)
    projected, inverse, probs, attention, kept, sent, out_local = forward(
        neighbours,
        tile_slot,
        stream,
        other_stream,
        weight,
        out_local,
        query_gain,
        key_gain,
        gate_scale,
    )
    kept = routed(kept, 0, 1)
    sent = routed(sent, 1, 1)
    gate_kept, gate_sent, grad_kept, grad_sent = backward(
        upstream,
        other_upstream,
        out_local,
        weight,
        turned_weight,
        projected,
        inverse,
        probs,
        attention,
        query_gain,
        key_gain,
        gate_scale,
    )
    grad_sent = routed(grad_sent, 1, -1)
    grad_kept = routed(grad_kept, 0, -1)
    segment_output = (kept.astype(F32) + sent.astype(F32)).astype(BF16)
    segment_output, gate_sent = lax.optimization_barrier((segment_output, gate_sent))
    gate_sent = routed(gate_sent, 1, 0)
    token_grad, gate_grad = sums(grad_sent, grad_kept, gate_kept, gate_sent)
    return (segment_output[None], token_grad[None], gate_grad)


def solution(mesh):
    in_specs = (
        P("pipe", ("dp", "seq"), None),
        P("pipe", ("dp", "seq"), None),
        P("pipe", None, "seq", None),
        P("pipe", "seq", None),
        P("pipe", None),
        P("pipe", None),
        P("pipe", None),
        P("dp", None),
        P("dp"),
    )
    out_specs = (
        P("pipe", ("dp", "seq"), None),
        P("pipe", ("dp", "seq"), None),
        P(("dp", "pipe"), "seq"),
    )

    def body(*args):
        one_tile_each = args[0].shape[1] == TILE and args[8].shape[0] == 2
        if mesh.shape["seq"] == 2 and one_tile_each and args[2].shape[2] % GROUP == 0:
            return pair_body(*args)
        return general_body(*args)

    return jax.shard_map(body, mesh=mesh, in_specs=in_specs, out_specs=out_specs, check_vma=False)
```

```python
import functools
import math

import jax
import jax.numpy as jnp
from jax import lax
from jax.experimental import pallas as pl
from jax.experimental.pallas import tpu as pltpu
from jax.sharding import PartitionSpec as P

TILE = 64
EPSILON = 1e-06
F32 = jnp.float32
BF16 = jnp.bfloat16
MIB = 1024 * 1024
GROUP = 4
TURNED = 6


def passed_along(block, axis, distance):
    devices = range(lax.axis_size(axis))
    route = [((i - distance) % len(devices), i) for i in devices]
    return lax.ppermute(block, axis, route)


def slot_lists(neighbours, tile_slot):
    tile_count = tile_slot.shape[0]
    numbering = jnp.arange(tile_count, dtype=jnp.int32)
    placed = (tile_slot[:, None] == numbering[None, :]).astype(jnp.int32)
    tile_of_slot = jnp.sum(placed * numbering[:, None], axis=0)
    chosen = (tile_of_slot[:, None] == numbering[None, :]).astype(jnp.int32)
    listed_tiles = jnp.sum(chosen[:, :, None] * neighbours[None, :, :], axis=1)
    key_valid = listed_tiles >= 0
    safe_tiles = jnp.maximum(listed_tiles, 0)
    matches = (safe_tiles[:, :, None] == numbering[None, None, :]).astype(jnp.int32)
    key_slots = jnp.sum(matches * tile_slot[None, None, :], axis=2)
    return (key_slots, key_valid)


def block_tiles(tile_count):
    return math.gcd(tile_count, max(1, 512 // TILE))


def unit_norm(values):
    spread = jnp.sqrt(jnp.mean(values * values, axis=-1, keepdims=True) + EPSILON)
    return (values / spread, spread)


def probabilities(query_block, key_rows, block_valid):
    scores = jnp.einsum(
        "aihd,ajhd->ahij", query_block, key_rows, preferred_element_type=jnp.float32
    ) * (1.0 / math.sqrt(query_block.shape[-1]))
    key_mask = jnp.repeat(block_valid, TILE, axis=1)
    scores = jnp.where(key_mask[:, None, None, :], scores, -jnp.inf)
    row_max = jnp.max(scores, axis=-1, keepdims=True)
    weights = jnp.exp(scores - row_max)
    return (weights / jnp.sum(weights, axis=-1, keepdims=True)).astype(jnp.bfloat16)


def gathered(tiles_array, block_slots):
    picked = tiles_array[block_slots]
    return picked.reshape(block_slots.shape[0], -1, tiles_array.shape[2], tiles_array.shape[3])


def attend_both(query_tiles, key_tiles, value_tiles, grad_tiles, key_slots, key_valid):
    tile_count = query_tiles.shape[0]
    span = block_tiles(tile_count)
    scale_factor = 1.0 / math.sqrt(query_tiles.shape[-1])
    empty_grad = jnp.zeros(query_tiles.shape, jnp.float32)

    def per_block(accumulators, block_index):
        key_total, value_total = accumulators
        first_tile = block_index * span
        query_block = lax.dynamic_slice_in_dim(query_tiles, first_tile, span, 0)
        grad_block = lax.dynamic_slice_in_dim(grad_tiles, first_tile, span, 0)
        block_slots = lax.dynamic_slice_in_dim(key_slots, first_tile, span, 0)
        block_valid = lax.dynamic_slice_in_dim(key_valid, first_tile, span, 0)
        key_rows = gathered(key_tiles, block_slots)
        value_rows = gathered(value_tiles, block_slots)
        weights = probabilities(query_block, key_rows, block_valid)
        attended = jnp.einsum(
            "ahij,ajhd->aihd", weights, value_rows, preferred_element_type=jnp.float32
        )
        value_part = jnp.einsum(
            "ahij,aihd->ajhd", weights, grad_block, preferred_element_type=jnp.float32
        )
        prob_grad = jnp.einsum(
            "aihd,ajhd->ahij", grad_block, value_rows, preferred_element_type=jnp.float32
        )
        weights_wide = weights.astype(jnp.float32)
        row_delta = jnp.sum(weights_wide * prob_grad, axis=-1, keepdims=True)
        score_grad = (weights_wide * (prob_grad - row_delta) * scale_factor).astype(jnp.bfloat16)
        query_part = jnp.einsum(
            "ahij,ajhd->aihd", score_grad, key_rows, preferred_element_type=jnp.float32
        )
        key_part = jnp.einsum(
            "ahij,aihd->ajhd", score_grad, query_block, preferred_element_type=jnp.float32
        )
        block_shape = (span, block_slots.shape[1]) + query_tiles.shape[1:]
        key_total = key_total.at[block_slots].add(key_part.reshape(block_shape))
        value_total = value_total.at[block_slots].add(value_part.reshape(block_shape))
        return ((key_total, value_total), (attended, query_part))

    totals, parts = lax.scan(
        per_block, (empty_grad, empty_grad), jnp.arange(tile_count // span, dtype=jnp.int32)
    )
    flat_shape = (-1,) + query_tiles.shape[2:]
    return (
        parts[0].reshape(flat_shape),
        parts[1].reshape(flat_shape),
        totals[0].reshape(flat_shape),
        totals[1].reshape(flat_shape),
    )


def general_body(
    segment_input,
    output_grad,
    qkv_weight,
    out_weight,
    query_gain,
    key_gain,
    gate_scale,
    neighbours,
    tile_slot,
):
    key_slots, key_valid = slot_lists(neighbours, tile_slot)
    stream = segment_input[0]
    upstream = output_grad[0]
    model_width = stream.shape[1]
    head_dim = query_gain.shape[1]
    local_heads = qkv_weight.shape[2]
    local_width = local_heads * head_dim
    proj_weight = qkv_weight[0].reshape(model_width, local_heads * 3 * head_dim)
    out_local = out_weight[0]
    gate_row = gate_scale[0]
    query_weights = query_gain[0]
    key_weights = key_gain[0]
    projected = jnp.dot(
        lax.all_gather(stream, "seq", axis=0, tiled=True),
        proj_weight,
        preferred_element_type=jnp.float32,
    )
    all_tokens = projected.shape[0]
    projected = projected.reshape(all_tokens, local_heads, 3, head_dim)
    query_unit, query_spread = unit_norm(projected[:, :, 0])
    key_unit, key_spread = unit_norm(projected[:, :, 1])
    queries = (query_unit * query_weights).astype(jnp.bfloat16)
    keys_normed = (key_unit * key_weights).astype(jnp.bfloat16)
    value_rows = projected[:, :, 2].astype(jnp.bfloat16)
    scaled = (upstream.astype(jnp.float32) * gate_row).astype(jnp.bfloat16)
    attended_grad = jnp.einsum(
        "td,cd->tc",
        lax.all_gather(scaled, "seq", axis=0, tiled=True),
        out_local,
        preferred_element_type=jnp.float32,
    ).astype(jnp.bfloat16)

    def as_tiles(values):
        return values.reshape(-1, TILE, local_heads, head_dim)

    attended, query_grad, key_grad, value_grad = attend_both(
        as_tiles(queries),
        as_tiles(keys_normed),
        as_tiles(value_rows),
        as_tiles(attended_grad),
        key_slots,
        key_valid,
    )
    attended_low = attended.astype(jnp.bfloat16).reshape(all_tokens, local_width)
    rows = attended_low
    attention_out = lax.psum_scatter(
        jnp.dot(rows, out_local, preferred_element_type=jnp.float32),
        "seq",
        scatter_dimension=0,
        tiled=True,
    )
    section_out = (stream.astype(jnp.float32) + gate_row * attention_out).astype(jnp.bfloat16)
    segment_output = passed_along(section_out, "pipe", 1)
    gate_local = lax.psum_scatter(
        jnp.sum(upstream.astype(jnp.float32) * attention_out, axis=0),
        "seq",
        scatter_dimension=0,
        tiled=True,
    )
    query_scaled = query_grad * query_weights
    query_part_grad = (
        query_scaled - query_unit * jnp.mean(query_scaled * query_unit, axis=-1, keepdims=True)
    ) / query_spread
    key_scaled = key_grad * key_weights
    key_part_grad = (
        key_scaled - key_unit * jnp.mean(key_scaled * key_unit, axis=-1, keepdims=True)
    ) / key_spread
    projected_grad = (
        jnp.stack([query_part_grad, key_part_grad, value_grad], axis=2)
        .astype(jnp.bfloat16)
        .reshape(all_tokens, local_heads * 3 * head_dim)
    )
    rows = projected_grad
    stream_grad = lax.psum_scatter(
        jnp.einsum("tc,dc->td", rows, proj_weight, preferred_element_type=jnp.float32).astype(
            jnp.bfloat16
        ),
        "seq",
        scatter_dimension=0,
        tiled=True,
    ).astype(jnp.float32)
    token_grad = (upstream.astype(jnp.float32) + stream_grad).astype(jnp.bfloat16)
    input_grad = passed_along(token_grad, "pipe", -1)
    return (segment_output[None], input_grad[None], gate_local[None])


def dot_nn(a, b):
    return lax.dot_general(a, b, (((1,), (0,)), ((), ())), preferred_element_type=F32)


def dot_nt(a, b):
    return lax.dot_general(a, b, (((1,), (1,)), ((), ())), preferred_element_type=F32)


def dot_tn(a, b):
    return lax.dot_general(a, b, (((0,), (0,)), ((), ())), preferred_element_type=F32)


def params(mebibytes):
    return pltpu.CompilerParams(vmem_limit_bytes=mebibytes * MIB)


class Copies:
    def __init__(self, pairs, semaphores, ahead):
        self.copies = [
            pltpu.make_async_copy(source, target, semaphores.at[i])
            for i, (source, target) in enumerate(pairs)
        ]
        self.ahead = ahead
        self.waited = 0
        for copy in self.copies[:ahead]:
            copy.start()

    def wait(self, count=1):
        for _ in range(count):
            self.copies[self.waited].wait()
            following = self.waited + self.ahead
            if following < len(self.copies):
                self.copies[following].start()
            self.waited += 1


def regroup_kernel(weight_ref, out_ref, turned_ref, read_ref, reads):
    depth, heads, width = weight_ref.shape
    slots, rows = read_ref.shape[:2]
    steps = depth // rows

    def part(step):
        return pl.ds(pl.multiple_of(step * rows, rows), rows)

    def read(step, slot):
        return pltpu.make_async_copy(
            weight_ref.at[part(step)], read_ref.at[slot], reads.at[slot]
        )

    for slot in range(slots):
        read(slot, slot).start()

    @pl.loop(0, steps)
    def _(step):
        slot = lax.rem(step, slots)
        read(step, slot).wait()
        by_head = jnp.swapaxes(read_ref[slot], 0, 1)
        for head in range(heads):
            left = (head % GROUP) * width
            out_ref[head // GROUP, part(step), left : left + width] = by_head[head]
            above = (head + 1) * width - (heads * width - turned_ref.shape[0])
            if above > 0:
                turned_ref[above - width : above, part(step)] = by_head[head].T

        @pl.when(step + slots < steps)
        def _():
            read(step + slots, slot).start()


def regroup(weight, rows, slots, turned):
    depth, heads, width = weight.shape
    out = (heads // GROUP, depth, GROUP * width)
    return pl.pallas_call(
        regroup_kernel,
        out_shape=(
            pltpu.VMEM(out, weight.dtype),
            pltpu.VMEM((turned * width, depth), weight.dtype),
        ),
        in_specs=[pl.BlockSpec(memory_space=pl.ANY)],
        out_specs=(pl.BlockSpec(memory_space=pltpu.VMEM),) * 2,
        scratch_shapes=[
            pltpu.VMEM((slots, rows, heads, width), weight.dtype),
            pltpu.SemaphoreType.DMA((slots,)),
        ],
        compiler_params=params(6),
        cost_estimate=pl.CostEstimate(
            flops=0, bytes_accessed=4 * depth * heads * width, transcendentals=0
        ),
        name="regroup",
    )(pltpu.with_memory_space_constraint(weight, pltpu.HBM))


def listed_slots(neighbours_ref, tile_slot_ref):
    tiles, places = neighbours_ref.shape
    one, zero = jnp.int32(1), jnp.int32(0)
    allowed = [[zero] * tiles for _ in range(tiles)]
    for t in range(tiles):
        for u in range(tiles):
            listed = zero
            for k in range(places):
                listed = jnp.where(neighbours_ref[t, k] == u, one, listed)
            for r in range(tiles):
                for c in range(tiles):
                    here = (tile_slot_ref[t] == r) & (tile_slot_ref[u] == c)
                    allowed[r][c] = jnp.where(here, listed, allowed[r][c])
    return allowed


def normed(rows, gain):
    inverse = lax.rsqrt(jnp.mean(rows * rows, axis=-1, keepdims=True) + EPSILON)
    unit = rows * inverse
    return unit, inverse, (unit * gain).astype(BF16)


def forward_kernel(
    neighbours_ref,
    tile_slot_ref,
    own_ref,
    other_ref,
    weight_ref,
    out_weight_ref,
    query_gain_ref,
    key_gain_ref,
    gate_ref,
    projected_ref,
    inverse_ref,
    probs_ref,
    attention_ref,
    kept_ref,
    sent_ref,
    out_weight_buffer,
    tokens_ref,
    semaphores,
):
    local, model = own_ref.shape
    tokens = 2 * local
    width = query_gain_ref.shape[1]
    groups = weight_ref.shape[0]
    rows = GROUP * width

    def out_weight_part(group):
        place = pl.ds(group * rows, rows)
        return out_weight_ref.at[place], out_weight_buffer.at[place]

    copies = Copies([out_weight_part(group) for group in range(groups)], semaphores, groups)

    tokens_ref[:local, :] = own_ref[...]
    tokens_ref[local:, :] = other_ref[...]
    allowed = listed_slots(neighbours_ref, tile_slot_ref)
    mine = lax.axis_index("seq")
    row_half = lax.broadcasted_iota(jnp.int32, (tokens, tokens), 0) // local
    column_half = lax.broadcasted_iota(jnp.int32, (tokens, tokens), 1) // local
    row_slot = jnp.where(row_half == 0, mine, 1 - mine)
    column_slot = jnp.where(column_half == 0, mine, 1 - mine)
    table = jnp.zeros((tokens, tokens), jnp.int32)
    for r in range(2):
        for c in range(2):
            table = jnp.where((row_slot == r) & (column_slot == c), allowed[r][c], table)
    bias = jnp.where(table > 0, 0.0, -jnp.inf).astype(F32)

    def project(group):
        projected_ref[group] = dot_nn(tokens_ref[...], weight_ref[group])

    def attend(group):
        heads = range(GROUP)
        operands = []
        for place in range(2 * GROUP):
            gain_ref = (query_gain_ref, key_gain_ref)[place % 2]
            left = (3 * (place // 2) + place % 2) * width
            part = slice(left, left + width)
            unit, inverse, operand = normed(projected_ref[group, :, part], gain_ref[...])
            projected_ref[group, :, part] = unit
            inverse_ref[group, :, place : place + 1] = inverse
            operands.append(operand)
        scale_factor = 1.0 / math.sqrt(width)
        scores = [dot_nt(operands[2 * h], operands[2 * h + 1]) * scale_factor + bias for h in heads]
        tops = [jnp.max(scores[h], axis=-1, keepdims=True) for h in heads]
        weights = [jnp.exp(scores[h] - tops[h]) for h in heads]
        sums = [jnp.sum(weights[h], axis=-1, keepdims=True) for h in heads]
        probs = [(weights[h] / sums[h]).astype(BF16) for h in heads]
        attended = []
        for h in heads:
            probs_ref[GROUP * group + h] = probs[h]
            left = (3 * h + 2) * width
            value = projected_ref[group, :, left : left + width].astype(BF16)
            attended.append(dot_nn(probs[h], value).astype(BF16))
        return jnp.concatenate(attended, axis=1)

    def share(group, attended):
        return dot_nn(attended, out_weight_buffer[group * rows : (group + 1) * rows, :])

    project(0)
    attended = attend(0)
    for group in range(1, groups):
        project(group)
        copies.wait()
        following = attend(group)
        if group == 1:
            attention_ref[...] = share(0, attended)
        else:
            attention_ref[...] += share(group - 1, attended)
        attended = following
    copies.wait()
    total = share(groups - 1, attended)
    if groups > 1:
        total += attention_ref[...]
    attention_ref[...] = total
    gate = gate_ref[...]
    kept_ref[...] = (own_ref[...].astype(F32) + gate * total[:local]).astype(BF16)
    sent_ref[...] = (gate * total[local:]).astype(BF16)


def forward(neighbours, tile_slot, own, other, weight, out_weight, query_gain, key_gain, gate):
    local, model = own.shape
    groups, _, wide = weight.shape
    tokens = 2 * local
    weight = pltpu.with_memory_space_constraint(weight, pltpu.VMEM)
    out_weight = pltpu.with_memory_space_constraint(out_weight, pltpu.HBM)
    smem = pl.BlockSpec(memory_space=pltpu.SMEM)
    vmem = pl.BlockSpec(memory_space=pltpu.VMEM)
    hbm = pl.BlockSpec(memory_space=pl.ANY)
    return pl.pallas_call(
        forward_kernel,
        out_shape=(
            jax.ShapeDtypeStruct((groups, tokens, wide), F32),
            jax.ShapeDtypeStruct((groups, tokens, 2 * GROUP), F32),
            jax.ShapeDtypeStruct((GROUP * groups, tokens, tokens), BF16),
            jax.ShapeDtypeStruct((tokens, model), F32),
            jax.ShapeDtypeStruct((local, model), BF16),
            jax.ShapeDtypeStruct((local, model), BF16),
            pltpu.VMEM(out_weight.shape, BF16),
        ),
        in_specs=[smem, smem, vmem, vmem, vmem, hbm, vmem, vmem, vmem],
        out_specs=(vmem,) * 7,
        scratch_shapes=[
            pltpu.VMEM((tokens, model), BF16),
            pltpu.SemaphoreType.DMA((groups,)),
        ],
        compiler_params=params(6),
        cost_estimate=pl.CostEstimate(
            flops=2 * tokens * (weight.size + out_weight.size),
            bytes_accessed=2 * (weight.size + out_weight.size),
            transcendentals=0,
        ),
        name="attention_forward",
    )(neighbours, tile_slot, own, other, weight, out_weight, query_gain, key_gain, gate)


def input_grad(grad_ref, weight_ref, turned_ref, own_ref, kept_ref, sent_ref):
    local, model = own_ref.shape
    groups, _, wide = grad_ref.shape
    streamed = groups * wide - turned_ref.shape[0]
    block = 512
    for start in range(0, model, block):
        part = slice(start, start + block)
        total = None
        for group in range(groups):
            first = group * wide
            cut = min(max(streamed - first, 0), wide)
            if cut < wide:
                rows = slice(first + cut - streamed, first + wide - streamed)
                product = dot_nn(grad_ref[group, :, cut:], turned_ref[rows, part])
                total = product if total is None else total + product
            if cut > 0:
                product = dot_nt(weight_ref[group, part, :cut], grad_ref[group, :, :cut]).T
                total = product if total is None else total + product
        kept_ref[:, part] = (own_ref[:, part].astype(F32) + total[:local]).astype(BF16)
        sent_ref[:, part] = total[local:].astype(BF16)


def backward_kernel(
    own_ref,
    other_ref,
    out_weight_ref,
    weight_ref,
    turned_ref,
    projected_ref,
    inverse_ref,
    probs_ref,
    attention_ref,
    query_gain_ref,
    key_gain_ref,
    gate_ref,
    gate_kept_ref,
    gate_sent_ref,
    kept_ref,
    sent_ref,
    grad_ref,
    scaled_ref,
    attended_grad_ref,
    gate_grad_ref,
):
    local = own_ref.shape[0]
    width = query_gain_ref.shape[1]
    groups = grad_ref.shape[0]
    rows = GROUP * width

    gate = gate_ref[...]
    own, other = own_ref[...].astype(F32), other_ref[...].astype(F32)
    scaled_ref[:local, :] = (own * gate).astype(BF16)
    scaled_ref[local:, :] = (other * gate).astype(BF16)
    gate_grad_ref[...] = jnp.sum(
        own * attention_ref[:local, :] + other * attention_ref[local:, :], axis=0, keepdims=True
    )
    half = gate_kept_ref.shape[1]
    mine = lax.axis_index("seq")
    gate_kept_ref[...] = gate_grad_ref[:, pl.ds(pl.multiple_of(mine * half, half), half)]
    gate_sent_ref[...] = gate_grad_ref[:, pl.ds(pl.multiple_of((1 - mine) * half, half), half)]

    def attended_grad(group):
        part = slice(group * rows, (group + 1) * rows)
        product = dot_nt(scaled_ref[...], out_weight_ref[part, :])
        attended_grad_ref[group] = product.astype(BF16)

    def attend_backward(group):
        heads = range(GROUP)
        query_gain, key_gain = query_gain_ref[...], key_gain_ref[...]
        scale_factor = 1.0 / math.sqrt(width)

        def part(head, index):
            left = (3 * head + index) * width
            return slice(left, left + width)

        def inverse(head, index):
            return inverse_ref[group, :, 2 * head + index : 2 * head + index + 1]

        grads = [attended_grad_ref[group, :, h * width : (h + 1) * width] for h in heads]
        values = [projected_ref[group, :, part(h, 2)].astype(BF16) for h in heads]
        prob_grads = [dot_nt(grads[h], values[h]) for h in heads]
        for h in heads:
            product = dot_tn(probs_ref[GROUP * group + h], grads[h])
            grad_ref[group, :, part(h, 2)] = product.astype(BF16)
        wide = [probs_ref[GROUP * group + h].astype(F32) for h in heads]
        deltas = [jnp.sum(wide[h] * prob_grads[h], axis=-1, keepdims=True) for h in heads]
        score_grads = [
            (wide[h] * (prob_grads[h] - deltas[h]) * scale_factor).astype(BF16) for h in heads
        ]
        units = [[projected_ref[group, :, part(h, index)] for index in range(2)] for h in heads]
        keys = [(units[h][1] * key_gain).astype(BF16) for h in heads]
        queries = [(units[h][0] * query_gain).astype(BF16) for h in heads]
        scaled = [
            [
                dot_nn(score_grads[h], keys[h]) * query_gain,
                dot_tn(score_grads[h], queries[h]) * key_gain,
            ]
            for h in heads
        ]
        means = [
            [jnp.mean(scaled[h][i] * units[h][i], axis=-1, keepdims=True) for i in range(2)]
            for h in heads
        ]
        for h in heads:
            for i in range(2):
                grad_ref[group, :, part(h, i)] = (
                    (scaled[h][i] - units[h][i] * means[h][i]) * inverse(h, i)
                ).astype(BF16)

    attended_grad(0)
    for group in range(groups):
        if group + 1 < groups:
            attended_grad(group + 1)
        attend_backward(group)
    input_grad(grad_ref, weight_ref, turned_ref, own_ref, kept_ref, sent_ref)


def backward(
    own,
    other,
    out_weight,
    weight,
    turned,
    projected,
    inverse,
    probs,
    attention,
    query_gain,
    key_gain,
    gate,
):
    local, model = own.shape
    groups, tokens, wide = projected.shape
    head_dim = query_gain.shape[1]
    out_weight = pltpu.with_memory_space_constraint(out_weight, pltpu.VMEM)
    weight = pltpu.with_memory_space_constraint(weight, pltpu.VMEM)
    turned = pltpu.with_memory_space_constraint(turned, pltpu.VMEM)
    vmem = pl.BlockSpec(memory_space=pltpu.VMEM)
    return pl.pallas_call(
        backward_kernel,
        out_shape=(
            jax.ShapeDtypeStruct((1, model // 2), F32),
            jax.ShapeDtypeStruct((1, model // 2), F32),
            jax.ShapeDtypeStruct((local, model), BF16),
            jax.ShapeDtypeStruct((local, model), BF16),
        ),
        in_specs=[vmem] * 12,
        out_specs=(vmem,) * 4,
        scratch_shapes=[
            pltpu.VMEM((groups, tokens, wide), BF16),
            pltpu.VMEM((tokens, model), BF16),
            pltpu.VMEM((groups, tokens, GROUP * head_dim), BF16),
            pltpu.VMEM((1, model), F32),
        ],
        compiler_params=params(6),
        cost_estimate=pl.CostEstimate(
            flops=2 * tokens * (out_weight.size + weight.size),
            bytes_accessed=2 * (out_weight.size + weight.size),
            transcendentals=0,
        ),
        name="attention_backward",
    )(
        own,
        other,
        out_weight,
        weight,
        turned,
        projected,
        inverse,
        probs,
        attention,
        query_gain,
        key_gain,
        gate,
    )


def sums_kernel(kept_ref, sent_ref, gate_kept_ref, gate_sent_ref, grad_ref, gate_ref):
    grad_ref[...] = (kept_ref[...].astype(F32) + sent_ref[...].astype(F32)).astype(BF16)
    gate_ref[...] = gate_kept_ref[...] + gate_sent_ref[...]


def sums(kept, sent, gate_kept, gate_sent):
    vmem = pl.BlockSpec(memory_space=pltpu.VMEM)
    return pl.pallas_call(
        sums_kernel,
        out_shape=(
            jax.ShapeDtypeStruct(kept.shape, BF16),
            jax.ShapeDtypeStruct(gate_kept.shape, F32),
        ),
        in_specs=[vmem] * 4,
        out_specs=(vmem, vmem),
        compiler_params=params(8),
        name="sums",
    )(kept, sent, gate_kept, gate_sent)


def routed(block, seq_step, pipe_step):
    seq_size, pipe_size = lax.axis_size("seq"), lax.axis_size("pipe")
    route = []
    for i in range(seq_size):
        for j in range(pipe_size):
            target = (i + seq_step) % seq_size * pipe_size + (j + pipe_step) % pipe_size
            route.append((i * pipe_size + j, target))
    return lax.ppermute(block, ("seq", "pipe"), route)


def pair_body(
    segment_input,
    output_grad,
    qkv_weight,
    out_weight,
    query_gain,
    key_gain,
    gate_scale,
    neighbours,
    tile_slot,
):
    stream = segment_input[0]
    upstream = output_grad[0]
    out_local = out_weight[0]
    other_stream = routed(stream, 1, 0)
    weight, turned_weight = regroup(qkv_weight[0], 128, 4, TURNED)
    other_upstream = routed(upstream, 1, 0)
    projected, inverse, probs, attention, kept, sent, out_local = forward(
        neighbours,
        tile_slot,
        stream,
        other_stream,
        weight,
        out_local,
        query_gain,
        key_gain,
        gate_scale,
    )
    kept = routed(kept, 0, 1)
    sent = routed(sent, 1, 1)
    gate_kept, gate_sent, grad_kept, grad_sent = backward(
        upstream,
        other_upstream,
        out_local,
        weight,
        turned_weight,
        projected,
        inverse,
        probs,
        attention,
        query_gain,
        key_gain,
        gate_scale,
    )
    grad_kept = routed(grad_kept, 0, -1)
    grad_sent = routed(grad_sent, 1, -1)
    segment_output = (kept.astype(F32) + sent.astype(F32)).astype(BF16)
    segment_output, gate_sent = lax.optimization_barrier((segment_output, gate_sent))
    gate_sent = routed(gate_sent, 1, 0)
    token_grad, gate_grad = sums(grad_kept, grad_sent, gate_kept, gate_sent)
    return (segment_output[None], token_grad[None], gate_grad)


def solution(mesh):
    in_specs = (
        P("pipe", ("dp", "seq"), None),
        P("pipe", ("dp", "seq"), None),
        P("pipe", None, "seq", None),
        P("pipe", "seq", None),
        P("pipe", None),
        P("pipe", None),
        P("pipe", None),
        P("dp", None),
        P("dp"),
    )
    out_specs = (
        P("pipe", ("dp", "seq"), None),
        P("pipe", ("dp", "seq"), None),
        P(("dp", "pipe"), "seq"),
    )

    def body(*args):
        one_tile_each = args[0].shape[1] == TILE and args[8].shape[0] == 2
        if mesh.shape["seq"] == 2 and one_tile_each and args[2].shape[2] % GROUP == 0:
            return pair_body(*args)
        return general_body(*args)

    return jax.shard_map(body, mesh=mesh, in_specs=in_specs, out_specs=out_specs, check_vma=False)
```

```python
import functools
import math

import jax
import jax.numpy as jnp
from jax import lax
from jax.experimental import pallas as pl
from jax.experimental.pallas import tpu as pltpu
from jax.sharding import PartitionSpec as P

TILE = 64
EPSILON = 1e-06
F32 = jnp.float32
BF16 = jnp.bfloat16
MIB = 1024 * 1024
GROUP = 4
TURNED = 6


def passed_along(block, axis, distance):
    devices = range(lax.axis_size(axis))
    route = [((i - distance) % len(devices), i) for i in devices]
    return lax.ppermute(block, axis, route)


def slot_lists(neighbours, tile_slot):
    tile_count = tile_slot.shape[0]
    numbering = jnp.arange(tile_count, dtype=jnp.int32)
    placed = (tile_slot[:, None] == numbering[None, :]).astype(jnp.int32)
    tile_of_slot = jnp.sum(placed * numbering[:, None], axis=0)
    chosen = (tile_of_slot[:, None] == numbering[None, :]).astype(jnp.int32)
    listed_tiles = jnp.sum(chosen[:, :, None] * neighbours[None, :, :], axis=1)
    key_valid = listed_tiles >= 0
    safe_tiles = jnp.maximum(listed_tiles, 0)
    matches = (safe_tiles[:, :, None] == numbering[None, None, :]).astype(jnp.int32)
    key_slots = jnp.sum(matches * tile_slot[None, None, :], axis=2)
    return (key_slots, key_valid)


def block_tiles(tile_count):
    return math.gcd(tile_count, max(1, 512 // TILE))


def unit_norm(values):
    spread = jnp.sqrt(jnp.mean(values * values, axis=-1, keepdims=True) + EPSILON)
    return (values / spread, spread)


def probabilities(query_block, key_rows, block_valid):
    scores = jnp.einsum(
        "aihd,ajhd->ahij", query_block, key_rows, preferred_element_type=jnp.float32
    ) * (1.0 / math.sqrt(query_block.shape[-1]))
    key_mask = jnp.repeat(block_valid, TILE, axis=1)
    scores = jnp.where(key_mask[:, None, None, :], scores, -jnp.inf)
    row_max = jnp.max(scores, axis=-1, keepdims=True)
    weights = jnp.exp(scores - row_max)
    return (weights / jnp.sum(weights, axis=-1, keepdims=True)).astype(jnp.bfloat16)


def gathered(tiles_array, block_slots):
    picked = tiles_array[block_slots]
    return picked.reshape(block_slots.shape[0], -1, tiles_array.shape[2], tiles_array.shape[3])


def attend_both(query_tiles, key_tiles, value_tiles, grad_tiles, key_slots, key_valid):
    tile_count = query_tiles.shape[0]
    span = block_tiles(tile_count)
    scale_factor = 1.0 / math.sqrt(query_tiles.shape[-1])
    empty_grad = jnp.zeros(query_tiles.shape, jnp.float32)

    def per_block(accumulators, block_index):
        key_total, value_total = accumulators
        first_tile = block_index * span
        query_block = lax.dynamic_slice_in_dim(query_tiles, first_tile, span, 0)
        grad_block = lax.dynamic_slice_in_dim(grad_tiles, first_tile, span, 0)
        block_slots = lax.dynamic_slice_in_dim(key_slots, first_tile, span, 0)
        block_valid = lax.dynamic_slice_in_dim(key_valid, first_tile, span, 0)
        key_rows = gathered(key_tiles, block_slots)
        value_rows = gathered(value_tiles, block_slots)
        weights = probabilities(query_block, key_rows, block_valid)
        attended = jnp.einsum(
            "ahij,ajhd->aihd", weights, value_rows, preferred_element_type=jnp.float32
        )
        value_part = jnp.einsum(
            "ahij,aihd->ajhd", weights, grad_block, preferred_element_type=jnp.float32
        )
        prob_grad = jnp.einsum(
            "aihd,ajhd->ahij", grad_block, value_rows, preferred_element_type=jnp.float32
        )
        weights_wide = weights.astype(jnp.float32)
        row_delta = jnp.sum(weights_wide * prob_grad, axis=-1, keepdims=True)
        score_grad = (weights_wide * (prob_grad - row_delta) * scale_factor).astype(jnp.bfloat16)
        query_part = jnp.einsum(
            "ahij,ajhd->aihd", score_grad, key_rows, preferred_element_type=jnp.float32
        )
        key_part = jnp.einsum(
            "ahij,aihd->ajhd", score_grad, query_block, preferred_element_type=jnp.float32
        )
        block_shape = (span, block_slots.shape[1]) + query_tiles.shape[1:]
        key_total = key_total.at[block_slots].add(key_part.reshape(block_shape))
        value_total = value_total.at[block_slots].add(value_part.reshape(block_shape))
        return ((key_total, value_total), (attended, query_part))

    totals, parts = lax.scan(
        per_block, (empty_grad, empty_grad), jnp.arange(tile_count // span, dtype=jnp.int32)
    )
    flat_shape = (-1,) + query_tiles.shape[2:]
    return (
        parts[0].reshape(flat_shape),
        parts[1].reshape(flat_shape),
        totals[0].reshape(flat_shape),
        totals[1].reshape(flat_shape),
    )


def general_body(
    segment_input,
    output_grad,
    qkv_weight,
    out_weight,
    query_gain,
    key_gain,
    gate_scale,
    neighbours,
    tile_slot,
):
    key_slots, key_valid = slot_lists(neighbours, tile_slot)
    stream = segment_input[0]
    upstream = output_grad[0]
    model_width = stream.shape[1]
    head_dim = query_gain.shape[1]
    local_heads = qkv_weight.shape[2]
    local_width = local_heads * head_dim
    proj_weight = qkv_weight[0].reshape(model_width, local_heads * 3 * head_dim)
    out_local = out_weight[0]
    gate_row = gate_scale[0]
    query_weights = query_gain[0]
    key_weights = key_gain[0]
    projected = jnp.dot(
        lax.all_gather(stream, "seq", axis=0, tiled=True),
        proj_weight,
        preferred_element_type=jnp.float32,
    )
    all_tokens = projected.shape[0]
    projected = projected.reshape(all_tokens, local_heads, 3, head_dim)
    query_unit, query_spread = unit_norm(projected[:, :, 0])
    key_unit, key_spread = unit_norm(projected[:, :, 1])
    queries = (query_unit * query_weights).astype(jnp.bfloat16)
    keys_normed = (key_unit * key_weights).astype(jnp.bfloat16)
    value_rows = projected[:, :, 2].astype(jnp.bfloat16)
    scaled = (upstream.astype(jnp.float32) * gate_row).astype(jnp.bfloat16)
    attended_grad = jnp.einsum(
        "td,cd->tc",
        lax.all_gather(scaled, "seq", axis=0, tiled=True),
        out_local,
        preferred_element_type=jnp.float32,
    ).astype(jnp.bfloat16)

    def as_tiles(values):
        return values.reshape(-1, TILE, local_heads, head_dim)

    attended, query_grad, key_grad, value_grad = attend_both(
        as_tiles(queries),
        as_tiles(keys_normed),
        as_tiles(value_rows),
        as_tiles(attended_grad),
        key_slots,
        key_valid,
    )
    attended_low = attended.astype(jnp.bfloat16).reshape(all_tokens, local_width)
    rows = attended_low
    attention_out = lax.psum_scatter(
        jnp.dot(rows, out_local, preferred_element_type=jnp.float32),
        "seq",
        scatter_dimension=0,
        tiled=True,
    )
    section_out = (stream.astype(jnp.float32) + gate_row * attention_out).astype(jnp.bfloat16)
    segment_output = passed_along(section_out, "pipe", 1)
    gate_local = lax.psum_scatter(
        jnp.sum(upstream.astype(jnp.float32) * attention_out, axis=0),
        "seq",
        scatter_dimension=0,
        tiled=True,
    )
    query_scaled = query_grad * query_weights
    query_part_grad = (
        query_scaled - query_unit * jnp.mean(query_scaled * query_unit, axis=-1, keepdims=True)
    ) / query_spread
    key_scaled = key_grad * key_weights
    key_part_grad = (
        key_scaled - key_unit * jnp.mean(key_scaled * key_unit, axis=-1, keepdims=True)
    ) / key_spread
    projected_grad = (
        jnp.stack([query_part_grad, key_part_grad, value_grad], axis=2)
        .astype(jnp.bfloat16)
        .reshape(all_tokens, local_heads * 3 * head_dim)
    )
    rows = projected_grad
    stream_grad = lax.psum_scatter(
        jnp.einsum("tc,dc->td", rows, proj_weight, preferred_element_type=jnp.float32).astype(
            jnp.bfloat16
        ),
        "seq",
        scatter_dimension=0,
        tiled=True,
    ).astype(jnp.float32)
    token_grad = (upstream.astype(jnp.float32) + stream_grad).astype(jnp.bfloat16)
    input_grad = passed_along(token_grad, "pipe", -1)
    return (segment_output[None], input_grad[None], gate_local[None])


def dot_nn(a, b):
    return lax.dot_general(a, b, (((1,), (0,)), ((), ())), preferred_element_type=F32)


def dot_nt(a, b):
    return lax.dot_general(a, b, (((1,), (1,)), ((), ())), preferred_element_type=F32)


def dot_tn(a, b):
    return lax.dot_general(a, b, (((0,), (0,)), ((), ())), preferred_element_type=F32)


def params(mebibytes):
    return pltpu.CompilerParams(vmem_limit_bytes=mebibytes * MIB)


class Copies:
    def __init__(self, pairs, semaphores, ahead):
        self.copies = [
            pltpu.make_async_copy(source, target, semaphores.at[i])
            for i, (source, target) in enumerate(pairs)
        ]
        self.ahead = ahead
        self.waited = 0
        for copy in self.copies[:ahead]:
            copy.start()

    def wait(self, count=1):
        for _ in range(count):
            self.copies[self.waited].wait()
            following = self.waited + self.ahead
            if following < len(self.copies):
                self.copies[following].start()
            self.waited += 1


def regroup_kernel(weight_ref, out_ref, turned_ref, read_ref, reads):
    depth, heads, width = weight_ref.shape
    slots, rows = read_ref.shape[:2]
    steps = depth // rows

    def part(step):
        return pl.ds(pl.multiple_of(step * rows, rows), rows)

    def read(step, slot):
        return pltpu.make_async_copy(
            weight_ref.at[part(step)], read_ref.at[slot], reads.at[slot]
        )

    for slot in range(slots):
        read(slot, slot).start()

    @pl.loop(0, steps)
    def _(step):
        slot = lax.rem(step, slots)
        read(step, slot).wait()
        by_head = jnp.swapaxes(read_ref[slot], 0, 1)
        for head in range(heads):
            left = (head % GROUP) * width
            out_ref[head // GROUP, part(step), left : left + width] = by_head[head]
            above = (head + 1) * width - (heads * width - turned_ref.shape[0])
            if above > 0:
                turned_ref[above - width : above, part(step)] = by_head[head].T

        @pl.when(step + slots < steps)
        def _():
            read(step + slots, slot).start()


def regroup(weight, rows, slots, turned):
    depth, heads, width = weight.shape
    out = (heads // GROUP, depth, GROUP * width)
    return pl.pallas_call(
        regroup_kernel,
        out_shape=(
            pltpu.VMEM(out, weight.dtype),
            pltpu.VMEM((turned * width, depth), weight.dtype),
        ),
        in_specs=[pl.BlockSpec(memory_space=pl.ANY)],
        out_specs=(pl.BlockSpec(memory_space=pltpu.VMEM),) * 2,
        scratch_shapes=[
            pltpu.VMEM((slots, rows, heads, width), weight.dtype),
            pltpu.SemaphoreType.DMA((slots,)),
        ],
        compiler_params=params(6),
        cost_estimate=pl.CostEstimate(
            flops=0, bytes_accessed=4 * depth * heads * width, transcendentals=0
        ),
        name="regroup",
    )(pltpu.with_memory_space_constraint(weight, pltpu.HBM))


def listed_slots(neighbours_ref, tile_slot_ref):
    tiles, places = neighbours_ref.shape
    one, zero = jnp.int32(1), jnp.int32(0)
    allowed = [[zero] * tiles for _ in range(tiles)]
    for t in range(tiles):
        for u in range(tiles):
            listed = zero
            for k in range(places):
                listed = jnp.where(neighbours_ref[t, k] == u, one, listed)
            for r in range(tiles):
                for c in range(tiles):
                    here = (tile_slot_ref[t] == r) & (tile_slot_ref[u] == c)
                    allowed[r][c] = jnp.where(here, listed, allowed[r][c])
    return allowed


def normed(rows, gain):
    inverse = lax.rsqrt(jnp.mean(rows * rows, axis=-1, keepdims=True) + EPSILON)
    unit = rows * inverse
    return unit, inverse, (unit * gain).astype(BF16)


def forward_kernel(
    neighbours_ref,
    tile_slot_ref,
    own_ref,
    other_ref,
    weight_ref,
    out_weight_ref,
    query_gain_ref,
    key_gain_ref,
    gate_ref,
    projected_ref,
    inverse_ref,
    probs_ref,
    attention_ref,
    kept_ref,
    sent_ref,
    out_weight_buffer,
    tokens_ref,
    semaphores,
):
    local, model = own_ref.shape
    tokens = 2 * local
    width = query_gain_ref.shape[1]
    groups = weight_ref.shape[0]
    rows = GROUP * width

    def out_weight_part(group):
        place = pl.ds(group * rows, rows)
        return out_weight_ref.at[place], out_weight_buffer.at[place]

    copies = Copies([out_weight_part(group) for group in range(groups)], semaphores, groups)

    tokens_ref[:local, :] = own_ref[...]
    tokens_ref[local:, :] = other_ref[...]
    allowed = listed_slots(neighbours_ref, tile_slot_ref)
    mine = lax.axis_index("seq")
    row_half = lax.broadcasted_iota(jnp.int32, (tokens, tokens), 0) // local
    column_half = lax.broadcasted_iota(jnp.int32, (tokens, tokens), 1) // local
    row_slot = jnp.where(row_half == 0, mine, 1 - mine)
    column_slot = jnp.where(column_half == 0, mine, 1 - mine)
    table = jnp.zeros((tokens, tokens), jnp.int32)
    for r in range(2):
        for c in range(2):
            table = jnp.where((row_slot == r) & (column_slot == c), allowed[r][c], table)
    bias = jnp.where(table > 0, 0.0, -jnp.inf).astype(F32)

    def project(group):
        projected_ref[group] = dot_nn(tokens_ref[...], weight_ref[group])

    def attend(group):
        heads = range(GROUP)
        operands = []
        for place in range(2 * GROUP):
            gain_ref = (query_gain_ref, key_gain_ref)[place % 2]
            left = (3 * (place // 2) + place % 2) * width
            part = slice(left, left + width)
            unit, inverse, operand = normed(projected_ref[group, :, part], gain_ref[...])
            projected_ref[group, :, part] = unit
            inverse_ref[group, :, place : place + 1] = inverse
            operands.append(operand)
        scale_factor = 1.0 / math.sqrt(width)
        scores = [dot_nt(operands[2 * h], operands[2 * h + 1]) * scale_factor + bias for h in heads]
        tops = [jnp.max(scores[h], axis=-1, keepdims=True) for h in heads]
        weights = [jnp.exp(scores[h] - tops[h]) for h in heads]
        sums = [jnp.sum(weights[h], axis=-1, keepdims=True) for h in heads]
        probs = [(weights[h] / sums[h]).astype(BF16) for h in heads]
        attended = []
        for h in heads:
            probs_ref[GROUP * group + h] = probs[h]
            left = (3 * h + 2) * width
            value = projected_ref[group, :, left : left + width].astype(BF16)
            attended.append(dot_nn(probs[h], value).astype(BF16))
        return jnp.concatenate(attended, axis=1)

    def share(group, attended):
        return dot_nn(attended, out_weight_buffer[group * rows : (group + 1) * rows, :])

    project(0)
    attended = attend(0)
    for group in range(1, groups):
        project(group)
        copies.wait()
        following = attend(group)
        if group == 1:
            attention_ref[...] = share(0, attended)
        else:
            attention_ref[...] += share(group - 1, attended)
        attended = following
    copies.wait()
    total = share(groups - 1, attended)
    if groups > 1:
        total += attention_ref[...]
    attention_ref[...] = total
    gate = gate_ref[...]
    kept_ref[...] = (own_ref[...].astype(F32) + gate * total[:local]).astype(BF16)
    sent_ref[...] = (gate * total[local:]).astype(BF16)


def forward(neighbours, tile_slot, own, other, weight, out_weight, query_gain, key_gain, gate):
    local, model = own.shape
    groups, _, wide = weight.shape
    tokens = 2 * local
    weight = pltpu.with_memory_space_constraint(weight, pltpu.VMEM)
    out_weight = pltpu.with_memory_space_constraint(out_weight, pltpu.HBM)
    smem = pl.BlockSpec(memory_space=pltpu.SMEM)
    vmem = pl.BlockSpec(memory_space=pltpu.VMEM)
    hbm = pl.BlockSpec(memory_space=pl.ANY)
    return pl.pallas_call(
        forward_kernel,
        out_shape=(
            jax.ShapeDtypeStruct((groups, tokens, wide), F32),
            jax.ShapeDtypeStruct((groups, tokens, 2 * GROUP), F32),
            jax.ShapeDtypeStruct((GROUP * groups, tokens, tokens), BF16),
            jax.ShapeDtypeStruct((tokens, model), F32),
            jax.ShapeDtypeStruct((local, model), BF16),
            jax.ShapeDtypeStruct((local, model), BF16),
            pltpu.VMEM(out_weight.shape, BF16),
        ),
        in_specs=[smem, smem, vmem, vmem, vmem, hbm, vmem, vmem, vmem],
        out_specs=(vmem,) * 7,
        scratch_shapes=[
            pltpu.VMEM((tokens, model), BF16),
            pltpu.SemaphoreType.DMA((groups,)),
        ],
        compiler_params=params(6),
        cost_estimate=pl.CostEstimate(
            flops=2 * tokens * (weight.size + out_weight.size),
            bytes_accessed=2 * (weight.size + out_weight.size),
            transcendentals=0,
        ),
        name="attention_forward",
    )(neighbours, tile_slot, own, other, weight, out_weight, query_gain, key_gain, gate)


def input_grad(grad_ref, weight_ref, turned_ref, own_ref, kept_ref, sent_ref):
    local, model = own_ref.shape
    groups, _, wide = grad_ref.shape
    streamed = groups * wide - turned_ref.shape[0]
    block = 512
    for start in range(0, model, block):
        part = slice(start, start + block)
        total = None
        for group in range(groups):
            first = group * wide
            cut = min(max(streamed - first, 0), wide)
            if cut < wide:
                rows = slice(first + cut - streamed, first + wide - streamed)
                product = dot_nn(grad_ref[group, :, cut:], turned_ref[rows, part])
                total = product if total is None else total + product
            if cut > 0:
                product = dot_nt(weight_ref[group, part, :cut], grad_ref[group, :, :cut]).T
                total = product if total is None else total + product
        kept_ref[:, part] = (own_ref[:, part].astype(F32) + total[:local]).astype(BF16)
        sent_ref[:, part] = total[local:].astype(BF16)


def backward_kernel(
    own_ref,
    other_ref,
    out_weight_ref,
    weight_ref,
    turned_ref,
    projected_ref,
    inverse_ref,
    probs_ref,
    attention_ref,
    query_gain_ref,
    key_gain_ref,
    gate_ref,
    gate_kept_ref,
    gate_sent_ref,
    kept_ref,
    sent_ref,
    grad_ref,
    scaled_ref,
    attended_grad_ref,
    gate_grad_ref,
):
    local = own_ref.shape[0]
    width = query_gain_ref.shape[1]
    groups = grad_ref.shape[0]
    rows = GROUP * width

    gate = gate_ref[...]
    own, other = own_ref[...].astype(F32), other_ref[...].astype(F32)
    scaled_ref[:local, :] = (own * gate).astype(BF16)
    scaled_ref[local:, :] = (other * gate).astype(BF16)
    gate_grad_ref[...] = jnp.sum(
        own * attention_ref[:local, :] + other * attention_ref[local:, :], axis=0, keepdims=True
    )
    half = gate_kept_ref.shape[1]
    mine = lax.axis_index("seq")
    gate_kept_ref[...] = gate_grad_ref[:, pl.ds(pl.multiple_of(mine * half, half), half)]
    gate_sent_ref[...] = gate_grad_ref[:, pl.ds(pl.multiple_of((1 - mine) * half, half), half)]

    def attended_grad(group):
        part = slice(group * rows, (group + 1) * rows)
        product = dot_nt(scaled_ref[...], out_weight_ref[part, :])
        attended_grad_ref[group] = product.astype(BF16)

    def attend_backward(group):
        heads = range(GROUP)
        query_gain, key_gain = query_gain_ref[...], key_gain_ref[...]
        scale_factor = 1.0 / math.sqrt(width)

        def part(head, index):
            left = (3 * head + index) * width
            return slice(left, left + width)

        def inverse(head, index):
            return inverse_ref[group, :, 2 * head + index : 2 * head + index + 1]

        grads = [attended_grad_ref[group, :, h * width : (h + 1) * width] for h in heads]
        values = [projected_ref[group, :, part(h, 2)].astype(BF16) for h in heads]
        prob_grads = [dot_nt(grads[h], values[h]) for h in heads]
        for h in heads:
            product = dot_tn(probs_ref[GROUP * group + h], grads[h])
            grad_ref[group, :, part(h, 2)] = product.astype(BF16)
        wide = [probs_ref[GROUP * group + h].astype(F32) for h in heads]
        deltas = [jnp.sum(wide[h] * prob_grads[h], axis=-1, keepdims=True) for h in heads]
        score_grads = [
            (wide[h] * (prob_grads[h] - deltas[h]) * scale_factor).astype(BF16) for h in heads
        ]
        units = [[projected_ref[group, :, part(h, index)] for index in range(2)] for h in heads]
        keys = [(units[h][1] * key_gain).astype(BF16) for h in heads]
        queries = [(units[h][0] * query_gain).astype(BF16) for h in heads]
        scaled = [
            [
                dot_nn(score_grads[h], keys[h]) * query_gain,
                dot_tn(score_grads[h], queries[h]) * key_gain,
            ]
            for h in heads
        ]
        means = [
            [jnp.mean(scaled[h][i] * units[h][i], axis=-1, keepdims=True) for i in range(2)]
            for h in heads
        ]
        for h in heads:
            for i in range(2):
                grad_ref[group, :, part(h, i)] = (
                    (scaled[h][i] - units[h][i] * means[h][i]) * inverse(h, i)
                ).astype(BF16)

    attended_grad(0)
    for group in range(groups):
        if group + 1 < groups:
            attended_grad(group + 1)
        attend_backward(group)
    input_grad(grad_ref, weight_ref, turned_ref, own_ref, kept_ref, sent_ref)


def backward(
    own,
    other,
    out_weight,
    weight,
    turned,
    projected,
    inverse,
    probs,
    attention,
    query_gain,
    key_gain,
    gate,
):
    local, model = own.shape
    groups, tokens, wide = projected.shape
    head_dim = query_gain.shape[1]
    out_weight = pltpu.with_memory_space_constraint(out_weight, pltpu.VMEM)
    weight = pltpu.with_memory_space_constraint(weight, pltpu.VMEM)
    turned = pltpu.with_memory_space_constraint(turned, pltpu.VMEM)
    vmem = pl.BlockSpec(memory_space=pltpu.VMEM)
    return pl.pallas_call(
        backward_kernel,
        out_shape=(
            jax.ShapeDtypeStruct((1, model // 2), F32),
            jax.ShapeDtypeStruct((1, model // 2), F32),
            jax.ShapeDtypeStruct((local, model), BF16),
            jax.ShapeDtypeStruct((local, model), BF16),
        ),
        in_specs=[vmem] * 12,
        out_specs=(vmem,) * 4,
        scratch_shapes=[
            pltpu.VMEM((groups, tokens, wide), BF16),
            pltpu.VMEM((tokens, model), BF16),
            pltpu.VMEM((groups, tokens, GROUP * head_dim), BF16),
            pltpu.VMEM((1, model), F32),
        ],
        compiler_params=params(6),
        cost_estimate=pl.CostEstimate(
            flops=2 * tokens * (out_weight.size + weight.size),
            bytes_accessed=2 * (out_weight.size + weight.size),
            transcendentals=0,
        ),
        name="attention_backward",
    )(
        own,
        other,
        out_weight,
        weight,
        turned,
        projected,
        inverse,
        probs,
        attention,
        query_gain,
        key_gain,
        gate,
    )


def sums_kernel(kept_ref, sent_ref, gate_kept_ref, gate_sent_ref, grad_ref, gate_ref):
    grad_ref[...] = (kept_ref[...].astype(F32) + sent_ref[...].astype(F32)).astype(BF16)
    gate_ref[...] = gate_kept_ref[...] + gate_sent_ref[...]


def sums(kept, sent, gate_kept, gate_sent):
    vmem = pl.BlockSpec(memory_space=pltpu.VMEM)
    return pl.pallas_call(
        sums_kernel,
        out_shape=(
            jax.ShapeDtypeStruct(kept.shape, BF16),
            jax.ShapeDtypeStruct(gate_kept.shape, F32),
        ),
        in_specs=[vmem] * 4,
        out_specs=(vmem, vmem),
        compiler_params=params(8),
        name="sums",
    )(kept, sent, gate_kept, gate_sent)


def routed(block, seq_step, pipe_step):
    seq_size, pipe_size = lax.axis_size("seq"), lax.axis_size("pipe")
    route = []
    for i in range(seq_size):
        for j in range(pipe_size):
            target = (i + seq_step) % seq_size * pipe_size + (j + pipe_step) % pipe_size
            route.append((i * pipe_size + j, target))
    return lax.ppermute(block, ("seq", "pipe"), route)


def pair_body(
    segment_input,
    output_grad,
    qkv_weight,
    out_weight,
    query_gain,
    key_gain,
    gate_scale,
    neighbours,
    tile_slot,
):
    stream = segment_input[0]
    upstream = output_grad[0]
    out_local = out_weight[0]
    other_stream = routed(stream, 1, 0)
    weight, turned_weight = regroup(qkv_weight[0], 128, 4, TURNED)
    other_upstream = routed(upstream, 1, 0)
    projected, inverse, probs, attention, kept, sent, out_local = forward(
        neighbours,
        tile_slot,
        stream,
        other_stream,
        weight,
        out_local,
        query_gain,
        key_gain,
        gate_scale,
    )
    kept = routed(kept, 0, 1)
    sent = routed(sent, 1, 1)
    gate_kept, gate_sent, grad_kept, grad_sent = backward(
        upstream,
        other_upstream,
        out_local,
        weight,
        turned_weight,
        projected,
        inverse,
        probs,
        attention,
        query_gain,
        key_gain,
        gate_scale,
    )
    grad_kept = routed(grad_kept, 0, -1)
    grad_sent = routed(grad_sent, 1, -1)
    segment_output = (kept.astype(F32) + sent.astype(F32)).astype(BF16)
    gate_sent = routed(gate_sent, 1, 0)
    token_grad, gate_grad = sums(grad_kept, grad_sent, gate_kept, gate_sent)
    return (segment_output[None], token_grad[None], gate_grad)


def solution(mesh):
    in_specs = (
        P("pipe", ("dp", "seq"), None),
        P("pipe", ("dp", "seq"), None),
        P("pipe", None, "seq", None),
        P("pipe", "seq", None),
        P("pipe", None),
        P("pipe", None),
        P("pipe", None),
        P("dp", None),
        P("dp"),
    )
    out_specs = (
        P("pipe", ("dp", "seq"), None),
        P("pipe", ("dp", "seq"), None),
        P(("dp", "pipe"), "seq"),
    )

    def body(*args):
        one_tile_each = args[0].shape[1] == TILE and args[8].shape[0] == 2
        if mesh.shape["seq"] == 2 and one_tile_each and args[2].shape[2] % GROUP == 0:
            return pair_body(*args)
        return general_body(*args)

    return jax.shard_map(body, mesh=mesh, in_specs=in_specs, out_specs=out_specs, check_vma=False)
```

```python
import functools
import math

import jax
import jax.numpy as jnp
from jax import lax
from jax.experimental import pallas as pl
from jax.experimental.pallas import tpu as pltpu
from jax.sharding import PartitionSpec as P

TILE = 64
EPSILON = 1e-06
F32 = jnp.float32
BF16 = jnp.bfloat16
MIB = 1024 * 1024
GROUP = 4
TURNED = 4


def passed_along(block, axis, distance):
    devices = range(lax.axis_size(axis))
    route = [((i - distance) % len(devices), i) for i in devices]
    return lax.ppermute(block, axis, route)


def slot_lists(neighbours, tile_slot):
    tile_count = tile_slot.shape[0]
    numbering = jnp.arange(tile_count, dtype=jnp.int32)
    placed = (tile_slot[:, None] == numbering[None, :]).astype(jnp.int32)
    tile_of_slot = jnp.sum(placed * numbering[:, None], axis=0)
    chosen = (tile_of_slot[:, None] == numbering[None, :]).astype(jnp.int32)
    listed_tiles = jnp.sum(chosen[:, :, None] * neighbours[None, :, :], axis=1)
    key_valid = listed_tiles >= 0
    safe_tiles = jnp.maximum(listed_tiles, 0)
    matches = (safe_tiles[:, :, None] == numbering[None, None, :]).astype(jnp.int32)
    key_slots = jnp.sum(matches * tile_slot[None, None, :], axis=2)
    return (key_slots, key_valid)


def block_tiles(tile_count):
    return math.gcd(tile_count, max(1, 512 // TILE))


def unit_norm(values):
    spread = jnp.sqrt(jnp.mean(values * values, axis=-1, keepdims=True) + EPSILON)
    return (values / spread, spread)


def probabilities(query_block, key_rows, block_valid):
    scores = jnp.einsum(
        "aihd,ajhd->ahij", query_block, key_rows, preferred_element_type=jnp.float32
    ) * (1.0 / math.sqrt(query_block.shape[-1]))
    key_mask = jnp.repeat(block_valid, TILE, axis=1)
    scores = jnp.where(key_mask[:, None, None, :], scores, -jnp.inf)
    row_max = jnp.max(scores, axis=-1, keepdims=True)
    weights = jnp.exp(scores - row_max)
    return (weights / jnp.sum(weights, axis=-1, keepdims=True)).astype(jnp.bfloat16)


def gathered(tiles_array, block_slots):
    picked = tiles_array[block_slots]
    return picked.reshape(block_slots.shape[0], -1, tiles_array.shape[2], tiles_array.shape[3])


def attend_both(query_tiles, key_tiles, value_tiles, grad_tiles, key_slots, key_valid):
    tile_count = query_tiles.shape[0]
    span = block_tiles(tile_count)
    scale_factor = 1.0 / math.sqrt(query_tiles.shape[-1])
    empty_grad = jnp.zeros(query_tiles.shape, jnp.float32)

    def per_block(accumulators, block_index):
        key_total, value_total = accumulators
        first_tile = block_index * span
        query_block = lax.dynamic_slice_in_dim(query_tiles, first_tile, span, 0)
        grad_block = lax.dynamic_slice_in_dim(grad_tiles, first_tile, span, 0)
        block_slots = lax.dynamic_slice_in_dim(key_slots, first_tile, span, 0)
        block_valid = lax.dynamic_slice_in_dim(key_valid, first_tile, span, 0)
        key_rows = gathered(key_tiles, block_slots)
        value_rows = gathered(value_tiles, block_slots)
        weights = probabilities(query_block, key_rows, block_valid)
        attended = jnp.einsum(
            "ahij,ajhd->aihd", weights, value_rows, preferred_element_type=jnp.float32
        )
        value_part = jnp.einsum(
            "ahij,aihd->ajhd", weights, grad_block, preferred_element_type=jnp.float32
        )
        prob_grad = jnp.einsum(
            "aihd,ajhd->ahij", grad_block, value_rows, preferred_element_type=jnp.float32
        )
        weights_wide = weights.astype(jnp.float32)
        row_delta = jnp.sum(weights_wide * prob_grad, axis=-1, keepdims=True)
        score_grad = (weights_wide * (prob_grad - row_delta) * scale_factor).astype(jnp.bfloat16)
        query_part = jnp.einsum(
            "ahij,ajhd->aihd", score_grad, key_rows, preferred_element_type=jnp.float32
        )
        key_part = jnp.einsum(
            "ahij,aihd->ajhd", score_grad, query_block, preferred_element_type=jnp.float32
        )
        block_shape = (span, block_slots.shape[1]) + query_tiles.shape[1:]
        key_total = key_total.at[block_slots].add(key_part.reshape(block_shape))
        value_total = value_total.at[block_slots].add(value_part.reshape(block_shape))
        return ((key_total, value_total), (attended, query_part))

    totals, parts = lax.scan(
        per_block, (empty_grad, empty_grad), jnp.arange(tile_count // span, dtype=jnp.int32)
    )
    flat_shape = (-1,) + query_tiles.shape[2:]
    return (
        parts[0].reshape(flat_shape),
        parts[1].reshape(flat_shape),
        totals[0].reshape(flat_shape),
        totals[1].reshape(flat_shape),
    )


def general_body(
    segment_input,
    output_grad,
    qkv_weight,
    out_weight,
    query_gain,
    key_gain,
    gate_scale,
    neighbours,
    tile_slot,
):
    key_slots, key_valid = slot_lists(neighbours, tile_slot)
    stream = segment_input[0]
    upstream = output_grad[0]
    model_width = stream.shape[1]
    head_dim = query_gain.shape[1]
    local_heads = qkv_weight.shape[2]
    local_width = local_heads * head_dim
    proj_weight = qkv_weight[0].reshape(model_width, local_heads * 3 * head_dim)
    out_local = out_weight[0]
    gate_row = gate_scale[0]
    query_weights = query_gain[0]
    key_weights = key_gain[0]
    projected = jnp.dot(
        lax.all_gather(stream, "seq", axis=0, tiled=True),
        proj_weight,
        preferred_element_type=jnp.float32,
    )
    all_tokens = projected.shape[0]
    projected = projected.reshape(all_tokens, local_heads, 3, head_dim)
    query_unit, query_spread = unit_norm(projected[:, :, 0])
    key_unit, key_spread = unit_norm(projected[:, :, 1])
    queries = (query_unit * query_weights).astype(jnp.bfloat16)
    keys_normed = (key_unit * key_weights).astype(jnp.bfloat16)
    value_rows = projected[:, :, 2].astype(jnp.bfloat16)
    scaled = (upstream.astype(jnp.float32) * gate_row).astype(jnp.bfloat16)
    attended_grad = jnp.einsum(
        "td,cd->tc",
        lax.all_gather(scaled, "seq", axis=0, tiled=True),
        out_local,
        preferred_element_type=jnp.float32,
    ).astype(jnp.bfloat16)

    def as_tiles(values):
        return values.reshape(-1, TILE, local_heads, head_dim)

    attended, query_grad, key_grad, value_grad = attend_both(
        as_tiles(queries),
        as_tiles(keys_normed),
        as_tiles(value_rows),
        as_tiles(attended_grad),
        key_slots,
        key_valid,
    )
    attended_low = attended.astype(jnp.bfloat16).reshape(all_tokens, local_width)
    rows = attended_low
    attention_out = lax.psum_scatter(
        jnp.dot(rows, out_local, preferred_element_type=jnp.float32),
        "seq",
        scatter_dimension=0,
        tiled=True,
    )
    section_out = (stream.astype(jnp.float32) + gate_row * attention_out).astype(jnp.bfloat16)
    segment_output = passed_along(section_out, "pipe", 1)
    gate_local = lax.psum_scatter(
        jnp.sum(upstream.astype(jnp.float32) * attention_out, axis=0),
        "seq",
        scatter_dimension=0,
        tiled=True,
    )
    query_scaled = query_grad * query_weights
    query_part_grad = (
        query_scaled - query_unit * jnp.mean(query_scaled * query_unit, axis=-1, keepdims=True)
    ) / query_spread
    key_scaled = key_grad * key_weights
    key_part_grad = (
        key_scaled - key_unit * jnp.mean(key_scaled * key_unit, axis=-1, keepdims=True)
    ) / key_spread
    projected_grad = (
        jnp.stack([query_part_grad, key_part_grad, value_grad], axis=2)
        .astype(jnp.bfloat16)
        .reshape(all_tokens, local_heads * 3 * head_dim)
    )
    rows = projected_grad
    stream_grad = lax.psum_scatter(
        jnp.einsum("tc,dc->td", rows, proj_weight, preferred_element_type=jnp.float32).astype(
            jnp.bfloat16
        ),
        "seq",
        scatter_dimension=0,
        tiled=True,
    ).astype(jnp.float32)
    token_grad = (upstream.astype(jnp.float32) + stream_grad).astype(jnp.bfloat16)
    input_grad = passed_along(token_grad, "pipe", -1)
    return (segment_output[None], input_grad[None], gate_local[None])


def dot_nn(a, b):
    return lax.dot_general(a, b, (((1,), (0,)), ((), ())), preferred_element_type=F32)


def dot_nt(a, b):
    return lax.dot_general(a, b, (((1,), (1,)), ((), ())), preferred_element_type=F32)


def dot_tn(a, b):
    return lax.dot_general(a, b, (((0,), (0,)), ((), ())), preferred_element_type=F32)


def params(mebibytes):
    return pltpu.CompilerParams(vmem_limit_bytes=mebibytes * MIB)


class Copies:
    def __init__(self, pairs, semaphores, ahead):
        self.copies = [
            pltpu.make_async_copy(source, target, semaphores.at[i])
            for i, (source, target) in enumerate(pairs)
        ]
        self.ahead = ahead
        self.waited = 0
        for copy in self.copies[:ahead]:
            copy.start()

    def wait(self, count=1):
        for _ in range(count):
            self.copies[self.waited].wait()
            following = self.waited + self.ahead
            if following < len(self.copies):
                self.copies[following].start()
            self.waited += 1


def regroup_kernel(weight_ref, out_ref, turned_ref, read_ref, reads):
    depth, heads, width = weight_ref.shape
    slots, rows = read_ref.shape[:2]
    steps = depth // rows

    def part(step):
        return pl.ds(pl.multiple_of(step * rows, rows), rows)

    def read(step, slot):
        return pltpu.make_async_copy(
            weight_ref.at[part(step)], read_ref.at[slot], reads.at[slot]
        )

    for slot in range(slots):
        read(slot, slot).start()

    @pl.loop(0, steps)
    def _(step):
        slot = lax.rem(step, slots)
        read(step, slot).wait()
        by_head = jnp.swapaxes(read_ref[slot], 0, 1)
        for head in range(heads):
            left = (head % GROUP) * width
            out_ref[head // GROUP, part(step), left : left + width] = by_head[head]
            above = (head + 1) * width - (heads * width - turned_ref.shape[0])
            if above > 0:
                turned_ref[above - width : above, part(step)] = by_head[head].T

        @pl.when(step + slots < steps)
        def _():
            read(step + slots, slot).start()


def regroup(weight, rows, slots, turned):
    depth, heads, width = weight.shape
    out = (heads // GROUP, depth, GROUP * width)
    return pl.pallas_call(
        regroup_kernel,
        out_shape=(
            pltpu.VMEM(out, weight.dtype),
            pltpu.VMEM((turned * width, depth), weight.dtype),
        ),
        in_specs=[pl.BlockSpec(memory_space=pl.ANY)],
        out_specs=(pl.BlockSpec(memory_space=pltpu.VMEM),) * 2,
        scratch_shapes=[
            pltpu.VMEM((slots, rows, heads, width), weight.dtype),
            pltpu.SemaphoreType.DMA((slots,)),
        ],
        compiler_params=params(9),
        cost_estimate=pl.CostEstimate(
            flops=0, bytes_accessed=4 * depth * heads * width, transcendentals=0
        ),
        name="regroup",
    )(pltpu.with_memory_space_constraint(weight, pltpu.HBM))


def listed_slots(neighbours_ref, tile_slot_ref):
    tiles, places = neighbours_ref.shape
    one, zero = jnp.int32(1), jnp.int32(0)
    allowed = [[zero] * tiles for _ in range(tiles)]
    for t in range(tiles):
        for u in range(tiles):
            listed = zero
            for k in range(places):
                listed = jnp.where(neighbours_ref[t, k] == u, one, listed)
            for r in range(tiles):
                for c in range(tiles):
                    here = (tile_slot_ref[t] == r) & (tile_slot_ref[u] == c)
                    allowed[r][c] = jnp.where(here, listed, allowed[r][c])
    return allowed


def normed(rows, gain):
    inverse = lax.rsqrt(jnp.mean(rows * rows, axis=-1, keepdims=True) + EPSILON)
    unit = rows * inverse
    return unit, inverse, (unit * gain).astype(BF16)


def forward_kernel(
    neighbours_ref,
    tile_slot_ref,
    own_ref,
    other_ref,
    weight_ref,
    out_weight_ref,
    query_gain_ref,
    key_gain_ref,
    gate_ref,
    projected_ref,
    inverse_ref,
    probs_ref,
    attention_ref,
    kept_ref,
    sent_ref,
    out_weight_buffer,
    tokens_ref,
    semaphores,
):
    local, model = own_ref.shape
    tokens = 2 * local
    width = query_gain_ref.shape[1]
    groups = weight_ref.shape[0]
    rows = GROUP * width

    def out_weight_part(group):
        place = pl.ds(group * rows, rows)
        return out_weight_ref.at[place], out_weight_buffer.at[place]

    copies = Copies([out_weight_part(group) for group in range(groups)], semaphores, groups)

    tokens_ref[:local, :] = own_ref[...]
    tokens_ref[local:, :] = other_ref[...]
    allowed = listed_slots(neighbours_ref, tile_slot_ref)
    mine = lax.axis_index("seq")
    row_half = lax.broadcasted_iota(jnp.int32, (tokens, tokens), 0) // local
    column_half = lax.broadcasted_iota(jnp.int32, (tokens, tokens), 1) // local
    row_slot = jnp.where(row_half == 0, mine, 1 - mine)
    column_slot = jnp.where(column_half == 0, mine, 1 - mine)
    table = jnp.zeros((tokens, tokens), jnp.int32)
    for r in range(2):
        for c in range(2):
            table = jnp.where((row_slot == r) & (column_slot == c), allowed[r][c], table)
    bias = jnp.where(table > 0, 0.0, -jnp.inf).astype(F32)

    def project(group):
        projected_ref[group] = dot_nn(tokens_ref[...], weight_ref[group])

    def attend(group):
        heads = range(GROUP)
        operands = []
        for place in range(2 * GROUP):
            gain_ref = (query_gain_ref, key_gain_ref)[place % 2]
            left = (3 * (place // 2) + place % 2) * width
            part = slice(left, left + width)
            unit, inverse, operand = normed(projected_ref[group, :, part], gain_ref[...])
            projected_ref[group, :, part] = unit
            inverse_ref[group, :, place : place + 1] = inverse
            operands.append(operand)
        scale_factor = 1.0 / math.sqrt(width)
        scores = [dot_nt(operands[2 * h], operands[2 * h + 1]) * scale_factor + bias for h in heads]
        tops = [jnp.max(scores[h], axis=-1, keepdims=True) for h in heads]
        weights = [jnp.exp(scores[h] - tops[h]) for h in heads]
        sums = [jnp.sum(weights[h], axis=-1, keepdims=True) for h in heads]
        probs = [(weights[h] / sums[h]).astype(BF16) for h in heads]
        attended = []
        for h in heads:
            probs_ref[GROUP * group + h] = probs[h]
            left = (3 * h + 2) * width
            value = projected_ref[group, :, left : left + width].astype(BF16)
            attended.append(dot_nn(probs[h], value).astype(BF16))
        return jnp.concatenate(attended, axis=1)

    def share(group, attended):
        return dot_nn(attended, out_weight_buffer[group * rows : (group + 1) * rows, :])

    project(0)
    attended = attend(0)
    for group in range(1, groups):
        project(group)
        copies.wait()
        following = attend(group)
        if group == 1:
            attention_ref[...] = share(0, attended)
        else:
            attention_ref[...] += share(group - 1, attended)
        attended = following
    copies.wait()
    total = share(groups - 1, attended)
    if groups > 1:
        total += attention_ref[...]
    attention_ref[...] = total
    gate = gate_ref[...]
    kept_ref[...] = (own_ref[...].astype(F32) + gate * total[:local]).astype(BF16)
    sent_ref[...] = (gate * total[local:]).astype(BF16)


def forward(neighbours, tile_slot, own, other, weight, out_weight, query_gain, key_gain, gate):
    local, model = own.shape
    groups, _, wide = weight.shape
    tokens = 2 * local
    weight = pltpu.with_memory_space_constraint(weight, pltpu.VMEM)
    out_weight = pltpu.with_memory_space_constraint(out_weight, pltpu.HBM)
    smem = pl.BlockSpec(memory_space=pltpu.SMEM)
    vmem = pl.BlockSpec(memory_space=pltpu.VMEM)
    hbm = pl.BlockSpec(memory_space=pl.ANY)
    return pl.pallas_call(
        forward_kernel,
        out_shape=(
            jax.ShapeDtypeStruct((groups, tokens, wide), F32),
            jax.ShapeDtypeStruct((groups, tokens, 2 * GROUP), F32),
            jax.ShapeDtypeStruct((GROUP * groups, tokens, tokens), BF16),
            jax.ShapeDtypeStruct((tokens, model), F32),
            jax.ShapeDtypeStruct((local, model), BF16),
            jax.ShapeDtypeStruct((local, model), BF16),
            pltpu.VMEM(out_weight.shape, BF16),
        ),
        in_specs=[smem, smem, vmem, vmem, vmem, hbm, vmem, vmem, vmem],
        out_specs=(vmem,) * 7,
        scratch_shapes=[
            pltpu.VMEM((tokens, model), BF16),
            pltpu.SemaphoreType.DMA((groups,)),
        ],
        compiler_params=params(6),
        cost_estimate=pl.CostEstimate(
            flops=2 * tokens * (weight.size + out_weight.size),
            bytes_accessed=2 * (weight.size + out_weight.size),
            transcendentals=0,
        ),
        name="attention_forward",
    )(neighbours, tile_slot, own, other, weight, out_weight, query_gain, key_gain, gate)


def input_grad(grad_ref, weight_ref, turned_ref, own_ref, kept_ref, sent_ref):
    local, model = own_ref.shape
    groups, _, wide = grad_ref.shape
    streamed = groups * wide - turned_ref.shape[0]
    block = 512
    for start in range(0, model, block):
        part = slice(start, start + block)
        total = None
        for group in range(groups):
            first = group * wide
            cut = min(max(streamed - first, 0), wide)
            if cut < wide:
                rows = slice(first + cut - streamed, first + wide - streamed)
                product = dot_nn(grad_ref[group, :, cut:], turned_ref[rows, part])
                total = product if total is None else total + product
            if cut > 0:
                product = dot_nt(weight_ref[group, part, :cut], grad_ref[group, :, :cut]).T
                total = product if total is None else total + product
        kept_ref[:, part] = (own_ref[:, part].astype(F32) + total[:local]).astype(BF16)
        sent_ref[:, part] = total[local:].astype(BF16)


def backward_kernel(
    own_ref,
    other_ref,
    out_weight_ref,
    weight_ref,
    turned_ref,
    projected_ref,
    inverse_ref,
    probs_ref,
    attention_ref,
    query_gain_ref,
    key_gain_ref,
    gate_ref,
    gate_kept_ref,
    gate_sent_ref,
    kept_ref,
    sent_ref,
    grad_ref,
    scaled_ref,
    attended_grad_ref,
    gate_grad_ref,
):
    local = own_ref.shape[0]
    width = query_gain_ref.shape[1]
    groups = grad_ref.shape[0]
    rows = GROUP * width

    gate = gate_ref[...]
    own, other = own_ref[...].astype(F32), other_ref[...].astype(F32)
    scaled_ref[:local, :] = (own * gate).astype(BF16)
    scaled_ref[local:, :] = (other * gate).astype(BF16)
    gate_grad_ref[...] = jnp.sum(
        own * attention_ref[:local, :] + other * attention_ref[local:, :], axis=0, keepdims=True
    )
    half = gate_kept_ref.shape[1]
    mine = lax.axis_index("seq")
    gate_kept_ref[...] = gate_grad_ref[:, pl.ds(pl.multiple_of(mine * half, half), half)]
    gate_sent_ref[...] = gate_grad_ref[:, pl.ds(pl.multiple_of((1 - mine) * half, half), half)]

    def attended_grad(group):
        part = slice(group * rows, (group + 1) * rows)
        product = dot_nt(scaled_ref[...], out_weight_ref[part, :])
        attended_grad_ref[group] = product.astype(BF16)

    def attend_backward(group):
        heads = range(GROUP)
        query_gain, key_gain = query_gain_ref[...], key_gain_ref[...]
        scale_factor = 1.0 / math.sqrt(width)

        def part(head, index):
            left = (3 * head + index) * width
            return slice(left, left + width)

        def inverse(head, index):
            return inverse_ref[group, :, 2 * head + index : 2 * head + index + 1]

        grads = [attended_grad_ref[group, :, h * width : (h + 1) * width] for h in heads]
        values = [projected_ref[group, :, part(h, 2)].astype(BF16) for h in heads]
        prob_grads = [dot_nt(grads[h], values[h]) for h in heads]
        for h in heads:
            product = dot_tn(probs_ref[GROUP * group + h], grads[h])
            grad_ref[group, :, part(h, 2)] = product.astype(BF16)
        wide = [probs_ref[GROUP * group + h].astype(F32) for h in heads]
        deltas = [jnp.sum(wide[h] * prob_grads[h], axis=-1, keepdims=True) for h in heads]
        score_grads = [
            (wide[h] * (prob_grads[h] - deltas[h]) * scale_factor).astype(BF16) for h in heads
        ]
        units = [[projected_ref[group, :, part(h, index)] for index in range(2)] for h in heads]
        keys = [(units[h][1] * key_gain).astype(BF16) for h in heads]
        queries = [(units[h][0] * query_gain).astype(BF16) for h in heads]
        scaled = [
            [
                dot_nn(score_grads[h], keys[h]) * query_gain,
                dot_tn(score_grads[h], queries[h]) * key_gain,
            ]
            for h in heads
        ]
        means = [
            [jnp.mean(scaled[h][i] * units[h][i], axis=-1, keepdims=True) for i in range(2)]
            for h in heads
        ]
        for h in heads:
            for i in range(2):
                grad_ref[group, :, part(h, i)] = (
                    (scaled[h][i] - units[h][i] * means[h][i]) * inverse(h, i)
                ).astype(BF16)

    attended_grad(0)
    for group in range(groups):
        if group + 1 < groups:
            attended_grad(group + 1)
        attend_backward(group)
    input_grad(grad_ref, weight_ref, turned_ref, own_ref, kept_ref, sent_ref)


def backward(
    own,
    other,
    out_weight,
    weight,
    turned,
    projected,
    inverse,
    probs,
    attention,
    query_gain,
    key_gain,
    gate,
):
    local, model = own.shape
    groups, tokens, wide = projected.shape
    head_dim = query_gain.shape[1]
    out_weight = pltpu.with_memory_space_constraint(out_weight, pltpu.VMEM)
    weight = pltpu.with_memory_space_constraint(weight, pltpu.VMEM)
    turned = pltpu.with_memory_space_constraint(turned, pltpu.VMEM)
    vmem = pl.BlockSpec(memory_space=pltpu.VMEM)
    return pl.pallas_call(
        backward_kernel,
        out_shape=(
            jax.ShapeDtypeStruct((1, model // 2), F32),
            jax.ShapeDtypeStruct((1, model // 2), F32),
            jax.ShapeDtypeStruct((local, model), BF16),
            jax.ShapeDtypeStruct((local, model), BF16),
        ),
        in_specs=[vmem] * 12,
        out_specs=(vmem,) * 4,
        scratch_shapes=[
            pltpu.VMEM((groups, tokens, wide), BF16),
            pltpu.VMEM((tokens, model), BF16),
            pltpu.VMEM((groups, tokens, GROUP * head_dim), BF16),
            pltpu.VMEM((1, model), F32),
        ],
        compiler_params=params(6),
        cost_estimate=pl.CostEstimate(
            flops=2 * tokens * (out_weight.size + weight.size),
            bytes_accessed=2 * (out_weight.size + weight.size),
            transcendentals=0,
        ),
        name="attention_backward",
    )(
        own,
        other,
        out_weight,
        weight,
        turned,
        projected,
        inverse,
        probs,
        attention,
        query_gain,
        key_gain,
        gate,
    )


def sums_kernel(sent_ref, kept_ref, gate_kept_ref, gate_sent_ref, grad_ref, gate_ref):
    grad_ref[...] = (kept_ref[...].astype(F32) + sent_ref[...].astype(F32)).astype(BF16)
    gate_ref[...] = gate_kept_ref[...] + gate_sent_ref[...]


def sums(sent, kept, gate_kept, gate_sent):
    vmem = pl.BlockSpec(memory_space=pltpu.VMEM)
    return pl.pallas_call(
        sums_kernel,
        out_shape=(
            jax.ShapeDtypeStruct(kept.shape, BF16),
            jax.ShapeDtypeStruct(gate_kept.shape, F32),
        ),
        in_specs=[vmem] * 4,
        out_specs=(vmem, vmem),
        compiler_params=params(8),
        name="sums",
    )(sent, kept, gate_kept, gate_sent)


def routed(block, seq_step, pipe_step):
    seq_size, pipe_size = lax.axis_size("seq"), lax.axis_size("pipe")
    route = []
    for i in range(seq_size):
        for j in range(pipe_size):
            target = (i + seq_step) % seq_size * pipe_size + (j + pipe_step) % pipe_size
            route.append((i * pipe_size + j, target))
    return lax.ppermute(block, ("seq", "pipe"), route)


def pair_body(
    segment_input,
    output_grad,
    qkv_weight,
    out_weight,
    query_gain,
    key_gain,
    gate_scale,
    neighbours,
    tile_slot,
):
    stream = segment_input[0]
    upstream = output_grad[0]
    out_local = out_weight[0]
    other_stream = routed(stream, 1, 0)
    weight, turned_weight = regroup(qkv_weight[0], 128, 6, TURNED)
    other_upstream = routed(upstream, 1, 0)
    projected, inverse, probs, attention, kept, sent, out_local = forward(
        neighbours,
        tile_slot,
        stream,
        other_stream,
        weight,
        out_local,
        query_gain,
        key_gain,
        gate_scale,
    )
    kept = routed(kept, 0, 1)
    sent = routed(sent, 1, 1)
    gate_kept, gate_sent, grad_kept, grad_sent = backward(
        upstream,
        other_upstream,
        out_local,
        weight,
        turned_weight,
        projected,
        inverse,
        probs,
        attention,
        query_gain,
        key_gain,
        gate_scale,
    )
    grad_sent = routed(grad_sent, 1, -1)
    grad_kept = routed(grad_kept, 0, -1)
    segment_output = (kept.astype(F32) + sent.astype(F32)).astype(BF16)
    segment_output, gate_sent = lax.optimization_barrier((segment_output, gate_sent))
    gate_sent = routed(gate_sent, 1, 0)
    token_grad, gate_grad = sums(grad_sent, grad_kept, gate_kept, gate_sent)
    return (segment_output[None], token_grad[None], gate_grad)


def solution(mesh):
    in_specs = (
        P("pipe", ("dp", "seq"), None),
        P("pipe", ("dp", "seq"), None),
        P("pipe", None, "seq", None),
        P("pipe", "seq", None),
        P("pipe", None),
        P("pipe", None),
        P("pipe", None),
        P("dp", None),
        P("dp"),
    )
    out_specs = (
        P("pipe", ("dp", "seq"), None),
        P("pipe", ("dp", "seq"), None),
        P(("dp", "pipe"), "seq"),
    )

    def body(*args):
        one_tile_each = args[0].shape[1] == TILE and args[8].shape[0] == 2
        if mesh.shape["seq"] == 2 and one_tile_each and args[2].shape[2] % GROUP == 0:
            return pair_body(*args)
        return general_body(*args)

    return jax.shard_map(body, mesh=mesh, in_specs=in_specs, out_specs=out_specs, check_vma=False)
```

```python
import functools
import math

import jax
import jax.numpy as jnp
from jax import lax
from jax.experimental import pallas as pl
from jax.experimental.pallas import tpu as pltpu
from jax.sharding import PartitionSpec as P

TILE = 64
EPSILON = 1e-06
F32 = jnp.float32
BF16 = jnp.bfloat16
MIB = 1024 * 1024
GROUP = 4
TURNED = 6


def passed_along(block, axis, distance):
    devices = range(lax.axis_size(axis))
    route = [((i - distance) % len(devices), i) for i in devices]
    return lax.ppermute(block, axis, route)


def slot_lists(neighbours, tile_slot):
    tile_count = tile_slot.shape[0]
    numbering = jnp.arange(tile_count, dtype=jnp.int32)
    placed = (tile_slot[:, None] == numbering[None, :]).astype(jnp.int32)
    tile_of_slot = jnp.sum(placed * numbering[:, None], axis=0)
    chosen = (tile_of_slot[:, None] == numbering[None, :]).astype(jnp.int32)
    listed_tiles = jnp.sum(chosen[:, :, None] * neighbours[None, :, :], axis=1)
    key_valid = listed_tiles >= 0
    safe_tiles = jnp.maximum(listed_tiles, 0)
    matches = (safe_tiles[:, :, None] == numbering[None, None, :]).astype(jnp.int32)
    key_slots = jnp.sum(matches * tile_slot[None, None, :], axis=2)
    return (key_slots, key_valid)


def block_tiles(tile_count):
    return math.gcd(tile_count, max(1, 512 // TILE))


def unit_norm(values):
    spread = jnp.sqrt(jnp.mean(values * values, axis=-1, keepdims=True) + EPSILON)
    return (values / spread, spread)


def probabilities(query_block, key_rows, block_valid):
    scores = jnp.einsum(
        "aihd,ajhd->ahij", query_block, key_rows, preferred_element_type=jnp.float32
    ) * (1.0 / math.sqrt(query_block.shape[-1]))
    key_mask = jnp.repeat(block_valid, TILE, axis=1)
    scores = jnp.where(key_mask[:, None, None, :], scores, -jnp.inf)
    row_max = jnp.max(scores, axis=-1, keepdims=True)
    weights = jnp.exp(scores - row_max)
    return (weights / jnp.sum(weights, axis=-1, keepdims=True)).astype(jnp.bfloat16)


def gathered(tiles_array, block_slots):
    picked = tiles_array[block_slots]
    return picked.reshape(block_slots.shape[0], -1, tiles_array.shape[2], tiles_array.shape[3])


def attend_both(query_tiles, key_tiles, value_tiles, grad_tiles, key_slots, key_valid):
    tile_count = query_tiles.shape[0]
    span = block_tiles(tile_count)
    scale_factor = 1.0 / math.sqrt(query_tiles.shape[-1])
    empty_grad = jnp.zeros(query_tiles.shape, jnp.float32)

    def per_block(accumulators, block_index):
        key_total, value_total = accumulators
        first_tile = block_index * span
        query_block = lax.dynamic_slice_in_dim(query_tiles, first_tile, span, 0)
        grad_block = lax.dynamic_slice_in_dim(grad_tiles, first_tile, span, 0)
        block_slots = lax.dynamic_slice_in_dim(key_slots, first_tile, span, 0)
        block_valid = lax.dynamic_slice_in_dim(key_valid, first_tile, span, 0)
        key_rows = gathered(key_tiles, block_slots)
        value_rows = gathered(value_tiles, block_slots)
        weights = probabilities(query_block, key_rows, block_valid)
        attended = jnp.einsum(
            "ahij,ajhd->aihd", weights, value_rows, preferred_element_type=jnp.float32
        )
        value_part = jnp.einsum(
            "ahij,aihd->ajhd", weights, grad_block, preferred_element_type=jnp.float32
        )
        prob_grad = jnp.einsum(
            "aihd,ajhd->ahij", grad_block, value_rows, preferred_element_type=jnp.float32
        )
        weights_wide = weights.astype(jnp.float32)
        row_delta = jnp.sum(weights_wide * prob_grad, axis=-1, keepdims=True)
        score_grad = (weights_wide * (prob_grad - row_delta) * scale_factor).astype(jnp.bfloat16)
        query_part = jnp.einsum(
            "ahij,ajhd->aihd", score_grad, key_rows, preferred_element_type=jnp.float32
        )
        key_part = jnp.einsum(
            "ahij,aihd->ajhd", score_grad, query_block, preferred_element_type=jnp.float32
        )
        block_shape = (span, block_slots.shape[1]) + query_tiles.shape[1:]
        key_total = key_total.at[block_slots].add(key_part.reshape(block_shape))
        value_total = value_total.at[block_slots].add(value_part.reshape(block_shape))
        return ((key_total, value_total), (attended, query_part))

    totals, parts = lax.scan(
        per_block, (empty_grad, empty_grad), jnp.arange(tile_count // span, dtype=jnp.int32)
    )
    flat_shape = (-1,) + query_tiles.shape[2:]
    return (
        parts[0].reshape(flat_shape),
        parts[1].reshape(flat_shape),
        totals[0].reshape(flat_shape),
        totals[1].reshape(flat_shape),
    )


def general_body(
    segment_input,
    output_grad,
    qkv_weight,
    out_weight,
    query_gain,
    key_gain,
    gate_scale,
    neighbours,
    tile_slot,
):
    key_slots, key_valid = slot_lists(neighbours, tile_slot)
    stream = segment_input[0]
    upstream = output_grad[0]
    model_width = stream.shape[1]
    head_dim = query_gain.shape[1]
    local_heads = qkv_weight.shape[2]
    local_width = local_heads * head_dim
    proj_weight = qkv_weight[0].reshape(model_width, local_heads * 3 * head_dim)
    out_local = out_weight[0]
    gate_row = gate_scale[0]
    query_weights = query_gain[0]
    key_weights = key_gain[0]
    projected = jnp.dot(
        lax.all_gather(stream, "seq", axis=0, tiled=True),
        proj_weight,
        preferred_element_type=jnp.float32,
    )
    all_tokens = projected.shape[0]
    projected = projected.reshape(all_tokens, local_heads, 3, head_dim)
    query_unit, query_spread = unit_norm(projected[:, :, 0])
    key_unit, key_spread = unit_norm(projected[:, :, 1])
    queries = (query_unit * query_weights).astype(jnp.bfloat16)
    keys_normed = (key_unit * key_weights).astype(jnp.bfloat16)
    value_rows = projected[:, :, 2].astype(jnp.bfloat16)
    scaled = (upstream.astype(jnp.float32) * gate_row).astype(jnp.bfloat16)
    attended_grad = jnp.einsum(
        "td,cd->tc",
        lax.all_gather(scaled, "seq", axis=0, tiled=True),
        out_local,
        preferred_element_type=jnp.float32,
    ).astype(jnp.bfloat16)

    def as_tiles(values):
        return values.reshape(-1, TILE, local_heads, head_dim)

    attended, query_grad, key_grad, value_grad = attend_both(
        as_tiles(queries),
        as_tiles(keys_normed),
        as_tiles(value_rows),
        as_tiles(attended_grad),
        key_slots,
        key_valid,
    )
    attended_low = attended.astype(jnp.bfloat16).reshape(all_tokens, local_width)
    rows = attended_low
    attention_out = lax.psum_scatter(
        jnp.dot(rows, out_local, preferred_element_type=jnp.float32),
        "seq",
        scatter_dimension=0,
        tiled=True,
    )
    section_out = (stream.astype(jnp.float32) + gate_row * attention_out).astype(jnp.bfloat16)
    segment_output = passed_along(section_out, "pipe", 1)
    gate_local = lax.psum_scatter(
        jnp.sum(upstream.astype(jnp.float32) * attention_out, axis=0),
        "seq",
        scatter_dimension=0,
        tiled=True,
    )
    query_scaled = query_grad * query_weights
    query_part_grad = (
        query_scaled - query_unit * jnp.mean(query_scaled * query_unit, axis=-1, keepdims=True)
    ) / query_spread
    key_scaled = key_grad * key_weights
    key_part_grad = (
        key_scaled - key_unit * jnp.mean(key_scaled * key_unit, axis=-1, keepdims=True)
    ) / key_spread
    projected_grad = (
        jnp.stack([query_part_grad, key_part_grad, value_grad], axis=2)
        .astype(jnp.bfloat16)
        .reshape(all_tokens, local_heads * 3 * head_dim)
    )
    rows = projected_grad
    stream_grad = lax.psum_scatter(
        jnp.einsum("tc,dc->td", rows, proj_weight, preferred_element_type=jnp.float32).astype(
            jnp.bfloat16
        ),
        "seq",
        scatter_dimension=0,
        tiled=True,
    ).astype(jnp.float32)
    token_grad = (upstream.astype(jnp.float32) + stream_grad).astype(jnp.bfloat16)
    input_grad = passed_along(token_grad, "pipe", -1)
    return (segment_output[None], input_grad[None], gate_local[None])


def dot_nn(a, b):
    return lax.dot_general(a, b, (((1,), (0,)), ((), ())), preferred_element_type=F32)


def dot_nt(a, b):
    return lax.dot_general(a, b, (((1,), (1,)), ((), ())), preferred_element_type=F32)


def dot_tn(a, b):
    return lax.dot_general(a, b, (((0,), (0,)), ((), ())), preferred_element_type=F32)


def params(mebibytes):
    return pltpu.CompilerParams(vmem_limit_bytes=mebibytes * MIB)


class Copies:
    def __init__(self, pairs, semaphores, ahead):
        self.copies = [
            pltpu.make_async_copy(source, target, semaphores.at[i])
            for i, (source, target) in enumerate(pairs)
        ]
        self.ahead = ahead
        self.waited = 0
        for copy in self.copies[:ahead]:
            copy.start()

    def wait(self, count=1):
        for _ in range(count):
            self.copies[self.waited].wait()
            following = self.waited + self.ahead
            if following < len(self.copies):
                self.copies[following].start()
            self.waited += 1


def regroup_kernel(weight_ref, out_ref, turned_ref, read_ref, reads):
    depth, heads, width = weight_ref.shape
    slots, rows = read_ref.shape[:2]
    steps = depth // rows

    def part(step):
        return pl.ds(pl.multiple_of(step * rows, rows), rows)

    def read(step, slot):
        return pltpu.make_async_copy(
            weight_ref.at[part(step)], read_ref.at[slot], reads.at[slot]
        )

    for slot in range(slots):
        read(slot, slot).start()

    @pl.loop(0, steps)
    def _(step):
        slot = lax.rem(step, slots)
        read(step, slot).wait()
        by_head = jnp.swapaxes(read_ref[slot], 0, 1)
        for head in range(heads):
            left = (head % GROUP) * width
            out_ref[head // GROUP, part(step), left : left + width] = by_head[head]
            above = (head + 1) * width - (heads * width - turned_ref.shape[0])
            if above > 0:
                turned_ref[above - width : above, part(step)] = by_head[head].T

        @pl.when(step + slots < steps)
        def _():
            read(step + slots, slot).start()


def regroup(weight, rows, slots, turned):
    depth, heads, width = weight.shape
    out = (heads // GROUP, depth, GROUP * width)
    return pl.pallas_call(
        regroup_kernel,
        out_shape=(
            pltpu.VMEM(out, weight.dtype),
            pltpu.VMEM((turned * width, depth), weight.dtype),
        ),
        in_specs=[pl.BlockSpec(memory_space=pl.ANY)],
        out_specs=(pl.BlockSpec(memory_space=pltpu.VMEM),) * 2,
        scratch_shapes=[
            pltpu.VMEM((slots, rows, heads, width), weight.dtype),
            pltpu.SemaphoreType.DMA((slots,)),
        ],
        compiler_params=params(6),
        cost_estimate=pl.CostEstimate(
            flops=0, bytes_accessed=4 * depth * heads * width, transcendentals=0
        ),
        name="regroup",
    )(pltpu.with_memory_space_constraint(weight, pltpu.HBM))


def listed_slots(neighbours_ref, tile_slot_ref):
    tiles, places = neighbours_ref.shape
    one, zero = jnp.int32(1), jnp.int32(0)
    allowed = [[zero] * tiles for _ in range(tiles)]
    for t in range(tiles):
        for u in range(tiles):
            listed = zero
            for k in range(places):
                listed = jnp.where(neighbours_ref[t, k] == u, one, listed)
            for r in range(tiles):
                for c in range(tiles):
                    here = (tile_slot_ref[t] == r) & (tile_slot_ref[u] == c)
                    allowed[r][c] = jnp.where(here, listed, allowed[r][c])
    return allowed


def normed(rows, gain):
    inverse = lax.rsqrt(jnp.mean(rows * rows, axis=-1, keepdims=True) + EPSILON)
    unit = rows * inverse
    return unit, inverse, (unit * gain).astype(BF16)


def forward_kernel(
    neighbours_ref,
    tile_slot_ref,
    own_ref,
    other_ref,
    weight_ref,
    out_weight_ref,
    query_gain_ref,
    key_gain_ref,
    gate_ref,
    projected_ref,
    inverse_ref,
    probs_ref,
    attention_ref,
    kept_ref,
    sent_ref,
    out_weight_buffer,
    tokens_ref,
    semaphores,
):
    local, model = own_ref.shape
    tokens = 2 * local
    width = query_gain_ref.shape[1]
    groups = weight_ref.shape[0]
    rows = GROUP * width

    def out_weight_part(group):
        place = pl.ds(group * rows, rows)
        return out_weight_ref.at[place], out_weight_buffer.at[place]

    copies = Copies([out_weight_part(group) for group in range(groups)], semaphores, groups)

    tokens_ref[:local, :] = own_ref[...]
    tokens_ref[local:, :] = other_ref[...]
    allowed = listed_slots(neighbours_ref, tile_slot_ref)
    mine = lax.axis_index("seq")
    row_half = lax.broadcasted_iota(jnp.int32, (tokens, tokens), 0) // local
    column_half = lax.broadcasted_iota(jnp.int32, (tokens, tokens), 1) // local
    row_slot = jnp.where(row_half == 0, mine, 1 - mine)
    column_slot = jnp.where(column_half == 0, mine, 1 - mine)
    table = jnp.zeros((tokens, tokens), jnp.int32)
    for r in range(2):
        for c in range(2):
            table = jnp.where((row_slot == r) & (column_slot == c), allowed[r][c], table)
    bias = jnp.where(table > 0, 0.0, -jnp.inf).astype(F32)

    def project(group):
        projected_ref[group] = dot_nn(tokens_ref[...], weight_ref[group])

    def attend(group):
        heads = range(GROUP)
        operands = []
        for place in range(2 * GROUP):
            gain_ref = (query_gain_ref, key_gain_ref)[place % 2]
            left = (3 * (place // 2) + place % 2) * width
            part = slice(left, left + width)
            unit, inverse, operand = normed(projected_ref[group, :, part], gain_ref[...])
            projected_ref[group, :, part] = unit
            inverse_ref[group, :, place : place + 1] = inverse
            operands.append(operand)
        scale_factor = 1.0 / math.sqrt(width)
        scores = [dot_nt(operands[2 * h], operands[2 * h + 1]) * scale_factor + bias for h in heads]
        tops = [jnp.max(scores[h], axis=-1, keepdims=True) for h in heads]
        weights = [jnp.exp(scores[h] - tops[h]) for h in heads]
        sums = [jnp.sum(weights[h], axis=-1, keepdims=True) for h in heads]
        probs = [(weights[h] / sums[h]).astype(BF16) for h in heads]
        attended = []
        for h in heads:
            probs_ref[GROUP * group + h] = probs[h]
            left = (3 * h + 2) * width
            value = projected_ref[group, :, left : left + width].astype(BF16)
            attended.append(dot_nn(probs[h], value).astype(BF16))
        return jnp.concatenate(attended, axis=1)

    def share(group, attended):
        return dot_nn(attended, out_weight_buffer[group * rows : (group + 1) * rows, :])

    project(0)
    attended = attend(0)
    for group in range(1, groups):
        project(group)
        copies.wait()
        following = attend(group)
        if group == 1:
            attention_ref[...] = share(0, attended)
        else:
            attention_ref[...] += share(group - 1, attended)
        attended = following
    copies.wait()
    total = share(groups - 1, attended)
    if groups > 1:
        total += attention_ref[...]
    attention_ref[...] = total
    gate = gate_ref[...]
    kept_ref[...] = (own_ref[...].astype(F32) + gate * total[:local]).astype(BF16)
    sent_ref[...] = (gate * total[local:]).astype(BF16)


def forward(neighbours, tile_slot, own, other, weight, out_weight, query_gain, key_gain, gate):
    local, model = own.shape
    groups, _, wide = weight.shape
    tokens = 2 * local
    weight = pltpu.with_memory_space_constraint(weight, pltpu.VMEM)
    out_weight = pltpu.with_memory_space_constraint(out_weight, pltpu.HBM)
    smem = pl.BlockSpec(memory_space=pltpu.SMEM)
    vmem = pl.BlockSpec(memory_space=pltpu.VMEM)
    hbm = pl.BlockSpec(memory_space=pl.ANY)
    return pl.pallas_call(
        forward_kernel,
        out_shape=(
            jax.ShapeDtypeStruct((groups, tokens, wide), F32),
            jax.ShapeDtypeStruct((groups, tokens, 2 * GROUP), F32),
            jax.ShapeDtypeStruct((GROUP * groups, tokens, tokens), BF16),
            jax.ShapeDtypeStruct((tokens, model), F32),
            jax.ShapeDtypeStruct((local, model), BF16),
            jax.ShapeDtypeStruct((local, model), BF16),
            pltpu.VMEM(out_weight.shape, BF16),
        ),
        in_specs=[smem, smem, vmem, vmem, vmem, hbm, vmem, vmem, vmem],
        out_specs=(vmem,) * 7,
        scratch_shapes=[
            pltpu.VMEM((tokens, model), BF16),
            pltpu.SemaphoreType.DMA((groups,)),
        ],
        compiler_params=params(6),
        cost_estimate=pl.CostEstimate(
            flops=2 * tokens * (weight.size + out_weight.size),
            bytes_accessed=2 * (weight.size + out_weight.size),
            transcendentals=0,
        ),
        name="attention_forward",
    )(neighbours, tile_slot, own, other, weight, out_weight, query_gain, key_gain, gate)


def input_grad(grad_ref, weight_ref, turned_ref, own_ref, kept_ref, sent_ref):
    local, model = own_ref.shape
    groups, _, wide = grad_ref.shape
    streamed = groups * wide - turned_ref.shape[0]
    block = 512
    for start in range(0, model, block):
        part = slice(start, start + block)
        total = None
        for group in range(groups):
            first = group * wide
            cut = min(max(streamed - first, 0), wide)
            if cut < wide:
                rows = slice(first + cut - streamed, first + wide - streamed)
                product = dot_nn(grad_ref[group, :, cut:], turned_ref[rows, part])
                total = product if total is None else total + product
            if cut > 0:
                product = dot_nt(weight_ref[group, part, :cut], grad_ref[group, :, :cut]).T
                total = product if total is None else total + product
        kept_ref[:, part] = (own_ref[:, part].astype(F32) + total[:local]).astype(BF16)
        sent_ref[:, part] = total[local:].astype(BF16)


def backward_kernel(
    own_ref,
    other_ref,
    out_weight_ref,
    weight_ref,
    turned_ref,
    projected_ref,
    inverse_ref,
    probs_ref,
    attention_ref,
    query_gain_ref,
    key_gain_ref,
    gate_ref,
    gate_kept_ref,
    gate_sent_ref,
    kept_ref,
    sent_ref,
    grad_ref,
    scaled_ref,
    attended_grad_ref,
    gate_grad_ref,
):
    local = own_ref.shape[0]
    width = query_gain_ref.shape[1]
    groups = grad_ref.shape[0]
    rows = GROUP * width

    gate = gate_ref[...]
    own, other = own_ref[...].astype(F32), other_ref[...].astype(F32)
    scaled_ref[:local, :] = (own * gate).astype(BF16)
    scaled_ref[local:, :] = (other * gate).astype(BF16)
    gate_grad_ref[...] = jnp.sum(
        own * attention_ref[:local, :] + other * attention_ref[local:, :], axis=0, keepdims=True
    )
    half = gate_kept_ref.shape[1]
    mine = lax.axis_index("seq")
    gate_kept_ref[...] = gate_grad_ref[:, pl.ds(pl.multiple_of(mine * half, half), half)]
    gate_sent_ref[...] = gate_grad_ref[:, pl.ds(pl.multiple_of((1 - mine) * half, half), half)]

    def attended_grad(group):
        part = slice(group * rows, (group + 1) * rows)
        product = dot_nt(scaled_ref[...], out_weight_ref[part, :])
        attended_grad_ref[group] = product.astype(BF16)

    def attend_backward(group):
        heads = range(GROUP)
        query_gain, key_gain = query_gain_ref[...], key_gain_ref[...]
        scale_factor = 1.0 / math.sqrt(width)

        def part(head, index):
            left = (3 * head + index) * width
            return slice(left, left + width)

        def inverse(head, index):
            return inverse_ref[group, :, 2 * head + index : 2 * head + index + 1]

        grads = [attended_grad_ref[group, :, h * width : (h + 1) * width] for h in heads]
        values = [projected_ref[group, :, part(h, 2)].astype(BF16) for h in heads]
        prob_grads = [dot_nt(grads[h], values[h]) for h in heads]
        for h in heads:
            product = dot_tn(probs_ref[GROUP * group + h], grads[h])
            grad_ref[group, :, part(h, 2)] = product.astype(BF16)
        wide = [probs_ref[GROUP * group + h].astype(F32) for h in heads]
        deltas = [jnp.sum(wide[h] * prob_grads[h], axis=-1, keepdims=True) for h in heads]
        score_grads = [
            (wide[h] * (prob_grads[h] - deltas[h]) * scale_factor).astype(BF16) for h in heads
        ]
        units = [[projected_ref[group, :, part(h, index)] for index in range(2)] for h in heads]
        keys = [(units[h][1] * key_gain).astype(BF16) for h in heads]
        queries = [(units[h][0] * query_gain).astype(BF16) for h in heads]
        scaled = [
            [
                dot_nn(score_grads[h], keys[h]) * query_gain,
                dot_tn(score_grads[h], queries[h]) * key_gain,
            ]
            for h in heads
        ]
        means = [
            [jnp.mean(scaled[h][i] * units[h][i], axis=-1, keepdims=True) for i in range(2)]
            for h in heads
        ]
        for h in heads:
            for i in range(2):
                grad_ref[group, :, part(h, i)] = (
                    (scaled[h][i] - units[h][i] * means[h][i]) * inverse(h, i)
                ).astype(BF16)

    attended_grad(0)
    for group in range(groups):
        if group + 1 < groups:
            attended_grad(group + 1)
        attend_backward(group)
    input_grad(grad_ref, weight_ref, turned_ref, own_ref, kept_ref, sent_ref)


def backward(
    own,
    other,
    out_weight,
    weight,
    turned,
    projected,
    inverse,
    probs,
    attention,
    query_gain,
    key_gain,
    gate,
):
    local, model = own.shape
    groups, tokens, wide = projected.shape
    head_dim = query_gain.shape[1]
    out_weight = pltpu.with_memory_space_constraint(out_weight, pltpu.VMEM)
    weight = pltpu.with_memory_space_constraint(weight, pltpu.VMEM)
    turned = pltpu.with_memory_space_constraint(turned, pltpu.VMEM)
    vmem = pl.BlockSpec(memory_space=pltpu.VMEM)
    return pl.pallas_call(
        backward_kernel,
        out_shape=(
            jax.ShapeDtypeStruct((1, model // 2), F32),
            jax.ShapeDtypeStruct((1, model // 2), F32),
            jax.ShapeDtypeStruct((local, model), BF16),
            jax.ShapeDtypeStruct((local, model), BF16),
        ),
        in_specs=[vmem] * 12,
        out_specs=(vmem,) * 4,
        scratch_shapes=[
            pltpu.VMEM((groups, tokens, wide), BF16),
            pltpu.VMEM((tokens, model), BF16),
            pltpu.VMEM((groups, tokens, GROUP * head_dim), BF16),
            pltpu.VMEM((1, model), F32),
        ],
        compiler_params=params(6),
        cost_estimate=pl.CostEstimate(
            flops=2 * tokens * (out_weight.size + weight.size),
            bytes_accessed=2 * (out_weight.size + weight.size),
            transcendentals=0,
        ),
        name="attention_backward",
    )(
        own,
        other,
        out_weight,
        weight,
        turned,
        projected,
        inverse,
        probs,
        attention,
        query_gain,
        key_gain,
        gate,
    )


def sums_kernel(sent_ref, kept_ref, gate_kept_ref, gate_sent_ref, grad_ref, gate_ref):
    grad_ref[...] = (kept_ref[...].astype(F32) + sent_ref[...].astype(F32)).astype(BF16)
    gate_ref[...] = gate_kept_ref[...] + gate_sent_ref[...]


def sums(sent, kept, gate_kept, gate_sent):
    vmem = pl.BlockSpec(memory_space=pltpu.VMEM)
    return pl.pallas_call(
        sums_kernel,
        out_shape=(
            jax.ShapeDtypeStruct(kept.shape, BF16),
            jax.ShapeDtypeStruct(gate_kept.shape, F32),
        ),
        in_specs=[vmem] * 4,
        out_specs=(vmem, vmem),
        compiler_params=params(8),
        name="sums",
    )(sent, kept, gate_kept, gate_sent)


def routed(block, seq_step, pipe_step):
    seq_size, pipe_size = lax.axis_size("seq"), lax.axis_size("pipe")
    route = []
    for i in range(seq_size):
        for j in range(pipe_size):
            target = (i + seq_step) % seq_size * pipe_size + (j + pipe_step) % pipe_size
            route.append((i * pipe_size + j, target))
    return lax.ppermute(block, ("seq", "pipe"), route)


def pair_body(
    segment_input,
    output_grad,
    qkv_weight,
    out_weight,
    query_gain,
    key_gain,
    gate_scale,
    neighbours,
    tile_slot,
):
    stream = segment_input[0]
    upstream = output_grad[0]
    out_local = out_weight[0]
    other_stream = routed(stream, 1, 0)
    weight, turned_weight = regroup(qkv_weight[0], 128, 4, TURNED)
    other_upstream = routed(upstream, 1, 0)
    projected, inverse, probs, attention, kept, sent, out_local = forward(
        neighbours,
        tile_slot,
        stream,
        other_stream,
        weight,
        out_local,
        query_gain,
        key_gain,
        gate_scale,
    )
    sent = routed(sent, 1, 1)
    kept = routed(kept, 0, 1)
    gate_kept, gate_sent, grad_kept, grad_sent = backward(
        upstream,
        other_upstream,
        out_local,
        weight,
        turned_weight,
        projected,
        inverse,
        probs,
        attention,
        query_gain,
        key_gain,
        gate_scale,
    )
    grad_sent = routed(grad_sent, 1, -1)
    grad_kept = routed(grad_kept, 0, -1)
    segment_output = (sent.astype(F32) + kept.astype(F32)).astype(BF16)
    segment_output, gate_sent = lax.optimization_barrier((segment_output, gate_sent))
    gate_sent = routed(gate_sent, 1, 0)
    token_grad, gate_grad = sums(grad_sent, grad_kept, gate_kept, gate_sent)
    return (segment_output[None], token_grad[None], gate_grad)


def solution(mesh):
    in_specs = (
        P("pipe", ("dp", "seq"), None),
        P("pipe", ("dp", "seq"), None),
        P("pipe", None, "seq", None),
        P("pipe", "seq", None),
        P("pipe", None),
        P("pipe", None),
        P("pipe", None),
        P("dp", None),
        P("dp"),
    )
    out_specs = (
        P("pipe", ("dp", "seq"), None),
        P("pipe", ("dp", "seq"), None),
        P(("dp", "pipe"), "seq"),
    )

    def body(*args):
        one_tile_each = args[0].shape[1] == TILE and args[8].shape[0] == 2
        if mesh.shape["seq"] == 2 and one_tile_each and args[2].shape[2] % GROUP == 0:
            return pair_body(*args)
        return general_body(*args)

    return jax.shard_map(body, mesh=mesh, in_specs=in_specs, out_specs=out_specs, check_vma=False)
```
